32 devices in a mesh: dp: 4 (over y, x), wide: 8 (over z, core).
Axes of the slice: x: 2, y: 2, z: 4, core: 2. Of those that a mesh axis runs over, the one named last changes fastest.
Arguments:
- doc_tokens: bfloat16 [2, 32, 512, 768], P(None, ('dp', 'wide')), may hold values from -6 to 6
- query_tokens: bfloat16 [2, 64, 32, 768], P(None, ('dp', 'wide')), may hold values from -6 to 6
- query_lengths: int32 [2, 64], P(None, ('dp', 'wide')), may hold values from 8 to 32
- retrieved: int32 [2, 64, 32, 32], P(None, ('dp', 'wide')), may hold values from 0 to 4095
- targets: int32 [2, 64], P(None, ('dp', 'wide')), may hold values from 0 to 7
- q_weight: bfloat16 [768, 768], P(('dp', 'wide')), may hold values from -0.02734375 to 0.02734375
- k_weight: bfloat16 [768, 768], P(('dp', 'wide')), may hold values from -0.21875 to 0.21875
- v_weight: bfloat16 [768, 768], P(('dp', 'wide')), may hold values from -0.21875 to 0.21875
- o_weight: bfloat16 [768, 768], P(('dp', 'wide')), may hold values from -1.25 to 1.25
- gate_weight: bfloat16 [768, 2048], P(('dp', 'wide')), may hold values from -0.21875 to 0.21875
- up_weight: bfloat16 [768, 2048], P(('dp', 'wide')), may hold values from -0.21875 to 0.21875
- down_weight: bfloat16 [2048, 768], P(('dp', 'wide')), may hold values from -0.21875 to 0.21875
- proj_weight: bfloat16 [768, 128], P(('dp', 'wide')), may hold values from -0.21875 to 0.21875
- attn_gain: bfloat16 [768], P(('dp', 'wide')), may hold values from 0.5 to 1.5
- ffn_gain: bfloat16 [768], P(('dp', 'wide')), may hold values from 0.5 to 1.5
- final_gain: bfloat16 [768], P(('dp', 'wide')), may hold values from 0.5 to 1.5
- rel_bias: bfloat16 [32, 12], replicated, may hold values from -4 to 4
Outputs:
- losses: float32 [2, 64], P(None, ('dp', 'wide'))
- doc_grad: float32 [2, 32, 512, 768], P(None, ('dp', 'wide'))
- query_grad: float32 [2, 64, 32, 768], P(None, ('dp', 'wide'))
- q_grad: float32 [768, 768], P(('dp', 'wide'))
- k_grad: float32 [768, 768], P(('dp', 'wide'))
- v_grad: float32 [768, 768], P(('dp', 'wide'))
- o_grad: float32 [768, 768], P(('dp', 'wide'))
- gate_grad: float32 [768, 2048], P(('dp', 'wide'))
- up_grad: float32 [768, 2048], P(('dp', 'wide'))
- down_grad: float32 [2048, 768], P(('dp', 'wide'))
- proj_grad: float32 [768, 128], P(('dp', 'wide'))
- attn_gain_grad: float32 [768], P(('dp', 'wide'))
- ffn_gain_grad: float32 [768], P(('dp', 'wide'))
- final_gain_grad: float32 [768], P(('dp', 'wide'))
- bias_grad: float32 [32, 12], replicated
The draws below stay inside these ranges and needn't reach their ends.
Inputs may be any that keep to these rules, and one draw needn't show every extreme that they name: `retrieved`: each entry names a token of a document of the same micro-batch and group: document w, token t as w * 512 + t; entries may repeat. `targets`: the positive document's number within the group.
All inputs are finite; a program needn't handle non-finite values.
Results may differ from the reference program's by a relative error of at most 0.023.
Values may be sent and summed in bfloat16 or wider, within the bound.
A program may use at most 256 MiB of HBM per device.

```python
import jax
import jax.numpy as jnp
from jax import lax

D = 768
H = 12
DH = 64
FF = 2048
NB = 32
P_SIZE = 128
DOC_LEN = 512
QLEN = 32
K = 32
QPD = 2
MB = 2
DOCS = 32
QUERIES = 64
N_DP = 4
N_WIDE = 8


def set_ends(array, stream_key, smallest, largest):
    spot = [jax.random.randint(jax.random.fold_in(stream_key, axis), (), 0, length) for axis, length in enumerate(array.shape)]
    longest = array.shape.index(max(array.shape))
    beside = spot[:longest] + [(spot[longest] + 1) % array.shape[longest]] + spot[longest + 1:]
    return array.at[tuple(spot)].set(smallest).at[tuple(beside)].set(largest)


def steps_of(own_key, extent, shards, smallest, high):
    gain = 1.0
    for dim, blocks in shards:
        steps = jax.random.uniform(jax.random.fold_in(jax.random.fold_in(own_key, 6), dim), (blocks,), jnp.float32, smallest / len(shards), high / len(shards))
        gain = gain * jnp.repeat(jnp.exp(steps), extent[dim] // blocks).reshape((-1,) + (1,) * (len(extent) - 1 - dim))
    return gain


def scatter_about(own_key, dims, scale, bound, cuts=(), kind=jnp.bfloat16):
    values = scale * jax.random.normal(own_key, dims, jnp.float32)
    if cuts:
        values = values * steps_of(own_key, dims, cuts, -0.22, 0.18)
    return jnp.clip(values, -bound, bound).astype(kind)


def setup_inputs(seed: int = 0) -> dict:
    key_list = jax.random.split(jax.random.key(seed), 18)
    doc_tokens = scatter_about(key_list[0], (MB, DOCS, DOC_LEN, D), 1.0, 6.0, ((1, 32),))
    query_tokens = scatter_about(key_list[1], (MB, QUERIES, QLEN, D), 1.0, 6.0, ((1, 32),))
    query_lengths = set_ends(jax.random.randint(key_list[2], (MB, QUERIES), QLEN // 4, QLEN + 1), jax.random.fold_in(key_list[2], 1), QLEN // 4, QLEN).astype(jnp.int32)
    retrieved = set_ends(jax.random.randint(key_list[3], (MB, QUERIES, QLEN, K), 0, N_WIDE * DOC_LEN), jax.random.fold_in(key_list[3], 1), 0, (N_WIDE * DOC_LEN) - 1).astype(jnp.int32)
    targets = set_ends(jax.random.randint(key_list[4], (MB, QUERIES), 0, N_WIDE), jax.random.fold_in(key_list[4], 1), 0, N_WIDE - 1).astype(jnp.int32)
    q_weight = scatter_about(key_list[5], (D, D), (D * DH) ** -0.5, 0.02734375, ((0, 32),))
    k_weight = scatter_about(key_list[6], (D, D), D ** -0.5, 0.21875, ((0, 32),))
    v_weight = scatter_about(key_list[7], (D, D), D ** -0.5, 0.21875, ((0, 32),))
    o_weight = scatter_about(key_list[8], (D, D), (D // 32) ** -0.5, 1.25, ((0, 32),))
    gate_weight = scatter_about(key_list[9], (D, FF), D ** -0.5, 0.21875, ((0, 32),))
    up_weight = scatter_about(key_list[10], (D, FF), D ** -0.5, 0.21875, ((0, 32),))
    down_weight = scatter_about(key_list[11], (FF, D), (FF // 3) ** -0.5, 0.21875, ((0, 32),))
    proj_weight = scatter_about(key_list[12], (D, P_SIZE), D ** -0.5, 0.21875, ((0, 32),))
    attn_gain = jnp.clip(1.0 + 0.1 * jax.random.normal(key_list[13], (D,), jnp.float32), 0.5, 1.5).astype(jnp.bfloat16)
    ffn_gain = jnp.clip(1.0 + 0.1 * jax.random.normal(key_list[14], (D,), jnp.float32), 0.5, 1.5).astype(jnp.bfloat16)
    final_gain = jnp.clip(1.0 + 0.1 * jax.random.normal(key_list[15], (D,), jnp.float32), 0.5, 1.5).astype(jnp.bfloat16)
    rel_bias = scatter_about(key_list[16], (NB, H), 1.0, 4.0)
    return dict(doc_tokens=doc_tokens, query_tokens=query_tokens, query_lengths=query_lengths, retrieved=retrieved, targets=targets, q_weight=q_weight, k_weight=k_weight, v_weight=v_weight, o_weight=o_weight, gate_weight=gate_weight, up_weight=up_weight, down_weight=down_weight, proj_weight=proj_weight, attn_gain=attn_gain, ffn_gain=ffn_gain, final_gain=final_gain, rel_bias=rel_bias)


@jax.custom_vjp
def low(v):
    return lax.optimization_barrier(v.astype(jnp.bfloat16)).astype(jnp.float32)

@jax.custom_vjp
def low_back(v):
    return v

def low_keep(v):
    return (low(v), None)

def low_pass(kept, grad):
    return (grad,)

def back_keep(v):
    return (v, None)

def back_low(kept, grad):
    return (low(grad),)
low.defvjp(low_keep, low_pass)
low_back.defvjp(back_keep, back_low)
eps_norm = 1e-06
score_scale = 6.0
mask_fill = -1000000000.0
top_precision = lax.Precision.HIGHEST

def matmul(left_mat, right_mat):
    return jnp.dot(left_mat, right_mat, precision=top_precision)

def rms_scale(values, gain_vec):
    return values * lax.rsqrt(lax.optimization_barrier(jnp.mean(values * values, axis=-1, keepdims=True)) + eps_norm) * gain_vec

def bucket_onehot(length, bucket_count):
    places = jnp.arange(length, dtype=jnp.int32)
    offset_ij = places[None, :] - places[:, None]
    distance = jnp.abs(offset_ij)
    steps_far = jnp.zeros_like(distance)
    for power_step in range(1, 8):
        steps_far = steps_far + (distance * distance >= 64 * 2 ** power_step).astype(jnp.int32)
    bucket_ids = jnp.where(offset_ij > 0, 16, 0) + jnp.where(distance < 8, distance, 8 + steps_far)
    return (bucket_ids[:, :, None] == jnp.arange(bucket_count, dtype=jnp.int32)[None, None, :]).astype(jnp.float32)

def encode(tokens, valid_keys, params):
    w_query, w_key, w_value, w_out, w_gate, w_up, w_down, w_proj, gain_attn, gain_ffn, gain_final, bias_table = params
    batch_size, length, width_size = tokens.shape
    head_count = bias_table.shape[1]
    flat_rows = tokens.reshape(batch_size * length, width_size)
    normed = low(rms_scale(flat_rows, gain_attn))

    def split_heads(weight):
        return low_back(low(matmul(normed, weight))).reshape(batch_size, length, head_count, -1)
    queries_h = split_heads(w_query)
    keys_h = split_heads(w_key)
    values_h = split_heads(w_value)
    bias_full = jnp.einsum('ijb,bh->hij', bucket_onehot(length, bias_table.shape[0]), bias_table, precision=top_precision)
    scores = low_back(jnp.einsum('bqhd,bkhd->bhqk', queries_h, keys_h, precision=top_precision)) + bias_full[None]
    scores = jnp.where(valid_keys[:, None, None, :], scores, mask_fill)
    shifted = jnp.exp(scores - lax.optimization_barrier(jnp.max(scores, axis=-1, keepdims=True)))
    probs_attn = shifted / lax.optimization_barrier(jnp.sum(shifted, axis=-1, keepdims=True))
    context = jnp.einsum('bhqk,bkhd->bqhd', low(probs_attn), values_h, precision=top_precision)
    context = low_back(low(context)).reshape(batch_size * length, width_size)
    hidden = flat_rows + low_back(matmul(context, w_out))
    normed_two = low(rms_scale(hidden, gain_ffn))
    gate_pre = low_back(matmul(normed_two, w_gate))
    up_pre = low_back(matmul(normed_two, w_up))
    activated = low(jax.nn.gelu(gate_pre) * up_pre)
    layer_out = hidden + low_back(matmul(activated, w_down))
    normed_end = low(rms_scale(layer_out, gain_final))
    embedded = low_back(low(matmul(normed_end, w_proj)))
    return embedded.reshape(batch_size, length, -1)

def group_loss(doc_embs, query_embs, picks_all, lengths, goal_ids):

    def one_doc(bundle):
        doc_emb, doc_index = bundle
        scores_raw = low_back(matmul(query_embs, doc_emb.T)) * P_SIZE ** (-0.5)
        positions = doc_index * DOC_LEN + jnp.arange(DOC_LEN, dtype=jnp.int32)
        multiple = lax.optimization_barrier(jnp.sum((picks_all[:, :, None] == positions[None, None, :]).astype(jnp.float32), axis=1))
        present = lax.optimization_barrier(jnp.sum(multiple, axis=-1))
        return jnp.log(lax.optimization_barrier(jnp.sum(multiple * jnp.exp(scores_raw), axis=-1)) + (present == 0).astype(jnp.float32))
    doc_ids = jnp.arange(N_WIDE, dtype=jnp.int32)
    pooled = lax.map(jax.checkpoint(one_doc), (doc_embs, doc_ids))
    owner_doc = picks_all // DOC_LEN
    hit_mask = jnp.any(owner_doc[None, :, :] == doc_ids[:, None, None], axis=-1).astype(jnp.float32)
    query_count = lengths.shape[0]
    valid_mask = (jnp.arange(QLEN, dtype=jnp.int32)[None, :] < lengths[:, None]).astype(jnp.float32).reshape(-1)
    counts = lax.optimization_barrier(jnp.sum((hit_mask * valid_mask).reshape(N_WIDE, query_count, QLEN), axis=-1))
    summed = lax.optimization_barrier(jnp.sum((pooled * valid_mask).reshape(N_WIDE, query_count, QLEN), axis=-1))
    logits = score_scale * summed / jnp.maximum(counts, 1.0)
    col_top = lax.optimization_barrier(jnp.max(logits, axis=0))
    log_total = col_top + jnp.log(lax.optimization_barrier(jnp.sum(jnp.exp(logits - col_top[None, :]), axis=0)))
    chosen = (doc_ids[:, None] == goal_ids[None, :]).astype(jnp.float32)
    return log_total - lax.optimization_barrier(jnp.sum(chosen * logits, axis=0))

def forward(params, doc_values, query_values, query_lengths, retrieved, targets):
    doc_valid = jnp.ones((1, DOC_LEN), dtype=bool)
    doc_in = doc_values.reshape(MB * DOCS, 1, DOC_LEN, D)
    doc_emb = lax.map(jax.checkpoint(lambda item_doc: encode(item_doc, doc_valid, params)), doc_in)
    group_count = MB * N_DP
    group_queries = QPD * N_WIDE
    doc_emb = doc_emb.reshape(group_count, N_WIDE, DOC_LEN, P_SIZE)
    lengths_group = query_lengths.reshape(group_count, group_queries)
    query_in = query_values.reshape(group_count, group_queries, QLEN, D)
    slot_ids = jnp.arange(QLEN, dtype=jnp.int32)

    def encode_queries(bundle):
        tokens_g, lengths_g = bundle
        return encode(tokens_g, slot_ids[None, :] < lengths_g[:, None], params)
    query_emb = lax.map(jax.checkpoint(encode_queries), (query_in, lengths_group))
    query_emb = query_emb.reshape(group_count, group_queries * QLEN, P_SIZE)
    picks_group = retrieved.reshape(group_count, group_queries * QLEN, K)
    goals_group = targets.reshape(group_count, group_queries)

    def one_group(bundle):
        return group_loss(bundle[0], bundle[1], bundle[2], bundle[3], bundle[4])
    losses = lax.map(jax.checkpoint(one_group), (doc_emb, query_emb, picks_group, lengths_group, goals_group))
    return losses.reshape(MB, QUERIES)

def reference(doc_tokens, query_tokens, query_lengths, retrieved, targets, q_weight, k_weight, v_weight, o_weight, gate_weight, up_weight, down_weight, proj_weight, attn_gain, ffn_gain, final_gain, rel_bias):
    params = tuple((weight.astype(jnp.float32) for weight in (q_weight, k_weight, v_weight, o_weight, gate_weight, up_weight, down_weight, proj_weight, attn_gain, ffn_gain, final_gain, rel_bias)))
    doc_values = doc_tokens.astype(jnp.float32)
    query_values = query_tokens.astype(jnp.float32)

    def objective(params_in, docs_in, queries_in):
        return forward(params_in, docs_in, queries_in, query_lengths, retrieved, targets)
    losses, pull_back = jax.vjp(objective, params, doc_values, query_values)
    grad_list, doc_grad, query_grad = pull_back(jnp.ones_like(losses))
    return (losses, doc_grad, query_grad, grad_list[0], grad_list[1], grad_list[2], grad_list[3], grad_list[4], grad_list[5], grad_list[6], grad_list[7], grad_list[8], grad_list[9], grad_list[10], grad_list[11])
```

```python
import functools

import jax
import jax.numpy as jnp
from jax import lax
from jax.experimental import pallas as pl
from jax.experimental.pallas import tpu as pltpu
from jax.sharding import PartitionSpec as P

eps_norm = 1e-06
score_scale = 6.0
mask_fill = -1000000000.0
top_precision = lax.Precision.HIGHEST
block_rows = 512


MESH = pl.DeviceIdType.MESH

def gray(p):
    return p + (p // 2) * (1 - 2 * (p % 2))

class Place:
    def __init__(self, zc):
        self.zc = zc
        d = lax.axis_index("dp"); w = lax.axis_index("wide")
        self.d, self.w = d, w
        self.z, self.c = w // 2, w % 2
        p = gray(d)
        self.right = gray((p + 1) % 4); self.left = gray((p + 3) % 4); self.opp = gray((p + 2) % 4)
    def dev(self, d=None, z=None, c=None):
        d = self.d if d is None else d
        z = self.z if z is None else z
        c = self.c if c is None else c
        return (d, z * 2 + c)

def enter(pos):
    barrier = pltpu.get_barrier_semaphore()
    for dev in (pos.dev(d=pos.right), pos.dev(d=pos.left), pos.dev(c=1 - pos.c)):
        pl.semaphore_signal(barrier, inc=1, device_id=dev, device_id_type=MESH)
    @pl.when(pos.z > 0)
    def _():
        pl.semaphore_signal(barrier, inc=1, device_id=pos.dev(z=pos.z - 1), device_id_type=MESH)
    @pl.when(pos.z < pos.zc - 1)
    def _():
        pl.semaphore_signal(barrier, inc=1, device_id=pos.dev(z=pos.z + 1), device_id_type=MESH)
    zc = pos.zc
    peers = 3 + (pos.z + zc - 1) // zc + (2 * zc - 2 - pos.z) // zc
    pl.semaphore_wait(barrier, peers)

def gather_kernel(zc, count, *refs):
    pos = Place(zc)
    shard = refs[:count]
    out = refs[count:2 * count]
    rest = refs[2 * count:]
    comp = rest[:count]; mine = rest[count:2 * count]
    (s_col, s_ring, s_fwd, s_mate, s_pair, s_own, r_col, r_left, r_right, r_opp, r_mate, r_pair) = rest[2 * count:]
    z, c, d = pos.z, pos.c, pos.d
    enter(pos)
    rows = [o.shape[0] // (4 * zc) for o in out]
    half = [o.shape[1] // 2 for o in out]

    def part(a, ref, blk, core):
        return ref.at[pl.ds(pl.multiple_of(blk * rows[a], 16), rows[a]), pl.ds(pl.multiple_of(core * half[a], 128), half[a])]
    def own(a, core):
        return comp[a].at[:, pl.ds(pl.multiple_of(core * half[a], 128), half[a])]
    def rdma(a, src, blk, dev, ss, rs):
        return pltpu.make_async_remote_copy(src_ref=src, dst_ref=part(a, out[a], blk, c), send_sem=ss, recv_sem=rs, device_id=dev, device_id_type=MESH)
    def blk(dd, zz):
        return dd * zc + zz
    mate_dev = pos.dev(c=1 - c)
    def pair(a):
        return pltpu.make_async_remote_copy(src_ref=shard[a], dst_ref=mine[a], send_sem=s_pair.at[a], recv_sem=r_pair.at[a], device_id=mate_dev, device_id_type=MESH)
    def keep(a):
        return pltpu.make_async_copy(comp[a], out[a].at[pl.ds(pl.multiple_of(blk(d, z) * rows[a], 16), rows[a]), :], s_own.at[a])
    def up(a, src, zz):
        return rdma(a, src, blk(d, zz), pos.dev(z=lax.rem(z + 1, zc)), s_col.at[a, 0, zz], r_col.at[a, zz])
    def down(a, src, zz):
        return rdma(a, src, blk(d, zz), pos.dev(z=lax.rem(z + zc - 1, zc)), s_col.at[a, 1, zz], r_col.at[a, zz])
    def right(a, src, zz):
        return rdma(a, src, blk(d, zz), pos.dev(d=pos.right), s_ring.at[a, 0, zz], r_left.at[a, zz])
    def left(a, src, zz):
        return rdma(a, src, blk(d, zz), pos.dev(d=pos.left), s_ring.at[a, 1, zz], r_right.at[a, zz])
    def fwd_right(a, zz):
        b = blk(pos.left, zz)
        return rdma(a, part(a, out[a], b, c), b, pos.dev(d=pos.right), s_fwd.at[a, zz], r_opp.at[a, zz])
    def fwd_left(a, zz):
        b = blk(pos.right, zz)
        return rdma(a, part(a, out[a], b, c), b, pos.dev(d=pos.left), s_fwd.at[a, zz], r_opp.at[a, zz])
    def mate(a, b):
        return rdma(a, part(a, out[a], b, c), b, mate_dev, s_mate.at[a, b], r_mate.at[a, b])
    def got(a, b, sem):
        return rdma(a, part(a, out[a], b, c), b, mate_dev, s_mate.at[a, b], sem).wait_recv()
    def mate_got(a, b):
        piece = part(a, out[a], b, 1 - c)
        pltpu.make_async_remote_copy(src_ref=piece, dst_ref=piece, send_sem=s_mate.at[a, b], recv_sem=r_mate.at[a, b], device_id=mate_dev, device_id_type=MESH).wait_recv()

    for a in range(count):
        pair(a).start()
    for a in range(count):
        pair(a).wait_recv()
        r2 = rows[a] // 2
        step = 256 if half[a] * 2 % 256 == 0 else 128
        @pl.loop(0, half[a] * 2 // step)
        def _(t):
            cols = pl.ds(pl.multiple_of(t * step, 128), step)
            mn = shard[a][:, cols].astype(jnp.float32)[:r2]
            ot = mine[a][:, cols].astype(jnp.float32)[:r2]
            first = jnp.where(c == 0, mn, ot)
            second = jnp.where(c == 0, ot, mn)
            comp[a][:, cols] = jnp.concatenate([first, second], axis=0).astype(jnp.bfloat16)
        right(a, own(a, c), z).start()
        left(a, own(a, c), z).start()
        pl.when(z < zc - 1)(lambda: up(a, own(a, c), z).start())
        pl.when(z > 0)(lambda: down(a, own(a, c), z).start())
        keep(a).start()

    def column(a, j):
        @pl.when(z - j >= 0)
        def _():
            zz = z - j
            got(a, blk(d, zz), r_col.at[a, zz])
            src = part(a, out[a], blk(d, zz), c)
            pl.when(z < zc - 1)(lambda: up(a, src, zz).start())
            right(a, src, zz).start(); left(a, src, zz).start()
            mate(a, blk(d, zz)).start()
        @pl.when(z + j < zc)
        def _():
            zz = z + j
            got(a, blk(d, zz), r_col.at[a, zz])
            src = part(a, out[a], blk(d, zz), c)
            pl.when(z > 0)(lambda: down(a, src, zz).start())
            right(a, src, zz).start(); left(a, src, zz).start()
            mate(a, blk(d, zz)).start()
    def ring_one(a, zz):
        got(a, blk(pos.left, zz), r_left.at[a, zz])
        pl.when(zz % 2 == 0)(lambda: fwd_right(a, zz).start())
        mate(a, blk(pos.left, zz)).start()
        got(a, blk(pos.right, zz), r_right.at[a, zz])
        pl.when(zz % 2 == 1)(lambda: fwd_left(a, zz).start())
        mate(a, blk(pos.right, zz)).start()
    def opp_one(a, zz):
        got(a, blk(pos.opp, zz), r_opp.at[a, zz])
        mate(a, blk(pos.opp, zz)).start()
    def spread(fn, a, j):
        if j == 0:
            fn(a, z); return
        pl.when(z - j >= 0)(lambda: fn(a, z - j))
        pl.when(z + j < zc)(lambda: fn(a, z + j))
    for a in range(count):
        for t in range(zc + 2):
            if 1 <= t < zc:
                column(a, t)
            if 1 <= t <= zc:
                spread(ring_one, a, t - 1)
            if 2 <= t:
                spread(opp_one, a, t - 2)
    for a in range(count):
        pair(a).wait_send(); keep(a).wait()
        @pl.loop(0, zc)
        def _(zz):
            src = part(a, out[a], blk(d, zz), c)
            right(a, src, zz).wait_send(); left(a, src, zz).wait_send()
            pl.when((z < zc - 1) & (zz <= z))(lambda: up(a, src, zz).wait_send())
            pl.when((z > 0) & (zz >= z))(lambda: down(a, src, zz).wait_send())
            fwd_right(a, zz).wait_send()
        @pl.loop(0, 4 * zc)
        def _(b):
            @pl.when(b != blk(d, z))
            def _():
                mate(a, b).wait_send()
                mate_got(a, b)

def gather(shards, zc, n_dev):
    count = len(shards)
    outs, comps, mines = [], [], []
    for s, rows in shards:
        outs.append(jax.ShapeDtypeStruct((rows * n_dev, s.shape[1]), s.dtype))
        comps.append(pltpu.VMEM((rows * 2, s.shape[1]), s.dtype))
        mines.append(pltpu.VMEM(s.shape, s.dtype))
    dma = pltpu.SemaphoreType.DMA
    sems = [dma((count, 2, zc)), dma((count, 2, zc)), dma((count, zc)), dma((count, 4 * zc)), dma((count,)), dma((count,)),
            dma((count, zc)), dma((count, zc)), dma((count, zc)), dma((count, zc)), dma((count, 4 * zc)), dma((count,))]
    return pl.pallas_call(
        functools.partial(gather_kernel, zc, count),
        out_shape=outs,
        in_specs=[pl.BlockSpec(memory_space=pltpu.VMEM)] * count,
        out_specs=[pl.BlockSpec(memory_space=pl.ANY)] * count,
        scratch_shapes=comps + mines + sems,
        compiler_params=pltpu.CompilerParams(collective_id=0, has_side_effects=True, vmem_limit_bytes=32 << 20),
        name="gather_weights",
    )(*[s for s, _ in shards])


F32 = jnp.float32; BF = jnp.bfloat16

def reduce_kernel(zc, count, *refs):
    pos = Place(zc)
    z, c, d = pos.z, pos.c, pos.d
    g = refs[:count]; table = refs[count]
    out = refs[count + 1:2 * count + 1]; table_out = refs[2 * count + 1]
    rest = refs[2 * count + 2:]
    loc = rest[:count]; rxp = rest[count:2 * count]; rxf = rest[2 * count:3 * count]
    rxl = rest[3 * count:4 * count]; rxr = rest[4 * count:5 * count]
    rxu = rest[5 * count:6 * count]; rxd = rest[6 * count:7 * count]
    fin = rest[7 * count:8 * count]; rxm = rest[8 * count:9 * count]
    (tabs, s_tab, r_tab, s_pair, r_pair, s_loc, s_ring, r_fwd, r_left, r_right, s_z, r_up, r_dn, s_fin, r_fin) = rest[9 * count:]
    rows = [x.shape[0] // (4 * zc) for x in g]
    half = [x.shape[1] // 2 for x in g]
    n_dev = 8 * zc
    me = d * (2 * zc) + pos.w
    barrier = pltpu.get_barrier_semaphore()
    @pl.loop(1, n_dev)
    def _(k):
        o = lax.rem(me + k, n_dev)
        pl.semaphore_signal(barrier, inc=1, device_id=(o // (2 * zc), lax.rem(o, 2 * zc)), device_id_type=MESH)
    pl.semaphore_wait(barrier, n_dev - 1)
    mate_dev = pos.dev(c=1 - c)
    right_dev = pos.dev(d=pos.right); left_dev = pos.dev(d=pos.left)
    def remote(src, dst, ss, rs, dev):
        return pltpu.make_async_remote_copy(src_ref=src, dst_ref=dst, send_sem=ss, recv_sem=rs, device_id=dev, device_id_type=MESH)
    def tab_copy(k):
        o = lax.rem(me + k, n_dev)
        return remote(table, tabs.at[me], s_tab.at[k], r_tab.at[me], (o // (2 * zc), lax.rem(o, 2 * zc)))
    def tab_got(k):
        o = lax.rem(me + k, n_dev)
        return remote(table, tabs.at[o], s_tab.at[k], r_tab.at[o], (o // (2 * zc), lax.rem(o, 2 * zc)))
    def strip(a, dd):
        return pl.ds(pl.multiple_of(dd * zc * rows[a], 16), zc * rows[a])
    def cols(a, core):
        return pl.ds(pl.multiple_of(core * half[a], 128), half[a])
    def pair(a, dd):
        return remote(g[a].at[strip(a, dd), cols(a, 1 - c)], rxp[a].at[strip(a, dd), :], s_pair.at[a, dd], r_pair.at[a, dd], mate_dev)
    def local(a, dd):
        return pltpu.make_async_copy(g[a].at[strip(a, dd), cols(a, c)], loc[a].at[strip(a, dd), :], s_loc.at[a, dd])
    def row(a, dd, zz):
        return pl.ds(pl.multiple_of((dd * zc + zz) * rows[a], 16), rows[a])
    def slot(a, zz):
        return pl.ds(pl.multiple_of(zz * rows[a], 16), rows[a])
    def add(a, dst, terms, out_ref=None):
        step = 128 if half[a] % 256 else 256
        @pl.loop(0, half[a] // step)
        def _(t):
            cc = pl.ds(pl.multiple_of(t * step, 128), step)
            total = None
            for ref, rr in terms:
                v = ref[rr, cc].astype(F32)
                total = v if total is None else total + v
            dst[0][dst[1], cc] = total.astype(dst[0].dtype)
    def pair_sum(a, dd, zz, extra=()):
        r = row(a, dd, zz)
        add(a, (loc[a], r), [(loc[a], r), (rxp[a], r)] + list(extra))
    def first_right(a, zz):
        return remote(loc[a].at[row(a, pos.opp, zz), :], rxf[a].at[slot(a, zz), :], s_ring.at[a, 0, zz], r_fwd.at[a, zz], right_dev)
    def first_left(a, zz):
        return remote(loc[a].at[row(a, pos.opp, zz), :], rxf[a].at[slot(a, zz), :], s_ring.at[a, 0, zz], r_fwd.at[a, zz], left_dev)
    def to_right(a, zz):
        return remote(loc[a].at[row(a, pos.right, zz), :], rxl[a].at[slot(a, zz), :], s_ring.at[a, 1, zz], r_left.at[a, zz], right_dev)
    def to_left(a, zz):
        return remote(loc[a].at[row(a, pos.left, zz), :], rxr[a].at[slot(a, zz), :], s_ring.at[a, 2, zz], r_right.at[a, zz], left_dev)
    def up(a, zt):
        return remote(loc[a].at[row(a, d, zt), :], rxu[a].at[slot(a, zt), :], s_z.at[a, zt], r_up.at[a, zt], pos.dev(z=lax.rem(z + 1, zc)))
    def down(a, zt):
        return remote(loc[a].at[row(a, d, zt), :], rxd[a].at[slot(a, zt), :], s_z.at[a, zt], r_dn.at[a, zt], pos.dev(z=lax.rem(z + zc - 1, zc)))
    def mate_rows(a):
        r2 = rows[a] // 2
        return pl.ds(pl.multiple_of((1 - c) * r2, 8), r2)
    def my_rows(a):
        r2 = rows[a] // 2
        return pl.ds(pl.multiple_of(c * r2, 8), r2)
    def final(a):
        return remote(fin[a].at[mate_rows(a), :], rxm[a], s_fin.at[a], r_fin.at[a], mate_dev)

    for a in range(count):
        for dd in (pos.opp, pos.right, pos.left, d):
            pair(a, dd).start(); local(a, dd).start()
    @pl.loop(1, n_dev)
    def _(k):
        tab_copy(k).start()

    def phase_p(a):
        dd = pos.opp
        pair(a, dd).wait_recv(); local(a, dd).wait()
        for zz in range(zc):
            pair_sum(a, dd, zz)
            (first_right if zz % 2 == 0 else first_left)(a, zz).start()
        dd = pos.right
        pair(a, dd).wait_recv(); local(a, dd).wait()
        dd = pos.left
        pair(a, dd).wait_recv(); local(a, dd).wait()
        for zz in range(zc):
            if zz % 2:
                pair_sum(a, pos.right, zz); to_right(a, zz).start()
            else:
                pair_sum(a, pos.left, zz); to_left(a, zz).start()
    def phase_q(a):
        for zz in range(zc):
            if zz % 2 == 0:
                first_right(a, zz).wait_recv()
                pair_sum(a, pos.right, zz, [(rxf[a], slot(a, zz))]); to_right(a, zz).start()
            else:
                first_left(a, zz).wait_recv()
                pair_sum(a, pos.left, zz, [(rxf[a], slot(a, zz))]); to_left(a, zz).start()
        pair(a, d).wait_recv(); local(a, d).wait()
    def phase_r(a):
        def column(zz, dst, extra=()):
            r = row(a, d, zz)
            add(a, dst, [(loc[a], r), (rxp[a], r), (rxl[a], slot(a, zz)), (rxr[a], slot(a, zz))] + list(extra))
        def arrived(zz):
            to_right(a, zz).wait_recv(); to_left(a, zz).wait_recv()
        for zt in range(zc):
            arrived(zt)
        for i in range(zc - 1):
            zt = zc - 1 - i
            @pl.when(z < zt)
            def _():
                r = row(a, d, zt)
                @pl.when(z > 0)
                def _():
                    up(a, zt).wait_recv()
                    column(zt, (loc[a], r), [(rxu[a], slot(a, zt))])
                @pl.when(z == 0)
                def _():
                    column(zt, (loc[a], r))
                up(a, zt).start()
            zs = i
            @pl.when(z > zs)
            def _():
                r = row(a, d, zs)
                @pl.when(z < zc - 1)
                def _():
                    down(a, zs).wait_recv()
                    column(zs, (loc[a], r), [(rxd[a], slot(a, zs))])
                @pl.when(z == zc - 1)
                def _():
                    column(zs, (loc[a], r))
                down(a, zs).start()
        full = (fin[a], slice(None))
        zz = z
        @pl.when(z > 0)
        def _():
            up(a, zz).wait_recv()
        @pl.when(z < zc - 1)
        def _():
            down(a, zz).wait_recv()
        @pl.when(z == 0)
        def _():
            column(zz, full, [(rxd[a], slot(a, zz))])
        @pl.when(z == zc - 1)
        def _():
            column(zz, full, [(rxu[a], slot(a, zz))])
        @pl.when((z > 0) & (z < zc - 1))
        def _():
            column(zz, full, [(rxu[a], slot(a, zz)), (rxd[a], slot(a, zz))])
        final(a).start()
    def phase_s(a):
        out[a][:, cols(a, c)] = fin[a][my_rows(a), :]
        final(a).wait_recv()
        out[a][:, cols(a, 1 - c)] = rxm[a][...]
    for t in range(count + 2):
        if t < count: phase_p(t)
        if 1 <= t <= count: phase_q(t - 1)
        if 2 <= t: phase_r(t - 2)
    for a in range(count):
        phase_s(a)
    tabs[me] = table[...]
    @pl.loop(1, n_dev)
    def _(k):
        tab_got(k).wait_recv()
        tab_copy(k).wait_send()
    total = tabs[0]
    for k in range(1, n_dev):
        total = total + tabs[k]
    table_out[...] = total
    for a in range(count):
        for dd in range(4):
            pair(a, dd).wait_send()
        for zz in range(zc):
            (first_right if zz % 2 == 0 else first_left)(a, zz).wait_send()
            to_right(a, zz).wait_send(); to_left(a, zz).wait_send()
            @pl.when(zz != z)
            def _():
                up(a, zz).wait_send()
        final(a).wait_send()

def reduce_scatter(grads, table, zc):
    count = len(grads)
    n_dev = 8 * zc
    V = pltpu.VMEM
    outs = [jax.ShapeDtypeStruct((x.shape[0] // n_dev, x.shape[1]), F32) for x in grads] + [jax.ShapeDtypeStruct(table.shape, F32)]
    rows = [x.shape[0] // (4 * zc) for x in grads]; half = [x.shape[1] // 2 for x in grads]
    scratch = []
    scratch += [V((x.shape[0], h), BF) for x, h in zip(grads, half)]
    scratch += [V((x.shape[0], h), BF) for x, h in zip(grads, half)]
    for _ in range(5):
        scratch += [V((zc * r, h), BF) for r, h in zip(rows, half)]
    scratch += [V((r, h), F32) for r, h in zip(rows, half)]
    scratch += [V((r // 2, h), F32) for r, h in zip(rows, half)]
    dma = pltpu.SemaphoreType.DMA
    scratch += [V((n_dev,) + table.shape, F32), dma((n_dev,)), dma((n_dev,)), dma((count, 4)), dma((count, 4)), dma((count, 4)), dma((count, 3, zc)),
                dma((count, zc)), dma((count, zc)), dma((count, zc)), dma((count, zc)), dma((count, zc)), dma((count, zc)), dma((count,)), dma((count,))]
    return pl.pallas_call(
        functools.partial(reduce_kernel, zc, count),
        out_shape=outs,
        in_specs=[pl.BlockSpec(memory_space=pl.ANY)] * count + [pl.BlockSpec(memory_space=pltpu.VMEM)],
        out_specs=[pl.BlockSpec(memory_space=pltpu.VMEM)] * (count + 1),
        scratch_shapes=scratch,
        compiler_params=pltpu.CompilerParams(collective_id=1, has_side_effects=True, vmem_limit_bytes=48 << 20),
        name="reduce_grads",
    )(*grads, table)


def two_level(q_weight, down_weight):
    zc = lax.axis_size("wide") // 2
    return (
        lax.axis_size("dp") == 4
        and lax.axis_size("wide") % 4 == 0
        and q_weight.shape[0] % 8 == 0
        and down_weight.shape[0] % 8 == 0
    )


def gathered(*weights):
    q_w, k_w, v_w, o_w, gate_w, up_w, down_w, proj_w, g_a, g_f, g_e = weights
    if not two_level(q_w, down_w):
        return tuple(lax.all_gather(w, ("dp", "wide"), axis=0, tiled=True) for w in weights)
    zc = lax.axis_size("wide") // 2
    rows, width = q_w.shape
    ff = gate_w.shape[1]
    gains = jnp.pad(jnp.stack([g_a, g_f, g_e], axis=1), ((0, 0), (0, proj_w.shape[1] - 3)))
    one = jnp.concatenate([q_w, k_w, v_w, o_w, proj_w, gains], axis=1)
    two = jnp.concatenate([gate_w, up_w], axis=1)
    spare = -rows % 16
    one = jnp.pad(one, ((0, spare), (0, 0)))
    two = jnp.pad(two, ((0, spare), (0, 0)))
    one, two, down = gather([(one, rows), (two, rows), (down_w, down_w.shape[0])], zc, 8 * zc)
    cuts = [one[:, i * width : (i + 1) * width] for i in range(4)]
    last = one[:, 4 * width :]
    p = proj_w.shape[1]
    return (*cuts, two[:, :ff], two[:, ff:], down, last[:, :p], last[:, p], last[:, p + 1], last[:, p + 2])


def scattered(grads, table):
    q_g, k_g, v_g, o_g, gate_g, up_g, down_g, proj_g, a_g, f_g, e_g = grads
    n_dev = lax.axis_size("dp") * lax.axis_size("wide")
    rows = q_g.shape[0] // n_dev
    if not two_level(q_g[:rows], down_g[: down_g.shape[0] // n_dev]):
        shards = [lax.psum_scatter(g, ("dp", "wide"), scatter_dimension=0, tiled=True) for g in grads]
        return (*shards, lax.psum(table, ("dp", "wide")))
    zc = lax.axis_size("wide") // 2
    width = q_g.shape[1]
    p = proj_g.shape[1]
    low = jnp.bfloat16
    gains = jnp.pad(jnp.stack([a_g, f_g, e_g], axis=1), ((0, 0), (0, p - 3)))
    one = jnp.concatenate([g.astype(low) for g in (q_g, k_g, v_g, o_g, proj_g, gains)], axis=1)
    two = jnp.concatenate([gate_g.astype(low), up_g.astype(low)], axis=1)
    flat = table.reshape(-1)
    spare = -flat.shape[0] % 1024
    packed = jnp.pad(flat, (0, spare)).reshape(-1, 128)
    one, two, down, packed = reduce_scatter([one, two, down_g.astype(low)], packed, zc)
    ff = gate_g.shape[1]
    cuts = [one[:, i * width : (i + 1) * width] for i in range(4)]
    last = one[:, 4 * width :]
    return (
        *cuts,
        two[:, :ff],
        two[:, ff:],
        down,
        last[:, :p],
        last[:, p],
        last[:, p + 1],
        last[:, p + 2],
        packed.reshape(-1)[: flat.shape[0]].reshape(table.shape),
    )


def cut_along(x, dim, length):
    shape = x.shape
    tiles = x.reshape(*shape[:dim], length, shape[dim] // length, *shape[dim + 1 :])
    return jnp.moveaxis(tiles, dim, 0)


def sent_and_summed(x, axis, dim):
    length = lax.axis_size(axis)
    tiles = lax.all_to_all(cut_along(x, dim, length), axis, 0, 0, tiled=True)
    return jnp.sum(tiles.astype(jnp.float32), axis=0)


def contract_rows(left_mat, right_mat):
    return lax.dot_general(
        left_mat, right_mat, (((0,), (0,)), ((), ())), preferred_element_type=jnp.float32
    )


def contract_cols(left_mat, right_mat):
    return lax.dot_general(
        left_mat, right_mat, (((1,), (1,)), ((), ())), preferred_element_type=jnp.float32
    )


def matmul(left_mat, right_mat):
    return jnp.dot(left_mat, right_mat, preferred_element_type=jnp.float32)


def rms_forward(values, gain_vec):
    inverse = lax.rsqrt(jnp.mean(values * values, axis=-1, keepdims=True) + eps_norm)
    return (values * inverse * gain_vec, inverse)


def rms_backward(values, inverse, gain_vec, upstream):
    scaled = upstream * gain_vec
    gain_grad = jnp.sum(upstream * values * inverse, axis=0)
    inner_mean = jnp.mean(scaled * values, axis=-1, keepdims=True)
    return (inverse * scaled - values * inverse * inverse * inverse * inner_mean, gain_grad)


def bucket_onehot(length, bucket_count):
    places = jnp.arange(length, dtype=jnp.int32)
    offset_ij = places[None, :] - places[:, None]
    distance = jnp.abs(offset_ij)
    steps_far = jnp.zeros_like(distance)
    for power_step in range(1, 8):
        steps_far = steps_far + (distance * distance >= 64 * 2**power_step).astype(jnp.int32)
    bucket_ids = jnp.where(offset_ij > 0, 16, 0) + jnp.where(distance < 8, distance, 8 + steps_far)
    return (
        bucket_ids[:, :, None] == jnp.arange(bucket_count, dtype=jnp.int32)[None, None, :]
    ).astype(jnp.float32)


def attention_scores(queries_h, keys_h, bias_full, valid_keys):
    scores = (
        jnp.einsum("bqhd,bkhd->bhqk", queries_h, keys_h, preferred_element_type=jnp.float32)
        + bias_full[None]
    )
    return jnp.where(valid_keys[:, None, None, :], scores, mask_fill)


def encode_forward(tokens, valid_keys, bias_full, full_weights):
    (
        w_query,
        w_key,
        w_value,
        w_out,
        w_gate,
        w_up,
        w_down,
        w_proj,
        gain_attn,
        gain_ffn,
        gain_final,
    ) = full_weights
    batch_size, length, width_size = tokens.shape
    head_count = bias_full.shape[0]
    flat_rows = tokens.astype(jnp.float32).reshape(batch_size * length, width_size)
    normed_full, inverse_one = rms_forward(flat_rows, gain_attn.astype(jnp.float32))
    normed = normed_full.astype(jnp.bfloat16)

    def split_heads(weight):
        return (
            matmul(normed, weight).astype(jnp.bfloat16).reshape(batch_size, length, head_count, -1)
        )

    queries_h = split_heads(w_query)
    keys_h = split_heads(w_key)
    values_h = split_heads(w_value)
    scores = attention_scores(queries_h, keys_h, bias_full, valid_keys)
    row_top = jnp.max(scores, axis=-1, keepdims=True)
    shifted = jnp.exp(scores - row_top)
    row_totals = jnp.sum(shifted, axis=-1, keepdims=True)
    probs_attn = shifted / row_totals
    log_total = row_top + jnp.log(row_totals)
    context = jnp.einsum(
        "bhqk,bkhd->bqhd",
        probs_attn.astype(jnp.bfloat16),
        values_h,
        preferred_element_type=jnp.float32,
    )
    context = context.astype(jnp.bfloat16).reshape(batch_size * length, width_size)
    hidden = flat_rows + matmul(context, w_out)
    normed_two_full, inverse_two = rms_forward(hidden, gain_ffn.astype(jnp.float32))
    normed_two = normed_two_full.astype(jnp.bfloat16)
    gate_pre = matmul(normed_two, w_gate)
    up_pre = matmul(normed_two, w_up)
    activated = (jax.nn.gelu(gate_pre) * up_pre).astype(jnp.bfloat16)
    layer_out = hidden + matmul(activated, w_down)
    normed_end_full, inverse_end = rms_forward(layer_out, gain_final.astype(jnp.float32))
    normed_end = normed_end_full.astype(jnp.bfloat16)
    embedded = matmul(normed_end, w_proj).astype(jnp.bfloat16)
    kept_state = (
        flat_rows,
        inverse_one,
        normed,
        queries_h,
        keys_h,
        values_h,
        log_total,
        context,
        hidden,
        inverse_two,
        normed_two,
        gate_pre,
        up_pre,
        activated,
        layer_out,
        inverse_end,
        normed_end,
    )
    return (embedded, kept_state)


def encode_backward(grad_emb, kept_state, valid_keys, bias_full, onehot_table, full_weights):
    (
        w_query,
        w_key,
        w_value,
        w_out,
        w_gate,
        w_up,
        w_down,
        w_proj,
        gain_attn,
        gain_ffn,
        gain_final,
    ) = full_weights
    (
        flat_rows,
        inverse_one,
        normed,
        queries_h,
        keys_h,
        values_h,
        log_total,
        context,
        hidden,
        inverse_two,
        normed_two,
        gate_pre,
        up_pre,
        activated,
        layer_out,
        inverse_end,
        normed_end,
    ) = kept_state
    row_count, width_size = flat_rows.shape
    grad_low = grad_emb.astype(jnp.bfloat16)
    proj_grad = contract_rows(normed_end, grad_low)
    d_normed_end = contract_cols(grad_low, w_proj)
    d_layer, final_gain_grad = rms_backward(
        layer_out, inverse_end, gain_final.astype(jnp.float32), d_normed_end
    )
    d_layer_low = d_layer.astype(jnp.bfloat16)
    down_grad = contract_rows(activated, d_layer_low)
    d_activated = contract_cols(d_layer_low, w_down)
    unused_value, pull_back = jax.vjp(
        lambda first_arg, second_arg: jax.nn.gelu(first_arg) * second_arg, gate_pre, up_pre
    )
    d_gate, d_up = pull_back(d_activated)
    d_gate = d_gate.astype(jnp.bfloat16)
    d_up = d_up.astype(jnp.bfloat16)
    gate_grad = contract_rows(normed_two, d_gate)
    up_grad = contract_rows(normed_two, d_up)
    d_normed_two = contract_cols(d_gate, w_gate) + contract_cols(d_up, w_up)
    d_hidden_norm, ffn_gain_grad = rms_backward(
        hidden, inverse_two, gain_ffn.astype(jnp.float32), d_normed_two
    )
    d_hidden = d_layer + d_hidden_norm
    d_hidden_low = d_hidden.astype(jnp.bfloat16)
    out_grad = contract_rows(context, d_hidden_low)
    d_context = contract_cols(d_hidden_low, w_out).astype(jnp.bfloat16).reshape(queries_h.shape)
    scores = attention_scores(queries_h, keys_h, bias_full, valid_keys)
    probs_attn = jnp.exp(scores - log_total)
    d_probs = jnp.einsum("bqhd,bkhd->bhqk", d_context, values_h, preferred_element_type=jnp.float32)
    d_values = jnp.einsum(
        "bhqk,bqhd->bkhd",
        probs_attn.astype(jnp.bfloat16),
        d_context,
        preferred_element_type=jnp.float32,
    )
    d_values = d_values.astype(jnp.bfloat16).reshape(row_count, width_size)
    d_scores = probs_attn * (d_probs - jnp.sum(probs_attn * d_probs, axis=-1, keepdims=True))
    table_grad = jnp.einsum(
        "hij,ijb->bh", jnp.sum(d_scores, axis=0), onehot_table, precision=top_precision
    )
    d_scores_low = d_scores.astype(jnp.bfloat16)
    d_queries = jnp.einsum(
        "bhqk,bkhd->bqhd", d_scores_low, keys_h, preferred_element_type=jnp.float32
    )
    d_queries = d_queries.astype(jnp.bfloat16).reshape(row_count, width_size)
    d_keys = jnp.einsum(
        "bhqk,bqhd->bkhd", d_scores_low, queries_h, preferred_element_type=jnp.float32
    )
    d_keys = d_keys.astype(jnp.bfloat16).reshape(row_count, width_size)
    query_w_grad = contract_rows(normed, d_queries)
    key_w_grad = contract_rows(normed, d_keys)
    value_w_grad = contract_rows(normed, d_values)
    d_normed = (
        contract_cols(d_queries, w_query)
        + contract_cols(d_keys, w_key)
        + contract_cols(d_values, w_value)
    )
    d_flat, attn_gain_grad = rms_backward(
        flat_rows, inverse_one, gain_attn.astype(jnp.float32), d_normed
    )
    grad_list = (
        query_w_grad,
        key_w_grad,
        value_w_grad,
        out_grad,
        gate_grad,
        up_grad,
        down_grad,
        proj_grad,
        attn_gain_grad,
        ffn_gain_grad,
        final_gain_grad,
    )
    return (d_hidden + d_flat, grad_list, table_grad)


def pool_rows(row_block, picks_block, doc_emb, positions):
    scores_raw = contract_cols(row_block, doc_emb) * doc_emb.shape[1] ** (-0.5)
    multiple = jnp.sum(
        (picks_block[:, :, None] == positions[None, None, :]).astype(jnp.float32), axis=1
    )
    present = jnp.sum(multiple, axis=-1)
    totals_sum = jnp.sum(multiple * jnp.exp(scores_raw), axis=-1) + (present == 0).astype(
        jnp.float32
    )
    return (scores_raw, multiple, totals_sum)


def score_forward(query_all, picks_all, doc_emb, positions):
    row_count = query_all.shape[0]
    block_size = min(block_rows, row_count)
    block_count = row_count // block_size

    def one_block(bundle):
        scores_raw, multiple, totals_sum = pool_rows(bundle[0], bundle[1], doc_emb, positions)
        return jnp.log(totals_sum)

    pooled = lax.map(
        one_block,
        (
            query_all.reshape(block_count, block_size, -1),
            picks_all.reshape(block_count, block_size, -1),
        ),
    )
    return pooled.reshape(row_count)


def score_backward(query_all, picks_all, doc_emb, positions, pooled_grad):
    row_count = query_all.shape[0]
    block_size = min(block_rows, row_count)
    block_count = row_count // block_size
    scale_factor = doc_emb.shape[1] ** (-0.5)

    def one_block(doc_acc, bundle):
        row_block, picks_block, grad_block = bundle
        scores_raw, multiple, totals_sum = pool_rows(row_block, picks_block, doc_emb, positions)
        d_raw = (grad_block / totals_sum)[:, None] * multiple * jnp.exp(scores_raw) * scale_factor
        d_low = d_raw.astype(jnp.bfloat16)
        return (doc_acc + contract_rows(d_low, row_block), matmul(d_low, doc_emb))

    start_acc = jnp.zeros(doc_emb.shape, jnp.float32)
    doc_grad, query_blocks = lax.scan(
        one_block,
        start_acc,
        (
            query_all.reshape(block_count, block_size, -1),
            picks_all.reshape(block_count, block_size, -1),
            pooled_grad.reshape(block_count, block_size),
        ),
    )
    return (doc_grad, query_blocks.reshape(row_count, -1))


def query_loss(pooled_query, own_picks, lengths, goal_ids, doc_len):
    wide_count, token_count = pooled_query.shape
    query_count = lengths.shape[0]
    slot_count = token_count // query_count
    owner_doc = own_picks // doc_len
    doc_ids = jnp.arange(wide_count, dtype=jnp.int32)
    hit_mask = jnp.any(owner_doc[None, :, :] == doc_ids[:, None, None], axis=-1).astype(jnp.float32)
    valid_mask = (
        (jnp.arange(slot_count, dtype=jnp.int32)[None, :] < lengths[:, None])
        .astype(jnp.float32)
        .reshape(token_count)
    )
    counts = jnp.sum((hit_mask * valid_mask).reshape(wide_count, query_count, slot_count), axis=-1)
    divisor = jnp.maximum(counts, 1.0)
    summed = jnp.sum(
        (pooled_query * valid_mask).reshape(wide_count, query_count, slot_count), axis=-1
    )
    logits = score_scale * summed / divisor
    col_top = jnp.max(logits, axis=0, keepdims=True)
    shifted = jnp.exp(logits - col_top)
    col_totals = jnp.sum(shifted, axis=0, keepdims=True)
    chosen = (doc_ids[:, None] == goal_ids[None, :]).astype(jnp.float32)
    losses = col_top[0] + jnp.log(col_totals[0]) - jnp.sum(chosen * logits, axis=0)
    d_logits = shifted / col_totals - chosen
    d_pooled = (score_scale * d_logits / divisor)[:, :, None] * valid_mask.reshape(
        1, query_count, slot_count
    )
    return (losses, d_pooled.reshape(wide_count, token_count))


def local(
    doc_tokens,
    query_tokens,
    query_lengths,
    retrieved,
    targets,
    q_weight,
    k_weight,
    v_weight,
    o_weight,
    gate_weight,
    up_weight,
    down_weight,
    proj_weight,
    attn_gain,
    ffn_gain,
    final_gain,
    rel_bias,
):
    micro_count, _, doc_len, width = doc_tokens.shape
    query_count, slot_count = query_tokens.shape[1:3]
    picks_width = retrieved.shape[3]
    wide_count = lax.axis_size("wide")
    bias_table = rel_bias.astype(jnp.float32)
    onehot_doc = bucket_onehot(doc_len, rel_bias.shape[0])
    onehot_query = bucket_onehot(slot_count, rel_bias.shape[0])
    bias_doc = jnp.einsum("ijb,bh->hij", onehot_doc, bias_table, precision=top_precision)
    bias_query = jnp.einsum("ijb,bh->hij", onehot_query, bias_table, precision=top_precision)
    doc_valid = jnp.ones((1, doc_len), dtype=bool)
    slot_ids = jnp.arange(slot_count, dtype=jnp.int32)
    positions = lax.axis_index("wide") * doc_len + jnp.arange(doc_len, dtype=jnp.int32)
    full_weights = gathered(q_weight, k_weight, v_weight, o_weight, gate_weight, up_weight, down_weight, proj_weight, attn_gain, ffn_gain, final_gain)
    picks_group = lax.all_gather(retrieved, "wide", axis=1, tiled=True)
    docs = doc_tokens.reshape(micro_count, doc_len, width)
    queries = query_tokens.reshape(micro_count * query_count, slot_count, width)
    query_valid = slot_ids[None, :] < query_lengths.reshape(-1)[:, None]
    doc_emb, doc_state = encode_forward(docs, doc_valid, bias_doc, full_weights)
    query_emb, query_state = encode_forward(queries, query_valid, bias_query, full_weights)
    doc_emb = doc_emb.reshape(micro_count, doc_len, -1)
    query_emb = query_emb.reshape(micro_count, query_count * slot_count, -1)
    query_all = lax.all_gather(query_emb, "wide", axis=1, tiled=True)
    pooled = jnp.stack([
        score_forward(query_all[m], picks_group[m].reshape(-1, picks_width), doc_emb[m], positions)
        for m in range(micro_count)
    ])
    pooled_query = lax.all_to_all(
        pooled.reshape(micro_count, wide_count, -1), "wide", split_axis=1, concat_axis=1, tiled=True
    )
    results = [
        query_loss(pooled_query[m], retrieved[m].reshape(-1, picks_width), query_lengths[m], targets[m], doc_len)
        for m in range(micro_count)
    ]
    losses_out = jnp.stack([r[0] for r in results])
    d_pooled = jnp.stack([r[1] for r in results])
    d_pooled_doc = lax.all_to_all(d_pooled, "wide", split_axis=1, concat_axis=1, tiled=True)
    backs = [
        score_backward(
            query_all[m],
            picks_group[m].reshape(-1, picks_width),
            doc_emb[m],
            positions,
            d_pooled_doc[m].reshape(-1),
        )
        for m in range(micro_count)
    ]
    doc_emb_grad = jnp.concatenate([b[0] for b in backs])
    query_all_grad = jnp.stack([b[1] for b in backs])
    query_emb_grad = sent_and_summed(query_all_grad.astype(jnp.bfloat16), "wide", 1)
    doc_in_grad, doc_grads, doc_table = encode_backward(
        doc_emb_grad, doc_state, doc_valid, bias_doc, onehot_doc, full_weights
    )
    query_in_grad, query_grads, query_table = encode_backward(
        query_emb_grad.reshape(-1, query_emb_grad.shape[-1]), query_state, query_valid, bias_query, onehot_query, full_weights
    )
    grads = jax.tree.map(jnp.add, doc_grads, query_grads)
    shards = scattered(grads, doc_table + query_table)
    return (
        losses_out,
        doc_in_grad.reshape(doc_tokens.shape),
        query_in_grad.reshape(query_tokens.shape),
        *shards,
    )


def solution(mesh):
    placed = (
        P(None, ("dp", "wide"), None, None),
        P(None, ("dp", "wide"), None, None),
        P(None, ("dp", "wide")),
        P(None, ("dp", "wide"), None, None),
        P(None, ("dp", "wide")),
        P(("dp", "wide"), None),
        P(("dp", "wide"), None),
        P(("dp", "wide"), None),
        P(("dp", "wide"), None),
        P(("dp", "wide"), None),
        P(("dp", "wide"), None),
        P(("dp", "wide"), None),
        P(("dp", "wide"), None),
        P(("dp", "wide")),
        P(("dp", "wide")),
        P(("dp", "wide")),
        P(),
    )
    return jax.shard_map(
        local,
        mesh=mesh,
        in_specs=placed,
        out_specs=(
            P(None, ("dp", "wide")),
            P(None, ("dp", "wide"), None, None),
            P(None, ("dp", "wide"), None, None),
            P(("dp", "wide"), None),
            P(("dp", "wide"), None),
            P(("dp", "wide"), None),
            P(("dp", "wide"), None),
            P(("dp", "wide"), None),
            P(("dp", "wide"), None),
            P(("dp", "wide"), None),
            P(("dp", "wide"), None),
            P(("dp", "wide")),
            P(("dp", "wide")),
            P(("dp", "wide")),
            P(),
        ),
        check_vma=False,
    )
```

```python
import functools

import jax
import jax.numpy as jnp
from jax import lax
from jax.experimental import pallas as pl
from jax.experimental.pallas import tpu as pltpu
from jax.sharding import PartitionSpec as P

eps_norm = 1e-06
score_scale = 6.0
mask_fill = -1000000000.0
top_precision = lax.Precision.HIGHEST
F32 = jnp.float32
BF = jnp.bfloat16


MESH = pl.DeviceIdType.MESH

def gray(p):
    return p + (p // 2) * (1 - 2 * (p % 2))

class Place:
    def __init__(self, zc):
        self.zc = zc
        d = lax.axis_index("dp"); w = lax.axis_index("wide")
        self.d, self.w = d, w
        self.z, self.c = w // 2, w % 2
        p = gray(d)
        self.right = gray((p + 1) % 4); self.left = gray((p + 3) % 4); self.opp = gray((p + 2) % 4)
    def dev(self, d=None, z=None, c=None):
        d = self.d if d is None else d
        z = self.z if z is None else z
        c = self.c if c is None else c
        return (d, z * 2 + c)

def enter(pos):
    barrier = pltpu.get_barrier_semaphore()
    for dev in (pos.dev(d=pos.right), pos.dev(d=pos.left), pos.dev(c=1 - pos.c)):
        pl.semaphore_signal(barrier, inc=1, device_id=dev, device_id_type=MESH)
    @pl.when(pos.z > 0)
    def _():
        pl.semaphore_signal(barrier, inc=1, device_id=pos.dev(z=pos.z - 1), device_id_type=MESH)
    @pl.when(pos.z < pos.zc - 1)
    def _():
        pl.semaphore_signal(barrier, inc=1, device_id=pos.dev(z=pos.z + 1), device_id_type=MESH)
    zc = pos.zc
    peers = 3 + (pos.z + zc - 1) // zc + (2 * zc - 2 - pos.z) // zc
    pl.semaphore_wait(barrier, peers)

def gather_kernel(zc, count, *refs):
    pos = Place(zc)
    shard = refs[:count]
    out = refs[count:2 * count]
    rest = refs[2 * count:]
    comp = rest[:count]; mine = rest[count:2 * count]
    (s_col, s_ring, s_fwd, s_mate, s_pair, s_own, r_col, r_left, r_right, r_opp, r_mate, r_pair) = rest[2 * count:]
    z, c, d = pos.z, pos.c, pos.d
    enter(pos)
    rows = [o.shape[0] // (4 * zc) for o in out]
    half = [o.shape[1] // 2 for o in out]

    def part(a, ref, blk, core):
        return ref.at[pl.ds(pl.multiple_of(blk * rows[a], 16), rows[a]), pl.ds(pl.multiple_of(core * half[a], 128), half[a])]
    def own(a, core):
        return comp[a].at[:, pl.ds(pl.multiple_of(core * half[a], 128), half[a])]
    def rdma(a, src, blk, dev, ss, rs):
        return pltpu.make_async_remote_copy(src_ref=src, dst_ref=part(a, out[a], blk, c), send_sem=ss, recv_sem=rs, device_id=dev, device_id_type=MESH)
    def blk(dd, zz):
        return dd * zc + zz
    mate_dev = pos.dev(c=1 - c)
    def pair(a):
        return pltpu.make_async_remote_copy(src_ref=shard[a], dst_ref=mine[a], send_sem=s_pair.at[a], recv_sem=r_pair.at[a], device_id=mate_dev, device_id_type=MESH)
    def keep(a):
        return pltpu.make_async_copy(comp[a], out[a].at[pl.ds(pl.multiple_of(blk(d, z) * rows[a], 16), rows[a]), :], s_own.at[a])
    def up(a, src, zz):
        return rdma(a, src, blk(d, zz), pos.dev(z=lax.rem(z + 1, zc)), s_col.at[a, 0, zz], r_col.at[a, zz])
    def down(a, src, zz):
        return rdma(a, src, blk(d, zz), pos.dev(z=lax.rem(z + zc - 1, zc)), s_col.at[a, 1, zz], r_col.at[a, zz])
    def right(a, src, zz):
        return rdma(a, src, blk(d, zz), pos.dev(d=pos.right), s_ring.at[a, 0, zz], r_left.at[a, zz])
    def left(a, src, zz):
        return rdma(a, src, blk(d, zz), pos.dev(d=pos.left), s_ring.at[a, 1, zz], r_right.at[a, zz])
    def fwd_right(a, zz):
        b = blk(pos.left, zz)
        return rdma(a, part(a, out[a], b, c), b, pos.dev(d=pos.right), s_fwd.at[a, zz], r_opp.at[a, zz])
    def fwd_left(a, zz):
        b = blk(pos.right, zz)
        return rdma(a, part(a, out[a], b, c), b, pos.dev(d=pos.left), s_fwd.at[a, zz], r_opp.at[a, zz])
    def mate(a, b):
        return rdma(a, part(a, out[a], b, c), b, mate_dev, s_mate.at[a, b], r_mate.at[a, b])
    def got(a, b, sem):
        return rdma(a, part(a, out[a], b, c), b, mate_dev, s_mate.at[a, b], sem).wait_recv()
    def mate_got(a, b):
        piece = part(a, out[a], b, 1 - c)
        pltpu.make_async_remote_copy(src_ref=piece, dst_ref=piece, send_sem=s_mate.at[a, b], recv_sem=r_mate.at[a, b], device_id=mate_dev, device_id_type=MESH).wait_recv()

    for a in range(count):
        pair(a).start()
    for a in range(count):
        pair(a).wait_recv()
        r2 = rows[a] // 2
        step = 256 if half[a] * 2 % 256 == 0 else 128
        @pl.loop(0, half[a] * 2 // step)
        def _(t):
            cols = pl.ds(pl.multiple_of(t * step, 128), step)
            mn = shard[a][:, cols].astype(jnp.float32)[:r2]
            ot = mine[a][:, cols].astype(jnp.float32)[:r2]
            first = jnp.where(c == 0, mn, ot)
            second = jnp.where(c == 0, ot, mn)
            comp[a][:, cols] = jnp.concatenate([first, second], axis=0).astype(jnp.bfloat16)
        right(a, own(a, c), z).start()
        left(a, own(a, c), z).start()
        pl.when(z < zc - 1)(lambda: up(a, own(a, c), z).start())
        pl.when(z > 0)(lambda: down(a, own(a, c), z).start())
        keep(a).start()

    def column(a, j):
        @pl.when(z - j >= 0)
        def _():
            zz = z - j
            got(a, blk(d, zz), r_col.at[a, zz])
            src = part(a, out[a], blk(d, zz), c)
            pl.when(z < zc - 1)(lambda: up(a, src, zz).start())
            right(a, src, zz).start(); left(a, src, zz).start()
            mate(a, blk(d, zz)).start()
        @pl.when(z + j < zc)
        def _():
            zz = z + j
            got(a, blk(d, zz), r_col.at[a, zz])
            src = part(a, out[a], blk(d, zz), c)
            pl.when(z > 0)(lambda: down(a, src, zz).start())
            right(a, src, zz).start(); left(a, src, zz).start()
            mate(a, blk(d, zz)).start()
    def ring_one(a, zz):
        got(a, blk(pos.left, zz), r_left.at[a, zz])
        pl.when(zz % 2 == 0)(lambda: fwd_right(a, zz).start())
        mate(a, blk(pos.left, zz)).start()
        got(a, blk(pos.right, zz), r_right.at[a, zz])
        pl.when(zz % 2 == 1)(lambda: fwd_left(a, zz).start())
        mate(a, blk(pos.right, zz)).start()
    def opp_one(a, zz):
        got(a, blk(pos.opp, zz), r_opp.at[a, zz])
        mate(a, blk(pos.opp, zz)).start()
    def spread(fn, a, j):
        if j == 0:
            fn(a, z); return
        pl.when(z - j >= 0)(lambda: fn(a, z - j))
        pl.when(z + j < zc)(lambda: fn(a, z + j))
    for a in range(count):
        for t in range(zc + 2):
            if 1 <= t < zc:
                column(a, t)
            if 1 <= t <= zc:
                spread(ring_one, a, t - 1)
            if 2 <= t:
                spread(opp_one, a, t - 2)
    for a in range(count):
        pair(a).wait_send(); keep(a).wait()
        @pl.loop(0, zc)
        def _(zz):
            src = part(a, out[a], blk(d, zz), c)
            right(a, src, zz).wait_send(); left(a, src, zz).wait_send()
            pl.when((z < zc - 1) & (zz <= z))(lambda: up(a, src, zz).wait_send())
            pl.when((z > 0) & (zz >= z))(lambda: down(a, src, zz).wait_send())
            fwd_right(a, zz).wait_send()
        @pl.loop(0, 4 * zc)
        def _(b):
            @pl.when(b != blk(d, z))
            def _():
                mate(a, b).wait_send()
                mate_got(a, b)

def gather(shards, zc, n_dev):
    count = len(shards)
    outs, comps, mines = [], [], []
    for s, rows in shards:
        outs.append(jax.ShapeDtypeStruct((rows * n_dev, s.shape[1]), s.dtype))
        comps.append(pltpu.VMEM((rows * 2, s.shape[1]), s.dtype))
        mines.append(pltpu.VMEM(s.shape, s.dtype))
    dma = pltpu.SemaphoreType.DMA
    sems = [dma((count, 2, zc)), dma((count, 2, zc)), dma((count, zc)), dma((count, 4 * zc)), dma((count,)), dma((count,)),
            dma((count, zc)), dma((count, zc)), dma((count, zc)), dma((count, zc)), dma((count, 4 * zc)), dma((count,))]
    return pl.pallas_call(
        functools.partial(gather_kernel, zc, count),
        out_shape=outs,
        in_specs=[pl.BlockSpec(memory_space=pltpu.VMEM)] * count,
        out_specs=[pl.BlockSpec(memory_space=pl.ANY)] * count,
        scratch_shapes=comps + mines + sems,
        compiler_params=pltpu.CompilerParams(collective_id=0, has_side_effects=True, vmem_limit_bytes=32 << 20),
        name="gather_weights",
    )(*[s for s, _ in shards])


def reduce_kernel(zc, count, *refs):
    pos = Place(zc)
    z, c, d = pos.z, pos.c, pos.d
    g = refs[:count]; table = refs[count]
    out = refs[count + 1:2 * count + 1]; table_out = refs[2 * count + 1]
    rest = refs[2 * count + 2:]
    loc = rest[:count]; rxp = rest[count:2 * count]; rxf = rest[2 * count:3 * count]
    rxl = rest[3 * count:4 * count]; rxr = rest[4 * count:5 * count]
    rxu = rest[5 * count:6 * count]; rxd = rest[6 * count:7 * count]
    fin = rest[7 * count:8 * count]; rxm = rest[8 * count:9 * count]
    (tabs, s_tab, r_tab, s_pair, r_pair, s_loc, s_ring, r_fwd, r_left, r_right, s_z, r_up, r_dn, s_fin, r_fin) = rest[9 * count:]
    rows = [x.shape[0] // (4 * zc) for x in g]
    half = [x.shape[1] // 2 for x in g]
    n_dev = 8 * zc
    me = d * (2 * zc) + pos.w
    barrier = pltpu.get_barrier_semaphore()
    @pl.loop(1, n_dev)
    def _(k):
        o = lax.rem(me + k, n_dev)
        pl.semaphore_signal(barrier, inc=1, device_id=(o // (2 * zc), lax.rem(o, 2 * zc)), device_id_type=MESH)
    pl.semaphore_wait(barrier, n_dev - 1)
    mate_dev = pos.dev(c=1 - c)
    right_dev = pos.dev(d=pos.right); left_dev = pos.dev(d=pos.left)
    def remote(src, dst, ss, rs, dev):
        return pltpu.make_async_remote_copy(src_ref=src, dst_ref=dst, send_sem=ss, recv_sem=rs, device_id=dev, device_id_type=MESH)
    def tab_copy(k):
        o = lax.rem(me + k, n_dev)
        return remote(table, tabs.at[me], s_tab.at[k], r_tab.at[me], (o // (2 * zc), lax.rem(o, 2 * zc)))
    def tab_got(k):
        o = lax.rem(me + k, n_dev)
        return remote(table, tabs.at[o], s_tab.at[k], r_tab.at[o], (o // (2 * zc), lax.rem(o, 2 * zc)))
    def strip(a, dd):
        return pl.ds(pl.multiple_of(dd * zc * rows[a], 16), zc * rows[a])
    def cols(a, core):
        return pl.ds(pl.multiple_of(core * half[a], 128), half[a])
    def pair(a, dd):
        return remote(g[a].at[strip(a, dd), cols(a, 1 - c)], rxp[a].at[strip(a, dd), :], s_pair.at[a, dd], r_pair.at[a, dd], mate_dev)
    def local(a, dd):
        return pltpu.make_async_copy(g[a].at[strip(a, dd), cols(a, c)], loc[a].at[strip(a, dd), :], s_loc.at[a, dd])
    def row(a, dd, zz):
        return pl.ds(pl.multiple_of((dd * zc + zz) * rows[a], 16), rows[a])
    def slot(a, zz):
        return pl.ds(pl.multiple_of(zz * rows[a], 16), rows[a])
    def add(a, dst, terms, out_ref=None):
        step = 128 if half[a] % 256 else 256
        @pl.loop(0, half[a] // step)
        def _(t):
            cc = pl.ds(pl.multiple_of(t * step, 128), step)
            total = None
            for ref, rr in terms:
                v = ref[rr, cc].astype(F32)
                total = v if total is None else total + v
            dst[0][dst[1], cc] = total.astype(dst[0].dtype)
    def pair_sum(a, dd, zz, extra=()):
        r = row(a, dd, zz)
        add(a, (loc[a], r), [(loc[a], r), (rxp[a], r)] + list(extra))
    def first_right(a, zz):
        return remote(loc[a].at[row(a, pos.opp, zz), :], rxf[a].at[slot(a, zz), :], s_ring.at[a, 0, zz], r_fwd.at[a, zz], right_dev)
    def first_left(a, zz):
        return remote(loc[a].at[row(a, pos.opp, zz), :], rxf[a].at[slot(a, zz), :], s_ring.at[a, 0, zz], r_fwd.at[a, zz], left_dev)
    def to_right(a, zz):
        return remote(loc[a].at[row(a, pos.right, zz), :], rxl[a].at[slot(a, zz), :], s_ring.at[a, 1, zz], r_left.at[a, zz], right_dev)
    def to_left(a, zz):
        return remote(loc[a].at[row(a, pos.left, zz), :], rxr[a].at[slot(a, zz), :], s_ring.at[a, 2, zz], r_right.at[a, zz], left_dev)
    def up(a, zt):
        return remote(loc[a].at[row(a, d, zt), :], rxu[a].at[slot(a, zt), :], s_z.at[a, zt], r_up.at[a, zt], pos.dev(z=lax.rem(z + 1, zc)))
    def down(a, zt):
        return remote(loc[a].at[row(a, d, zt), :], rxd[a].at[slot(a, zt), :], s_z.at[a, zt], r_dn.at[a, zt], pos.dev(z=lax.rem(z + zc - 1, zc)))
    def mate_rows(a):
        r2 = rows[a] // 2
        return pl.ds(pl.multiple_of((1 - c) * r2, 8), r2)
    def my_rows(a):
        r2 = rows[a] // 2
        return pl.ds(pl.multiple_of(c * r2, 8), r2)
    def final(a):
        return remote(fin[a].at[mate_rows(a), :], rxm[a], s_fin.at[a], r_fin.at[a], mate_dev)

    for a in range(count):
        for dd in (pos.opp, pos.right, pos.left, d):
            pair(a, dd).start(); local(a, dd).start()
    @pl.loop(1, n_dev)
    def _(k):
        tab_copy(k).start()

    def phase_p(a):
        dd = pos.opp
        pair(a, dd).wait_recv(); local(a, dd).wait()
        for zz in range(zc):
            pair_sum(a, dd, zz)
            (first_right if zz % 2 == 0 else first_left)(a, zz).start()
        dd = pos.right
        pair(a, dd).wait_recv(); local(a, dd).wait()
        dd = pos.left
        pair(a, dd).wait_recv(); local(a, dd).wait()
        for zz in range(zc):
            if zz % 2:
                pair_sum(a, pos.right, zz); to_right(a, zz).start()
            else:
                pair_sum(a, pos.left, zz); to_left(a, zz).start()
    def phase_q(a):
        for zz in range(zc):
            if zz % 2 == 0:
                first_right(a, zz).wait_recv()
                pair_sum(a, pos.right, zz, [(rxf[a], slot(a, zz))]); to_right(a, zz).start()
            else:
                first_left(a, zz).wait_recv()
                pair_sum(a, pos.left, zz, [(rxf[a], slot(a, zz))]); to_left(a, zz).start()
        pair(a, d).wait_recv(); local(a, d).wait()
    def phase_r(a):
        def column(zz, dst, extra=()):
            r = row(a, d, zz)
            add(a, dst, [(loc[a], r), (rxp[a], r), (rxl[a], slot(a, zz)), (rxr[a], slot(a, zz))] + list(extra))
        def arrived(zz):
            to_right(a, zz).wait_recv(); to_left(a, zz).wait_recv()
        for zt in range(zc):
            arrived(zt)
        for i in range(zc - 1):
            zt = zc - 1 - i
            @pl.when(z < zt)
            def _():
                r = row(a, d, zt)
                @pl.when(z > 0)
                def _():
                    up(a, zt).wait_recv()
                    column(zt, (loc[a], r), [(rxu[a], slot(a, zt))])
                @pl.when(z == 0)
                def _():
                    column(zt, (loc[a], r))
                up(a, zt).start()
            zs = i
            @pl.when(z > zs)
            def _():
                r = row(a, d, zs)
                @pl.when(z < zc - 1)
                def _():
                    down(a, zs).wait_recv()
                    column(zs, (loc[a], r), [(rxd[a], slot(a, zs))])
                @pl.when(z == zc - 1)
                def _():
                    column(zs, (loc[a], r))
                down(a, zs).start()
        full = (fin[a], slice(None))
        zz = z
        @pl.when(z > 0)
        def _():
            up(a, zz).wait_recv()
        @pl.when(z < zc - 1)
        def _():
            down(a, zz).wait_recv()
        @pl.when(z == 0)
        def _():
            column(zz, full, [(rxd[a], slot(a, zz))])
        @pl.when(z == zc - 1)
        def _():
            column(zz, full, [(rxu[a], slot(a, zz))])
        @pl.when((z > 0) & (z < zc - 1))
        def _():
            column(zz, full, [(rxu[a], slot(a, zz)), (rxd[a], slot(a, zz))])
        final(a).start()
    def phase_s(a):
        out[a][:, cols(a, c)] = fin[a][my_rows(a), :]
        final(a).wait_recv()
        out[a][:, cols(a, 1 - c)] = rxm[a][...]
    for t in range(count + 2):
        if t < count: phase_p(t)
        if 1 <= t <= count: phase_q(t - 1)
        if 2 <= t: phase_r(t - 2)
    for a in range(count):
        phase_s(a)
    tabs[me] = table[...]
    @pl.loop(1, n_dev)
    def _(k):
        tab_got(k).wait_recv()
        tab_copy(k).wait_send()
    total = tabs[0]
    for k in range(1, n_dev):
        total = total + tabs[k]
    table_out[...] = total
    for a in range(count):
        for dd in range(4):
            pair(a, dd).wait_send()
        for zz in range(zc):
            (first_right if zz % 2 == 0 else first_left)(a, zz).wait_send()
            to_right(a, zz).wait_send(); to_left(a, zz).wait_send()
            @pl.when(zz != z)
            def _():
                up(a, zz).wait_send()
        final(a).wait_send()

def reduce_scatter(grads, table, zc):
    count = len(grads)
    n_dev = 8 * zc
    V = pltpu.VMEM
    outs = [jax.ShapeDtypeStruct((x.shape[0] // n_dev, x.shape[1]), F32) for x in grads] + [jax.ShapeDtypeStruct(table.shape, F32)]
    rows = [x.shape[0] // (4 * zc) for x in grads]; half = [x.shape[1] // 2 for x in grads]
    scratch = []
    scratch += [V((x.shape[0], h), BF) for x, h in zip(grads, half)]
    scratch += [V((x.shape[0], h), BF) for x, h in zip(grads, half)]
    for _ in range(5):
        scratch += [V((zc * r, h), BF) for r, h in zip(rows, half)]
    scratch += [V((r, h), F32) for r, h in zip(rows, half)]
    scratch += [V((r // 2, h), F32) for r, h in zip(rows, half)]
    dma = pltpu.SemaphoreType.DMA
    scratch += [V((n_dev,) + table.shape, F32), dma((n_dev,)), dma((n_dev,)), dma((count, 4)), dma((count, 4)), dma((count, 4)), dma((count, 3, zc)),
                dma((count, zc)), dma((count, zc)), dma((count, zc)), dma((count, zc)), dma((count, zc)), dma((count, zc)), dma((count,)), dma((count,))]
    return pl.pallas_call(
        functools.partial(reduce_kernel, zc, count),
        out_shape=outs,
        in_specs=[pl.BlockSpec(memory_space=pl.ANY)] * count + [pl.BlockSpec(memory_space=pltpu.VMEM)],
        out_specs=[pl.BlockSpec(memory_space=pltpu.VMEM)] * (count + 1),
        scratch_shapes=scratch,
        compiler_params=pltpu.CompilerParams(collective_id=1, has_side_effects=True, vmem_limit_bytes=48 << 20),
        name="reduce_grads",
    )(*grads, table)


def bucket_of(n):
    far = jnp.zeros_like(n)
    dist = jnp.abs(n)
    for power_step in range(1, 8):
        far = far + (dist * dist >= 64 * 2**power_step).astype(jnp.int32)
    return jnp.where(n > 0, 16, 0) + jnp.where(dist < 8, dist, 8 + far)

def diagonal_onehot(doc_len, bucket_count):
    span = 2 * doc_len
    i = jnp.arange(span, dtype=jnp.int32)
    base = doc_len - 128
    n = base - jnp.where(i >= span - 127, i - span, i)
    inside = (n > -doc_len) & (n < doc_len)
    hot = (bucket_of(n)[:, None] == jnp.arange(bucket_count, dtype=jnp.int32)[None, :]) & inside[:, None]
    return hot.astype(F32)

def cols_dot(a, b):
    return lax.dot_general(a, b, (((1,), (1,)), ((), ())), preferred_element_type=F32)

def tiles_of(table, keys, q_from, q_len, doc_len):
    parts = []
    for kb in range(keys // 128):
        at = doc_len - 128 - 128 * kb + q_from
        parts.append(table[:, at : at + q_len])
    return jnp.concatenate(parts, axis=0) if len(parts) > 1 else parts[0]

def attend_kernel(doc_len, doc_count, block, qkv_ref, diag_ref, mask_ref, ctx_ref, lse_ref, table_ref):
    span = 2 * doc_len
    hd = 64
    for h in range(2):
        wide = jnp.broadcast_to(diag_ref[0, h : h + 1, :], (128, span))
        table_ref[h] = pltpu.roll(wide, 0, 1, stride=1, stride_axis=0)[:, : span - 128]
    lane = lax.broadcasted_iota(jnp.int32, (1, 128), 1)
    def part(rows, keys_from, keys, q_at, q_len, mask):
        q2 = qkv_ref[pl.ds(rows + q_at, q_len), 0:128]
        k2 = qkv_ref[pl.ds(rows + keys_from, keys), 128:256]
        v2 = qkv_ref[pl.ds(rows + keys_from, keys), 256:384]
        v2t = v2.astype(F32).T.astype(BF)
        outs = []
        for h in range(2):
            qm = jnp.where((lane < hd) == (h == 0), q2, jnp.zeros_like(q2))
            s = cols_dot(k2, qm) + tiles_of(table_ref.at[h], keys, q_at, q_len, doc_len)
            if mask is not None:
                s = jnp.where(mask > 0, s, mask_fill)
            top = jnp.max(s, axis=0, keepdims=True)
            e = jnp.exp(s - top)
            total = jnp.sum(e, axis=0, keepdims=True)
            p = (e * (1.0 / total)).astype(BF)
            lse_ref[0, h : h + 1, pl.ds(rows + q_at, q_len)] = top + jnp.log(total)
            outs.append(jnp.dot(v2t[h * hd : (h + 1) * hd], p, preferred_element_type=F32))
        ctx_ref[pl.ds(rows + q_at, q_len), :] = jnp.concatenate(outs, axis=0).T.astype(BF)
    for m in range(doc_count):
        for q_at in range(0, doc_len, block):
            part(m * doc_len, 0, doc_len, q_at, block, None)
    rest = qkv_ref.shape[0] - doc_count * doc_len
    for i in range(rest // 128):
        part(doc_count * doc_len + 128 * i, 0, 128, 0, 128, mask_ref[i])

def attend(qkv, diag, mask, doc_len, doc_count):
    total, width = qkv.shape
    pairs = width // 384
    span = 2 * doc_len
    return pl.pallas_call(
        functools.partial(attend_kernel, doc_len, doc_count, 256),
        grid=(pairs,),
        in_specs=[
            pl.BlockSpec((total, 384), lambda j: (0, j)),
            pl.BlockSpec((1, 8, span), lambda j: (j, 0, 0)),
            pl.BlockSpec(mask.shape, lambda j: (0, 0, 0)),
        ],
        out_specs=[
            pl.BlockSpec((total, 128), lambda j: (0, j)),
            pl.BlockSpec((1, 8, total), lambda j: (j, 0, 0)),
            pl.BlockSpec((2, 128, span - 128), lambda j: (j, 0, 0)),
        ],
        out_shape=[
            jax.ShapeDtypeStruct((total, pairs * 128), BF),
            jax.ShapeDtypeStruct((pairs, 8, total), F32),
            jax.ShapeDtypeStruct((pairs * 2, 128, span - 128), F32),
        ],
        compiler_params=pltpu.CompilerParams(vmem_limit_bytes=40 << 20),
        name="attend",
    )(qkv, diag, mask)

def attend_back_kernel(doc_len, doc_count, block, qkv_ref, do_ref, lse_ref, table_ref, mask_ref, dqkv_ref, diag_ref, acc):
    span = 2 * doc_len
    hd = 64
    acc[...] = jnp.zeros_like(acc)
    lane = lax.broadcasted_iota(jnp.int32, (1, 128), 1)
    def part(rows, keys, q_len, mask):
        k2 = qkv_ref[pl.ds(rows, keys), 128:256]
        v2 = qkv_ref[pl.ds(rows, keys), 256:384]
        k2t = k2.astype(F32).T.astype(BF)
        dk = jnp.zeros((keys, 128), F32)
        dv = jnp.zeros((keys, 128), F32)
        for q_at in range(0, keys, q_len):
            qr = pl.ds(rows + q_at, q_len)
            q2 = qkv_ref[qr, 0:128]
            do2 = do_ref[qr, :]
            outs = []
            for h in range(2):
                mine = (lane < hd) == (h == 0)
                qm = jnp.where(mine, q2, jnp.zeros_like(q2))
                dom = jnp.where(mine, do2, jnp.zeros_like(do2))
                s = cols_dot(k2, qm) + tiles_of(table_ref.at[h], keys, q_at, q_len, doc_len)
                if mask is not None:
                    s = jnp.where(mask > 0, s, mask_fill)
                p = jnp.exp(s - lse_ref[0, h : h + 1, qr])
                dp = cols_dot(v2, dom)
                ds = p * (dp - jnp.sum(p * dp, axis=0, keepdims=True))
                for kb in range(keys // 128):
                    at = doc_len - 128 - 128 * kb + q_at
                    acc[h, :, at : at + q_len] += ds[128 * kb : 128 * (kb + 1)]
                low = ds.astype(BF)
                dv += jnp.dot(p.astype(BF), dom, preferred_element_type=F32)
                dk += jnp.dot(low, qm, preferred_element_type=F32)
                outs.append(jnp.dot(k2t[h * hd : (h + 1) * hd], low, preferred_element_type=F32))
            dqkv_ref[qr, 0:128] = jnp.concatenate(outs, axis=0).T.astype(BF)
        dqkv_ref[pl.ds(rows, keys), 128:256] = dk.astype(BF)
        dqkv_ref[pl.ds(rows, keys), 256:384] = dv.astype(BF)
    for m in range(doc_count):
        part(m * doc_len, doc_len, block, None)
    rest = qkv_ref.shape[0] - doc_count * doc_len
    for i in range(rest // 128):
        part(doc_count * doc_len + 128 * i, 128, 128, mask_ref[i])
    for h in range(2):
        eight = acc[h, 0:8]
        for g in range(1, 16):
            eight = eight + pltpu.roll(acc[h, 8 * g : 8 * g + 8], span - 8 * g, 1)
        one = eight[0:1]
        for r in range(1, 8):
            one = one + pltpu.roll(eight, span - r, 1)[r : r + 1]
        diag_ref[0, h : h + 1, :] = one

def attend_back(qkv, d_ctx, lse, table, mask, doc_len, doc_count):
    total, width = qkv.shape
    pairs = width // 384
    span = 2 * doc_len
    return pl.pallas_call(
        functools.partial(attend_back_kernel, doc_len, doc_count, 256),
        grid=(pairs,),
        in_specs=[
            pl.BlockSpec((total, 384), lambda j: (0, j)),
            pl.BlockSpec((total, 128), lambda j: (0, j)),
            pl.BlockSpec((1, 8, total), lambda j: (j, 0, 0)),
            pl.BlockSpec((2, 128, span - 128), lambda j: (j, 0, 0)),
            pl.BlockSpec(mask.shape, lambda j: (0, 0, 0)),
        ],
        out_specs=[
            pl.BlockSpec((total, 384), lambda j: (0, j)),
            pl.BlockSpec((1, 8, span), lambda j: (j, 0, 0)),
        ],
        out_shape=[
            jax.ShapeDtypeStruct((total, width), BF),
            jax.ShapeDtypeStruct((pairs, 8, span), F32),
        ],
        scratch_shapes=[pltpu.VMEM((2, 128, span), F32)],
        compiler_params=pltpu.CompilerParams(vmem_limit_bytes=40 << 20),
        name="attend_back",
    )(qkv, d_ctx, lse, table, mask)

def query_mask(lengths, slots):
    per = 128 // slots
    live = (jnp.arange(slots, dtype=jnp.int32)[None, :] < lengths[:, None]).reshape(-1, 128)
    owner = jnp.arange(128, dtype=jnp.int32) // slots
    same = owner[:, None] == owner[None, :]
    return (live[:, :, None] & same[None]).astype(F32)

def pair_columns(w):
    q, k, v = w
    rows, width = q.shape
    pack = jnp.stack([x.reshape(rows, width // 128, 128) for x in (q, k, v)], axis=2)
    return pack.reshape(rows, 3 * width)


def score_kernel(peers, doc_len, slots, emb_ref, picks_ref, live_ref, goal_ref, loss_ref, d_emb_ref,
                 q_own, q_all, p_all, weighed, totals, pool_out, pool_in, grad_out, grad_in, dq_out, dq_in, docs_t, d_docs,
                 s_q, r_q, s_p, r_p, s_pool, r_pool, s_grad, r_grad, s_dq, r_dq):
    dp = lax.axis_index("dp"); me = lax.axis_index("wide")
    tokens = q_own.shape[0]
    feat = emb_ref.shape[1]
    half = tokens // 2
    scale = feat ** -0.5
    barrier = pltpu.get_barrier_semaphore()
    def other(k):
        return lax.rem(me + k, peers)
    def each(fn):
        @pl.loop(1, peers)
        def _(k):
            fn(other(k))
    each(lambda o: pl.semaphore_signal(barrier, inc=1, device_id=(dp, o), device_id_type=MESH))
    q_own[...] = emb_ref[2 * doc_len :, :]
    q_all[me] = q_own[...]
    p_all[me] = picks_ref[...]
    pl.semaphore_wait(barrier, peers - 1)
    def send(src, dst, ss, rs, o):
        return pltpu.make_async_remote_copy(src_ref=src, dst_ref=dst, send_sem=ss, recv_sem=rs, device_id=(dp, o), device_id_type=MESH)
    def picks_to(o): return send(picks_ref, p_all.at[me], s_p.at[o], r_p.at[me], o)
    def picks_from(o): return send(picks_ref, p_all.at[o], s_p.at[o], r_p.at[o], o)
    def q_to(o): return send(q_own, q_all.at[me], s_q.at[o], r_q.at[me], o)
    def q_from(o): return send(q_own, q_all.at[o], s_q.at[o], r_q.at[o], o)
    def pool_to(o): return send(pool_out.at[o], pool_in.at[me], s_pool.at[o], r_pool.at[me], o)
    def pool_from(o): return send(pool_out.at[o], pool_in.at[o], s_pool.at[o], r_pool.at[o], o)
    def grad_to(o): return send(grad_out.at[o], grad_in.at[me], s_grad.at[o], r_grad.at[me], o)
    def grad_from(o): return send(grad_out.at[o], grad_in.at[o], s_grad.at[o], r_grad.at[o], o)
    def dq_to(o): return send(dq_out.at[o], dq_in.at[me], s_dq.at[o], r_dq.at[me], o)
    def dq_from(o): return send(dq_out.at[o], dq_in.at[o], s_dq.at[o], r_dq.at[o], o)
    def started(o):
        picks_to(o).start(); q_to(o).start()
    each(started)
    docs2 = jnp.concatenate([emb_ref[0:doc_len, :], emb_ref[doc_len : 2 * doc_len, :]], axis=1)
    docs_t[...] = docs2.astype(F32).T.astype(BF)
    row = lax.broadcasted_iota(jnp.int32, (tokens, 1), 0)
    lane = lax.broadcasted_iota(jnp.int32, (1, tokens), 1)
    def two_docs(o):
        q = q_all[o]
        none = jnp.zeros_like(q)
        return jnp.concatenate([jnp.where(row < half, q, none), jnp.where(row < half, none, q)], axis=1)
    chunk = 64
    base = me * doc_len
    def forward(o):
        picks = p_all[o] - base
        found = jnp.zeros((1, tokens), F32)
        weight = jnp.zeros((1, tokens), F32)
        s = lax.dot_general(docs2, two_docs(o), (((1,), (1,)), ((), ())), preferred_element_type=F32) * scale
        e = jnp.exp(s)
        for at in range(0, doc_len, chunk):
            place = lax.broadcasted_iota(jnp.int32, (chunk, tokens), 0) + at
            count = jnp.zeros((chunk, tokens), jnp.int32)
            for k in range(picks.shape[0]):
                count = count + (picks[k : k + 1, :] == place).astype(jnp.int32)
            multiple = count.astype(F32)
            w = multiple * e[at : at + chunk]
            weighed[o, at : at + chunk, :] = w
            found = found + jnp.sum(multiple, axis=0, keepdims=True)
            weight = weight + jnp.sum(w, axis=0, keepdims=True)
        weight = weight + (found == 0).astype(F32)
        totals[o] = jnp.broadcast_to(weight, (8, tokens))
        pool_out[o] = jnp.broadcast_to(jnp.log(weight), (8, tokens))
    def forward_peer(o):
        picks_from(o).wait_recv(); q_from(o).wait_recv()
        forward(o)
        pool_to(o).start()
    forward(me)
    pool_in[me] = pool_out[me]
    each(forward_peer)
    each(lambda o: pool_from(o).wait_recv())
    pooled = pool_in[:, 0, :]
    mine = picks_ref[...]
    hits = []
    for w in range(peers):
        inside = ((mine >= w * doc_len) & (mine < (w + 1) * doc_len)).astype(F32)
        hits.append(jnp.max(inside, axis=0, keepdims=True))
    hit = jnp.concatenate(hits, axis=0)
    live = live_ref[0:1, :]
    own_row = lax.broadcasted_iota(jnp.int32, (tokens, tokens), 0) // slots
    own_col = lax.broadcasted_iota(jnp.int32, (tokens, tokens), 1) // slots
    same = (own_row == own_col).astype(F32)
    def per_query(v):
        return jnp.dot(v, same, precision=lax.Precision.HIGHEST, preferred_element_type=F32)
    divisor = jnp.maximum(per_query(hit * live), 1.0)
    logits = score_scale * per_query(pooled * live) / divisor
    top = jnp.max(logits, axis=0, keepdims=True)
    shifted = jnp.exp(logits - top)
    total = jnp.sum(shifted, axis=0, keepdims=True)
    doc_id = lax.broadcasted_iota(jnp.int32, (peers, tokens), 0)
    chosen = (doc_id == goal_ref[0:1, :]).astype(F32)
    loss = top + jnp.log(total) - jnp.sum(chosen * logits, axis=0, keepdims=True)
    loss_ref[...] = jnp.broadcast_to(loss, loss_ref.shape)
    d_pooled = score_scale * (shifted / total - chosen) / divisor * live
    for w in range(peers):
        grad_out[w] = jnp.broadcast_to(d_pooled[w : w + 1], (8, tokens))
    each(lambda o: grad_to(o).start())
    grad_in[me] = grad_out[me]
    d_docs[...] = jnp.zeros_like(d_docs)
    def backward(o):
        factor = grad_in[o][0:1] / totals[o][0:1] * scale
        d_raw = (weighed[o] * factor).astype(BF)
        d_docs[...] += jnp.dot(d_raw, two_docs(o), preferred_element_type=F32)
        both = jnp.dot(docs_t[...], d_raw, preferred_element_type=F32)
        d_q = jnp.where(lane < half, both[0:feat], both[feat : 2 * feat])
        dq_out[o] = d_q.T.astype(BF)
    def backward_peer(o):
        grad_from(o).wait_recv()
        backward(o)
        dq_to(o).start()
    each(backward_peer)
    backward(me)
    d_emb_ref[0:doc_len, :] = d_docs[:, 0:feat].astype(BF)
    d_emb_ref[doc_len : 2 * doc_len, :] = d_docs[:, feat : 2 * feat].astype(BF)
    dq_in[me] = dq_out[me]
    each(lambda o: dq_from(o).wait_recv())
    total_q = dq_in[0].astype(F32)
    for w in range(1, peers):
        total_q = total_q + dq_in[w].astype(F32)
    d_emb_ref[2 * doc_len :, :] = total_q.astype(BF)
    def sent(o):
        picks_to(o).wait_send(); q_to(o).wait_send(); pool_to(o).wait_send(); grad_to(o).wait_send(); dq_to(o).wait_send()
    each(sent)

def score(emb, picks, live, goal, doc_len, slots, peers):
    tokens = picks.shape[1]
    feat = emb.shape[1]
    V = pltpu.VMEM
    dma = pltpu.SemaphoreType.DMA
    return pl.pallas_call(
        functools.partial(score_kernel, peers, doc_len, slots),
        out_shape=[jax.ShapeDtypeStruct((8, tokens), F32), jax.ShapeDtypeStruct(emb.shape, BF)],
        in_specs=[pl.BlockSpec(memory_space=pltpu.VMEM)] * 4,
        out_specs=[pl.BlockSpec(memory_space=pltpu.VMEM)] * 2,
        scratch_shapes=[
            V((tokens, feat), BF), V((peers, tokens, feat), BF), V((peers,) + picks.shape, jnp.int32),
            V((peers, doc_len, tokens), F32), V((peers, 8, tokens), F32),
            V((peers, 8, tokens), F32), V((peers, 8, tokens), F32), V((peers, 8, tokens), F32), V((peers, 8, tokens), F32),
            V((peers, tokens, feat), BF), V((peers, tokens, feat), BF), V((2 * feat, doc_len), BF), V((doc_len, 2 * feat), F32),
        ] + [dma((peers,))] * 10,
        compiler_params=pltpu.CompilerParams(collective_id=2, has_side_effects=True, vmem_limit_bytes=48 << 20),
        name="score",
    )(emb, picks, live, goal)


def contract_rows(left_mat, right_mat):
    return lax.dot_general(
        left_mat, right_mat, (((0,), (0,)), ((), ())), preferred_element_type=jnp.float32
    )


def contract_cols(left_mat, right_mat):
    return lax.dot_general(
        left_mat, right_mat, (((1,), (1,)), ((), ())), preferred_element_type=jnp.float32
    )


def matmul(left_mat, right_mat):
    return jnp.dot(left_mat, right_mat, preferred_element_type=jnp.float32)


def rms_forward(values, gain_vec):
    inverse = lax.rsqrt(jnp.mean(values * values, axis=-1, keepdims=True) + eps_norm)
    return (values * inverse * gain_vec, inverse)


def rms_backward(values, inverse, gain_vec, upstream):
    scaled = upstream * gain_vec
    gain_grad = jnp.sum(upstream * values * inverse, axis=0)
    inner_mean = jnp.mean(scaled * values, axis=-1, keepdims=True)
    return (inverse * scaled - values * inverse * inverse * inverse * inner_mean, gain_grad)


def two_level(shards):
    return (
        lax.axis_size("dp") == 4
        and lax.axis_size("wide") % 4 == 0
        and all(s.shape[0] % 8 == 0 for s in shards)
    )


def gathered(shards):
    if not two_level(shards):
        return [lax.all_gather(s, ("dp", "wide"), axis=0, tiled=True) for s in shards]
    zc = lax.axis_size("wide") // 2
    padded = [(jnp.pad(s, ((0, -s.shape[0] % 16), (0, 0))), s.shape[0]) for s in shards]
    return gather(padded, zc, 8 * zc)


def scattered(grads, table):
    n_dev = lax.axis_size("dp") * lax.axis_size("wide")
    if not two_level([g[: g.shape[0] // n_dev] for g in grads]):
        shards = [
            lax.psum_scatter(g.astype(F32), ("dp", "wide"), scatter_dimension=0, tiled=True)
            for g in grads
        ]
        return [*shards, lax.psum(table, ("dp", "wide"))]
    flat = table.reshape(-1)
    packed = jnp.pad(flat, (0, -flat.shape[0] % 1024)).reshape(-1, 128)
    *shards, packed = reduce_scatter(grads, packed, lax.axis_size("wide") // 2)
    return [*shards, packed.reshape(-1)[: flat.shape[0]].reshape(table.shape)]


def local(
    doc_tokens,
    query_tokens,
    query_lengths,
    retrieved,
    targets,
    q_weight,
    k_weight,
    v_weight,
    o_weight,
    gate_weight,
    up_weight,
    down_weight,
    proj_weight,
    attn_gain,
    ffn_gain,
    final_gain,
    rel_bias,
):
    micro_count, _, doc_len, width = doc_tokens.shape
    slots = query_tokens.shape[2]
    doc_rows = micro_count * doc_len
    wide_count = lax.axis_size("wide")
    p_size = proj_weight.shape[1]
    bucket_count, head_count = rel_bias.shape
    pairs = width // 128
    gains = jnp.stack([attn_gain, ffn_gain, final_gain], axis=1)
    last = jnp.concatenate([proj_weight, jnp.pad(gains, ((0, 0), (0, 128 - gains.shape[1])))], axis=1)
    w_qkv, w_out, w_last, w_gate, w_up, w_down = gathered(
        [pair_columns((q_weight, k_weight, v_weight)), o_weight, last, gate_weight, up_weight, down_weight]
    )
    w_proj = w_last[:, :p_size]
    gain_attn, gain_ffn, gain_final = (w_last[:, p_size + i].astype(F32) for i in range(3))
    hot = diagonal_onehot(doc_len, bucket_count)
    diag = jnp.dot(rel_bias.astype(F32).T, hot.T, precision=top_precision)
    diag = jnp.pad(diag.reshape(pairs, 2, -1), ((0, 0), (0, 6), (0, 0)))
    mask = query_mask(query_lengths.reshape(-1), slots)
    rows = jnp.concatenate(
        [doc_tokens.reshape(doc_rows, width), query_tokens.reshape(-1, width)], axis=0
    ).astype(F32)
    normed_full, inverse_one = rms_forward(rows, gain_attn)
    normed = normed_full.astype(BF)
    qkv = matmul(normed, w_qkv).astype(BF)
    context, lse, table = attend(qkv, diag, mask, doc_len, micro_count)
    hidden = rows + matmul(context, w_out)
    normed_two_full, inverse_two = rms_forward(hidden, gain_ffn)
    normed_two = normed_two_full.astype(BF)
    gate_pre = matmul(normed_two, w_gate)
    up_pre = matmul(normed_two, w_up)
    activated = (jax.nn.gelu(gate_pre) * up_pre).astype(BF)
    layer_out = hidden + matmul(activated, w_down)
    normed_end_full, inverse_end = rms_forward(layer_out, gain_final)
    normed_end = normed_end_full.astype(BF)
    embedded = matmul(normed_end, w_proj).astype(BF)
    picks = retrieved.reshape(-1, retrieved.shape[3]).T
    tokens = picks.shape[1]
    live = (jnp.arange(slots, dtype=jnp.int32)[None, :] < query_lengths.reshape(-1)[:, None]).astype(F32)
    live = jnp.broadcast_to(live.reshape(1, tokens), (8, tokens))
    goal = jnp.broadcast_to(jnp.repeat(targets.reshape(-1), slots)[None, :], (8, tokens))
    loss_rows, d_embedded = score(embedded, picks, live, goal, doc_len, slots, wide_count)
    losses_out = loss_rows[0].reshape(-1, slots)[:, 0].reshape(targets.shape)
    proj_grad = contract_rows(normed_end, d_embedded)
    d_normed_end = contract_cols(d_embedded, w_proj)
    d_layer, final_gain_grad = rms_backward(layer_out, inverse_end, gain_final, d_normed_end)
    d_layer_low = d_layer.astype(BF)
    down_grad = contract_rows(activated, d_layer_low).astype(BF)
    d_activated = contract_cols(d_layer_low, w_down)
    _, pull_back = jax.vjp(
        lambda first_arg, second_arg: jax.nn.gelu(first_arg) * second_arg, gate_pre, up_pre
    )
    d_gate, d_up = pull_back(d_activated)
    d_gate = d_gate.astype(BF)
    d_up = d_up.astype(BF)
    gate_grad = contract_rows(normed_two, d_gate).astype(BF)
    up_grad = contract_rows(normed_two, d_up).astype(BF)
    d_normed_two = contract_cols(d_gate, w_gate) + contract_cols(d_up, w_up)
    d_hidden_norm, ffn_gain_grad = rms_backward(hidden, inverse_two, gain_ffn, d_normed_two)
    d_hidden = d_layer + d_hidden_norm
    d_hidden_low = d_hidden.astype(BF)
    out_grad = contract_rows(context, d_hidden_low).astype(BF)
    d_context = contract_cols(d_hidden_low, w_out).astype(BF)
    d_qkv, d_diag = attend_back(qkv, d_context, lse, table, mask, doc_len, micro_count)
    table_grad = jnp.dot(hot.T, d_diag[:, :2].reshape(head_count, -1).T, precision=top_precision)
    qkv_grad = contract_rows(normed, d_qkv).astype(BF)
    d_normed = contract_cols(d_qkv, w_qkv)
    d_rows, attn_gain_grad = rms_backward(rows, inverse_one, gain_attn, d_normed)
    d_rows = d_hidden + d_rows
    gain_grads = jnp.stack([attn_gain_grad, ffn_gain_grad, final_gain_grad], axis=1)
    last_grad = jnp.concatenate([proj_grad, jnp.pad(gain_grads, ((0, 0), (0, 125)))], axis=1).astype(BF)
    s_qkv, s_out, s_last, s_gate, s_up, s_down, s_table = scattered(
        [qkv_grad, out_grad, last_grad, gate_grad, up_grad, down_grad], table_grad
    )
    apart = s_qkv.reshape(-1, pairs, 3, 128)
    return (
        losses_out,
        d_rows[:doc_rows].reshape(doc_tokens.shape),
        d_rows[doc_rows:].reshape(query_tokens.shape),
        apart[:, :, 0].reshape(-1, width),
        apart[:, :, 1].reshape(-1, width),
        apart[:, :, 2].reshape(-1, width),
        s_out,
        s_gate,
        s_up,
        s_down,
        s_last[:, :p_size],
        s_last[:, p_size],
        s_last[:, p_size + 1],
        s_last[:, p_size + 2],
        s_table,
    )


def solution(mesh):
    placed = (
        P(None, ("dp", "wide"), None, None),
        P(None, ("dp", "wide"), None, None),
        P(None, ("dp", "wide")),
        P(None, ("dp", "wide"), None, None),
        P(None, ("dp", "wide")),
        P(("dp", "wide"), None),
        P(("dp", "wide"), None),
        P(("dp", "wide"), None),
        P(("dp", "wide"), None),
        P(("dp", "wide"), None),
        P(("dp", "wide"), None),
        P(("dp", "wide"), None),
        P(("dp", "wide"), None),
        P(("dp", "wide")),
        P(("dp", "wide")),
        P(("dp", "wide")),
        P(),
    )
    return jax.shard_map(
        local,
        mesh=mesh,
        in_specs=placed,
        out_specs=(
            P(None, ("dp", "wide")),
            P(None, ("dp", "wide"), None, None),
            P(None, ("dp", "wide"), None, None),
            P(("dp", "wide"), None),
            P(("dp", "wide"), None),
            P(("dp", "wide"), None),
            P(("dp", "wide"), None),
            P(("dp", "wide"), None),
            P(("dp", "wide"), None),
            P(("dp", "wide"), None),
            P(("dp", "wide"), None),
            P(("dp", "wide")),
            P(("dp", "wide")),
            P(("dp", "wide")),
            P(),
        ),
        check_vma=False,
    )
```

```python
import functools

import jax
import jax.numpy as jnp
from jax import lax
from jax.experimental import pallas as pl
from jax.experimental.pallas import tpu as pltpu
from jax.sharding import PartitionSpec as P

eps_norm = 1e-06
score_scale = 6.0
mask_fill = -1000000000.0
top_precision = lax.Precision.HIGHEST
F32 = jnp.float32
BF = jnp.bfloat16


MESH = pl.DeviceIdType.MESH

def gray(p):
    return p + (p // 2) * (1 - 2 * (p % 2))

class Place:
    def __init__(self, zc):
        self.zc = zc
        d = lax.axis_index("dp"); w = lax.axis_index("wide")
        self.d, self.w = d, w
        self.z, self.c = w // 2, w % 2
        p = gray(d)
        self.right = gray((p + 1) % 4); self.left = gray((p + 3) % 4); self.opp = gray((p + 2) % 4)
    def dev(self, d=None, z=None, c=None):
        d = self.d if d is None else d
        z = self.z if z is None else z
        c = self.c if c is None else c
        return (d, z * 2 + c)

def enter(pos):
    barrier = pltpu.get_barrier_semaphore()
    for dev in (pos.dev(d=pos.right), pos.dev(d=pos.left), pos.dev(c=1 - pos.c)):
        pl.semaphore_signal(barrier, inc=1, device_id=dev, device_id_type=MESH)
    @pl.loop(1, pos.zc)
    def _(k):
        pl.semaphore_signal(barrier, inc=1, device_id=pos.dev(z=lax.rem(pos.z + k, pos.zc)), device_id_type=MESH)
    pl.semaphore_wait(barrier, 2 + pos.zc)


def gather_events(zc, shard, out, rest):
    count = len(shard)
    pos = Place(zc)
    comp = rest[:count]; mine = rest[count:2 * count]
    (s_col, s_ring, s_fwd, s_mate, s_pair, s_own, r_col, r_left, r_right, r_opp, r_mate, r_pair) = rest[2 * count:]
    z, c, d = pos.z, pos.c, pos.d
    rows = [o.shape[0] // (4 * zc) for o in out]
    half = [o.shape[1] // 2 for o in out]

    def part(a, ref, blk, core):
        return ref.at[pl.ds(pl.multiple_of(blk * rows[a], 16), rows[a]), pl.ds(pl.multiple_of(core * half[a], 128), half[a])]
    def own(a, core):
        return comp[a].at[:, pl.ds(pl.multiple_of(core * half[a], 128), half[a])]
    def rdma(a, src, blk, dev, ss, rs):
        return pltpu.make_async_remote_copy(src_ref=src, dst_ref=part(a, out[a], blk, c), send_sem=ss, recv_sem=rs, device_id=dev, device_id_type=MESH)
    def blk(dd, zz):
        return dd * zc + zz
    mate_dev = pos.dev(c=1 - c)
    def pair(a):
        return pltpu.make_async_remote_copy(src_ref=shard[a], dst_ref=mine[a], send_sem=s_pair.at[a], recv_sem=r_pair.at[a], device_id=mate_dev, device_id_type=MESH)
    def keep(a):
        return pltpu.make_async_copy(comp[a], out[a].at[pl.ds(pl.multiple_of(blk(d, z) * rows[a], 16), rows[a]), :], s_own.at[a])
    def up(a, src, zz):
        return rdma(a, src, blk(d, zz), pos.dev(z=lax.rem(z + 1, zc)), s_col.at[a, 0, zz], r_col.at[a, zz])
    def down(a, src, zz):
        return rdma(a, src, blk(d, zz), pos.dev(z=lax.rem(z + zc - 1, zc)), s_col.at[a, 1, zz], r_col.at[a, zz])
    def right(a, src, zz):
        return rdma(a, src, blk(d, zz), pos.dev(d=pos.right), s_ring.at[a, 0, zz], r_left.at[a, zz])
    def left(a, src, zz):
        return rdma(a, src, blk(d, zz), pos.dev(d=pos.left), s_ring.at[a, 1, zz], r_right.at[a, zz])
    def fwd_right(a, zz):
        b = blk(pos.left, zz)
        return rdma(a, part(a, out[a], b, c), b, pos.dev(d=pos.right), s_fwd.at[a, zz], r_opp.at[a, zz])
    def fwd_left(a, zz):
        b = blk(pos.right, zz)
        return rdma(a, part(a, out[a], b, c), b, pos.dev(d=pos.left), s_fwd.at[a, zz], r_opp.at[a, zz])
    def mate(a, b):
        return rdma(a, part(a, out[a], b, c), b, mate_dev, s_mate.at[a, b], r_mate.at[a, b])
    def got(a, b, sem):
        return rdma(a, part(a, out[a], b, c), b, mate_dev, s_mate.at[a, b], sem).wait_recv()
    def mate_got(a, b):
        piece = part(a, out[a], b, 1 - c)
        pltpu.make_async_remote_copy(src_ref=piece, dst_ref=piece, send_sem=s_mate.at[a, b], recv_sem=r_mate.at[a, b], device_id=mate_dev, device_id_type=MESH).wait_recv()

    def begin():
        enter(pos)
        for a in range(count):
            pair(a).start()
    def first(a):
        pair(a).wait_recv()
        r2 = rows[a] // 2
        step = 256 if half[a] * 2 % 256 == 0 else 128
        @pl.loop(0, half[a] * 2 // step)
        def _(t):
            cols = pl.ds(pl.multiple_of(t * step, 128), step)
            mn = shard[a][:, cols].astype(jnp.float32)[:r2]
            ot = mine[a][:, cols].astype(jnp.float32)[:r2]
            first = jnp.where(c == 0, mn, ot)
            second = jnp.where(c == 0, ot, mn)
            comp[a][:, cols] = jnp.concatenate([first, second], axis=0).astype(jnp.bfloat16)
        right(a, own(a, c), z).start()
        left(a, own(a, c), z).start()
        pl.when(z < zc - 1)(lambda: up(a, own(a, c), z).start())
        pl.when(z > 0)(lambda: down(a, own(a, c), z).start())
        keep(a).start()

    def column(a, j):
        @pl.when(z - j >= 0)
        def _():
            zz = z - j
            got(a, blk(d, zz), r_col.at[a, zz])
            src = part(a, out[a], blk(d, zz), c)
            pl.when(z < zc - 1)(lambda: up(a, src, zz).start())
            right(a, src, zz).start(); left(a, src, zz).start()
            mate(a, blk(d, zz)).start()
        @pl.when(z + j < zc)
        def _():
            zz = z + j
            got(a, blk(d, zz), r_col.at[a, zz])
            src = part(a, out[a], blk(d, zz), c)
            pl.when(z > 0)(lambda: down(a, src, zz).start())
            right(a, src, zz).start(); left(a, src, zz).start()
            mate(a, blk(d, zz)).start()
    def ring_one(a, zz):
        got(a, blk(pos.left, zz), r_left.at[a, zz])
        pl.when(zz % 2 == 0)(lambda: fwd_right(a, zz).start())
        mate(a, blk(pos.left, zz)).start()
        got(a, blk(pos.right, zz), r_right.at[a, zz])
        pl.when(zz % 2 == 1)(lambda: fwd_left(a, zz).start())
        mate(a, blk(pos.right, zz)).start()
    def opp_one(a, zz):
        got(a, blk(pos.opp, zz), r_opp.at[a, zz])
        mate(a, blk(pos.opp, zz)).start()
    def spread(fn, a, j):
        if j == 0:
            fn(a, z); return
        pl.when(z - j >= 0)(lambda: fn(a, z - j))
        pl.when(z + j < zc)(lambda: fn(a, z + j))
    def round_of(a, t):
        if 1 <= t < zc:
            column(a, t)
        if 1 <= t <= zc:
            spread(ring_one, a, t - 1)
        if 2 <= t:
            spread(opp_one, a, t - 2)
    def finish():
        for a in range(count):
            finish_one(a)
    def finish_one(a):
        pair(a).wait_send(); keep(a).wait()
        @pl.loop(0, zc)
        def _(zz):
            src = part(a, out[a], blk(d, zz), c)
            right(a, src, zz).wait_send(); left(a, src, zz).wait_send()
            pl.when((z < zc - 1) & (zz <= z))(lambda: up(a, src, zz).wait_send())
            pl.when((z > 0) & (zz >= z))(lambda: down(a, src, zz).wait_send())
            fwd_right(a, zz).wait_send()
        @pl.loop(0, 4 * zc)
        def _(b):
            @pl.when(b != blk(d, z))
            def _():
                mate(a, b).wait_send()
                mate_got(a, b)
    return begin, first, round_of, finish


def gather_kernel(zc, count, *refs):
    begin, first, round_of, finish = gather_events(zc, refs[:count], refs[count : 2 * count], refs[2 * count :])
    begin()
    for a in range(count):
        first(a)
    for a in range(count):
        for t in range(1, zc + 2):
            round_of(a, t)
    finish()


def gather_scratch(shards, zc):
    count = len(shards)
    comps = [pltpu.VMEM((rows * 2, s.shape[1]), s.dtype) for s, rows in shards]
    mines = [pltpu.VMEM(s.shape, s.dtype) for s, rows in shards]
    dma = pltpu.SemaphoreType.DMA
    sems = [dma((count, 2, zc)), dma((count, 2, zc)), dma((count, zc)), dma((count, 4 * zc)), dma((count,)), dma((count,)),
            dma((count, zc)), dma((count, zc)), dma((count, zc)), dma((count, zc)), dma((count, 4 * zc)), dma((count,))]
    return comps + mines + sems


def gather(shards, zc, n_dev):
    count = len(shards)
    return pl.pallas_call(
        functools.partial(gather_kernel, zc, count),
        out_shape=[jax.ShapeDtypeStruct((rows * n_dev, s.shape[1]), s.dtype) for s, rows in shards],
        in_specs=[pl.BlockSpec(memory_space=pltpu.VMEM)] * count,
        out_specs=[pl.BlockSpec(memory_space=pl.ANY)] * count,
        scratch_shapes=gather_scratch(shards, zc),
        compiler_params=pltpu.CompilerParams(collective_id=0, has_side_effects=True, vmem_limit_bytes=32 << 20),
        name="gather_weights",
    )(*[s for s, _ in shards])


def reduce_events(zc, g, out, rest):
    count = len(g)
    pos = Place(zc)
    z, c, d = pos.z, pos.c, pos.d
    loc = rest[:count]; rxp = rest[count:2 * count]; rxf = rest[2 * count:3 * count]
    rxl = rest[3 * count:4 * count]; rxr = rest[4 * count:5 * count]
    rxz = rest[5 * count:6 * count]
    fin = rest[6 * count:7 * count]; rxm = rest[7 * count:8 * count]
    (s_pair, r_pair, s_loc, s_ring, r_fwd, r_left, r_right, s_z, r_z, s_fin, r_fin) = rest[8 * count:]
    rows = [x.shape[0] // (4 * zc) for x in g]
    half = [x.shape[1] // 2 for x in g]
    mate_dev = pos.dev(c=1 - c)
    right_dev = pos.dev(d=pos.right); left_dev = pos.dev(d=pos.left)
    def remote(src, dst, ss, rs, dev):
        return pltpu.make_async_remote_copy(src_ref=src, dst_ref=dst, send_sem=ss, recv_sem=rs, device_id=dev, device_id_type=MESH)
    def strip(a, dd):
        return pl.ds(pl.multiple_of(dd * zc * rows[a], 16), zc * rows[a])
    def cols(a, core):
        return pl.ds(pl.multiple_of(core * half[a], 128), half[a])
    def pair(a, dd):
        return remote(g[a].at[strip(a, dd), cols(a, 1 - c)], rxp[a].at[strip(a, dd), :], s_pair.at[a, dd], r_pair.at[a, dd], mate_dev)
    def local(a, dd):
        return pltpu.make_async_copy(g[a].at[strip(a, dd), cols(a, c)], loc[a].at[strip(a, dd), :], s_loc.at[a, dd])
    def first_row(a, dd, zz):
        return (dd * zc + zz) * rows[a]
    def row(a, dd, zz):
        return pl.ds(pl.multiple_of(first_row(a, dd, zz), 16), rows[a])
    def slot(a, zz):
        return pl.ds(pl.multiple_of(zz * rows[a], 16), rows[a])
    def add(a, dst, terms):
        group = 16
        while rows[a] % (2 * group) == 0 and 2 * group * half[a] <= 32768:
            group *= 2
        @pl.loop(0, rows[a] // group)
        def _(t):
            total = None
            for ref, at in terms:
                v = ref[pl.ds(pl.multiple_of(at + t * group, 16), group), :].astype(F32)
                total = v if total is None else total + v
            ref, at = dst
            ref[pl.ds(pl.multiple_of(at + t * group, 16), group), :] = total.astype(ref.dtype)
    def pair_sum(a, dd, zz, extra=()):
        r = first_row(a, dd, zz)
        add(a, (loc[a], r), [(loc[a], r), (rxp[a], r)] + list(extra))
    def first_right(a, zz):
        return remote(loc[a].at[row(a, pos.opp, zz), :], rxf[a].at[slot(a, zz), :], s_ring.at[a, 0, zz], r_fwd.at[a, zz], right_dev)
    def first_left(a, zz):
        return remote(loc[a].at[row(a, pos.opp, zz), :], rxf[a].at[slot(a, zz), :], s_ring.at[a, 0, zz], r_fwd.at[a, zz], left_dev)
    def to_right(a, zz):
        return remote(loc[a].at[row(a, pos.right, zz), :], rxl[a].at[slot(a, zz), :], s_ring.at[a, 1, zz], r_left.at[a, zz], right_dev)
    def to_left(a, zz):
        return remote(loc[a].at[row(a, pos.left, zz), :], rxr[a].at[slot(a, zz), :], s_ring.at[a, 2, zz], r_right.at[a, zz], left_dev)
    def to_line(a, zt):
        return remote(loc[a].at[row(a, d, zt), :], rxz[a].at[slot(a, z), :], s_z.at[a, zt], r_z.at[a, z], pos.dev(z=zt))
    def from_line(a, zs):
        return remote(loc[a].at[row(a, d, zs), :], rxz[a].at[slot(a, zs), :], s_z.at[a, zs], r_z.at[a, zs], pos.dev(z=zs))
    def mate_rows(a):
        r2 = rows[a] // 2
        return pl.ds(pl.multiple_of((1 - c) * r2, 8), r2)
    def my_rows(a):
        r2 = rows[a] // 2
        return pl.ds(pl.multiple_of(c * r2, 8), r2)
    def final(a):
        return remote(fin[a].at[mate_rows(a), :], rxm[a], s_fin.at[a], r_fin.at[a], mate_dev)

    order = []
    for i in range(zc // 2):
        order += [zc - 1 - i, i]
    head = order[0]
    def begin():
        for a in range(count):
            for dd in (pos.opp, pos.right, pos.left):
                pair(a, dd).start(); local(a, dd).start()
        for a in range(count):
            pair(a, d).start(); local(a, d).start()
    def opposite(a, zz):
        if zz == head:
            pair(a, pos.opp).wait_recv(); local(a, pos.opp).wait()
        pair_sum(a, pos.opp, zz)
        (first_right if zz % 2 == 0 else first_left)(a, zz).start()
    def beside(a, zz):
        if zz % 2:
            pair_sum(a, pos.right, zz); to_right(a, zz).start()
        else:
            pair_sum(a, pos.left, zz); to_left(a, zz).start()
    def neighbours(a):
        for dd in (pos.right, pos.left):
            pair(a, dd).wait_recv(); local(a, dd).wait()
    def onward(a, zz):
        if zz % 2 == 0:
            first_right(a, zz).wait_recv()
            pair_sum(a, pos.right, zz, [(rxf[a], zz * rows[a])]); to_right(a, zz).start()
        else:
            first_left(a, zz).wait_recv()
            pair_sum(a, pos.left, zz, [(rxf[a], zz * rows[a])]); to_left(a, zz).start()
    def column(a, zz, dst, extra=()):
        r = first_row(a, d, zz)
        add(a, dst, [(loc[a], r), (rxp[a], r), (rxl[a], zz * rows[a]), (rxr[a], zz * rows[a])] + list(extra))
    def arrived(a, zz):
        if zz == head:
            pair(a, d).wait_recv(); local(a, d).wait()
        to_right(a, zz).wait_recv(); to_left(a, zz).wait_recv()
    def line(a, zt):
        @pl.when(z != zt)
        def _():
            column(a, zt, (loc[a], first_row(a, d, zt)))
            to_line(a, zt).start()
    def mine(a):
        others = [lax.rem(z + k, zc) for k in range(1, zc)]
        for o in others:
            from_line(a, o).wait_recv()
        column(a, z, (fin[a], 0), [(rxz[a], o * rows[a]) for o in others])
        final(a).start()
    def whole(a):
        out[a][:, cols(a, c)] = fin[a][my_rows(a), :]
        final(a).wait_recv()
        out[a][:, cols(a, 1 - c)] = rxm[a][...]
    def steps_of(a):
        call = functools.partial
        cuts = [order[: zc // 2], order[zc // 2 :]]
        stages = [[call(opposite, a, zz) for zz in order] + [call(neighbours, a)]]
        for n, cut in enumerate(cuts):
            before = cuts[n - 1] if n else []
            stages.append(
                [call(arrived, a, zz) for zz in before]
                + [call(onward, a, zz) for zz in cut]
                + [call(beside, a, zz) for zz in cut]
                + [call(line, a, zz) for zz in before]
            )
        stages.append([call(arrived, a, zz) for zz in cuts[-1]] + [call(line, a, zz) for zz in cuts[-1]])
        stages.append([call(mine, a)])
        return stages
    def all_steps():
        parts = [steps_of(a) for a in range(count)]
        depth = len(parts[0])
        steps = []
        for t in range(count + depth - 1):
            for a in range(count):
                if 0 <= t - a < depth:
                    steps += parts[a][t - a]
        return steps + [functools.partial(whole, a) for a in range(count)]
    def finish():
        for a in range(count):
            for dd in range(4):
                pair(a, dd).wait_send()
            for zz in range(zc):
                (first_right if zz % 2 == 0 else first_left)(a, zz).wait_send()
                to_right(a, zz).wait_send(); to_left(a, zz).wait_send()
                @pl.when(zz != z)
                def _():
                    to_line(a, zz).wait_send()
            final(a).wait_send()
    return pos, begin, all_steps, finish


def reduce_kernel(zc, count, *refs):
    g = refs[:count]; table = refs[count]
    out = refs[count + 1:2 * count + 1]; table_out = refs[2 * count + 1]
    tabs, s_tab, r_tab = refs[2 * count + 2 : 2 * count + 5]
    pos, begin, all_steps, finish = reduce_events(zc, g, out, refs[2 * count + 5 :])
    n_dev = 8 * zc
    me = pos.d * (2 * zc) + pos.w
    def device(o):
        return (o // (2 * zc), lax.rem(o, 2 * zc))
    barrier = pltpu.get_barrier_semaphore()
    @pl.loop(1, n_dev)
    def _(k):
        pl.semaphore_signal(barrier, inc=1, device_id=device(lax.rem(me + k, n_dev)), device_id_type=MESH)
    pl.semaphore_wait(barrier, n_dev - 1)
    def tab_copy(k):
        o = lax.rem(me + k, n_dev)
        return pltpu.make_async_remote_copy(src_ref=table, dst_ref=tabs.at[me], send_sem=s_tab.at[k], recv_sem=r_tab.at[me], device_id=device(o), device_id_type=MESH)
    def tab_got(k):
        o = lax.rem(me + k, n_dev)
        return pltpu.make_async_remote_copy(src_ref=table, dst_ref=tabs.at[o], send_sem=s_tab.at[k], recv_sem=r_tab.at[o], device_id=device(o), device_id_type=MESH)
    begin()
    @pl.loop(1, n_dev)
    def _(k):
        tab_copy(k).start()
    for step in all_steps():
        step()
    tabs[me] = table[...]
    @pl.loop(1, n_dev)
    def _(k):
        tab_got(k).wait_recv()
        tab_copy(k).wait_send()
    total = tabs[0]
    for k in range(1, n_dev):
        total = total + tabs[k]
    table_out[...] = total
    finish()


def reduce_scratch(grads, zc):
    count = len(grads)
    V = pltpu.VMEM
    rows = [x.shape[0] // (4 * zc) for x in grads]; half = [x.shape[1] // 2 for x in grads]
    scratch = [V((x.shape[0], h), BF) for x, h in zip(grads, half)] * 2
    for _ in range(4):
        scratch += [V((zc * r, h), BF) for r, h in zip(rows, half)]
    scratch += [V((r, h), F32) for r, h in zip(rows, half)]
    scratch += [V((r // 2, h), F32) for r, h in zip(rows, half)]
    dma = pltpu.SemaphoreType.DMA
    return scratch + [dma((count, 4)), dma((count, 4)), dma((count, 4)), dma((count, 3, zc))] + [dma((count, zc))] * 5 + [dma((count,)), dma((count,))]


def reduce_shapes(grads, n_dev):
    return [jax.ShapeDtypeStruct((x.shape[0] // n_dev, x.shape[1]), F32) for x in grads]


def reduce_scatter(grads, table, zc):
    count = len(grads)
    n_dev = 8 * zc
    dma = pltpu.SemaphoreType.DMA
    return pl.pallas_call(
        functools.partial(reduce_kernel, zc, count),
        out_shape=reduce_shapes(grads, n_dev) + [jax.ShapeDtypeStruct(table.shape, F32)],
        in_specs=[pl.BlockSpec(memory_space=pl.ANY)] * count + [pl.BlockSpec(memory_space=pltpu.VMEM)],
        out_specs=[pl.BlockSpec(memory_space=pltpu.VMEM)] * (count + 1),
        scratch_shapes=[pltpu.VMEM((n_dev,) + table.shape, F32), dma((n_dev,)), dma((n_dev,))] + reduce_scratch(grads, zc),
        compiler_params=pltpu.CompilerParams(collective_id=1, has_side_effects=True, vmem_limit_bytes=48 << 20),
        name="reduce_grads",
    )(*grads, table)


def bucket_of(n):
    far = jnp.zeros_like(n)
    dist = jnp.abs(n)
    for power_step in range(1, 8):
        far = far + (dist * dist >= 64 * 2**power_step).astype(jnp.int32)
    return jnp.where(n > 0, 16, 0) + jnp.where(dist < 8, dist, 8 + far)

def diagonal_onehot(doc_len, bucket_count):
    span = 2 * doc_len
    i = jnp.arange(span, dtype=jnp.int32)
    base = doc_len - 128
    n = base - jnp.where(i >= span - 127, i - span, i)
    inside = (n > -doc_len) & (n < doc_len)
    hot = (bucket_of(n)[:, None] == jnp.arange(bucket_count, dtype=jnp.int32)[None, :]) & inside[:, None]
    return hot.astype(F32)

def cols_dot(a, b):
    return lax.dot_general(a, b, (((1,), (1,)), ((), ())), preferred_element_type=F32)

def tiles_of(table, keys, q_from, q_len, doc_len):
    parts = []
    for kb in range(keys // 128):
        at = doc_len - 128 - 128 * kb + q_from
        parts.append(table[:, at : at + q_len])
    return jnp.concatenate(parts, axis=0) if len(parts) > 1 else parts[0]

def spread_steps(steps, first_slot, slots):
    plan = {}
    for n, step in enumerate(steps):
        at = min(slots - 1, first_slot + (n * (slots - first_slot)) // len(steps))
        plan.setdefault(at, []).append(step)
    return plan


def attend_kernel(doc_len, doc_count, block, zc, count, rows_ref, gains_ref, w_ref, diag_ref, mask_ref, *refs):
    shards = refs[:count]
    normed_ref, qkv_ref, ctx_ref, lse_ref, table_ref = refs[count : count + 5]
    outs = refs[count + 5 : 2 * count + 5]
    j = pl.program_id(0)
    span = 2 * doc_len
    hd = 64
    total = rows_ref.shape[0]
    rest = total - doc_count * doc_len
    places = [(m * doc_len, doc_len, q_at, block, None) for m in range(doc_count) for q_at in range(0, doc_len, block)]
    places += [(doc_count * doc_len + 128 * i, 128, 0, 128, i) for i in range(rest // 128)]
    slots = len(places)
    plan = {}
    if count:
        begin, first, round_of, finish = gather_events(zc, shards, outs, refs[2 * count + 5 :])
        steps = [functools.partial(round_of, a, t) for t in range(1, zc + 2) for a in range(count)]
        plan = spread_steps(steps, 2, slots * (rows_ref.shape[1] // 128))
    def now(i):
        for slot, steps in plan.items():
            if slot % slots == i:
                @pl.when(j == slot // slots)
                def _():
                    for step in steps:
                        step()
    @pl.when(j == 0)
    def _():
        if count:
            begin()
        for c in chunks_of(total, 4):
            x = rows_ref[c, :].astype(F32)
            normed_ref[c, :] = (x * inverse_rms(x) * gains_ref[0:1, :]).astype(BF)
        for a in range(count):
            first(a)
    for c in chunks_of(total, 4):
        qkv_ref[c, :] = dot(normed_ref[c, :], w_ref[...]).astype(BF)
    for h in range(2):
        wide = jnp.broadcast_to(diag_ref[0, h : h + 1, :], (128, span))
        table_ref[h] = pltpu.roll(wide, 0, 1, stride=1, stride_axis=0)[:, : span - 128]
    lane = lax.broadcasted_iota(jnp.int32, (1, 128), 1)
    def part(rows, keys, q_at, q_len, mask):
        q2 = qkv_ref[pl.ds(rows + q_at, q_len), 0:128]
        k2 = qkv_ref[pl.ds(rows, keys), 128:256]
        v2 = qkv_ref[pl.ds(rows, keys), 256:384]
        v2t = v2.astype(F32).T.astype(BF)
        outs = []
        for h in range(2):
            qm = jnp.where((lane < hd) == (h == 0), q2, jnp.zeros_like(q2))
            s = dot_nt(k2, qm) + tiles_of(table_ref.at[h], keys, q_at, q_len, doc_len)
            if mask is not None:
                s = jnp.where(mask_ref[mask] > 0, s, mask_fill)
            top = jnp.max(s, axis=0, keepdims=True)
            e = jnp.exp(s - top)
            total = jnp.sum(e, axis=0, keepdims=True)
            p = (e * (1.0 / total)).astype(BF)
            lse_ref[0, h : h + 1, pl.ds(rows + q_at, q_len)] = top + jnp.log(total)
            outs.append(dot(v2t[h * hd : (h + 1) * hd], p))
        ctx_ref[pl.ds(rows + q_at, q_len), :] = jnp.concatenate(outs, axis=0).T.astype(BF)
    for i, place in enumerate(places):
        now(i)
        part(*place)
    if count:
        @pl.when(j == pl.num_programs(0) - 1)
        def _():
            finish()


def attend(rows, gains, w_one, diag, mask, doc_len, doc_count, shards, zc, n_dev):
    total, width = rows.shape
    pairs = width // 128
    span = 2 * doc_len
    count = len(shards)
    once = pl.Buffered(1)
    remote = dict(collective_id=3, has_side_effects=True) if count else {}
    return pl.pallas_call(
        functools.partial(attend_kernel, doc_len, doc_count, 256, zc, count),
        grid=(pairs,),
        in_specs=[
            pl.BlockSpec((total, width), lambda j: (0, 0), pipeline_mode=once),
            pl.BlockSpec(gains.shape, lambda j: (0, 0)),
            pl.BlockSpec((width, 384), lambda j: (0, j)),
            pl.BlockSpec((1, 8, span), lambda j: (j, 0, 0)),
            pl.BlockSpec(mask.shape, lambda j: (0, 0, 0)),
        ] + [pl.BlockSpec(memory_space=pltpu.VMEM)] * count,
        out_specs=[
            pl.BlockSpec((total, width), lambda j: (0, 0), pipeline_mode=once),
            pl.BlockSpec((total, 384), lambda j: (0, j)),
            pl.BlockSpec((total, 128), lambda j: (0, j)),
            pl.BlockSpec((1, 8, total), lambda j: (j, 0, 0)),
            pl.BlockSpec((2, 128, span - 128), lambda j: (j, 0, 0)),
        ] + [pl.BlockSpec(memory_space=pl.ANY)] * count,
        out_shape=[
            jax.ShapeDtypeStruct((total, width), BF),
            jax.ShapeDtypeStruct((total, pairs * 384), BF),
            jax.ShapeDtypeStruct((total, width), BF),
            jax.ShapeDtypeStruct((pairs, 8, total), F32),
            jax.ShapeDtypeStruct((pairs * 2, 128, span - 128), F32),
        ] + [jax.ShapeDtypeStruct((r * n_dev, s.shape[1]), s.dtype) for s, r in shards],
        scratch_shapes=gather_scratch(shards, zc) if count else [],
        compiler_params=pltpu.CompilerParams(vmem_limit_bytes=48 << 20, **remote),
        name="attend",
    )(rows, gains, w_one, diag, mask, *[s for s, _ in shards])


def attend_back_kernel(doc_len, doc_count, block, zc, count, pairs_total, qkv_ref, do_ref, lse_ref, table_ref, mask_ref, *refs):
    grads = refs[:count]
    dqkv_ref, diag_ref = refs[count : count + 2]
    outs = refs[count + 2 : 2 * count + 2]
    acc = refs[2 * count + 2]
    j = pl.program_id(0)
    span = 2 * doc_len
    hd = 64
    rest = qkv_ref.shape[0] - doc_count * doc_len
    slots = doc_count * (doc_len // block) + rest // 128
    pairs = pairs_total
    plan = {}
    if count:
        pos, begin, all_steps, finish = reduce_events(zc, grads, outs, refs[2 * count + 3 :])
        plan = spread_steps(all_steps(), 1, slots * pairs)
        @pl.when(j == 0)
        def _():
            enter(pos)
            begin()
    slot = [0]
    def now():
        for at, steps in plan.items():
            if at % slots == slot[0]:
                @pl.when(j == at // slots)
                def _():
                    for step in steps:
                        step()
        slot[0] += 1
    acc[...] = jnp.zeros_like(acc)
    lane = lax.broadcasted_iota(jnp.int32, (1, 128), 1)
    def part(rows, keys, q_len, mask):
        k2 = qkv_ref[pl.ds(rows, keys), 128:256]
        v2 = qkv_ref[pl.ds(rows, keys), 256:384]
        k2t = k2.astype(F32).T.astype(BF)
        dk = jnp.zeros((keys, 128), F32)
        dv = jnp.zeros((keys, 128), F32)
        for q_at in range(0, keys, q_len):
            now()
            qr = pl.ds(rows + q_at, q_len)
            q2 = qkv_ref[qr, 0:128]
            do2 = do_ref[qr, :]
            outs = []
            for h in range(2):
                mine = (lane < hd) == (h == 0)
                qm = jnp.where(mine, q2, jnp.zeros_like(q2))
                dom = jnp.where(mine, do2, jnp.zeros_like(do2))
                s = dot_nt(k2, qm) + tiles_of(table_ref.at[h], keys, q_at, q_len, doc_len)
                if mask is not None:
                    s = jnp.where(mask_ref[mask] > 0, s, mask_fill)
                p = jnp.exp(s - lse_ref[0, h : h + 1, qr])
                dp = dot_nt(v2, dom)
                ds = p * (dp - jnp.sum(p * dp, axis=0, keepdims=True))
                for kb in range(keys // 128):
                    at = doc_len - 128 - 128 * kb + q_at
                    acc[h, :, at : at + q_len] += ds[128 * kb : 128 * (kb + 1)]
                low = ds.astype(BF)
                dv += dot(p.astype(BF), dom)
                dk += dot(low, qm)
                outs.append(dot(k2t[h * hd : (h + 1) * hd], low))
            dqkv_ref[qr, 0:128] = jnp.concatenate(outs, axis=0).T.astype(BF)
        dqkv_ref[pl.ds(rows, keys), 128:256] = dk.astype(BF)
        dqkv_ref[pl.ds(rows, keys), 256:384] = dv.astype(BF)
    for m in range(doc_count):
        part(m * doc_len, doc_len, block, None)
    for i in range(rest // 128):
        part(doc_count * doc_len + 128 * i, 128, 128, i)
    for h in range(2):
        eight = acc[h, 0:8]
        for g in range(1, 16):
            eight = eight + pltpu.roll(acc[h, 8 * g : 8 * g + 8], span - 8 * g, 1)
        one = eight[0:1]
        for r in range(1, 8):
            one = one + pltpu.roll(eight, span - r, 1)[r : r + 1]
        diag_ref[0, h : h + 1, :] = one
    if count:
        @pl.when(j == pl.num_programs(0) - 1)
        def _():
            finish()


def attend_back(qkv, d_ctx, lse, table, mask, doc_len, doc_count, grads, zc, n_dev):
    total, width = qkv.shape
    pairs = width // 384
    span = 2 * doc_len
    count = len(grads)
    remote = dict(collective_id=4, has_side_effects=True) if count else {}
    shapes = reduce_shapes(grads, n_dev)
    return pl.pallas_call(
        functools.partial(attend_back_kernel, doc_len, doc_count, 256, zc, count, pairs),
        grid=(pairs,),
        in_specs=[
            pl.BlockSpec((total, 384), lambda j: (0, j)),
            pl.BlockSpec((total, 128), lambda j: (0, j)),
            pl.BlockSpec((1, 8, total), lambda j: (j, 0, 0)),
            pl.BlockSpec((2, 128, span - 128), lambda j: (j, 0, 0)),
            pl.BlockSpec(mask.shape, lambda j: (0, 0, 0)),
        ] + [pl.BlockSpec(memory_space=pl.ANY)] * count,
        out_specs=[
            pl.BlockSpec((total, 384), lambda j: (0, j)),
            pl.BlockSpec((1, 8, span), lambda j: (j, 0, 0)),
        ] + [pl.BlockSpec(memory_space=pltpu.VMEM)] * count,
        out_shape=[
            jax.ShapeDtypeStruct((total, width), BF),
            jax.ShapeDtypeStruct((pairs, 8, span), F32),
        ] + shapes,
        scratch_shapes=[pltpu.VMEM((2, 128, span), F32)] + (reduce_scratch(grads, zc) if count else []),
        compiler_params=pltpu.CompilerParams(vmem_limit_bytes=60 << 20, **remote),
        name="attend_back",
    )(qkv, d_ctx, lse, table, mask, *grads)


def query_mask(lengths, slots):
    per = 128 // slots
    live = (jnp.arange(slots, dtype=jnp.int32)[None, :] < lengths[:, None]).reshape(-1, 128)
    owner = jnp.arange(128, dtype=jnp.int32) // slots
    same = owner[:, None] == owner[None, :]
    return (live[:, :, None] & same[None]).astype(F32)

def pair_columns(w):
    q, k, v = w
    rows, width = q.shape
    pack = jnp.stack([x.reshape(rows, width // 128, 128) for x in (q, k, v)], axis=2)
    return pack.reshape(rows, 3 * width)


def score_kernel(peers, doc_len, slots, emb_ref, picks_ref, live_ref, goal_ref, loss_ref, d_emb_ref,
                 q_own, q_all, p_all, weighed, totals, pool_out, pool_in, grad_out, grad_in, dq_out, dq_in, docs_t, d_docs,
                 s_q, r_q, s_p, r_p, s_pool, r_pool, s_grad, r_grad, s_dq, r_dq):
    dp = lax.axis_index("dp"); me = lax.axis_index("wide")
    tokens = q_own.shape[0]
    feat = emb_ref.shape[1]
    half = tokens // 2
    scale = feat ** -0.5
    barrier = pltpu.get_barrier_semaphore()
    def other(k):
        return lax.rem(me + k, peers)
    def each(fn):
        @pl.loop(1, peers)
        def _(k):
            fn(other(k))
    each(lambda o: pl.semaphore_signal(barrier, inc=1, device_id=(dp, o), device_id_type=MESH))
    q_own[...] = emb_ref[2 * doc_len :, :]
    q_all[me] = q_own[...]
    p_all[me] = picks_ref[...]
    pl.semaphore_wait(barrier, peers - 1)
    def send(src, dst, ss, rs, o):
        return pltpu.make_async_remote_copy(src_ref=src, dst_ref=dst, send_sem=ss, recv_sem=rs, device_id=(dp, o), device_id_type=MESH)
    def picks_to(o): return send(picks_ref, p_all.at[me], s_p.at[o], r_p.at[me], o)
    def picks_from(o): return send(picks_ref, p_all.at[o], s_p.at[o], r_p.at[o], o)
    def q_to(o): return send(q_own, q_all.at[me], s_q.at[o], r_q.at[me], o)
    def q_from(o): return send(q_own, q_all.at[o], s_q.at[o], r_q.at[o], o)
    def pool_to(o): return send(pool_out.at[o], pool_in.at[me], s_pool.at[o], r_pool.at[me], o)
    def pool_from(o): return send(pool_out.at[o], pool_in.at[o], s_pool.at[o], r_pool.at[o], o)
    def grad_to(o): return send(grad_out.at[o], grad_in.at[me], s_grad.at[o], r_grad.at[me], o)
    def grad_from(o): return send(grad_out.at[o], grad_in.at[o], s_grad.at[o], r_grad.at[o], o)
    def dq_to(o): return send(dq_out.at[o], dq_in.at[me], s_dq.at[o], r_dq.at[me], o)
    def dq_from(o): return send(dq_out.at[o], dq_in.at[o], s_dq.at[o], r_dq.at[o], o)
    def started(o):
        picks_to(o).start(); q_to(o).start()
    each(started)
    docs2 = jnp.concatenate([emb_ref[0:doc_len, :], emb_ref[doc_len : 2 * doc_len, :]], axis=1)
    docs_t[...] = docs2.astype(F32).T.astype(BF)
    row = lax.broadcasted_iota(jnp.int32, (tokens, 1), 0)
    lane = lax.broadcasted_iota(jnp.int32, (1, tokens), 1)
    def two_docs(o):
        q = q_all[o]
        none = jnp.zeros_like(q)
        return jnp.concatenate([jnp.where(row < half, q, none), jnp.where(row < half, none, q)], axis=1)
    chunk = 64
    base = me * doc_len
    def forward(o):
        picks = p_all[o] - base
        found = jnp.zeros((1, tokens), F32)
        weight = jnp.zeros((1, tokens), F32)
        s = lax.dot_general(docs2, two_docs(o), (((1,), (1,)), ((), ())), preferred_element_type=F32) * scale
        e = jnp.exp(s)
        for at in range(0, doc_len, chunk):
            place = lax.broadcasted_iota(jnp.int32, (chunk, tokens), 0) + at
            count = jnp.zeros((chunk, tokens), jnp.int32)
            for k in range(picks.shape[0]):
                count = count + (picks[k : k + 1, :] == place).astype(jnp.int32)
            multiple = count.astype(F32)
            w = multiple * e[at : at + chunk]
            weighed[o, at : at + chunk, :] = w
            found = found + jnp.sum(multiple, axis=0, keepdims=True)
            weight = weight + jnp.sum(w, axis=0, keepdims=True)
        weight = weight + (found == 0).astype(F32)
        totals[o] = jnp.broadcast_to(weight, (8, tokens))
        pool_out[o] = jnp.broadcast_to(jnp.log(weight), (8, tokens))
    def forward_peer(o):
        picks_from(o).wait_recv(); q_from(o).wait_recv()
        forward(o)
        pool_to(o).start()
    forward(me)
    pool_in[me] = pool_out[me]
    each(forward_peer)
    each(lambda o: pool_from(o).wait_recv())
    pooled = pool_in[:, 0, :]
    mine = picks_ref[...]
    hits = []
    for w in range(peers):
        inside = ((mine >= w * doc_len) & (mine < (w + 1) * doc_len)).astype(F32)
        hits.append(jnp.max(inside, axis=0, keepdims=True))
    hit = jnp.concatenate(hits, axis=0)
    live = live_ref[0:1, :]
    own_row = lax.broadcasted_iota(jnp.int32, (tokens, tokens), 0) // slots
    own_col = lax.broadcasted_iota(jnp.int32, (tokens, tokens), 1) // slots
    same = (own_row == own_col).astype(F32)
    def per_query(v):
        return jnp.dot(v, same, precision=lax.Precision.HIGHEST, preferred_element_type=F32)
    divisor = jnp.maximum(per_query(hit * live), 1.0)
    logits = score_scale * per_query(pooled * live) / divisor
    top = jnp.max(logits, axis=0, keepdims=True)
    shifted = jnp.exp(logits - top)
    total = jnp.sum(shifted, axis=0, keepdims=True)
    doc_id = lax.broadcasted_iota(jnp.int32, (peers, tokens), 0)
    chosen = (doc_id == goal_ref[0:1, :]).astype(F32)
    loss = top + jnp.log(total) - jnp.sum(chosen * logits, axis=0, keepdims=True)
    loss_ref[...] = jnp.broadcast_to(loss, loss_ref.shape)
    d_pooled = score_scale * (shifted / total - chosen) / divisor * live
    for w in range(peers):
        grad_out[w] = jnp.broadcast_to(d_pooled[w : w + 1], (8, tokens))
    each(lambda o: grad_to(o).start())
    grad_in[me] = grad_out[me]
    d_docs[...] = jnp.zeros_like(d_docs)
    def backward(o):
        factor = grad_in[o][0:1] / totals[o][0:1] * scale
        d_raw = (weighed[o] * factor).astype(BF)
        d_docs[...] += jnp.dot(d_raw, two_docs(o), preferred_element_type=F32)
        both = jnp.dot(docs_t[...], d_raw, preferred_element_type=F32)
        d_q = jnp.where(lane < half, both[0:feat], both[feat : 2 * feat])
        dq_out[o] = d_q.T.astype(BF)
    def backward_peer(o):
        grad_from(o).wait_recv()
        backward(o)
        dq_to(o).start()
    each(backward_peer)
    backward(me)
    d_emb_ref[0:doc_len, :] = d_docs[:, 0:feat].astype(BF)
    d_emb_ref[doc_len : 2 * doc_len, :] = d_docs[:, feat : 2 * feat].astype(BF)
    dq_in[me] = dq_out[me]
    each(lambda o: dq_from(o).wait_recv())
    total_q = dq_in[0].astype(F32)
    for w in range(1, peers):
        total_q = total_q + dq_in[w].astype(F32)
    d_emb_ref[2 * doc_len :, :] = total_q.astype(BF)
    def sent(o):
        picks_to(o).wait_send(); q_to(o).wait_send(); pool_to(o).wait_send(); grad_to(o).wait_send(); dq_to(o).wait_send()
    each(sent)

def score(emb, picks, live, goal, doc_len, slots, peers):
    tokens = picks.shape[1]
    feat = emb.shape[1]
    V = pltpu.VMEM
    dma = pltpu.SemaphoreType.DMA
    return pl.pallas_call(
        functools.partial(score_kernel, peers, doc_len, slots),
        out_shape=[jax.ShapeDtypeStruct((8, tokens), F32), jax.ShapeDtypeStruct(emb.shape, BF)],
        in_specs=[pl.BlockSpec(memory_space=pltpu.VMEM)] * 4,
        out_specs=[pl.BlockSpec(memory_space=pltpu.VMEM)] * 2,
        scratch_shapes=[
            V((tokens, feat), BF), V((peers, tokens, feat), BF), V((peers,) + picks.shape, jnp.int32),
            V((peers, doc_len, tokens), F32), V((peers, 8, tokens), F32),
            V((peers, 8, tokens), F32), V((peers, 8, tokens), F32), V((peers, 8, tokens), F32), V((peers, 8, tokens), F32),
            V((peers, tokens, feat), BF), V((peers, tokens, feat), BF), V((2 * feat, doc_len), BF), V((doc_len, 2 * feat), F32),
        ] + [dma((peers,))] * 10,
        compiler_params=pltpu.CompilerParams(collective_id=2, has_side_effects=True, vmem_limit_bytes=48 << 20),
        name="score",
    )(emb, picks, live, goal)


GELU_SCALE = 0.7978845608028654
GELU_CUBE = 0.044715

def dot(a, b):
    return jnp.dot(a, b, preferred_element_type=F32)

def dot_nt(a, b):
    return lax.dot_general(a, b, (((1,), (1,)), ((), ())), preferred_element_type=F32)

def dot_tn(a, b):
    return lax.dot_general(a, b, (((0,), (0,)), ((), ())), preferred_element_type=F32)

def inverse_rms(v):
    return lax.rsqrt(jnp.mean(v * v, axis=-1, keepdims=True) + eps_norm)

def chunks_of(total, parts):
    size = total // parts
    return [slice(i * size, (i + 1) * size) for i in range(parts)]

def ffn_kernel(parts, rows_ref, ctx_ref, wo_ref, wgu_ref, wd_ref, wp_ref, gains_ref, hidden_ref, n2_ref, gu_ref, lo_ref, ne_ref, emb_ref):
    j = pl.program_id(0)
    block = wd_ref.shape[0]
    chunks = chunks_of(rows_ref.shape[0], parts)
    @pl.when(j == 0)
    def _():
        for c in chunks:
            h = rows_ref[c, :].astype(F32) + dot(ctx_ref[c, :], wo_ref[...])
            hidden_ref[c, :] = h
            lo_ref[c, :] = h
            n2_ref[c, :] = (h * inverse_rms(h) * gains_ref[1:2, :]).astype(BF)
    for c in chunks:
        gu = dot(n2_ref[c, :], wgu_ref[...])
        gu_ref[c, :] = gu
        g = gu[:, :block]
        t = jnp.tanh(GELU_SCALE * (g + GELU_CUBE * (g * g * g)))
        act = (0.5 * g * (1.0 + t)) * gu[:, block:]
        lo_ref[c, :] += dot(act.astype(BF), wd_ref[...])
    @pl.when(j == pl.num_programs(0) - 1)
    def _():
        for c in chunks:
            lo = lo_ref[c, :]
            ne = (lo * inverse_rms(lo) * gains_ref[2:3, :]).astype(BF)
            ne_ref[c, :] = ne
            emb_ref[c, :] = dot(ne, wp_ref[...]).astype(BF)

def ffn(rows, ctx, w_one, w_gu, w_down, gains, p_size, block):
    total, width = rows.shape
    ff = w_down.shape[0]
    once = pl.Buffered(1)
    full = lambda cols, at=0: pl.BlockSpec((total, cols), lambda j: (0, 0), pipeline_mode=once)
    return pl.pallas_call(
        functools.partial(ffn_kernel, 4),
        grid=(ff // block,),
        in_specs=[
            full(width), full(width),
            pl.BlockSpec((width, width), lambda j: (0, 3), pipeline_mode=once),
            pl.BlockSpec((width, 2 * block), lambda j: (0, j)),
            pl.BlockSpec((block, width), lambda j: (j, 0)),
            pl.BlockSpec((width, p_size), lambda j: (0, 4 * width // p_size), pipeline_mode=once),
            pl.BlockSpec(gains.shape, lambda j: (0, 0)),
        ],
        out_specs=[full(width), full(width), pl.BlockSpec((total, 2 * block), lambda j: (0, j)), full(width), full(width), full(p_size)],
        out_shape=[
            jax.ShapeDtypeStruct((total, width), F32), jax.ShapeDtypeStruct((total, width), BF),
            jax.ShapeDtypeStruct((total, 2 * ff), F32), jax.ShapeDtypeStruct((total, width), F32),
            jax.ShapeDtypeStruct((total, width), BF), jax.ShapeDtypeStruct((total, p_size), BF),
        ],
        compiler_params=pltpu.CompilerParams(vmem_limit_bytes=56 << 20),
        name="feed_forward",
    )(rows, ctx, w_one, w_gu, w_down, w_one, gains)

def rms_pull(v, gain, upstream):
    inv = inverse_rms(v)
    scaled = upstream * gain
    d_gain = jnp.sum(upstream * (v * inv), axis=0, keepdims=True)
    inner = jnp.mean(scaled * v, axis=-1, keepdims=True)
    return inv * scaled - v * (inv * inv * inv * inner), d_gain

def ffn_back_kernel(parts, de_ref, lo_ref, ne_ref, hidden_ref, n2_ref, ctx_ref, wo_ref, wp_ref, gains_ref, gu_ref, wgu_ref, wd_ref,
                    dgu_w_ref, dd_w_ref, dp_w_ref, do_w_ref, dh_ref, dctx_ref, dgain_ref, dl_ref, low_ref, n2t_ref, acc_ref, dhl_ref):
    j = pl.program_id(0)
    block = wd_ref.shape[0]
    chunks = chunks_of(lo_ref.shape[0], parts)
    @pl.when(j == 0)
    def _():
        dgain_ref[...] = jnp.zeros_like(dgain_ref)
        for c in chunks:
            up = dot_nt(de_ref[c, :], wp_ref[...])
            dl, dg = rms_pull(lo_ref[c, :], gains_ref[2:3, :], up)
            dl_ref[c, :] = dl
            low_ref[c, :] = dl.astype(BF)
            dgain_ref[2:3, :] += dg
        dp_w_ref[...] = dot_tn(ne_ref[...], de_ref[...]).astype(BF)
        n2t_ref[...] = n2_ref[...].T
        acc_ref[...] = jnp.zeros_like(acc_ref)
    acts, dgus = [], []
    for c in chunks:
        da = dot_nt(low_ref[c, :], wd_ref[...])
        g = gu_ref[c, :block]
        u = gu_ref[c, block:]
        t = jnp.tanh(GELU_SCALE * (g + GELU_CUBE * (g * g * g)))
        cdf = 0.5 * (1.0 + t)
        gel = g * cdf
        acts.append((gel * u).astype(BF))
        slope = cdf + (0.5 * GELU_SCALE) * g * (1.0 - t * t) * (1.0 + (3.0 * GELU_CUBE) * (g * g))
        dgu = jnp.concatenate([(da * u * slope).astype(BF), (da * gel).astype(BF)], axis=1)
        dgus.append(dgu)
        acc_ref[c, :] += dot_nt(dgu, wgu_ref[...])
    dgu_w_ref[...] = dot(n2t_ref[...], jnp.concatenate(dgus, axis=0)).astype(BF)
    dd_w_ref[...] = dot_tn(jnp.concatenate(acts, axis=0), low_ref[...]).astype(BF)
    @pl.when(j == pl.num_programs(0) - 1)
    def _():
        for c in chunks:
            dv, dg = rms_pull(hidden_ref[c, :], gains_ref[1:2, :], acc_ref[c, :])
            dh = dl_ref[c, :] + dv
            dh_ref[c, :] = dh
            dhl = dh.astype(BF)
            dhl_ref[c, :] = dhl
            dgain_ref[1:2, :] += dg
            dctx_ref[c, :] = dot_nt(dhl, wo_ref[...]).astype(BF)
        do_w_ref[...] = dot_tn(ctx_ref[...], dhl_ref[...]).astype(BF)

def ffn_back(d_emb, lo, ne, hidden, n2, ctx, w_one, w_gu, w_down, gains, gu, p_size, block):
    total, width = lo.shape
    ff = w_down.shape[0]
    once = pl.Buffered(1)
    full = lambda cols: pl.BlockSpec((total, cols), lambda j: (0, 0), pipeline_mode=once)
    fixed = lambda shape: pl.BlockSpec(shape, lambda j: (0, 0), pipeline_mode=once)
    V = pltpu.VMEM
    return pl.pallas_call(
        functools.partial(ffn_back_kernel, 4),
        grid=(ff // block,),
        in_specs=[
            full(p_size), full(width), full(width), full(width), full(width), full(width),
            pl.BlockSpec((width, width), lambda j: (0, 3), pipeline_mode=once),
            pl.BlockSpec((width, p_size), lambda j: (0, 4 * width // p_size), pipeline_mode=once),
            fixed(gains.shape),
            pl.BlockSpec((total, 2 * block), lambda j: (0, j)),
            pl.BlockSpec((width, 2 * block), lambda j: (0, j)),
            pl.BlockSpec((block, width), lambda j: (j, 0)),
        ],
        out_specs=[
            pl.BlockSpec((width, 2 * block), lambda j: (0, j)),
            pl.BlockSpec((block, width), lambda j: (j, 0)),
            fixed((width, p_size)), fixed((width, width)), full(width), full(width), fixed((8, width)),
        ],
        out_shape=[
            jax.ShapeDtypeStruct((width, 2 * ff), BF), jax.ShapeDtypeStruct((ff, width), BF),
            jax.ShapeDtypeStruct((width, p_size), BF), jax.ShapeDtypeStruct((width, width), BF),
            jax.ShapeDtypeStruct((total, width), F32), jax.ShapeDtypeStruct((total, width), BF),
            jax.ShapeDtypeStruct((8, width), F32),
        ],
        scratch_shapes=[V((total, width), F32), V((total, width), BF), V((width, total), BF), V((total, width), F32), V((total, width), BF)],
        compiler_params=pltpu.CompilerParams(vmem_limit_bytes=60 << 20),
        name="feed_forward_back",
    )(d_emb, lo, ne, hidden, n2, ctx, w_one, w_one, gains, gu, w_gu, w_down)

def gate_up_columns(gate, up, block):
    rows, ff = gate.shape
    return jnp.stack([gate.reshape(rows, -1, block), up.reshape(rows, -1, block)], axis=2).reshape(rows, 2 * ff)


def contract_rows(left_mat, right_mat):
    return lax.dot_general(
        left_mat, right_mat, (((0,), (0,)), ((), ())), preferred_element_type=jnp.float32
    )


def contract_cols(left_mat, right_mat):
    return lax.dot_general(
        left_mat, right_mat, (((1,), (1,)), ((), ())), preferred_element_type=jnp.float32
    )


def matmul(left_mat, right_mat):
    return jnp.dot(left_mat, right_mat, preferred_element_type=jnp.float32)


def rms_forward(values, gain_vec):
    inverse = lax.rsqrt(jnp.mean(values * values, axis=-1, keepdims=True) + eps_norm)
    return (values * inverse * gain_vec, inverse)


def rms_backward(values, inverse, gain_vec, upstream):
    scaled = upstream * gain_vec
    gain_grad = jnp.sum(upstream * values * inverse, axis=0)
    inner_mean = jnp.mean(scaled * values, axis=-1, keepdims=True)
    return (inverse * scaled - values * inverse * inverse * inverse * inner_mean, gain_grad)


def two_level(shards):
    return (
        lax.axis_size("dp") == 4
        and lax.axis_size("wide") % 4 == 0
        and all(s.shape[0] % 8 == 0 for s in shards)
    )


def padded(shards):
    return [(jnp.pad(s, ((0, -s.shape[0] % 16), (0, 0))), s.shape[0]) for s in shards]


def gathered(shards):
    if not two_level(shards):
        return [lax.all_gather(s, ("dp", "wide"), axis=0, tiled=True) for s in shards]
    zc = lax.axis_size("wide") // 2
    return gather(padded(shards), zc, 8 * zc)


def scattered(grads, table):
    n_dev = lax.axis_size("dp") * lax.axis_size("wide")
    if not two_level([g[: g.shape[0] // n_dev] for g in grads]):
        shards = [
            lax.psum_scatter(g.astype(F32), ("dp", "wide"), scatter_dimension=0, tiled=True)
            for g in grads
        ]
        return [*shards, lax.psum(table, ("dp", "wide"))]
    flat = table.reshape(-1)
    packed = jnp.pad(flat, (0, -flat.shape[0] % 1024)).reshape(-1, 128)
    *shards, packed = reduce_scatter(grads, packed, lax.axis_size("wide") // 2)
    return [*shards, packed.reshape(-1)[: flat.shape[0]].reshape(table.shape)]


def local(
    doc_tokens,
    query_tokens,
    query_lengths,
    retrieved,
    targets,
    q_weight,
    k_weight,
    v_weight,
    o_weight,
    gate_weight,
    up_weight,
    down_weight,
    proj_weight,
    attn_gain,
    ffn_gain,
    final_gain,
    rel_bias,
):
    micro_count, _, doc_len, width = doc_tokens.shape
    slots = query_tokens.shape[2]
    doc_rows = micro_count * doc_len
    wide_count = lax.axis_size("wide")
    p_size = proj_weight.shape[1]
    bucket_count, head_count = rel_bias.shape
    pairs = width // 128
    ff_block = 256
    gains = jnp.stack([attn_gain, ffn_gain, final_gain], axis=1)
    shard_one = jnp.concatenate(
        [pair_columns((q_weight, k_weight, v_weight)), o_weight, proj_weight, jnp.pad(gains, ((0, 0), (0, 125)))],
        axis=1,
    )
    ffn_shards = [gate_up_columns(gate_weight, up_weight, ff_block), down_weight]
    beside = two_level([shard_one, *ffn_shards])
    (w_one,) = gathered([shard_one])
    w_qkv = w_one[:, : 3 * width]
    gains = jnp.pad(w_one[:, 4 * width + p_size :].astype(F32).T[:3], ((0, 5), (0, 0)))
    hot = diagonal_onehot(doc_len, bucket_count)
    diag = jnp.dot(rel_bias.astype(F32).T, hot.T, precision=top_precision)
    diag = jnp.pad(diag.reshape(pairs, 2, -1), ((0, 0), (0, 6), (0, 0)))
    mask = query_mask(query_lengths.reshape(-1), slots)
    rows_low = jnp.concatenate(
        [doc_tokens.reshape(doc_rows, width), query_tokens.reshape(-1, width)], axis=0
    )
    normed, qkv, context, lse, table, *ffn_weights = attend(
        rows_low,
        gains,
        w_one,
        diag,
        mask,
        doc_len,
        micro_count,
        padded(ffn_shards) if beside else [],
        wide_count // 2,
        lax.axis_size("dp") * wide_count,
    )
    w_gu, w_down = ffn_weights if beside else gathered(ffn_shards)
    hidden, normed_two, gate_up, layer_out, normed_end, embedded = ffn(
        rows_low, context, w_one, w_gu, w_down, gains, p_size, ff_block
    )
    picks = retrieved.reshape(-1, retrieved.shape[3]).T
    tokens = picks.shape[1]
    live = (jnp.arange(slots, dtype=jnp.int32)[None, :] < query_lengths.reshape(-1)[:, None]).astype(F32)
    live = jnp.broadcast_to(live.reshape(1, tokens), (8, tokens))
    goal = jnp.broadcast_to(jnp.repeat(targets.reshape(-1), slots)[None, :], (8, tokens))
    loss_rows, d_embedded = score(embedded, picks, live, goal, doc_len, slots, wide_count)
    losses_out = loss_rows[0].reshape(-1, slots)[:, 0].reshape(targets.shape)
    gu_grad, down_grad, proj_grad, out_grad, d_hidden, d_context, gain_grads = ffn_back(
        d_embedded, layer_out, normed_end, hidden, normed_two, context, w_one, w_gu, w_down, gains, gate_up, p_size, ff_block
    )
    d_qkv, d_diag, *ffn_sums = attend_back(
        qkv,
        d_context,
        lse,
        table,
        mask,
        doc_len,
        micro_count,
        [gu_grad, down_grad] if beside else [],
        wide_count // 2,
        lax.axis_size("dp") * wide_count,
    )
    table_grad = jnp.dot(hot.T, d_diag[:, :2].reshape(head_count, -1).T, precision=top_precision)
    qkv_grad = contract_rows(normed, d_qkv).astype(BF)
    d_normed = contract_cols(d_qkv, w_qkv)
    rows = rows_low.astype(F32)
    d_rows, attn_gain_grad = rms_backward(rows, inverse_rms(rows), gains[0], d_normed)
    d_rows = d_hidden + d_rows
    gain_cols = jnp.pad(jnp.stack([attn_gain_grad, gain_grads[1], gain_grads[2]], axis=1), ((0, 0), (0, 125)))
    one_grad = jnp.concatenate([qkv_grad, out_grad, proj_grad, gain_cols.astype(BF)], axis=1)
    if beside:
        s_gu, s_down = ffn_sums
        s_one, s_table = scattered([one_grad], table_grad)
    else:
        s_one, s_gu, s_down, s_table = scattered([one_grad, gu_grad, down_grad], table_grad)
    apart = s_one[:, : 3 * width].reshape(-1, pairs, 3, 128)
    halves = s_gu.reshape(s_gu.shape[0], -1, 2, ff_block)
    s_last = s_one[:, 4 * width :]
    return (
        losses_out,
        d_rows[:doc_rows].reshape(doc_tokens.shape),
        d_rows[doc_rows:].reshape(query_tokens.shape),
        apart[:, :, 0].reshape(-1, width),
        apart[:, :, 1].reshape(-1, width),
        apart[:, :, 2].reshape(-1, width),
        s_one[:, 3 * width : 4 * width],
        halves[:, :, 0].reshape(s_gu.shape[0], -1),
        halves[:, :, 1].reshape(s_gu.shape[0], -1),
        s_down,
        s_last[:, :p_size],
        s_last[:, p_size],
        s_last[:, p_size + 1],
        s_last[:, p_size + 2],
        s_table,
    )


def solution(mesh):
    placed = (
        P(None, ("dp", "wide"), None, None),
        P(None, ("dp", "wide"), None, None),
        P(None, ("dp", "wide")),
        P(None, ("dp", "wide"), None, None),
        P(None, ("dp", "wide")),
        P(("dp", "wide"), None),
        P(("dp", "wide"), None),
        P(("dp", "wide"), None),
        P(("dp", "wide"), None),
        P(("dp", "wide"), None),
        P(("dp", "wide"), None),
        P(("dp", "wide"), None),
        P(("dp", "wide"), None),
        P(("dp", "wide")),
        P(("dp", "wide")),
        P(("dp", "wide")),
        P(),
    )
    return jax.shard_map(
        local,
        mesh=mesh,
        in_specs=placed,
        out_specs=(
            P(None, ("dp", "wide")),
            P(None, ("dp", "wide"), None, None),
            P(None, ("dp", "wide"), None, None),
            P(("dp", "wide"), None),
            P(("dp", "wide"), None),
            P(("dp", "wide"), None),
            P(("dp", "wide"), None),
            P(("dp", "wide"), None),
            P(("dp", "wide"), None),
            P(("dp", "wide"), None),
            P(("dp", "wide"), None),
            P(("dp", "wide")),
            P(("dp", "wide")),
            P(("dp", "wide")),
            P(),
        ),
        check_vma=False,
    )
```

```python
import functools

import jax
import jax.numpy as jnp
from jax import lax
from jax.experimental import pallas as pl
from jax.experimental.pallas import tpu as pltpu
from jax.sharding import PartitionSpec as P

eps_norm = 1e-06
score_scale = 6.0
mask_fill = -1000000000.0
top_precision = lax.Precision.HIGHEST
F32 = jnp.float32
BF = jnp.bfloat16
VMEM_ALL = 62 << 20
FF_BLOCK = 512


MESH = pl.DeviceIdType.MESH

def gray(p):
    return p + (p // 2) * (1 - 2 * (p % 2))

class Place:
    def __init__(self, zc):
        self.zc = zc
        d = lax.axis_index("dp"); w = lax.axis_index("wide")
        self.d, self.w = d, w
        self.z, self.c = w // 2, w % 2
        p = gray(d)
        self.right = gray((p + 1) % 4); self.left = gray((p + 3) % 4); self.opp = gray((p + 2) % 4)
    def dev(self, d=None, z=None, c=None):
        d = self.d if d is None else d
        z = self.z if z is None else z
        c = self.c if c is None else c
        return (d, z * 2 + c)

def enter(pos, wide=False):
    barrier = pltpu.get_barrier_semaphore()
    def greet(dev):
        pl.semaphore_signal(barrier, inc=1, device_id=dev, device_id_type=MESH)
    greet(pos.dev(d=pos.right))
    greet(pos.dev(d=pos.left))
    if wide:
        @pl.loop(1, 2 * pos.zc)
        def _(k):
            greet((pos.d, lax.rem(pos.w + k, 2 * pos.zc)))
        pl.semaphore_wait(barrier, 1 + 2 * pos.zc)
    else:
        greet(pos.dev(c=1 - pos.c))
        @pl.loop(1, pos.zc)
        def _(k):
            greet(pos.dev(z=lax.rem(pos.z + k, pos.zc)))
        pl.semaphore_wait(barrier, 2 + pos.zc)


def gather_events(zc, shard, out, rest):
    count = len(shard)
    pos = Place(zc)
    comp = rest[:count]; mine = rest[count:2 * count]
    (s_col, s_ring, s_fwd, s_mate, s_pair, s_own, r_col, r_left, r_right, r_opp, r_mate, r_pair) = rest[2 * count:]
    z, c, d = pos.z, pos.c, pos.d
    rows = [o.shape[0] // (4 * zc) for o in out]
    half = [o.shape[1] // 2 for o in out]

    def part(a, ref, blk, core):
        return ref.at[pl.ds(pl.multiple_of(blk * rows[a], 16), rows[a]), pl.ds(pl.multiple_of(core * half[a], 128), half[a])]
    def own(a, core):
        return comp[a].at[:, pl.ds(pl.multiple_of(core * half[a], 128), half[a])]
    def rdma(a, src, blk, dev, ss, rs):
        return pltpu.make_async_remote_copy(src_ref=src, dst_ref=part(a, out[a], blk, c), send_sem=ss, recv_sem=rs, device_id=dev, device_id_type=MESH)
    def blk(dd, zz):
        return dd * zc + zz
    mate_dev = pos.dev(c=1 - c)
    def pair(a):
        return pltpu.make_async_remote_copy(src_ref=shard[a], dst_ref=mine[a], send_sem=s_pair.at[a], recv_sem=r_pair.at[a], device_id=mate_dev, device_id_type=MESH)
    def keep(a):
        return pltpu.make_async_copy(comp[a], out[a].at[pl.ds(pl.multiple_of(blk(d, z) * rows[a], 16), rows[a]), :], s_own.at[a])
    def up(a, src, zz):
        return rdma(a, src, blk(d, zz), pos.dev(z=lax.rem(z + 1, zc)), s_col.at[a, 0, zz], r_col.at[a, zz])
    def down(a, src, zz):
        return rdma(a, src, blk(d, zz), pos.dev(z=lax.rem(z + zc - 1, zc)), s_col.at[a, 1, zz], r_col.at[a, zz])
    def right(a, src, zz):
        return rdma(a, src, blk(d, zz), pos.dev(d=pos.right), s_ring.at[a, 0, zz], r_left.at[a, zz])
    def left(a, src, zz):
        return rdma(a, src, blk(d, zz), pos.dev(d=pos.left), s_ring.at[a, 1, zz], r_right.at[a, zz])
    def fwd_right(a, zz):
        b = blk(pos.left, zz)
        return rdma(a, part(a, out[a], b, c), b, pos.dev(d=pos.right), s_fwd.at[a, zz], r_opp.at[a, zz])
    def fwd_left(a, zz):
        b = blk(pos.right, zz)
        return rdma(a, part(a, out[a], b, c), b, pos.dev(d=pos.left), s_fwd.at[a, zz], r_opp.at[a, zz])
    def mate(a, b):
        return rdma(a, part(a, out[a], b, c), b, mate_dev, s_mate.at[a, b], r_mate.at[a, b])
    def got(a, b, sem):
        return rdma(a, part(a, out[a], b, c), b, mate_dev, s_mate.at[a, b], sem).wait_recv()
    def mate_got(a, b):
        piece = part(a, out[a], b, 1 - c)
        pltpu.make_async_remote_copy(src_ref=piece, dst_ref=piece, send_sem=s_mate.at[a, b], recv_sem=r_mate.at[a, b], device_id=mate_dev, device_id_type=MESH).wait_recv()

    def begin(wide=False):
        enter(pos, wide)
        for a in range(count):
            pair(a).start()
    def first(a):
        pair(a).wait_recv()
        r2 = rows[a] // 2
        step = 256 if half[a] * 2 % 256 == 0 else 128
        @pl.loop(0, half[a] * 2 // step)
        def _(t):
            cols = pl.ds(pl.multiple_of(t * step, 128), step)
            mn = shard[a][:, cols].astype(jnp.float32)[:r2]
            ot = mine[a][:, cols].astype(jnp.float32)[:r2]
            first = jnp.where(c == 0, mn, ot)
            second = jnp.where(c == 0, ot, mn)
            comp[a][:, cols] = jnp.concatenate([first, second], axis=0).astype(jnp.bfloat16)
        right(a, own(a, c), z).start()
        left(a, own(a, c), z).start()
        pl.when(z < zc - 1)(lambda: up(a, own(a, c), z).start())
        pl.when(z > 0)(lambda: down(a, own(a, c), z).start())
        keep(a).start()

    def column(a, j):
        @pl.when(z - j >= 0)
        def _():
            zz = z - j
            got(a, blk(d, zz), r_col.at[a, zz])
            src = part(a, out[a], blk(d, zz), c)
            pl.when(z < zc - 1)(lambda: up(a, src, zz).start())
            right(a, src, zz).start(); left(a, src, zz).start()
            mate(a, blk(d, zz)).start()
        @pl.when(z + j < zc)
        def _():
            zz = z + j
            got(a, blk(d, zz), r_col.at[a, zz])
            src = part(a, out[a], blk(d, zz), c)
            pl.when(z > 0)(lambda: down(a, src, zz).start())
            right(a, src, zz).start(); left(a, src, zz).start()
            mate(a, blk(d, zz)).start()
    def ring_one(a, zz):
        got(a, blk(pos.left, zz), r_left.at[a, zz])
        pl.when(zz % 2 == 0)(lambda: fwd_right(a, zz).start())
        mate(a, blk(pos.left, zz)).start()
        got(a, blk(pos.right, zz), r_right.at[a, zz])
        pl.when(zz % 2 == 1)(lambda: fwd_left(a, zz).start())
        mate(a, blk(pos.right, zz)).start()
    def opp_one(a, zz):
        got(a, blk(pos.opp, zz), r_opp.at[a, zz])
        mate(a, blk(pos.opp, zz)).start()
    def spread(fn, a, j):
        if j == 0:
            fn(a, z); return
        pl.when(z - j >= 0)(lambda: fn(a, z - j))
        pl.when(z + j < zc)(lambda: fn(a, z + j))
    def rounds(a):
        call = functools.partial
        steps = []
        for t in range(1, zc + 2):
            if t < zc:
                steps.append(call(column, a, t))
            if t <= zc:
                steps.append(call(spread, ring_one, a, t - 1))
            if t >= 2:
                steps.append(call(spread, opp_one, a, t - 2))
        return steps
    def finish():
        for a in range(count):
            finish_one(a)
    def finish_one(a):
        pair(a).wait_send(); keep(a).wait()
        @pl.loop(0, zc)
        def _(zz):
            src = part(a, out[a], blk(d, zz), c)
            right(a, src, zz).wait_send(); left(a, src, zz).wait_send()
            pl.when((z < zc - 1) & (zz <= z))(lambda: up(a, src, zz).wait_send())
            pl.when((z > 0) & (zz >= z))(lambda: down(a, src, zz).wait_send())
            fwd_right(a, zz).wait_send()
        @pl.loop(0, 4 * zc)
        def _(b):
            @pl.when(b != blk(d, z))
            def _():
                mate(a, b).wait_send()
                mate_got(a, b)
    return pos, begin, first, rounds, finish


def count_places(picks, first, out_ref, size):
    tokens = picks.shape[1]
    chunk = 64
    @pl.loop(0, size // chunk)
    def _(t):
        at = pl.multiple_of(t * chunk, chunk)
        place = lax.broadcasted_iota(jnp.int32, (chunk, tokens), 0) + (first + at)
        count = jnp.zeros((chunk, tokens), jnp.int32)
        for k in range(picks.shape[0]):
            count = count + (picks[k : k + 1, :] == place).astype(jnp.int32)
        out_ref[pl.ds(at, chunk), :] = count.astype(F32).astype(BF)


def count_kernel(doc_len, all_ref, out_ref):
    count_places(all_ref[0], lax.axis_index("wide") * doc_len, out_ref.at[0], doc_len)


def count_all(picks, doc_len, peers):
    everyone = lax.all_gather(picks, "wide", axis=0)
    shape = (1,) + picks.shape
    return pl.pallas_call(
        functools.partial(count_kernel, doc_len),
        grid=(peers,),
        in_specs=[pl.BlockSpec(shape, lambda i: (i, 0, 0))],
        out_specs=pl.BlockSpec((1, doc_len, picks.shape[1]), lambda i: (i, 0, 0)),
        out_shape=jax.ShapeDtypeStruct((peers, doc_len, picks.shape[1]), BF),
        name="count",
    )(everyone)


def put_columns(ref, at, x):
    spare = ref.shape[0] - x.shape[0]
    full = jnp.concatenate([x.astype(F32), jnp.zeros((spare, x.shape[1]), F32)], axis=0) if spare else x
    ref[:, at : at + x.shape[1]] = full.astype(ref.dtype)


def gather_kernel(zc, doc_len, q_ref, k_ref, v_ref, o_ref, p_ref, g_ref, picks_ref, full_ref, counts_ref, shard_ref, p_all, s_p, r_p, *rest):
    count = 1
    pos, begin, first, rounds, finish = gather_events(zc, [shard_ref], [full_ref], rest)
    width = q_ref.shape[1]
    for i in range(width // 128):
        for n, ref in enumerate((q_ref, k_ref, v_ref)):
            put_columns(shard_ref, 384 * i + 128 * n, ref[:, 128 * i : 128 * i + 128])
    put_columns(shard_ref, 3 * width, o_ref[...])
    put_columns(shard_ref, 4 * width, p_ref[...])
    put_columns(shard_ref, 4 * width + p_ref.shape[1], g_ref[...].T[: q_ref.shape[0]])
    peers = 2 * zc
    def picks_copy(k, there):
        o = lax.rem(pos.w + k, peers)
        slot = pos.w if there else o
        return pltpu.make_async_remote_copy(src_ref=picks_ref, dst_ref=p_all.at[slot], send_sem=s_p.at[o], recv_sem=r_p.at[slot], device_id=(pos.d, o), device_id_type=MESH)
    part = doc_len // 2
    def counted(k, h):
        o = lax.rem(pos.w + k, peers)
        if k and not h:
            picks_copy(k, False).wait_recv()
        picks = p_all[o] if k else picks_ref[...]
        count_places(picks, pos.w * doc_len + h * part, counts_ref.at[o, pl.ds(h * part, part)], part)
    begin(True)
    @pl.loop(1, peers)
    def _(k):
        picks_copy(k, True).start()
    for a in range(count):
        first(a)
    steps = [step for a in range(count) for step in rounds(a)]
    pieces = [(k, h) for k in range(peers) for h in range(2)]
    for n, step in enumerate(steps):
        for k, h in pieces[len(pieces) * n // len(steps) : len(pieces) * (n + 1) // len(steps)]:
            counted(k, h)
        step()
    @pl.loop(1, peers)
    def _(k):
        picks_copy(k, True).wait_send()
    finish()


def gather_scratch(shapes, zc):
    count = len(shapes)
    comps = [pltpu.VMEM((2 * rows, cols), BF) for rows, cols in shapes]
    mines = [pltpu.VMEM((rows + -rows % 16, cols), BF) for rows, cols in shapes]
    dma = pltpu.SemaphoreType.DMA
    sems = [dma((count, 2, zc)), dma((count, 2, zc)), dma((count, zc)), dma((count, 4 * zc)), dma((count,)), dma((count,)),
            dma((count, zc)), dma((count, zc)), dma((count, zc)), dma((count, zc)), dma((count, 4 * zc)), dma((count,))]
    return comps + mines + sems


def gather(weights, gains, picks, doc_len, zc, n_dev):
    peers = 2 * zc
    rows = weights[0].shape[0]
    cols = sum(w.shape[1] for w in weights) + 128
    dma = pltpu.SemaphoreType.DMA
    whole = pl.BlockSpec(memory_space=pltpu.VMEM)
    return pl.pallas_call(
        functools.partial(gather_kernel, zc, doc_len),
        out_shape=[jax.ShapeDtypeStruct((rows * n_dev, cols), BF), jax.ShapeDtypeStruct((peers, doc_len, picks.shape[1]), BF)],
        in_specs=[whole] * (len(weights) + 2),
        out_specs=[pl.BlockSpec(memory_space=pl.ANY), whole],
        scratch_shapes=[pltpu.VMEM((rows + -rows % 16, cols), BF), pltpu.VMEM((peers,) + picks.shape, jnp.int32), dma((peers,)), dma((peers,))]
        + gather_scratch([(rows, cols)], zc),
        compiler_params=pltpu.CompilerParams(collective_id=0, has_side_effects=True, vmem_limit_bytes=VMEM_ALL),
        name="gather_weights",
    )(*weights, gains, picks)


def reduce_events(zc, g, out, rest):
    count = len(g)
    pos = Place(zc)
    z, c, d = pos.z, pos.c, pos.d
    loc = rest[:count]; rxp = rest[count:2 * count]; rxf = rest[2 * count:3 * count]
    rxl = rest[3 * count:4 * count]; rxr = rest[4 * count:5 * count]
    rxz = rest[5 * count:6 * count]
    fin = rest[6 * count:7 * count]; rxm = rest[7 * count:8 * count]
    (s_pair, r_pair, s_loc, s_ring, r_fwd, r_left, r_right, s_z, r_z, s_fin, r_fin) = rest[8 * count:]
    rows = [x.shape[0] // (4 * zc) for x in g]
    half = [x.shape[1] // 2 for x in g]
    mate_dev = pos.dev(c=1 - c)
    right_dev = pos.dev(d=pos.right); left_dev = pos.dev(d=pos.left)
    def remote(src, dst, ss, rs, dev):
        return pltpu.make_async_remote_copy(src_ref=src, dst_ref=dst, send_sem=ss, recv_sem=rs, device_id=dev, device_id_type=MESH)
    def strip(a, dd):
        return pl.ds(pl.multiple_of(dd * zc * rows[a], 16), zc * rows[a])
    def cols(a, core):
        return pl.ds(pl.multiple_of(core * half[a], 128), half[a])
    def pair(a, dd):
        return remote(g[a].at[strip(a, dd), cols(a, 1 - c)], rxp[a].at[strip(a, dd), :], s_pair.at[a, dd], r_pair.at[a, dd], mate_dev)
    def local(a, dd):
        return pltpu.make_async_copy(g[a].at[strip(a, dd), cols(a, c)], loc[a].at[strip(a, dd), :], s_loc.at[a, dd])
    def first_row(a, dd, zz):
        return (dd * zc + zz) * rows[a]
    def row(a, dd, zz):
        return pl.ds(pl.multiple_of(first_row(a, dd, zz), 16), rows[a])
    def slot(a, zz):
        return pl.ds(pl.multiple_of(zz * rows[a], 16), rows[a])
    def add(a, dst, terms):
        group = 16
        while rows[a] % (2 * group) == 0 and 2 * group * half[a] <= 32768:
            group *= 2
        @pl.loop(0, rows[a] // group)
        def _(t):
            total = None
            for ref, at in terms:
                v = ref[pl.ds(pl.multiple_of(at + t * group, 16), group), :].astype(F32)
                total = v if total is None else total + v
            ref, at = dst
            ref[pl.ds(pl.multiple_of(at + t * group, 16), group), :] = total.astype(ref.dtype)
    def pair_sum(a, dd, zz, extra=()):
        r = first_row(a, dd, zz)
        add(a, (loc[a], r), [(loc[a], r), (rxp[a], r)] + list(extra))
    def first_right(a, zz):
        return remote(loc[a].at[row(a, pos.opp, zz), :], rxf[a].at[slot(a, zz), :], s_ring.at[a, 0, zz], r_fwd.at[a, zz], right_dev)
    def first_left(a, zz):
        return remote(loc[a].at[row(a, pos.opp, zz), :], rxf[a].at[slot(a, zz), :], s_ring.at[a, 0, zz], r_fwd.at[a, zz], left_dev)
    def to_right(a, zz):
        return remote(loc[a].at[row(a, pos.right, zz), :], rxl[a].at[slot(a, zz), :], s_ring.at[a, 1, zz], r_left.at[a, zz], right_dev)
    def to_left(a, zz):
        return remote(loc[a].at[row(a, pos.left, zz), :], rxr[a].at[slot(a, zz), :], s_ring.at[a, 2, zz], r_right.at[a, zz], left_dev)
    def to_line(a, zt):
        return remote(loc[a].at[row(a, d, zt), :], rxz[a].at[slot(a, z), :], s_z.at[a, zt], r_z.at[a, z], pos.dev(z=zt))
    def from_line(a, zs):
        return remote(loc[a].at[row(a, d, zs), :], rxz[a].at[slot(a, zs), :], s_z.at[a, zs], r_z.at[a, zs], pos.dev(z=zs))
    def mate_rows(a):
        r2 = rows[a] // 2
        return pl.ds(pl.multiple_of((1 - c) * r2, 8), r2)
    def my_rows(a):
        r2 = rows[a] // 2
        return pl.ds(pl.multiple_of(c * r2, 8), r2)
    def final(a):
        return remote(fin[a].at[mate_rows(a), :], rxm[a], s_fin.at[a], r_fin.at[a], mate_dev)

    order = []
    for i in range(zc // 2):
        order += [zc - 1 - i, i]
    head = order[0]
    def begin():
        for a in range(count):
            for dd in (pos.opp, pos.right, pos.left):
                pair(a, dd).start(); local(a, dd).start()
        for a in range(count):
            pair(a, d).start(); local(a, d).start()
    def opposite(a, zz):
        if zz == head:
            pair(a, pos.opp).wait_recv(); local(a, pos.opp).wait()
        pair_sum(a, pos.opp, zz)
        (first_right if zz % 2 == 0 else first_left)(a, zz).start()
    def beside(a, zz):
        if zz % 2:
            pair_sum(a, pos.right, zz); to_right(a, zz).start()
        else:
            pair_sum(a, pos.left, zz); to_left(a, zz).start()
    def neighbours(a):
        for dd in (pos.right, pos.left):
            pair(a, dd).wait_recv(); local(a, dd).wait()
    def onward(a, zz):
        if zz % 2 == 0:
            first_right(a, zz).wait_recv()
            pair_sum(a, pos.right, zz, [(rxf[a], zz * rows[a])]); to_right(a, zz).start()
        else:
            first_left(a, zz).wait_recv()
            pair_sum(a, pos.left, zz, [(rxf[a], zz * rows[a])]); to_left(a, zz).start()
    def column(a, zz, dst, extra=()):
        r = first_row(a, d, zz)
        add(a, dst, [(loc[a], r), (rxp[a], r), (rxl[a], zz * rows[a]), (rxr[a], zz * rows[a])] + list(extra))
    def arrived(a, zz):
        if zz == head:
            pair(a, d).wait_recv(); local(a, d).wait()
        to_right(a, zz).wait_recv(); to_left(a, zz).wait_recv()
    def line(a, zt):
        @pl.when(z != zt)
        def _():
            column(a, zt, (loc[a], first_row(a, d, zt)))
            to_line(a, zt).start()
    def mine(a):
        others = [lax.rem(z + k, zc) for k in range(1, zc)]
        for o in others:
            from_line(a, o).wait_recv()
        column(a, z, (fin[a], 0), [(rxz[a], o * rows[a]) for o in others])
        final(a).start()
    def whole(a):
        out[a][:, cols(a, c)] = fin[a][my_rows(a), :]
        final(a).wait_recv()
        out[a][:, cols(a, 1 - c)] = rxm[a][...]
    def steps_of(a):
        call = functools.partial
        cuts = [order[: zc // 2], order[zc // 2 :]]
        stages = [[call(opposite, a, zz) for zz in order] + [call(neighbours, a)]]
        for n, cut in enumerate(cuts):
            before = cuts[n - 1] if n else []
            stages.append(
                [call(arrived, a, zz) for zz in before]
                + [call(onward, a, zz) for zz in cut]
                + [call(beside, a, zz) for zz in cut]
                + [call(line, a, zz) for zz in before]
            )
        stages.append([call(arrived, a, zz) for zz in cuts[-1]] + [call(line, a, zz) for zz in cuts[-1]])
        stages.append([call(mine, a)])
        return stages
    def all_steps():
        parts = [steps_of(a) for a in range(count)]
        depth = len(parts[0])
        groups = []
        for t in range(count + depth - 1):
            group = []
            for a in range(count):
                if 0 <= t - a < depth:
                    group += parts[a][t - a]
            groups.append(group)
        return groups + [[functools.partial(whole, a) for a in range(count)]]
    def finish():
        for a in range(count):
            for dd in range(4):
                pair(a, dd).wait_send()
            for zz in range(zc):
                (first_right if zz % 2 == 0 else first_left)(a, zz).wait_send()
                to_right(a, zz).wait_send(); to_left(a, zz).wait_send()
                @pl.when(zz != z)
                def _():
                    to_line(a, zz).wait_send()
            final(a).wait_send()
    return pos, begin, all_steps, finish


ROW_BLOCK = 128


def input_grad(dqkv_ref, w_ref, rows_ref, dh_ref, gains_ref, dx_ref):
    up = dot_nt(dqkv_ref[...], w_ref[...])
    dv, _ = rms_pull(rows_ref[...].astype(F32), gains_ref[0:1, :], up)
    dx_ref[...] = dh_ref[...] + dv


def reduce_kernel(zc, count, rows_total, dqkv_ref, w_ref, rows_ref, dh_ref, gains_ref, *refs):
    if not count:
        input_grad(dqkv_ref, w_ref, rows_ref, dh_ref, gains_ref, refs[0])
        return
    i = pl.program_id(0)
    g = refs[:count]; table = refs[count]
    dx_ref = refs[count + 1]
    refs = refs[1:]
    out = refs[count + 1 : 2 * count + 1]
    table_out, tabs, s_tab, r_tab = refs[2 * count + 1 : 2 * count + 5]
    pos, begin, all_steps, finish = reduce_events(zc, g, out, refs[2 * count + 5 :])
    n_dev = 8 * zc
    me = pos.d * (2 * zc) + pos.w
    def device(o):
        return (o // (2 * zc), lax.rem(o, 2 * zc))
    def tab_copy(k):
        o = lax.rem(me + k, n_dev)
        return pltpu.make_async_remote_copy(src_ref=table, dst_ref=tabs.at[me], send_sem=s_tab.at[k], recv_sem=r_tab.at[me], device_id=device(o), device_id_type=MESH)
    def tab_got(k):
        o = lax.rem(me + k, n_dev)
        return pltpu.make_async_remote_copy(src_ref=table, dst_ref=tabs.at[o], send_sem=s_tab.at[k], recv_sem=r_tab.at[o], device_id=device(o), device_id_type=MESH)
    def enter_all():
        barrier = pltpu.get_barrier_semaphore()
        @pl.loop(1, n_dev)
        def _(k):
            pl.semaphore_signal(barrier, inc=1, device_id=device(lax.rem(me + k, n_dev)), device_id_type=MESH)
        pl.semaphore_wait(barrier, n_dev - 1)
        begin()
        @pl.loop(1, n_dev)
        def _(k):
            tab_copy(k).start()
    def leave():
        tabs[me] = table[...]
        @pl.loop(1, n_dev)
        def _(k):
            tab_got(k).wait_recv()
            tab_copy(k).wait_send()
        total = tabs[0]
        for k in range(1, n_dev):
            total = total + tabs[k]
        table_out[...] = total
        finish()
    blocks = pl.num_programs(0)
    @pl.when(i == 0)
    def _():
        enter_all()
    input_grad(dqkv_ref, w_ref, rows_ref, dh_ref, gains_ref, dx_ref)
    groups = all_steps()
    early, late = groups[: len(groups) - 2], groups[len(groups) - 2 :]
    places = max(1, rows_total // ROW_BLOCK - 1)
    for n, group in enumerate(early):
        @pl.when(i == min(places, (n * places) // len(early)))
        def _():
            for step in group:
                step()
    @pl.when(i == blocks - 1)
    def _():
        for group in late:
            for step in group:
                step()
        leave()


def reduce_scratch(grads, zc):
    count = len(grads)
    V = pltpu.VMEM
    rows = [x.shape[0] // (4 * zc) for x in grads]; half = [x.shape[1] // 2 for x in grads]
    scratch = [V((x.shape[0], h), BF) for x, h in zip(grads, half)] * 2
    for _ in range(4):
        scratch += [V((zc * r, h), BF) for r, h in zip(rows, half)]
    scratch += [V((r, h), F32) for r, h in zip(rows, half)]
    scratch += [V((r // 2, h), F32) for r, h in zip(rows, half)]
    dma = pltpu.SemaphoreType.DMA
    return scratch + [dma((count, 4)), dma((count, 4)), dma((count, 4)), dma((count, 3, zc))] + [dma((count, zc))] * 5 + [dma((count,)), dma((count,))]


def reduce_shapes(grads, n_dev):
    return [jax.ShapeDtypeStruct((x.shape[0] // n_dev, x.shape[1]), F32) for x in grads]


def reduce_scatter(dqkv, w_one, rows, d_hidden, gains, grads, table, zc):
    count = len(grads)
    n_dev = 8 * zc
    total, width = rows.shape
    dma = pltpu.SemaphoreType.DMA
    block = lambda cols: pl.BlockSpec((ROW_BLOCK, cols), lambda i: (i, 0))
    whole = pl.BlockSpec(memory_space=pltpu.VMEM)
    remote = dict(collective_id=1, has_side_effects=True) if count else {}
    extra = reduce_shapes(grads, n_dev) + [jax.ShapeDtypeStruct(table.shape, F32)] if count else []
    scratch = [pltpu.VMEM((n_dev,) + table.shape, F32), dma((n_dev,)), dma((n_dev,))] + reduce_scratch(grads, zc) if count else []
    return pl.pallas_call(
        functools.partial(reduce_kernel, zc, count, total),
        grid=(total // ROW_BLOCK,),
        out_shape=[jax.ShapeDtypeStruct(rows.shape, F32)] + extra,
        in_specs=[
            block(dqkv.shape[1]),
            pl.BlockSpec((width, dqkv.shape[1]), lambda i: (0, 0), pipeline_mode=pl.Buffered(1)),
            block(width), block(width),
            pl.BlockSpec(gains.shape, lambda i: (0, 0)),
        ] + ([pl.BlockSpec(memory_space=pl.ANY)] * count + [whole] if count else []),
        out_specs=[block(width)] + [whole] * len(extra),
        scratch_shapes=scratch,
        compiler_params=pltpu.CompilerParams(vmem_limit_bytes=VMEM_ALL, **remote),
        name="reduce_grads",
    )(dqkv, w_one, rows, d_hidden, gains, *([*grads, table] if count else []))


def apart_kernel(layouts, docs_in, queries_in, *refs):
    count = len(layouts)
    docs_ref, queries_ref = refs[count : count + 2]
    outs = list(refs[count + 2 :])
    docs_ref[...] = docs_in[...]
    @pl.when(pl.program_id(0) == 0)
    def _():
        queries_ref[...] = queries_in[...]
        for ref, layout in zip(refs[:count], layouts):
            for pieces in layout:
                out = outs.pop(0)
                to = 0
                for start, size in pieces:
                    out[:, to : to + size] = ref[:, start : start + size]
                    to += size


def apart(dx, sums, layouts, doc_rows):
    total, width = dx.shape
    rest = total - doc_rows
    shapes = [jax.ShapeDtypeStruct((doc_rows, width), F32), jax.ShapeDtypeStruct((rest, width), F32)]
    shapes += [
        jax.ShapeDtypeStruct((x.shape[0], sum(size for _, size in pieces)), F32)
        for x, layout in zip(sums, layouts)
        for pieces in layout
    ]
    fixed = lambda x: pl.BlockSpec(x.shape, lambda i: (0, 0), pipeline_mode=pl.Buffered(1))
    block = pl.BlockSpec((doc_rows // 4, width), lambda i: (i, 0))
    return pl.pallas_call(
        functools.partial(apart_kernel, layouts),
        grid=(4,),
        out_shape=shapes,
        in_specs=[block, pl.BlockSpec((rest, width), lambda i: (doc_rows // rest, 0), pipeline_mode=pl.Buffered(1))] + [fixed(x) for x in sums],
        out_specs=[block] + [fixed(x) for x in shapes[1:]],
        compiler_params=pltpu.CompilerParams(vmem_limit_bytes=VMEM_ALL),
        name="apart",
    )(dx, dx, *sums)


def bucket_of(n):
    far = jnp.zeros_like(n)
    dist = jnp.abs(n)
    for power_step in range(1, 8):
        far = far + (dist * dist >= 64 * 2**power_step).astype(jnp.int32)
    return jnp.where(n > 0, 16, 0) + jnp.where(dist < 8, dist, 8 + far)

def diagonal_onehot(doc_len, bucket_count):
    span = 2 * doc_len
    i = jnp.arange(span, dtype=jnp.int32)
    base = doc_len - 128
    n = base - jnp.where(i >= span - 127, i - span, i)
    inside = (n > -doc_len) & (n < doc_len)
    hot = (bucket_of(n)[:, None] == jnp.arange(bucket_count, dtype=jnp.int32)[None, :]) & inside[:, None]
    return hot.astype(F32)

def cols_dot(a, b):
    return lax.dot_general(a, b, (((1,), (1,)), ((), ())), preferred_element_type=F32)

def tiles_of(table, keys, q_from, q_len, doc_len):
    parts = []
    for kb in range(keys // 128):
        at = doc_len - 128 - 128 * kb + q_from
        parts.append(table[:, at : at + q_len])
    return jnp.concatenate(parts, axis=0) if len(parts) > 1 else parts[0]

def spread_steps(steps, first_slot, slots):
    plan = {}
    for n, step in enumerate(steps):
        at = min(slots - 1, first_slot + (n * (slots - first_slot)) // len(steps))
        plan.setdefault(at, []).append(step)
    return plan


def attend_kernel(doc_len, doc_count, block, zc, count, docs_ref, queries_ref, gain_ref, w_ref, diag_ref, mask_ref, *refs):
    raw = refs[: 3 if count else 0]
    at = len(raw)
    rows_ref, gains_ref, normed_ref, qkv_ref, ctx_ref, lse_ref, table_ref = refs[at : at + 7]
    outs = refs[at + 7 : at + 7 + count]
    shards = refs[at + 7 + count : at + 7 + 2 * count]
    scratch = refs[at + 7 + 2 * count :]
    j = pl.program_id(0)
    span = 2 * doc_len
    hd = 64
    total = rows_ref.shape[0]
    rest = total - doc_count * doc_len
    places = [(m * doc_len, doc_len, q_at, block, None) for m in range(doc_count) for q_at in range(0, doc_len, block)]
    places += [(doc_count * doc_len + 128 * i, 128, 0, 128, i) for i in range(rest // 128)]
    slots = len(places)
    plan = {}
    if count:
        _, begin, first, rounds, finish = gather_events(zc, shards, outs, scratch)
        every = [rounds(a) for a in range(count)]
        steps = [step for same in zip(*every) for step in same]
        plan = spread_steps(steps, 2, slots * (rows_ref.shape[1] // 128))
    def now(i):
        for slot, steps in plan.items():
            if slot % slots == i:
                @pl.when(j == slot // slots)
                def _():
                    for step in steps:
                        step()
    @pl.when(j == 0)
    def _():
        gains_ref[...] = gain_ref[...].astype(F32).T[0:8]
        if count:
            gate_ref, up_ref, down_ref = raw
            ff = gate_ref.shape[1]
            size = FF_BLOCK
            for i in range(ff // size):
                put_columns(shards[0], 2 * size * i, gate_ref[:, size * i : size * i + size])
                put_columns(shards[0], 2 * size * i + size, up_ref[:, size * i : size * i + size])
            put_columns(shards[1], 0, down_ref[...])
            begin()
        rows_ref[0 : docs_ref.shape[0], :] = docs_ref[...]
        rows_ref[docs_ref.shape[0] :, :] = queries_ref[...]
        for c in chunks_of(total, 4):
            x = rows_ref[c, :].astype(F32)
            normed_ref[c, :] = (x * inverse_rms(x) * gains_ref[0:1, :]).astype(BF)
        for a in range(count):
            first(a)
    for c in chunks_of(total, 4):
        qkv_ref[c, :] = dot(normed_ref[c, :], w_ref[...]).astype(BF)
    for h in range(2):
        wide = jnp.broadcast_to(diag_ref[0, h : h + 1, :], (128, span))
        table_ref[h] = pltpu.roll(wide, 0, 1, stride=1, stride_axis=0)[:, : span - 128]
    lane = lax.broadcasted_iota(jnp.int32, (1, 128), 1)
    def part(rows, keys, q_at, q_len, mask):
        q2 = qkv_ref[pl.ds(rows + q_at, q_len), 0:128]
        k2 = qkv_ref[pl.ds(rows, keys), 128:256]
        v2 = qkv_ref[pl.ds(rows, keys), 256:384]
        v2t = v2.astype(F32).T.astype(BF)
        outs = []
        for h in range(2):
            qm = jnp.where((lane < hd) == (h == 0), q2, jnp.zeros_like(q2))
            s = dot_nt(k2, qm) + tiles_of(table_ref.at[h], keys, q_at, q_len, doc_len)
            if mask is not None:
                s = jnp.where(mask_ref[mask] > 0, s, mask_fill)
            top = jnp.max(s, axis=0, keepdims=True)
            e = jnp.exp(s - top)
            total = jnp.sum(e, axis=0, keepdims=True)
            p = (e * (1.0 / total)).astype(BF)
            lse_ref[0, h : h + 1, pl.ds(rows + q_at, q_len)] = top + jnp.log(total)
            outs.append(dot(v2t[h * hd : (h + 1) * hd], p))
        ctx_ref[pl.ds(rows + q_at, q_len), :] = jnp.concatenate(outs, axis=0).T.astype(BF)
    for i, place in enumerate(places):
        now(i)
        part(*place)
    if count:
        @pl.when(j == pl.num_programs(0) - 1)
        def _():
            finish()


def attend(docs, queries, w_one, diag, mask, doc_len, doc_count, weights, zc, n_dev):
    width = docs.shape[1]
    total = docs.shape[0] + queries.shape[0]
    pairs = width // 128
    span = 2 * doc_len
    once = pl.Buffered(1)
    whole = pl.BlockSpec(memory_space=pltpu.VMEM)
    shapes = []
    if weights:
        shapes = [(weights[0].shape[0], 2 * weights[0].shape[1]), weights[2].shape]
    count = len(shapes)
    remote = dict(collective_id=3, has_side_effects=True) if count else {}
    fixed = lambda shape: pl.BlockSpec(shape, lambda j: (0, 0), pipeline_mode=once)
    return pl.pallas_call(
        functools.partial(attend_kernel, doc_len, doc_count, 256, zc, count),
        grid=(pairs,),
        in_specs=[
            fixed(docs.shape), fixed(queries.shape),
            pl.BlockSpec((width, 128), lambda j: (0, w_one.shape[1] // 128 - 1), pipeline_mode=once),
            pl.BlockSpec((width, 384), lambda j: (0, j)),
            pl.BlockSpec((1, 8, span), lambda j: (j, 0, 0)),
            pl.BlockSpec(mask.shape, lambda j: (0, 0, 0)),
        ] + [whole] * len(weights),
        out_specs=[
            fixed((total, width)), fixed((8, width)), fixed((total, width)),
            pl.BlockSpec((total, 384), lambda j: (0, j)),
            pl.BlockSpec((total, 128), lambda j: (0, j)),
            pl.BlockSpec((1, 8, total), lambda j: (j, 0, 0)),
            pl.BlockSpec((2, 128, span - 128), lambda j: (j, 0, 0)),
        ] + [pl.BlockSpec(memory_space=pl.ANY)] * count,
        out_shape=[
            jax.ShapeDtypeStruct((total, width), BF),
            jax.ShapeDtypeStruct((8, width), F32),
            jax.ShapeDtypeStruct((total, width), BF),
            jax.ShapeDtypeStruct((total, pairs * 384), BF),
            jax.ShapeDtypeStruct((total, width), BF),
            jax.ShapeDtypeStruct((pairs, 8, total), F32),
            jax.ShapeDtypeStruct((pairs * 2, 128, span - 128), F32),
        ] + [jax.ShapeDtypeStruct((r * n_dev, c), BF) for r, c in shapes],
        scratch_shapes=[pltpu.VMEM((r + -r % 16, c), BF) for r, c in shapes] + (gather_scratch(shapes, zc) if count else []),
        compiler_params=pltpu.CompilerParams(vmem_limit_bytes=VMEM_ALL, **remote),
        name="attend",
    )(docs, queries, w_one, w_one, diag, mask, *weights)


BACK_SHARES = (0.0, 0.27, 0.5, 0.78, 0.93, 0.97, 1.0)


def attend_back_kernel(doc_len, doc_count, block, zc, count, pairs_total, qkv_ref, do_ref, lse_ref, table_ref, mask_ref,
                       normed_ref, *refs):
    grads = refs[:count]
    wg_ref, diag_ref, dqkv_ref = refs[count : count + 3]
    outs = refs[count + 3 : 2 * count + 3]
    acc, normed_t = refs[2 * count + 3 : 2 * count + 5]
    j = pl.program_id(0)
    span = 2 * doc_len
    hd = 64
    rest = qkv_ref.shape[0] - doc_count * doc_len
    slots = doc_count * (doc_len // block) + rest // 128
    pairs = pairs_total
    plan = {}
    if count:
        pos, begin, all_steps, finish = reduce_events(zc, grads, outs, refs[2 * count + 5 :])
        for group, share in zip(all_steps(), BACK_SHARES):
            for n, step in enumerate(group):
                at = min(slots * pairs - 1, int(share * slots * pairs) + n // 4)
                plan.setdefault(at, []).append(step)
        @pl.when(j == 0)
        def _():
            enter(pos)
            begin()
    slot = [0]
    def now():
        for at, steps in plan.items():
            if at % slots == slot[0]:
                @pl.when(j == at // slots)
                def _():
                    for step in steps:
                        step()
        slot[0] += 1
    @pl.when(j == 0)
    def _():
        normed_t[...] = normed_ref[...].T
    acc[...] = jnp.zeros_like(acc)
    lane = lax.broadcasted_iota(jnp.int32, (1, 128), 1)
    def part(rows, keys, q_len, mask):
        k2 = qkv_ref[pl.ds(rows, keys), 128:256]
        v2 = qkv_ref[pl.ds(rows, keys), 256:384]
        k2t = k2.astype(F32).T.astype(BF)
        dk = jnp.zeros((keys, 128), F32)
        dv = jnp.zeros((keys, 128), F32)
        for q_at in range(0, keys, q_len):
            now()
            qr = pl.ds(rows + q_at, q_len)
            q2 = qkv_ref[qr, 0:128]
            do2 = do_ref[qr, :]
            outs = []
            for h in range(2):
                mine = (lane < hd) == (h == 0)
                qm = jnp.where(mine, q2, jnp.zeros_like(q2))
                dom = jnp.where(mine, do2, jnp.zeros_like(do2))
                s = dot_nt(k2, qm) + tiles_of(table_ref.at[h], keys, q_at, q_len, doc_len)
                if mask is not None:
                    s = jnp.where(mask_ref[mask] > 0, s, mask_fill)
                p = jnp.exp(s - lse_ref[0, h : h + 1, qr])
                dp = dot_nt(v2, dom)
                ds = p * (dp - jnp.sum(p * dp, axis=0, keepdims=True))
                for kb in range(keys // 128):
                    at = doc_len - 128 - 128 * kb + q_at
                    acc[h, :, at : at + q_len] += ds[128 * kb : 128 * (kb + 1)]
                low = ds.astype(BF)
                dv += dot(p.astype(BF), dom)
                dk += dot(low, qm)
                outs.append(dot(k2t[h * hd : (h + 1) * hd], low))
            dqkv_ref[qr, 0:128] = jnp.concatenate(outs, axis=0).T.astype(BF)
        dqkv_ref[pl.ds(rows, keys), 128:256] = dk.astype(BF)
        dqkv_ref[pl.ds(rows, keys), 256:384] = dv.astype(BF)
    for m in range(doc_count):
        part(m * doc_len, doc_len, block, None)
    for i in range(rest // 128):
        part(doc_count * doc_len + 128 * i, 128, 128, i)
    for h in range(2):
        eight = acc[h, 0:8]
        for g in range(1, 16):
            eight = eight + pltpu.roll(acc[h, 8 * g : 8 * g + 8], span - 8 * g, 1)
        one = eight[0:1]
        for r in range(1, 8):
            one = one + pltpu.roll(eight, span - r, 1)[r : r + 1]
        diag_ref[0, h : h + 1, :] = one
    wg_ref[...] = dot(normed_t[...], dqkv_ref[...]).astype(BF)
    if count:
        @pl.when(j == pl.num_programs(0) - 1)
        def _():
            finish()


def attend_back(qkv, d_ctx, lse, table, mask, normed, doc_len, doc_count, grads, zc, n_dev):
    total, width = qkv.shape
    pairs = width // 384
    span = 2 * doc_len
    count = len(grads)
    remote = dict(collective_id=4, has_side_effects=True) if count else {}
    fixed = lambda shape: pl.BlockSpec(shape, lambda j: (0, 0), pipeline_mode=pl.Buffered(1))
    shapes = reduce_shapes(grads, n_dev)
    return pl.pallas_call(
        functools.partial(attend_back_kernel, doc_len, doc_count, 256, zc, count, pairs),
        grid=(pairs,),
        in_specs=[
            pl.BlockSpec((total, 384), lambda j: (0, j)),
            pl.BlockSpec((total, 128), lambda j: (0, j)),
            pl.BlockSpec((1, 8, total), lambda j: (j, 0, 0)),
            pl.BlockSpec((2, 128, span - 128), lambda j: (j, 0, 0)),
            pl.BlockSpec(mask.shape, lambda j: (0, 0, 0)),
            fixed(normed.shape),
        ] + [pl.BlockSpec(memory_space=pl.ANY)] * count,
        out_specs=[
            pl.BlockSpec((normed.shape[1], 384), lambda j: (0, j)),
            pl.BlockSpec((1, 8, span), lambda j: (j, 0, 0)),
            pl.BlockSpec((total, 384), lambda j: (0, j)),
        ] + [pl.BlockSpec(memory_space=pltpu.VMEM)] * len(shapes),
        out_shape=[
            jax.ShapeDtypeStruct((normed.shape[1], width), BF),
            jax.ShapeDtypeStruct((pairs, 8, span), F32),
            jax.ShapeDtypeStruct((total, width), BF),
        ] + shapes,
        scratch_shapes=[
            pltpu.VMEM((2, 128, span), F32), pltpu.VMEM(normed.shape[::-1], BF),
        ] + (reduce_scratch(grads, zc) if count else []),
        compiler_params=pltpu.CompilerParams(vmem_limit_bytes=VMEM_ALL, **remote),
        name="attend_back",
    )(qkv, d_ctx, lse, table, mask, normed, *grads)


def columns_of(rows):
    n = rows[0].shape[1]
    return jnp.concatenate([*rows, jnp.zeros((128 - len(rows), n), F32)], axis=0).T


def query_mask(lengths, slots):
    per = 128 // slots
    live = (jnp.arange(slots, dtype=jnp.int32)[None, :] < lengths[:, None]).reshape(-1, 128)
    owner = jnp.arange(128, dtype=jnp.int32) // slots
    same = owner[:, None] == owner[None, :]
    return (live[:, :, None] & same[None]).astype(F32)

def pair_columns(w):
    q, k, v = w
    rows, width = q.shape
    pack = jnp.stack([x.reshape(rows, width // 128, 128) for x in (q, k, v)], axis=2)
    return pack.reshape(rows, 3 * width)


def score_kernel(peers, doc_len, slots, emb_ref, picks_ref, counts_ref, live_ref, goal_ref, loss_ref, d_emb_ref,
                 q_own, q_all, weighed, totals, pool_out, pool_in, grad_out, grad_in, dq_out, dq_in, docs_t, d_docs,
                 s_q, r_q, s_pool, r_pool, s_grad, r_grad, s_dq, r_dq):
    dp = lax.axis_index("dp"); me = lax.axis_index("wide")
    tokens = q_own.shape[0]
    feat = emb_ref.shape[1]
    half = tokens // 2
    scale = feat ** -0.5
    barrier = pltpu.get_barrier_semaphore()
    def other(k):
        return lax.rem(me + k, peers)
    def each(fn):
        @pl.loop(1, peers)
        def _(k):
            fn(other(k))
    each(lambda o: pl.semaphore_signal(barrier, inc=1, device_id=(dp, o), device_id_type=MESH))
    q_own[...] = emb_ref[2 * doc_len :, :]
    q_all[me] = q_own[...]
    pl.semaphore_wait(barrier, peers - 1)
    def send(src, dst, ss, rs, o):
        return pltpu.make_async_remote_copy(src_ref=src, dst_ref=dst, send_sem=ss, recv_sem=rs, device_id=(dp, o), device_id_type=MESH)
    def q_to(o): return send(q_own, q_all.at[me], s_q.at[o], r_q.at[me], o)
    def q_from(o): return send(q_own, q_all.at[o], s_q.at[o], r_q.at[o], o)
    def pool_to(o): return send(pool_out.at[o], pool_in.at[me], s_pool.at[o], r_pool.at[me], o)
    def pool_from(o): return send(pool_out.at[o], pool_in.at[o], s_pool.at[o], r_pool.at[o], o)
    def grad_to(o): return send(grad_out.at[o], grad_in.at[me], s_grad.at[o], r_grad.at[me], o)
    def grad_from(o): return send(grad_out.at[o], grad_in.at[o], s_grad.at[o], r_grad.at[o], o)
    def dq_to(o): return send(dq_out.at[o], dq_in.at[me], s_dq.at[o], r_dq.at[me], o)
    def dq_from(o): return send(dq_out.at[o], dq_in.at[o], s_dq.at[o], r_dq.at[o], o)
    def started(o):
        q_to(o).start()
    each(started)
    docs2 = jnp.concatenate([emb_ref[0:doc_len, :], emb_ref[doc_len : 2 * doc_len, :]], axis=1)
    docs_t[...] = docs2.astype(F32).T.astype(BF)
    row = lax.broadcasted_iota(jnp.int32, (tokens, 1), 0)
    lane = lax.broadcasted_iota(jnp.int32, (1, tokens), 1)
    def two_docs(o):
        q = q_all[o]
        none = jnp.zeros_like(q)
        return jnp.concatenate([jnp.where(row < half, q, none), jnp.where(row < half, none, q)], axis=1)
    def forward(o):
        s = lax.dot_general(docs2, two_docs(o), (((1,), (1,)), ((), ())), preferred_element_type=F32) * scale
        multiple = counts_ref[o].astype(F32)
        w = multiple * jnp.exp(s)
        weighed[o] = w
        found = jnp.sum(multiple, axis=0, keepdims=True)
        weight = jnp.sum(w, axis=0, keepdims=True) + (found == 0).astype(F32)
        totals[o] = jnp.broadcast_to(weight, (8, tokens))
        pool_out[o] = jnp.broadcast_to(jnp.log(weight), (8, tokens))
    def forward_peer(o):
        q_from(o).wait_recv()
        forward(o)
        pool_to(o).start()
    forward(me)
    pool_in[me] = pool_out[me]
    each(forward_peer)
    each(lambda o: pool_from(o).wait_recv())
    pooled = pool_in[:, 0, :]
    mine = picks_ref[...]
    hits = []
    for w in range(peers):
        inside = ((mine >= w * doc_len) & (mine < (w + 1) * doc_len)).astype(F32)
        hits.append(jnp.max(inside, axis=0, keepdims=True))
    hit = jnp.concatenate(hits, axis=0)
    live = live_ref[0:1, :]
    own_row = lax.broadcasted_iota(jnp.int32, (tokens, tokens), 0) // slots
    own_col = lax.broadcasted_iota(jnp.int32, (tokens, tokens), 1) // slots
    same = (own_row == own_col).astype(F32)
    def per_query(v):
        return jnp.dot(v, same, precision=lax.Precision.HIGHEST, preferred_element_type=F32)
    divisor = jnp.maximum(per_query(hit * live), 1.0)
    logits = score_scale * per_query(pooled * live) / divisor
    top = jnp.max(logits, axis=0, keepdims=True)
    shifted = jnp.exp(logits - top)
    total = jnp.sum(shifted, axis=0, keepdims=True)
    doc_id = lax.broadcasted_iota(jnp.int32, (peers, tokens), 0)
    chosen = (doc_id == goal_ref[0:1, :]).astype(F32)
    loss = top + jnp.log(total) - jnp.sum(chosen * logits, axis=0, keepdims=True)
    loss_ref[...] = jnp.broadcast_to(loss, loss_ref.shape)
    d_pooled = score_scale * (shifted / total - chosen) / divisor * live
    for w in range(peers):
        grad_out[w] = jnp.broadcast_to(d_pooled[w : w + 1], (8, tokens))
    each(lambda o: grad_to(o).start())
    grad_in[me] = grad_out[me]
    d_docs[...] = jnp.zeros_like(d_docs)
    def backward(o):
        factor = grad_in[o][0:1] / totals[o][0:1] * scale
        d_raw = (weighed[o] * factor).astype(BF)
        d_docs[...] += jnp.dot(d_raw, two_docs(o), preferred_element_type=F32)
        both = jnp.dot(docs_t[...], d_raw, preferred_element_type=F32)
        d_q = jnp.where(lane < half, both[0:feat], both[feat : 2 * feat])
        dq_out[o] = d_q.T.astype(BF)
    def backward_peer(o):
        grad_from(o).wait_recv()
        backward(o)
        dq_to(o).start()
    each(backward_peer)
    backward(me)
    d_emb_ref[0:doc_len, :] = d_docs[:, 0:feat].astype(BF)
    d_emb_ref[doc_len : 2 * doc_len, :] = d_docs[:, feat : 2 * feat].astype(BF)
    dq_in[me] = dq_out[me]
    each(lambda o: dq_from(o).wait_recv())
    total_q = dq_in[0].astype(F32)
    for w in range(1, peers):
        total_q = total_q + dq_in[w].astype(F32)
    d_emb_ref[2 * doc_len :, :] = total_q.astype(BF)
    def sent(o):
        q_to(o).wait_send(); pool_to(o).wait_send(); grad_to(o).wait_send(); dq_to(o).wait_send()
    each(sent)

def score(emb, picks, counts, live, goal, doc_len, slots, peers):
    tokens = picks.shape[1]
    feat = emb.shape[1]
    V = pltpu.VMEM
    dma = pltpu.SemaphoreType.DMA
    return pl.pallas_call(
        functools.partial(score_kernel, peers, doc_len, slots),
        out_shape=[jax.ShapeDtypeStruct((8, tokens), F32), jax.ShapeDtypeStruct(emb.shape, BF)],
        in_specs=[pl.BlockSpec(memory_space=pltpu.VMEM)] * 5,
        out_specs=[pl.BlockSpec(memory_space=pltpu.VMEM)] * 2,
        scratch_shapes=[
            V((tokens, feat), BF), V((peers, tokens, feat), BF),
            V((peers, doc_len, tokens), F32), V((peers, 8, tokens), F32),
            V((peers, 8, tokens), F32), V((peers, 8, tokens), F32), V((peers, 8, tokens), F32), V((peers, 8, tokens), F32),
            V((peers, tokens, feat), BF), V((peers, tokens, feat), BF), V((2 * feat, doc_len), BF), V((doc_len, 2 * feat), F32),
        ] + [dma((peers,))] * 8,
        compiler_params=pltpu.CompilerParams(collective_id=2, has_side_effects=True, vmem_limit_bytes=VMEM_ALL),
        name="score",
    )(emb, picks, counts, live, goal)


GELU_SCALE = 0.7978845608028654
GELU_CUBE = 0.044715

def dot(a, b):
    return jnp.dot(a, b, preferred_element_type=F32)

def dot_nt(a, b):
    return lax.dot_general(a, b, (((1,), (1,)), ((), ())), preferred_element_type=F32)

def dot_tn(a, b):
    return lax.dot_general(a, b, (((0,), (0,)), ((), ())), preferred_element_type=F32)

def inverse_rms(v):
    return lax.rsqrt(jnp.mean(v * v, axis=-1, keepdims=True) + eps_norm)

def chunks_of(total, parts):
    size = total // parts
    return [slice(i * size, (i + 1) * size) for i in range(parts)]

def ffn_kernel(parts, rows_ref, ctx_ref, wo_ref, wgu_ref, wd_ref, wp_ref, gains_ref, n2_ref, gu_ref, scale_ref, ne_ref, emb_ref, lo_ref):
    j = pl.program_id(0)
    block = wd_ref.shape[0]
    chunks = chunks_of(rows_ref.shape[0], parts)
    @pl.when(j == 0)
    def _():
        for c in chunks:
            h = rows_ref[c, :].astype(F32) + dot(ctx_ref[c, :], wo_ref[...])
            lo_ref[c, :] = h
            inv = inverse_rms(h)
            scale_ref[c, :] = jnp.broadcast_to(inv, scale_ref[c, :].shape)
            n2_ref[c, :] = (h * inv * gains_ref[1:2, :]).astype(BF)
    for c in chunks:
        gu = dot(n2_ref[c, :], wgu_ref[...])
        gu_ref[c, :] = gu.astype(BF)
        g = gu[:, :block]
        t = jnp.tanh(GELU_SCALE * (g + GELU_CUBE * (g * g * g)))
        act = (0.5 * g * (1.0 + t)) * gu[:, block:]
        lo_ref[c, :] += dot(act.astype(BF), wd_ref[...])
    @pl.when(j == pl.num_programs(0) - 1)
    def _():
        for c in chunks:
            lo = lo_ref[c, :]
            inv = inverse_rms(lo)
            lane = lax.broadcasted_iota(jnp.int32, (1, scale_ref.shape[1]), 1)
            scale_ref[c, :] = jnp.where(lane < 64, scale_ref[c, :], inv)
            ne = (lo * inv * gains_ref[2:3, :]).astype(BF)
            ne_ref[c, :] = ne
            emb_ref[c, :] = dot(ne, wp_ref[...]).astype(BF)

def ffn(rows, ctx, w_one, w_gu, w_down, gains, p_size, block):
    total, width = rows.shape
    ff = w_down.shape[0]
    once = pl.Buffered(1)
    full = lambda cols, at=0: pl.BlockSpec((total, cols), lambda j: (0, 0), pipeline_mode=once)
    return pl.pallas_call(
        functools.partial(ffn_kernel, 2),
        grid=(ff // block,),
        in_specs=[
            full(width), full(width),
            pl.BlockSpec((width, width), lambda j: (0, 3), pipeline_mode=once),
            pl.BlockSpec((width, 2 * block), lambda j: (0, j)),
            pl.BlockSpec((block, width), lambda j: (j, 0)),
            pl.BlockSpec((width, p_size), lambda j: (0, 4 * width // p_size), pipeline_mode=once),
            pl.BlockSpec(gains.shape, lambda j: (0, 0)),
        ],
        out_specs=[full(width), pl.BlockSpec((total, 2 * block), lambda j: (0, j)), full(128), full(width), full(p_size)],
        out_shape=[
            jax.ShapeDtypeStruct((total, width), BF), jax.ShapeDtypeStruct((total, 2 * ff), BF),
            jax.ShapeDtypeStruct((total, 128), F32), jax.ShapeDtypeStruct((total, width), BF),
            jax.ShapeDtypeStruct((total, p_size), BF),
        ],
        scratch_shapes=[pltpu.VMEM((total, width), F32)],
        compiler_params=pltpu.CompilerParams(vmem_limit_bytes=VMEM_ALL),
        name="feed_forward",
    )(rows, ctx, w_one, w_gu, w_down, w_one, gains)

def rms_pull_normed(normed, inv, gain, upstream):
    unit = normed.astype(F32) / gain
    scaled = upstream * gain
    d_gain = jnp.sum(upstream * unit, axis=0, keepdims=True)
    inner = jnp.mean(scaled * unit, axis=-1, keepdims=True)
    return inv * (scaled - unit * inner), d_gain


def rms_pull(v, gain, upstream):
    inv = inverse_rms(v)
    scaled = upstream * gain
    d_gain = jnp.sum(upstream * (v * inv), axis=0, keepdims=True)
    inner = jnp.mean(scaled * v, axis=-1, keepdims=True)
    return inv * scaled - v * (inv * inv * inv * inner), d_gain

def ffn_back_kernel(parts, de_ref, scale_ref, ne_ref, n2_ref, ctx_ref, wo_ref, wp_ref, gains_ref, gu_ref, wgu_ref, wd_ref,
                    dgu_w_ref, dd_w_ref, last_ref, dh_ref, dctx_ref, dgain_ref, dl_ref, low_ref, n2t_ref, acc_ref, dhl_ref):
    j = pl.program_id(0)
    block = wd_ref.shape[0]
    chunks = chunks_of(ne_ref.shape[0], parts)
    @pl.when(j == 0)
    def _():
        dgain_ref[...] = jnp.zeros_like(dgain_ref)
        for c in chunks:
            up = dot_nt(de_ref[c, :], wp_ref[...])
            dl, dg = rms_pull_normed(ne_ref[c, :], scale_ref[c, 64:65], gains_ref[2:3, :], up)
            dl_ref[c, :] = dl
            low_ref[c, :] = dl.astype(BF)
            dgain_ref[2:3, :] += dg
        width = ne_ref.shape[1]
        last_ref[:, width : width + de_ref.shape[1]] = dot_tn(ne_ref[...], de_ref[...]).astype(BF)
        n2t_ref[...] = n2_ref[...].T
        acc_ref[...] = jnp.zeros_like(acc_ref)
    acts, dgus = [], []
    for c in chunks:
        da = dot_nt(low_ref[c, :], wd_ref[...])
        g = gu_ref[c, :block].astype(F32)
        u = gu_ref[c, block:].astype(F32)
        t = jnp.tanh(GELU_SCALE * (g + GELU_CUBE * (g * g * g)))
        cdf = 0.5 * (1.0 + t)
        gel = g * cdf
        acts.append((gel * u).astype(BF))
        slope = cdf + (0.5 * GELU_SCALE) * g * (1.0 - t * t) * (1.0 + (3.0 * GELU_CUBE) * (g * g))
        dgu = jnp.concatenate([(da * u * slope).astype(BF), (da * gel).astype(BF)], axis=1)
        dgus.append(dgu)
        acc_ref[c, :] += dot_nt(dgu, wgu_ref[...])
    dgu_w_ref[...] = dot(n2t_ref[...], jnp.concatenate(dgus, axis=0)).astype(BF)
    dd_w_ref[...] = dot_tn(jnp.concatenate(acts, axis=0), low_ref[...]).astype(BF)
    @pl.when(j == pl.num_programs(0) - 1)
    def _():
        for c in chunks:
            dv, dg = rms_pull_normed(n2_ref[c, :], scale_ref[c, 0:1], gains_ref[1:2, :], acc_ref[c, :])
            dh = dl_ref[c, :] + dv
            dh_ref[c, :] = dh
            dhl = dh.astype(BF)
            dhl_ref[c, :] = dhl
            dgain_ref[1:2, :] += dg
            dctx_ref[c, :] = dot_nt(dhl, wo_ref[...]).astype(BF)
        width = ne_ref.shape[1]
        last_ref[:, :width] = dot_tn(ctx_ref[...], dhl_ref[...]).astype(BF)
        last_ref[:, width + de_ref.shape[1] :] = columns_of([dgain_ref[i : i + 1, :] for i in range(3)]).astype(BF)

def ffn_back(d_emb, scale, ne, n2, ctx, w_one, w_gu, w_down, gains, gu, p_size, block):
    total, width = ne.shape
    ff = w_down.shape[0]
    once = pl.Buffered(1)
    full = lambda cols: pl.BlockSpec((total, cols), lambda j: (0, 0), pipeline_mode=once)
    fixed = lambda shape: pl.BlockSpec(shape, lambda j: (0, 0), pipeline_mode=once)
    V = pltpu.VMEM
    return pl.pallas_call(
        functools.partial(ffn_back_kernel, 2),
        grid=(ff // block,),
        in_specs=[
            full(p_size), full(128), full(width), full(width), full(width),
            pl.BlockSpec((width, width), lambda j: (0, 3), pipeline_mode=once),
            pl.BlockSpec((width, p_size), lambda j: (0, 4 * width // p_size), pipeline_mode=once),
            fixed(gains.shape),
            pl.BlockSpec((total, 2 * block), lambda j: (0, j)),
            pl.BlockSpec((width, 2 * block), lambda j: (0, j)),
            pl.BlockSpec((block, width), lambda j: (j, 0)),
        ],
        out_specs=[
            pl.BlockSpec((width, 2 * block), lambda j: (0, j)),
            pl.BlockSpec((block, width), lambda j: (j, 0)),
            fixed((width, width + p_size + 128)), full(width), full(width),
        ],
        out_shape=[
            jax.ShapeDtypeStruct((width, 2 * ff), BF), jax.ShapeDtypeStruct((ff, width), BF),
            jax.ShapeDtypeStruct((width, width + p_size + 128), BF),
            jax.ShapeDtypeStruct((total, width), F32), jax.ShapeDtypeStruct((total, width), BF),
        ],
        scratch_shapes=[V((8, width), F32), V((total, width), F32), V((total, width), BF), V((width, total), BF), V((total, width), F32), V((total, width), BF)],
        compiler_params=pltpu.CompilerParams(vmem_limit_bytes=VMEM_ALL),
        name="feed_forward_back",
    )(d_emb, scale, ne, n2, ctx, w_one, w_one, gains, gu, w_gu, w_down)

def gate_up_columns(gate, up, block):
    rows, ff = gate.shape
    return jnp.stack([gate.reshape(rows, -1, block), up.reshape(rows, -1, block)], axis=2).reshape(rows, 2 * ff)


def contract_rows(left_mat, right_mat):
    return lax.dot_general(
        left_mat, right_mat, (((0,), (0,)), ((), ())), preferred_element_type=jnp.float32
    )


def contract_cols(left_mat, right_mat):
    return lax.dot_general(
        left_mat, right_mat, (((1,), (1,)), ((), ())), preferred_element_type=jnp.float32
    )


def matmul(left_mat, right_mat):
    return jnp.dot(left_mat, right_mat, preferred_element_type=jnp.float32)


def rms_forward(values, gain_vec):
    inverse = lax.rsqrt(jnp.mean(values * values, axis=-1, keepdims=True) + eps_norm)
    return (values * inverse * gain_vec, inverse)


def rms_backward(values, inverse, gain_vec, upstream):
    scaled = upstream * gain_vec
    gain_grad = jnp.sum(upstream * values * inverse, axis=0)
    inner_mean = jnp.mean(scaled * values, axis=-1, keepdims=True)
    return (inverse * scaled - values * inverse * inverse * inverse * inner_mean, gain_grad)


def two_level(shards):
    return (
        lax.axis_size("dp") == 4
        and lax.axis_size("wide") % 4 == 0
        and all(s.shape[0] % 8 == 0 for s in shards)
    )


def gathered(shards):
    return [lax.all_gather(s, ("dp", "wide"), axis=0, tiled=True) for s in shards]


def summed(grads, table):
    sums = [lax.psum_scatter(g.astype(F32), ("dp", "wide"), scatter_dimension=0, tiled=True) for g in grads]
    return [*sums, lax.psum(table, ("dp", "wide"))]


def local(
    doc_tokens,
    query_tokens,
    query_lengths,
    retrieved,
    targets,
    q_weight,
    k_weight,
    v_weight,
    o_weight,
    gate_weight,
    up_weight,
    down_weight,
    proj_weight,
    attn_gain,
    ffn_gain,
    final_gain,
    rel_bias,
):
    micro_count, _, doc_len, width = doc_tokens.shape
    slots = query_tokens.shape[2]
    doc_rows = micro_count * doc_len
    wide_count = lax.axis_size("wide")
    p_size = proj_weight.shape[1]
    bucket_count, head_count = rel_bias.shape
    pairs = width // 128
    ff_block = FF_BLOCK
    weights = [q_weight, k_weight, v_weight, o_weight, proj_weight]
    ffn_raw = [gate_weight, up_weight, down_weight]
    beside = two_level(weights + ffn_raw)
    picks = retrieved.reshape(-1, retrieved.shape[3]).T
    tokens = picks.shape[1]
    gains = jnp.stack([attn_gain, ffn_gain, final_gain]).astype(F32)
    n_dev = lax.axis_size("dp") * wide_count
    if beside:
        spare = ((0, 128 - gains.shape[0]), (0, 128 - gains.shape[1]))
        w_one, counts = gather(weights, jnp.pad(gains, spare), picks, doc_len, wide_count // 2, n_dev)
    else:
        shard_one = jnp.concatenate(
            [pair_columns(weights[:3]), o_weight, proj_weight, jnp.pad(gains.T.astype(BF), ((0, 0), (0, 125)))], axis=1
        )
        (w_one,) = gathered([shard_one])
        counts = count_all(picks, doc_len, wide_count)
    hot = diagonal_onehot(doc_len, bucket_count)
    diag = jnp.dot(rel_bias.astype(F32).T, hot.T, precision=top_precision)
    diag = jnp.pad(diag.reshape(pairs, 2, -1), ((0, 0), (0, 6), (0, 0)))
    mask = query_mask(query_lengths.reshape(-1), slots)
    rows_low, gains, normed, qkv, context, lse, table, *ffn_weights = attend(
        doc_tokens.reshape(doc_rows, width),
        query_tokens.reshape(-1, width),
        w_one,
        diag,
        mask,
        doc_len,
        micro_count,
        ffn_raw if beside else [],
        wide_count // 2,
        n_dev,
    )
    w_gu, w_down = (
        ffn_weights if beside else gathered([gate_up_columns(gate_weight, up_weight, ff_block), down_weight])
    )
    normed_two, gate_up, scale, normed_end, embedded = ffn(
        rows_low, context, w_one, w_gu, w_down, gains, p_size, ff_block
    )
    live = (jnp.arange(slots, dtype=jnp.int32)[None, :] < query_lengths.reshape(-1)[:, None]).astype(F32)
    live = jnp.broadcast_to(live.reshape(1, tokens), (8, tokens))
    goal = jnp.broadcast_to(jnp.repeat(targets.reshape(-1), slots)[None, :], (8, tokens))
    loss_rows, d_embedded = score(embedded, picks, counts, live, goal, doc_len, slots, wide_count)
    losses_out = loss_rows[0].reshape(-1, slots)[:, 0].reshape(targets.shape)
    gu_grad, down_grad, last_grad, d_hidden, d_context = ffn_back(
        d_embedded, scale, normed_end, normed_two, context, w_one, w_gu, w_down, gains, gate_up, p_size, ff_block
    )
    ff = down_grad.shape[0]
    ffn_layouts = [
        [[(2 * ff_block * i + at, ff_block) for i in range(ff // ff_block)] for at in (0, ff_block)],
        [[(0, width)]],
    ]
    one_layouts = [
        [[(384 * i + 128 * n, 128) for i in range(pairs)] for n in range(3)],
        [[(0, width)], [(width, p_size)], [(width + p_size, 128)]],
    ]
    zc = wide_count // 2 if beside else 0
    qkv_grad, d_diag, d_qkv, *ffn_sums = attend_back(
        qkv,
        d_context,
        lse,
        table,
        mask,
        normed,
        doc_len,
        micro_count,
        [gu_grad, down_grad] if beside else [],
        zc,
        n_dev,
    )
    table_grad = jnp.dot(hot.T, d_diag[:, :2].reshape(head_count, -1).T, precision=top_precision)
    packed = jnp.pad(table_grad.reshape(-1), (0, -table_grad.size % 1024)).reshape(-1, 128)
    d_rows, *one_sums = reduce_scatter(
        d_qkv, w_one, rows_low, d_hidden, gains, [qkv_grad, last_grad] if beside else [], packed, zc
    )
    if beside:
        *one_sums, s_table = one_sums
    else:
        *one_sums, s_gu, s_down, s_table = summed([qkv_grad, last_grad, gu_grad, down_grad], packed)
        ffn_sums = [s_gu, s_down]
    s_table = s_table.reshape(-1)[: table_grad.size].reshape(table_grad.shape)
    d_docs, d_queries, s_q, s_k, s_v, s_o, s_proj, s_gains, s_gate, s_up, s_down = apart(
        d_rows, [*one_sums, *ffn_sums], one_layouts + ffn_layouts, doc_rows
    )
    weighed = sum(w.astype(F32) * g for w, g in ((q_weight, s_q), (k_weight, s_k), (v_weight, s_v)))
    attn_gain_grad = jnp.sum(weighed, axis=1) / attn_gain.astype(F32)
    return (
        losses_out,
        d_docs.reshape(doc_tokens.shape),
        d_queries.reshape(query_tokens.shape),
        s_q,
        s_k,
        s_v,
        s_o,
        s_gate,
        s_up,
        s_down,
        s_proj,
        attn_gain_grad,
        s_gains[:, 1],
        s_gains[:, 2],
        s_table,
    )


def solution(mesh):
    placed = (
        P(None, ("dp", "wide"), None, None),
        P(None, ("dp", "wide"), None, None),
        P(None, ("dp", "wide")),
        P(None, ("dp", "wide"), None, None),
        P(None, ("dp", "wide")),
        P(("dp", "wide"), None),
        P(("dp", "wide"), None),
        P(("dp", "wide"), None),
        P(("dp", "wide"), None),
        P(("dp", "wide"), None),
        P(("dp", "wide"), None),
        P(("dp", "wide"), None),
        P(("dp", "wide"), None),
        P(("dp", "wide")),
        P(("dp", "wide")),
        P(("dp", "wide")),
        P(),
    )
    return jax.shard_map(
        local,
        mesh=mesh,
        in_specs=placed,
        out_specs=(
            P(None, ("dp", "wide")),
            P(None, ("dp", "wide"), None, None),
            P(None, ("dp", "wide"), None, None),
            P(("dp", "wide"), None),
            P(("dp", "wide"), None),
            P(("dp", "wide"), None),
            P(("dp", "wide"), None),
            P(("dp", "wide"), None),
            P(("dp", "wide"), None),
            P(("dp", "wide"), None),
            P(("dp", "wide"), None),
            P(("dp", "wide")),
            P(("dp", "wide")),
            P(("dp", "wide")),
            P(),
        ),
        check_vma=False,
    )
```

```python
import functools

import jax
import jax.numpy as jnp
from jax import lax
from jax.experimental import pallas as pl
from jax.experimental.pallas import tpu as pltpu
from jax.sharding import PartitionSpec as P

eps_norm = 1e-06
score_scale = 6.0
mask_fill = -1000000000.0
top_precision = lax.Precision.HIGHEST
F32 = jnp.float32
BF = jnp.bfloat16
VMEM_ALL = 62 << 20
FF_BLOCK = 512


MESH = pl.DeviceIdType.MESH

def gray(p):
    return p + (p // 2) * (1 - 2 * (p % 2))

class Place:
    def __init__(self, zc):
        self.zc = zc
        d = lax.axis_index("dp"); w = lax.axis_index("wide")
        self.d, self.w = d, w
        self.z, self.c = w // 2, w % 2
        p = gray(d)
        self.right = gray((p + 1) % 4); self.left = gray((p + 3) % 4); self.opp = gray((p + 2) % 4)
    def dev(self, d=None, z=None, c=None):
        d = self.d if d is None else d
        z = self.z if z is None else z
        c = self.c if c is None else c
        return (d, z * 2 + c)

def enter(pos, wide=False):
    barrier = pltpu.get_barrier_semaphore()
    def greet(dev):
        pl.semaphore_signal(barrier, inc=1, device_id=dev, device_id_type=MESH)
    greet(pos.dev(d=pos.right))
    greet(pos.dev(d=pos.left))
    if wide:
        @pl.loop(1, 2 * pos.zc)
        def _(k):
            greet((pos.d, lax.rem(pos.w + k, 2 * pos.zc)))
        pl.semaphore_wait(barrier, 1 + 2 * pos.zc)
    else:
        greet(pos.dev(c=1 - pos.c))
        @pl.loop(1, pos.zc)
        def _(k):
            greet(pos.dev(z=lax.rem(pos.z + k, pos.zc)))
        pl.semaphore_wait(barrier, 2 + pos.zc)


def gather_events(zc, shard, out, rest):
    count = len(shard)
    pos = Place(zc)
    comp = rest[:count]; mine = rest[count:2 * count]
    (s_col, s_ring, s_fwd, s_mate, s_pair, s_own, r_col, r_left, r_right, r_opp, r_mate, r_pair) = rest[2 * count:]
    z, c, d = pos.z, pos.c, pos.d
    rows = [o.shape[0] // (4 * zc) for o in out]
    half = [o.shape[1] // 2 for o in out]

    def part(a, ref, blk, core):
        return ref.at[pl.ds(pl.multiple_of(blk * rows[a], 16), rows[a]), pl.ds(pl.multiple_of(core * half[a], 128), half[a])]
    def own(a, core):
        return comp[a].at[:, pl.ds(pl.multiple_of(core * half[a], 128), half[a])]
    def rdma(a, src, blk, dev, ss, rs):
        return pltpu.make_async_remote_copy(src_ref=src, dst_ref=part(a, out[a], blk, c), send_sem=ss, recv_sem=rs, device_id=dev, device_id_type=MESH)
    def blk(dd, zz):
        return dd * zc + zz
    mate_dev = pos.dev(c=1 - c)
    def pair(a):
        return pltpu.make_async_remote_copy(src_ref=shard[a], dst_ref=mine[a], send_sem=s_pair.at[a], recv_sem=r_pair.at[a], device_id=mate_dev, device_id_type=MESH)
    def keep(a):
        return pltpu.make_async_copy(comp[a], out[a].at[pl.ds(pl.multiple_of(blk(d, z) * rows[a], 16), rows[a]), :], s_own.at[a])
    def up(a, src, zz):
        return rdma(a, src, blk(d, zz), pos.dev(z=lax.rem(z + 1, zc)), s_col.at[a, 0, zz], r_col.at[a, zz])
    def down(a, src, zz):
        return rdma(a, src, blk(d, zz), pos.dev(z=lax.rem(z + zc - 1, zc)), s_col.at[a, 1, zz], r_col.at[a, zz])
    def right(a, src, zz):
        return rdma(a, src, blk(d, zz), pos.dev(d=pos.right), s_ring.at[a, 0, zz], r_left.at[a, zz])
    def left(a, src, zz):
        return rdma(a, src, blk(d, zz), pos.dev(d=pos.left), s_ring.at[a, 1, zz], r_right.at[a, zz])
    def fwd_right(a, zz):
        b = blk(pos.left, zz)
        return rdma(a, part(a, out[a], b, c), b, pos.dev(d=pos.right), s_fwd.at[a, zz], r_opp.at[a, zz])
    def fwd_left(a, zz):
        b = blk(pos.right, zz)
        return rdma(a, part(a, out[a], b, c), b, pos.dev(d=pos.left), s_fwd.at[a, zz], r_opp.at[a, zz])
    def mate(a, b):
        return rdma(a, part(a, out[a], b, c), b, mate_dev, s_mate.at[a, b], r_mate.at[a, b])
    def got(a, b, sem):
        return rdma(a, part(a, out[a], b, c), b, mate_dev, s_mate.at[a, b], sem).wait_recv()
    def mate_got(a, b):
        piece = part(a, out[a], b, 1 - c)
        pltpu.make_async_remote_copy(src_ref=piece, dst_ref=piece, send_sem=s_mate.at[a, b], recv_sem=r_mate.at[a, b], device_id=mate_dev, device_id_type=MESH).wait_recv()

    def begin(wide=False):
        enter(pos, wide)
        for a in range(count):
            pair(a).start()
    def first(a):
        pair(a).wait_recv()
        r2 = rows[a] // 2
        step = 256 if half[a] * 2 % 256 == 0 else 128
        @pl.loop(0, half[a] * 2 // step)
        def _(t):
            cols = pl.ds(pl.multiple_of(t * step, 128), step)
            mn = shard[a][:, cols].astype(jnp.float32)[:r2]
            ot = mine[a][:, cols].astype(jnp.float32)[:r2]
            first = jnp.where(c == 0, mn, ot)
            second = jnp.where(c == 0, ot, mn)
            comp[a][:, cols] = jnp.concatenate([first, second], axis=0).astype(jnp.bfloat16)
        right(a, own(a, c), z).start()
        left(a, own(a, c), z).start()
        pl.when(z < zc - 1)(lambda: up(a, own(a, c), z).start())
        pl.when(z > 0)(lambda: down(a, own(a, c), z).start())
        keep(a).start()

    def column(a, j):
        @pl.when(z - j >= 0)
        def _():
            zz = z - j
            got(a, blk(d, zz), r_col.at[a, zz])
            src = part(a, out[a], blk(d, zz), c)
            pl.when(z < zc - 1)(lambda: up(a, src, zz).start())
            right(a, src, zz).start(); left(a, src, zz).start()
            mate(a, blk(d, zz)).start()
        @pl.when(z + j < zc)
        def _():
            zz = z + j
            got(a, blk(d, zz), r_col.at[a, zz])
            src = part(a, out[a], blk(d, zz), c)
            pl.when(z > 0)(lambda: down(a, src, zz).start())
            right(a, src, zz).start(); left(a, src, zz).start()
            mate(a, blk(d, zz)).start()
    def ring_one(a, zz):
        got(a, blk(pos.left, zz), r_left.at[a, zz])
        pl.when(zz % 2 == 0)(lambda: fwd_right(a, zz).start())
        mate(a, blk(pos.left, zz)).start()
        got(a, blk(pos.right, zz), r_right.at[a, zz])
        pl.when(zz % 2 == 1)(lambda: fwd_left(a, zz).start())
        mate(a, blk(pos.right, zz)).start()
    def opp_one(a, zz):
        got(a, blk(pos.opp, zz), r_opp.at[a, zz])
        mate(a, blk(pos.opp, zz)).start()
    def spread(fn, a, j):
        if j == 0:
            fn(a, z); return
        pl.when(z - j >= 0)(lambda: fn(a, z - j))
        pl.when(z + j < zc)(lambda: fn(a, z + j))
    def rounds(a):
        call = functools.partial
        steps = []
        for t in range(1, zc + 2):
            if t < zc:
                steps.append(call(column, a, t))
            if t <= zc:
                steps.append(call(spread, ring_one, a, t - 1))
            if t >= 2:
                steps.append(call(spread, opp_one, a, t - 2))
        return steps
    def finish_one(a):
        pair(a).wait_send(); keep(a).wait()
        @pl.loop(0, zc)
        def _(zz):
            src = part(a, out[a], blk(d, zz), c)
            right(a, src, zz).wait_send(); left(a, src, zz).wait_send()
            pl.when((z < zc - 1) & (zz <= z))(lambda: up(a, src, zz).wait_send())
            pl.when((z > 0) & (zz >= z))(lambda: down(a, src, zz).wait_send())
            fwd_right(a, zz).wait_send()
        @pl.loop(0, 4 * zc)
        def _(b):
            @pl.when(b != blk(d, z))
            def _():
                mate(a, b).wait_send()
                mate_got(a, b)
    return pos, begin, first, rounds, finish_one


def count_places(picks, first, out_ref, size):
    tokens = picks.shape[1]
    chunk = 64
    @pl.loop(0, size // chunk)
    def _(t):
        at = pl.multiple_of(t * chunk, chunk)
        place = lax.broadcasted_iota(jnp.int32, (chunk, tokens), 0) + (first + at)
        count = jnp.zeros((chunk, tokens), jnp.int32)
        for k in range(picks.shape[0]):
            count = count + (picks[k : k + 1, :] == place).astype(jnp.int32)
        out_ref[pl.ds(at, chunk), :] = count.astype(F32).astype(BF)


def count_kernel(doc_len, all_ref, out_ref):
    count_places(all_ref[0], lax.axis_index("wide") * doc_len, out_ref.at[0], doc_len)


def count_all(picks, doc_len, peers):
    everyone = lax.all_gather(picks, "wide", axis=0)
    shape = (1,) + picks.shape
    return pl.pallas_call(
        functools.partial(count_kernel, doc_len),
        grid=(peers,),
        in_specs=[pl.BlockSpec(shape, lambda i: (i, 0, 0))],
        out_specs=pl.BlockSpec((1, doc_len, picks.shape[1]), lambda i: (i, 0, 0)),
        out_shape=jax.ShapeDtypeStruct((peers, doc_len, picks.shape[1]), BF),
        name="count",
    )(everyone)


def put_columns(ref, at, x):
    spare = ref.shape[0] - x.shape[0]
    full = jnp.concatenate([x.astype(F32), jnp.zeros((spare, x.shape[1]), F32)], axis=0) if spare else x
    ref[:, at : at + x.shape[1]] = full.astype(ref.dtype)


def picks_events(pos, doc_len, picks_ref, counts_ref, p_all, s_p, r_p):
    peers = 2 * pos.zc
    part = doc_len // 2
    def picks_copy(k, there):
        o = lax.rem(pos.w + k, peers)
        slot = pos.w if there else o
        return pltpu.make_async_remote_copy(src_ref=picks_ref, dst_ref=p_all.at[slot], send_sem=s_p.at[o], recv_sem=r_p.at[slot], device_id=(pos.d, o), device_id_type=MESH)
    def begin():
        @pl.loop(1, peers)
        def _(k):
            picks_copy(k, True).start()
    def counted(k, h):
        o = lax.rem(pos.w + k, peers)
        if k and not h:
            picks_copy(k, False).wait_recv()
        picks = p_all[o] if k else picks_ref[...]
        count_places(picks, pos.w * doc_len + h * part, counts_ref.at[o, pl.ds(h * part, part)], part)
    def finish():
        @pl.loop(1, peers)
        def _(k):
            picks_copy(k, True).wait_send()
    return begin, [functools.partial(counted, k, h) for k in range(peers) for h in range(2)], finish


def gather_scratch(shapes, zc):
    count = len(shapes)
    comps = [pltpu.VMEM((2 * rows, cols), BF) for rows, cols in shapes]
    mines = [pltpu.VMEM((rows + -rows % 16, cols), BF) for rows, cols in shapes]
    dma = pltpu.SemaphoreType.DMA
    sems = [dma((count, 2, zc)), dma((count, 2, zc)), dma((count, zc)), dma((count, 4 * zc)), dma((count,)), dma((count,)),
            dma((count, zc)), dma((count, zc)), dma((count, zc)), dma((count, zc)), dma((count, 4 * zc)), dma((count,))]
    return comps + mines + sems


def reduce_events(zc, g, out, rest):
    count = len(g)
    pos = Place(zc)
    z, c, d = pos.z, pos.c, pos.d
    loc = rest[:count]; rxp = rest[count:2 * count]; rxf = rest[2 * count:3 * count]
    rxl = rest[3 * count:4 * count]; rxr = rest[4 * count:5 * count]
    rxz = rest[5 * count:6 * count]
    fin = rest[6 * count:7 * count]; rxm = rest[7 * count:8 * count]
    (s_pair, r_pair, s_loc, s_ring, r_fwd, r_left, r_right, s_z, r_z, s_fin, r_fin) = rest[8 * count:]
    rows = [x.shape[0] // (4 * zc) for x in g]
    half = [x.shape[1] // 2 for x in g]
    mate_dev = pos.dev(c=1 - c)
    right_dev = pos.dev(d=pos.right); left_dev = pos.dev(d=pos.left)
    def remote(src, dst, ss, rs, dev):
        return pltpu.make_async_remote_copy(src_ref=src, dst_ref=dst, send_sem=ss, recv_sem=rs, device_id=dev, device_id_type=MESH)
    def strip(a, dd):
        return pl.ds(pl.multiple_of(dd * zc * rows[a], 16), zc * rows[a])
    def cols(a, core):
        return pl.ds(pl.multiple_of(core * half[a], 128), half[a])
    def pair(a, dd):
        return remote(g[a].at[strip(a, dd), cols(a, 1 - c)], rxp[a].at[strip(a, dd), :], s_pair.at[a, dd], r_pair.at[a, dd], mate_dev)
    def local(a, dd):
        return pltpu.make_async_copy(g[a].at[strip(a, dd), cols(a, c)], loc[a].at[strip(a, dd), :], s_loc.at[a, dd])
    def first_row(a, dd, zz):
        return (dd * zc + zz) * rows[a]
    def row(a, dd, zz):
        return pl.ds(pl.multiple_of(first_row(a, dd, zz), 16), rows[a])
    def slot(a, zz):
        return pl.ds(pl.multiple_of(zz * rows[a], 16), rows[a])
    def add(a, dst, terms):
        group = 16
        while rows[a] % (2 * group) == 0 and 2 * group * half[a] <= 32768:
            group *= 2
        @pl.loop(0, rows[a] // group)
        def _(t):
            total = None
            for ref, at in terms:
                v = ref[pl.ds(pl.multiple_of(at + t * group, 16), group), :].astype(F32)
                total = v if total is None else total + v
            ref, at = dst
            ref[pl.ds(pl.multiple_of(at + t * group, 16), group), :] = total.astype(ref.dtype)
    def pair_sum(a, dd, zz, extra=()):
        r = first_row(a, dd, zz)
        add(a, (loc[a], r), [(loc[a], r), (rxp[a], r)] + list(extra))
    def first_right(a, zz):
        return remote(loc[a].at[row(a, pos.opp, zz), :], rxf[a].at[slot(a, zz), :], s_ring.at[a, 0, zz], r_fwd.at[a, zz], right_dev)
    def first_left(a, zz):
        return remote(loc[a].at[row(a, pos.opp, zz), :], rxf[a].at[slot(a, zz), :], s_ring.at[a, 0, zz], r_fwd.at[a, zz], left_dev)
    def to_right(a, zz):
        return remote(loc[a].at[row(a, pos.right, zz), :], rxl[a].at[slot(a, zz), :], s_ring.at[a, 1, zz], r_left.at[a, zz], right_dev)
    def to_left(a, zz):
        return remote(loc[a].at[row(a, pos.left, zz), :], rxr[a].at[slot(a, zz), :], s_ring.at[a, 2, zz], r_right.at[a, zz], left_dev)
    def to_line(a, zt):
        return remote(loc[a].at[row(a, d, zt), :], rxz[a].at[slot(a, z), :], s_z.at[a, zt], r_z.at[a, z], pos.dev(z=zt))
    def from_line(a, zs):
        return remote(loc[a].at[row(a, d, zs), :], rxz[a].at[slot(a, zs), :], s_z.at[a, zs], r_z.at[a, zs], pos.dev(z=zs))
    def mate_rows(a):
        r2 = rows[a] // 2
        return pl.ds(pl.multiple_of((1 - c) * r2, 8), r2)
    def my_rows(a):
        r2 = rows[a] // 2
        return pl.ds(pl.multiple_of(c * r2, 8), r2)
    def final(a):
        return remote(fin[a].at[mate_rows(a), :], rxm[a], s_fin.at[a], r_fin.at[a], mate_dev)

    order = []
    for i in range(zc // 2):
        order += [zc - 1 - i, i]
    head = order[0]
    def begin():
        for a in range(count):
            for dd in (pos.opp, pos.right, pos.left):
                pair(a, dd).start(); local(a, dd).start()
        for a in range(count):
            pair(a, d).start(); local(a, d).start()
    def opposite(a, zz):
        if zz == head:
            pair(a, pos.opp).wait_recv(); local(a, pos.opp).wait()
        pair_sum(a, pos.opp, zz)
        (first_right if zz % 2 == 0 else first_left)(a, zz).start()
    def beside(a, zz):
        if zz % 2:
            pair_sum(a, pos.right, zz); to_right(a, zz).start()
        else:
            pair_sum(a, pos.left, zz); to_left(a, zz).start()
    def neighbours(a):
        for dd in (pos.right, pos.left):
            pair(a, dd).wait_recv(); local(a, dd).wait()
    def onward(a, zz):
        if zz % 2 == 0:
            first_right(a, zz).wait_recv()
            pair_sum(a, pos.right, zz, [(rxf[a], zz * rows[a])]); to_right(a, zz).start()
        else:
            first_left(a, zz).wait_recv()
            pair_sum(a, pos.left, zz, [(rxf[a], zz * rows[a])]); to_left(a, zz).start()
    def column(a, zz, dst, extra=()):
        r = first_row(a, d, zz)
        add(a, dst, [(loc[a], r), (rxp[a], r), (rxl[a], zz * rows[a]), (rxr[a], zz * rows[a])] + list(extra))
    def arrived(a, zz):
        if zz == head:
            pair(a, d).wait_recv(); local(a, d).wait()
        to_right(a, zz).wait_recv(); to_left(a, zz).wait_recv()
    def line(a, zt):
        @pl.when(z != zt)
        def _():
            column(a, zt, (loc[a], first_row(a, d, zt)))
            to_line(a, zt).start()
    def mine(a):
        others = [lax.rem(z + k, zc) for k in range(1, zc)]
        for o in others:
            from_line(a, o).wait_recv()
        column(a, z, (fin[a], 0), [(rxz[a], o * rows[a]) for o in others])
        final(a).start()
    def whole(a):
        out[a][:, cols(a, c)] = fin[a][my_rows(a), :]
        final(a).wait_recv()
        out[a][:, cols(a, 1 - c)] = rxm[a][...]
    def steps_of(a):
        call = functools.partial
        cuts = [order[: zc // 2], order[zc // 2 :]]
        stages = [[call(opposite, a, zz) for zz in order] + [call(neighbours, a)]]
        for n, cut in enumerate(cuts):
            before = cuts[n - 1] if n else []
            stages.append(
                [call(arrived, a, zz) for zz in before]
                + [call(onward, a, zz) for zz in cut]
                + [call(beside, a, zz) for zz in cut]
                + [call(line, a, zz) for zz in before]
            )
        stages.append([call(arrived, a, zz) for zz in cuts[-1]] + [call(line, a, zz) for zz in cuts[-1]])
        stages.append([call(mine, a)])
        return stages
    def all_steps():
        parts = [steps_of(a) for a in range(count)]
        depth = len(parts[0])
        groups = []
        for t in range(count + depth - 1):
            group = []
            for a in range(count):
                if 0 <= t - a < depth:
                    group += parts[a][t - a]
            groups.append(group)
        return groups + [[functools.partial(whole, a) for a in range(count)]]
    def finish():
        for a in range(count):
            for dd in range(4):
                pair(a, dd).wait_send()
            for zz in range(zc):
                (first_right if zz % 2 == 0 else first_left)(a, zz).wait_send()
                to_right(a, zz).wait_send(); to_left(a, zz).wait_send()
                @pl.when(zz != z)
                def _():
                    to_line(a, zz).wait_send()
            final(a).wait_send()
    return pos, begin, all_steps, finish


ROW_BLOCK = 128


def input_grad(dqkv_ref, w_ref, rows_ref, dh_ref, gains_ref, dx_ref):
    up = dot_nt(dqkv_ref[...], w_ref[...])
    dv, _ = rms_pull(rows_ref[...].astype(F32), gains_ref[0:1, :], up)
    dx_ref[...] = dh_ref[...] + dv


def reduce_kernel(zc, count, rows_total, dqkv_ref, w_ref, rows_ref, dh_ref, gains_ref, *refs):
    if not count:
        input_grad(dqkv_ref, w_ref, rows_ref, dh_ref, gains_ref, refs[0])
        return
    i = pl.program_id(0)
    g = refs[:count]; table = refs[count]
    dx_ref = refs[count + 1]
    refs = refs[1:]
    out = refs[count + 1 : 2 * count + 1]
    table_out, tabs, s_tab, r_tab = refs[2 * count + 1 : 2 * count + 5]
    pos, begin, all_steps, finish = reduce_events(zc, g, out, refs[2 * count + 5 :])
    n_dev = 8 * zc
    me = pos.d * (2 * zc) + pos.w
    def device(o):
        return (o // (2 * zc), lax.rem(o, 2 * zc))
    def tab_copy(k):
        o = lax.rem(me + k, n_dev)
        return pltpu.make_async_remote_copy(src_ref=table, dst_ref=tabs.at[me], send_sem=s_tab.at[k], recv_sem=r_tab.at[me], device_id=device(o), device_id_type=MESH)
    def tab_got(k):
        o = lax.rem(me + k, n_dev)
        return pltpu.make_async_remote_copy(src_ref=table, dst_ref=tabs.at[o], send_sem=s_tab.at[k], recv_sem=r_tab.at[o], device_id=device(o), device_id_type=MESH)
    def enter_all():
        barrier = pltpu.get_barrier_semaphore()
        @pl.loop(1, n_dev)
        def _(k):
            pl.semaphore_signal(barrier, inc=1, device_id=device(lax.rem(me + k, n_dev)), device_id_type=MESH)
        pl.semaphore_wait(barrier, n_dev - 1)
        begin()
        @pl.loop(1, n_dev)
        def _(k):
            tab_copy(k).start()
    def leave():
        tabs[me] = table[...]
        @pl.loop(1, n_dev)
        def _(k):
            tab_got(k).wait_recv()
            tab_copy(k).wait_send()
        total = tabs[0]
        for k in range(1, n_dev):
            total = total + tabs[k]
        table_out[...] = total
        finish()
    blocks = pl.num_programs(0)
    @pl.when(i == 0)
    def _():
        enter_all()
    input_grad(dqkv_ref, w_ref, rows_ref, dh_ref, gains_ref, dx_ref)
    groups = all_steps()
    early, late = groups[: len(groups) - 2], groups[len(groups) - 2 :]
    places = max(1, rows_total // ROW_BLOCK - 1)
    for n, group in enumerate(early):
        @pl.when(i == min(places, (n * places) // len(early)))
        def _():
            for step in group:
                step()
    @pl.when(i == blocks - 1)
    def _():
        for group in late:
            for step in group:
                step()
        leave()


def reduce_scratch(grads, zc):
    count = len(grads)
    V = pltpu.VMEM
    rows = [x.shape[0] // (4 * zc) for x in grads]; half = [x.shape[1] // 2 for x in grads]
    scratch = [V((x.shape[0], h), BF) for x, h in zip(grads, half)] * 2
    for _ in range(4):
        scratch += [V((zc * r, h), BF) for r, h in zip(rows, half)]
    scratch += [V((r, h), F32) for r, h in zip(rows, half)]
    scratch += [V((r // 2, h), F32) for r, h in zip(rows, half)]
    dma = pltpu.SemaphoreType.DMA
    return scratch + [dma((count, 4)), dma((count, 4)), dma((count, 4)), dma((count, 3, zc))] + [dma((count, zc))] * 5 + [dma((count,)), dma((count,))]


def reduce_shapes(grads, n_dev):
    return [jax.ShapeDtypeStruct((x.shape[0] // n_dev, x.shape[1]), F32) for x in grads]


def reduce_scatter(dqkv, w_one, rows, d_hidden, gains, grads, table, zc):
    count = len(grads)
    n_dev = 8 * zc
    total, width = rows.shape
    dma = pltpu.SemaphoreType.DMA
    block = lambda cols: pl.BlockSpec((ROW_BLOCK, cols), lambda i: (i, 0))
    whole = pl.BlockSpec(memory_space=pltpu.VMEM)
    remote = dict(collective_id=1, has_side_effects=True) if count else {}
    extra = reduce_shapes(grads, n_dev) + [jax.ShapeDtypeStruct(table.shape, F32)] if count else []
    scratch = [pltpu.VMEM((n_dev,) + table.shape, F32), dma((n_dev,)), dma((n_dev,))] + reduce_scratch(grads, zc) if count else []
    return pl.pallas_call(
        functools.partial(reduce_kernel, zc, count, total),
        grid=(total // ROW_BLOCK,),
        out_shape=[jax.ShapeDtypeStruct(rows.shape, F32)] + extra,
        in_specs=[
            block(dqkv.shape[1]),
            pl.BlockSpec((width, dqkv.shape[1]), lambda i: (0, 0), pipeline_mode=pl.Buffered(1)),
            block(width), block(width),
            pl.BlockSpec(gains.shape, lambda i: (0, 0)),
        ] + ([pl.BlockSpec(memory_space=pl.ANY)] * count + [whole] if count else []),
        out_specs=[block(width)] + [whole] * len(extra),
        scratch_shapes=scratch,
        compiler_params=pltpu.CompilerParams(vmem_limit_bytes=VMEM_ALL, **remote),
        name="reduce_grads",
    )(dqkv, w_one, rows, d_hidden, gains, *([*grads, table] if count else []))


def apart_kernel(layouts, docs_in, queries_in, packed_ref, gain_ref, wq_ref, wk_ref, wv_ref, *refs):
    count = len(layouts)
    docs_ref, queries_ref, table_ref, g_attn, g_ffn, g_end = refs[count : count + 6]
    outs = list(refs[count + 6 :])
    docs_ref[...] = docs_in[...]
    @pl.when(pl.program_id(0) == 0)
    def _():
        queries_ref[...] = queries_in[...]
        done = []
        for ref, layout in zip(refs[:count], layouts):
            for pieces in layout:
                out = outs.pop(0)
                done.append(out)
                to = 0
                for start, size in pieces:
                    out[:, to : to + size] = ref[:, start : start + size]
                    to += size
        weighed = sum(w[...].astype(F32) * g[...] for w, g in zip((wq_ref, wk_ref, wv_ref), done))
        n = weighed.shape[0]
        g_attn[...] = turned(jnp.sum(weighed, axis=1, keepdims=True))[0:1, :n] / gain_ref[...].astype(F32)
        columns = refs[1][:, refs[1].shape[1] - 128 :]
        rows = turned(columns)
        g_ffn[...] = rows[1:2, :n]
        g_end[...] = rows[2:3, :n]
        heads, buckets = table_ref.shape
        pieces = [packed_ref[:, i * buckets : (i + 1) * buckets] for i in range(-(-heads // 8))]
        table_ref[...] = jnp.concatenate(pieces, axis=0)[:heads]


def apart(dx, packed, gain, weights, sums, layouts, doc_rows, table_shape):
    total, width = dx.shape
    rest = total - doc_rows
    n = weights[0].shape[0]
    shapes = [jax.ShapeDtypeStruct(s, F32) for s in ((doc_rows, width), (rest, width), table_shape, (1, n), (1, n), (1, n))]
    shapes += [
        jax.ShapeDtypeStruct((x.shape[0], sum(size for _, size in pieces)), F32)
        for x, layout in zip(sums, layouts)
        for pieces in layout
    ]
    fixed = lambda x: pl.BlockSpec(x.shape, lambda i: (0, 0), pipeline_mode=pl.Buffered(1))
    block = pl.BlockSpec((doc_rows // 4, width), lambda i: (i, 0))
    extra = [packed, gain, *weights, *sums]
    return pl.pallas_call(
        functools.partial(apart_kernel, layouts),
        grid=(4,),
        out_shape=shapes,
        in_specs=[block, pl.BlockSpec((rest, width), lambda i: (doc_rows // rest, 0), pipeline_mode=pl.Buffered(1))] + [fixed(x) for x in extra],
        out_specs=[block] + [fixed(x) for x in shapes[1:]],
        compiler_params=pltpu.CompilerParams(vmem_limit_bytes=VMEM_ALL),
        name="apart",
    )(dx, dx, *extra)


def bucket_of(n):
    far = jnp.zeros_like(n)
    dist = jnp.abs(n)
    for power_step in range(1, 8):
        far = far + (dist * dist >= 64 * 2**power_step).astype(jnp.int32)
    return jnp.where(n > 0, 16, 0) + jnp.where(dist < 8, dist, 8 + far)

def diagonal_hot(doc_len, rows):
    span = 2 * doc_len
    i = lax.broadcasted_iota(jnp.int32, (1, span), 1)
    n = doc_len - 128 - jnp.where(i >= span - 127, i - span, i)
    inside = (n > -doc_len) & (n < doc_len)
    bucket = jnp.where(inside, bucket_of(n), -1)
    return (lax.broadcasted_iota(jnp.int32, (rows, span), 0) == bucket).astype(F32)


def padded_tile(x):
    n, m = x.shape
    x = x.astype(F32)
    if m < 128:
        x = jnp.concatenate([x, jnp.zeros((n, 128 - m), F32)], axis=1)
    if n < 128:
        x = jnp.concatenate([x, jnp.zeros((128 - n, 128), F32)], axis=0)
    return x


def turned(x):
    return padded_tile(x).T


def per_token(values, first, shape, dim, slots):
    owner = lax.broadcasted_iota(jnp.int32, shape, dim) // slots
    out = jnp.zeros(shape, jnp.int32)
    for q in range(shape[dim] // slots):
        n = first + q
        out = jnp.where(owner == q, values[n // values.shape[1], n % values.shape[1]], out)
    return out


def live_tile(lengths, tile, slots):
    shape = (128, 128)
    key = lax.broadcasted_iota(jnp.int32, shape, 0)
    query = lax.broadcasted_iota(jnp.int32, shape, 1)
    limit = per_token(lengths, tile * (128 // slots), shape, 0, slots)
    return (lax.rem(key, slots) < limit) & (key // slots == query // slots)


def cols_dot(a, b):
    return lax.dot_general(a, b, (((1,), (1,)), ((), ())), preferred_element_type=F32)

def tiles_of(table, keys, q_from, q_len, doc_len):
    parts = []
    for kb in range(keys // 128):
        at = doc_len - 128 - 128 * kb + q_from
        parts.append(table[:, at : at + q_len])
    return jnp.concatenate(parts, axis=0) if len(parts) > 1 else parts[0]

def spread_steps(steps, first_slot, slots):
    plan = {}
    for n, step in enumerate(steps):
        at = min(slots - 1, first_slot + (n * (slots - first_slot)) // len(steps))
        plan.setdefault(at, []).append(step)
    return plan


def attend_kernel(doc_len, doc_count, block, zc, slot_count, docs_ref, queries_ref, rel_ref, lengths_ref, *refs):
    beside = zc > 0
    ins = 12 if beside else 1
    raw = refs[:ins]
    rows_ref, gains_ref, normed_ref, qkv_ref, ctx_ref, lse_ref, table_ref = refs[ins : ins + 7]
    j = pl.program_id(0)
    span = 2 * doc_len
    hd = 64
    total = rows_ref.shape[0]
    width = rows_ref.shape[1]
    rest = total - doc_count * doc_len
    places = [(m * doc_len, doc_len, q_at, block, None) for m in range(doc_count) for q_at in range(0, doc_len, block)]
    places += [(doc_count * doc_len + 128 * i, 128, 0, 128, i) for i in range(rest // 128)]
    slots = len(places)
    plan = {}
    if beside:
        q_ref, k_ref, v_ref, o_ref, p_ref, *g_refs, gate_ref, up_ref, down_ref, raw_picks = raw
        outs = refs[ins + 7 : ins + 10]
        counts_ref = refs[ins + 10]
        shards = refs[ins + 11 : ins + 14]
        w_ref, load, picks_ref, p_all, s_p, r_p = refs[ins + 14 : ins + 20]
        pos, begin, first, rounds, finish_one = gather_events(zc, shards, outs, refs[ins + 20 : -1])
        begin_picks, pieces, finish_picks = picks_events(pos, doc_len, picks_ref, counts_ref, p_all, s_p, r_p)
        every = [rounds(a) for a in (1, 2)]
        steps = [step for same in zip(*every) for step in same]
        plan = spread_steps(steps, 0, slots * (width // 128))
    else:
        (w_ref,) = raw
    diag_ref = refs[-1]
    def now(i):
        for slot, steps in plan.items():
            if slot % slots == i:
                @pl.when(j == slot // slots)
                def _():
                    for step in steps:
                        step()
    def assemble():
        for i in range(width // 128):
            for n, ref in enumerate((q_ref, k_ref, v_ref)):
                put_columns(shards[0], 384 * i + 128 * n, ref[:, 128 * i : 128 * i + 128])
        put_columns(shards[0], 3 * width, o_ref[...])
        put_columns(shards[0], 4 * width, p_ref[...])
        gains = jnp.concatenate([g[...].astype(F32) for g in g_refs], axis=0)
        put_columns(shards[0], 4 * width + p_ref.shape[1], turned(gains)[: q_ref.shape[0]])
        picks_ref[...] = turned(raw_picks[...])[: picks_ref.shape[0]].astype(jnp.int32)
        size = FF_BLOCK
        for i in range(gate_ref.shape[1] // size):
            put_columns(shards[1], 2 * size * i, gate_ref[:, size * i : size * i + size])
            put_columns(shards[1], 2 * size * i + size, up_ref[:, size * i : size * i + size])
        put_columns(shards[2], 0, down_ref[...])
    @pl.when(j == 0)
    def _():
        if beside:
            assemble()
            begin(True)
            begin_picks()
            first(0)
        table = padded_tile(rel_ref[...])[: diag_ref.shape[0]].astype(BF)
        diag_ref[...] = dot(table, diagonal_hot(doc_len, 128).astype(BF))
        rows_ref[0 : docs_ref.shape[0], :] = docs_ref[...]
        rows_ref[docs_ref.shape[0] :, :] = queries_ref[...]
        if beside:
            steps = rounds(0)
            for n, step in enumerate(steps):
                if n == len(steps) - 3:
                    first(1)
                    first(2)
                for piece in pieces[len(pieces) * n // len(steps) : len(pieces) * (n + 1) // len(steps)]:
                    piece()
                step()
            finish_one(0)
            loading = pltpu.make_async_copy(outs[0], w_ref, load)
            loading.start()
            loading.wait()
        gains_ref[...] = w_ref[:, w_ref.shape[1] - 128 :].astype(F32).T[0:8]
        for c in chunks_of(total, 4):
            x = rows_ref[c, :].astype(F32)
            normed_ref[c, :] = (x * inverse_rms(x) * gains_ref[0:1, :]).astype(BF)
    w_now = w_ref[:, pl.ds(pl.multiple_of(j * 384, 128), 384)]
    for c in chunks_of(total, 4):
        qkv_ref[c, :] = dot(normed_ref[c, :], w_now).astype(BF)
    for h in range(2):
        wide = jnp.broadcast_to(diag_ref[pl.ds(2 * j + h, 1), :], (128, span))
        table_ref[h] = pltpu.roll(wide, 0, 1, stride=1, stride_axis=0)[:, : span - 128]
    lane = lax.broadcasted_iota(jnp.int32, (1, 128), 1)
    def part(rows, keys, q_at, q_len, mask):
        q2 = qkv_ref[pl.ds(rows + q_at, q_len), 0:128]
        k2 = qkv_ref[pl.ds(rows, keys), 128:256]
        v2 = qkv_ref[pl.ds(rows, keys), 256:384]
        v2t = v2.astype(F32).T.astype(BF)
        outs = []
        for h in range(2):
            qm = jnp.where((lane < hd) == (h == 0), q2, jnp.zeros_like(q2))
            s = dot_nt(k2, qm) + tiles_of(table_ref.at[h], keys, q_at, q_len, doc_len)
            if mask is not None:
                s = jnp.where(live_tile(lengths_ref, mask, slot_count), s, mask_fill)
            top = jnp.max(s, axis=0, keepdims=True)
            e = jnp.exp(s - top)
            total = jnp.sum(e, axis=0, keepdims=True)
            p = (e * (1.0 / total)).astype(BF)
            lse_ref[0, h : h + 1, pl.ds(rows + q_at, q_len)] = top + jnp.log(total)
            outs.append(dot(v2t[h * hd : (h + 1) * hd], p))
        ctx_ref[pl.ds(rows + q_at, q_len), :] = jnp.concatenate(outs, axis=0).T.astype(BF)
    for i, place in enumerate(places):
        now(i)
        part(*place)
    if beside:
        @pl.when(j == pl.num_programs(0) - 1)
        def _():
            finish_one(1)
            finish_one(2)
            finish_picks()


def attend(docs, queries, rel, lengths, slots, doc_len, doc_count, weights, picks, w_one, zc, n_dev):
    width = docs.shape[1]
    total = docs.shape[0] + queries.shape[0]
    pairs = width // 128
    span = 2 * doc_len
    once = pl.Buffered(1)
    whole = pl.BlockSpec(memory_space=pltpu.VMEM)
    fixed = lambda shape: pl.BlockSpec(shape, lambda j: (0, 0), pipeline_mode=once)
    extra_in, extra_out, extra_specs, scratch, remote = [w_one], [], [], [], {}
    if zc:
        peers = 2 * zc
        dma = pltpu.SemaphoreType.DMA
        one, (gate, up, down) = weights[:5], weights[8:]
        turned_picks = picks.shape[::-1]
        shapes = [(one[0].shape[0], sum(w.shape[1] for w in one) + 128), (gate.shape[0], 2 * gate.shape[1]), down.shape]
        extra_in = [*weights, picks]
        extra_out = [jax.ShapeDtypeStruct((r * n_dev, c), BF) for r, c in shapes]
        extra_out += [jax.ShapeDtypeStruct((peers, doc_len, picks.shape[0]), BF)]
        extra_specs = [pl.BlockSpec(memory_space=pl.ANY)] * 3 + [whole]
        scratch = [pltpu.VMEM((r + -r % 16, c), BF) for r, c in shapes]
        scratch += [pltpu.VMEM(extra_out[0].shape, BF), dma, pltpu.VMEM(turned_picks, jnp.int32), pltpu.VMEM((peers,) + turned_picks, jnp.int32), dma((peers,)), dma((peers,))]
        scratch += gather_scratch(shapes, zc)
        remote = dict(collective_id=3, has_side_effects=True)
    return pl.pallas_call(
        functools.partial(attend_kernel, doc_len, doc_count, 256, zc, slots),
        grid=(pairs,),
        in_specs=[
            fixed(docs.shape), fixed(queries.shape),
            fixed(rel.shape), pl.BlockSpec(memory_space=pltpu.SMEM),
        ] + [whole] * len(extra_in),
        out_specs=[
            fixed((total, width)), fixed((8, width)), fixed((total, width)),
            pl.BlockSpec((total, 384), lambda j: (0, j)),
            pl.BlockSpec((total, 128), lambda j: (0, j)),
            pl.BlockSpec((1, 8, total), lambda j: (j, 0, 0)),
            pl.BlockSpec((2, 128, span - 128), lambda j: (j, 0, 0)),
        ] + extra_specs,
        out_shape=[
            jax.ShapeDtypeStruct((total, width), BF),
            jax.ShapeDtypeStruct((8, width), F32),
            jax.ShapeDtypeStruct((total, width), BF),
            jax.ShapeDtypeStruct((total, pairs * 384), BF),
            jax.ShapeDtypeStruct((total, width), BF),
            jax.ShapeDtypeStruct((pairs, 8, total), F32),
            jax.ShapeDtypeStruct((pairs * 2, 128, span - 128), F32),
        ] + extra_out,
        scratch_shapes=scratch + [pltpu.VMEM((2 * pairs + -2 * pairs % 16, span), F32)],
        compiler_params=pltpu.CompilerParams(vmem_limit_bytes=VMEM_ALL, **remote),
        name="attend",
    )(docs, queries, rel, lengths, *extra_in)


BACK_SHARES = (0.0, 0.27, 0.5, 0.78, 0.93, 0.97, 1.0)


def attend_back_kernel(doc_len, doc_count, block, zc, count, pairs_total, slot_count, bucket_count, qkv_ref, do_ref, lse_ref, table_ref, lengths_ref,
                       normed_ref, *refs):
    grads = refs[:count]
    wg_ref, packed_ref, dqkv_ref = refs[count : count + 3]
    outs = refs[count + 3 : 2 * count + 3]
    acc, normed_t, diag_ref = refs[2 * count + 3 : 2 * count + 6]
    j = pl.program_id(0)
    span = 2 * doc_len
    hd = 64
    rest = qkv_ref.shape[0] - doc_count * doc_len
    slots = doc_count * (doc_len // block) + rest // 128
    pairs = pairs_total
    plan = {}
    if count:
        pos, begin, all_steps, finish = reduce_events(zc, grads, outs, refs[2 * count + 6 :])
        for group, share in zip(all_steps(), BACK_SHARES):
            for n, step in enumerate(group):
                at = min(slots * pairs - 1, int(share * slots * pairs) + n // 4)
                plan.setdefault(at, []).append(step)
        @pl.when(j == 0)
        def _():
            enter(pos)
            begin()
    slot = [0]
    def now():
        for at, steps in plan.items():
            if at % slots == slot[0]:
                @pl.when(j == at // slots)
                def _():
                    for step in steps:
                        step()
        slot[0] += 1
    @pl.when(j == 0)
    def _():
        normed_t[...] = normed_ref[...].T
    acc[...] = jnp.zeros_like(acc)
    lane = lax.broadcasted_iota(jnp.int32, (1, 128), 1)
    def part(rows, keys, q_len, mask):
        k2 = qkv_ref[pl.ds(rows, keys), 128:256]
        v2 = qkv_ref[pl.ds(rows, keys), 256:384]
        k2t = k2.astype(F32).T.astype(BF)
        dk = jnp.zeros((keys, 128), F32)
        dv = jnp.zeros((keys, 128), F32)
        for q_at in range(0, keys, q_len):
            now()
            qr = pl.ds(rows + q_at, q_len)
            q2 = qkv_ref[qr, 0:128]
            do2 = do_ref[qr, :]
            outs = []
            for h in range(2):
                mine = (lane < hd) == (h == 0)
                qm = jnp.where(mine, q2, jnp.zeros_like(q2))
                dom = jnp.where(mine, do2, jnp.zeros_like(do2))
                s = dot_nt(k2, qm) + tiles_of(table_ref.at[h], keys, q_at, q_len, doc_len)
                if mask is not None:
                    s = jnp.where(live_tile(lengths_ref, mask, slot_count), s, mask_fill)
                p = jnp.exp(s - lse_ref[0, h : h + 1, qr])
                dp = dot_nt(v2, dom)
                ds = p * (dp - jnp.sum(p * dp, axis=0, keepdims=True))
                for kb in range(keys // 128):
                    at = doc_len - 128 - 128 * kb + q_at
                    acc[h, :, at : at + q_len] += ds[128 * kb : 128 * (kb + 1)]
                low = ds.astype(BF)
                dv += dot(p.astype(BF), dom)
                dk += dot(low, qm)
                outs.append(dot(k2t[h * hd : (h + 1) * hd], low))
            dqkv_ref[qr, 0:128] = jnp.concatenate(outs, axis=0).T.astype(BF)
        dqkv_ref[pl.ds(rows, keys), 128:256] = dk.astype(BF)
        dqkv_ref[pl.ds(rows, keys), 256:384] = dv.astype(BF)
    for m in range(doc_count):
        part(m * doc_len, doc_len, block, None)
    for i in range(rest // 128):
        part(doc_count * doc_len + 128 * i, 128, 128, i)
    for h in range(2):
        eight = acc[h, 0:8]
        for g in range(1, 16):
            eight = eight + pltpu.roll(acc[h, 8 * g : 8 * g + 8], span - 8 * g, 1)
        one = eight[0:1]
        for r in range(1, 8):
            one = one + pltpu.roll(eight, span - r, 1)[r : r + 1]
        diag_ref[pl.ds(2 * j + h, 1), :] = one
    wg_ref[...] = dot(normed_t[...], dqkv_ref[...]).astype(BF)
    @pl.when(j == pl.num_programs(0) - 1)
    def _():
        hot = diagonal_hot(doc_len, bucket_count)
        table = lax.dot_general(
            diag_ref[...], hot, (((1,), (1,)), ((), ())), precision=lax.Precision.HIGHEST, preferred_element_type=F32
        )
        pieces = [table[8 * i : 8 * i + 8] for i in range(table.shape[0] // 8)]
        spare = jnp.zeros((8, packed_ref.shape[1] - bucket_count * len(pieces)), F32)
        packed_ref[...] = jnp.concatenate([*pieces, spare], axis=1)
    if count:
        @pl.when(j == pl.num_programs(0) - 1)
        def _():
            finish()


def attend_back(qkv, d_ctx, lse, table, lengths, slots, bucket_count, normed, doc_len, doc_count, grads, zc, n_dev):
    total, width = qkv.shape
    pairs = width // 384
    span = 2 * doc_len
    count = len(grads)
    remote = dict(collective_id=4, has_side_effects=True) if count else {}
    fixed = lambda shape: pl.BlockSpec(shape, lambda j: (0, 0), pipeline_mode=pl.Buffered(1))
    shapes = reduce_shapes(grads, n_dev)
    return pl.pallas_call(
        functools.partial(attend_back_kernel, doc_len, doc_count, 256, zc, count, pairs, slots, bucket_count),
        grid=(pairs,),
        in_specs=[
            pl.BlockSpec((total, 384), lambda j: (0, j)),
            pl.BlockSpec((total, 128), lambda j: (0, j)),
            pl.BlockSpec((1, 8, total), lambda j: (j, 0, 0)),
            pl.BlockSpec((2, 128, span - 128), lambda j: (j, 0, 0)),
            pl.BlockSpec(memory_space=pltpu.SMEM),
            fixed(normed.shape),
        ] + [pl.BlockSpec(memory_space=pl.ANY)] * count,
        out_specs=[
            pl.BlockSpec((normed.shape[1], 384), lambda j: (0, j)),
            fixed((8, 128)),
            pl.BlockSpec((total, 384), lambda j: (0, j)),
        ] + [pl.BlockSpec(memory_space=pltpu.VMEM)] * len(shapes),
        out_shape=[
            jax.ShapeDtypeStruct((normed.shape[1], width), BF),
            jax.ShapeDtypeStruct((8, 128), F32),
            jax.ShapeDtypeStruct((total, width), BF),
        ] + shapes,
        scratch_shapes=[
            pltpu.VMEM((2, 128, span), F32), pltpu.VMEM(normed.shape[::-1], BF),
            pltpu.VMEM((2 * pairs + -2 * pairs % 16, span), F32),
        ] + (reduce_scratch(grads, zc) if count else []),
        compiler_params=pltpu.CompilerParams(vmem_limit_bytes=VMEM_ALL, **remote),
        name="attend_back",
    )(qkv, d_ctx, lse, table, lengths, normed, *grads)


def columns_of(rows):
    n = rows[0].shape[1]
    return jnp.concatenate([*rows, jnp.zeros((128 - len(rows), n), F32)], axis=0).T


def pair_columns(w):
    q, k, v = w
    rows, width = q.shape
    pack = jnp.stack([x.reshape(rows, width // 128, 128) for x in (q, k, v)], axis=2)
    return pack.reshape(rows, 3 * width)


def score_kernel(peers, doc_len, slots, emb_ref, picks_ref, counts_ref, lengths_ref, goals_ref, loss_ref, d_emb_ref,
                 q_own, q_all, q_two, d_raw, weighed, totals, pool_out, pool_in, grad_out, grad_in, dq_out, dq_in, docs_t, d_docs,
                 s_q, r_q, s_pool, r_pool, s_grad, r_grad, s_dq, r_dq):
    dp = lax.axis_index("dp"); me = lax.axis_index("wide")
    tokens = q_own.shape[0]
    feat = emb_ref.shape[1]
    half = tokens // 2
    scale = feat ** -0.5
    barrier = pltpu.get_barrier_semaphore()
    def other(k):
        return lax.rem(me + k, peers)
    def each(fn):
        @pl.loop(1, peers)
        def _(k):
            fn(other(k))
    each(lambda o: pl.semaphore_signal(barrier, inc=1, device_id=(dp, o), device_id_type=MESH))
    q_own[...] = emb_ref[2 * doc_len :, :]
    q_all[me] = q_own[...]
    pl.semaphore_wait(barrier, peers - 1)
    def send(src, dst, ss, rs, o):
        return pltpu.make_async_remote_copy(src_ref=src, dst_ref=dst, send_sem=ss, recv_sem=rs, device_id=(dp, o), device_id_type=MESH)
    def q_to(o): return send(q_own, q_all.at[me], s_q.at[o], r_q.at[me], o)
    def q_from(o): return send(q_own, q_all.at[o], s_q.at[o], r_q.at[o], o)
    def pool_to(o): return send(pool_out.at[o], pool_in.at[me], s_pool.at[o], r_pool.at[me], o)
    def pool_from(o): return send(pool_out.at[o], pool_in.at[o], s_pool.at[o], r_pool.at[o], o)
    def grad_to(o): return send(grad_out.at[o], grad_in.at[me], s_grad.at[o], r_grad.at[me], o)
    def grad_from(o): return send(grad_out.at[o], grad_in.at[o], s_grad.at[o], r_grad.at[o], o)
    def dq_to(o): return send(dq_out.at[o], dq_in.at[me], s_dq.at[o], r_dq.at[me], o)
    def dq_from(o): return send(dq_out.at[o], dq_in.at[o], s_dq.at[o], r_dq.at[o], o)
    def started(o):
        q_to(o).start()
    each(started)
    docs2 = jnp.concatenate([emb_ref[0:doc_len, :], emb_ref[doc_len : 2 * doc_len, :]], axis=1)
    docs_t[...] = docs2.astype(F32).T.astype(BF)
    row = lax.broadcasted_iota(jnp.int32, (tokens, 1), 0)
    lane = lax.broadcasted_iota(jnp.int32, (1, tokens), 1)
    group = min(8, peers)
    groups = range(peers // group)
    def members(n):
        return [(n * group + i, slice(i * tokens, (i + 1) * tokens)) for i in range(group)]
    def forward(n):
        for o, at in members(n):
            q = q_all[o]
            none = jnp.zeros_like(q)
            q_two[n, at, :] = jnp.concatenate([jnp.where(row < half, q, none), jnp.where(row < half, none, q)], axis=1)
        s = lax.dot_general(docs2, q_two[n], (((1,), (1,)), ((), ())), preferred_element_type=F32) * scale
        for o, at in members(n):
            multiple = counts_ref[o].astype(F32)
            w = multiple * jnp.exp(s[:, at])
            weighed[o] = w
            found = jnp.sum(multiple, axis=0, keepdims=True)
            weight = jnp.sum(w, axis=0, keepdims=True) + (found == 0).astype(F32)
            totals[o] = jnp.broadcast_to(weight, (8, tokens))
            pool_out[o] = jnp.broadcast_to(jnp.log(weight), (8, tokens))
    each(lambda o: q_from(o).wait_recv())
    for n in groups:
        forward(n)
    pool_in[me] = pool_out[me]
    each(lambda o: pool_to(o).start())
    each(lambda o: pool_from(o).wait_recv())
    pooled = pool_in[:, 0, :]
    mine = turned(picks_ref[...])[: picks_ref.shape[1]].astype(jnp.int32)
    hits = []
    for w in range(peers):
        inside = ((mine >= w * doc_len) & (mine < (w + 1) * doc_len)).astype(F32)
        hits.append(jnp.max(inside, axis=0, keepdims=True))
    hit = jnp.concatenate(hits, axis=0)
    live = (lax.rem(lane, slots) < per_token(lengths_ref, 0, lane.shape, 1, slots)).astype(F32)
    own_row = lax.broadcasted_iota(jnp.int32, (tokens, tokens), 0) // slots
    own_col = lax.broadcasted_iota(jnp.int32, (tokens, tokens), 1) // slots
    same = (own_row == own_col).astype(F32)
    def per_query(v):
        return jnp.dot(v, same, precision=lax.Precision.HIGHEST, preferred_element_type=F32)
    divisor = jnp.maximum(per_query(hit * live), 1.0)
    logits = score_scale * per_query(pooled * live) / divisor
    top = jnp.max(logits, axis=0, keepdims=True)
    shifted = jnp.exp(logits - top)
    total = jnp.sum(shifted, axis=0, keepdims=True)
    doc_id = lax.broadcasted_iota(jnp.int32, (peers, tokens), 0)
    chosen = (doc_id == per_token(goals_ref, 0, lane.shape, 1, slots)).astype(F32)
    loss = top + jnp.log(total) - jnp.sum(chosen * logits, axis=0, keepdims=True)
    queries = tokens // slots
    chosen_lane = (lax.broadcasted_iota(jnp.int32, (tokens, 128), 0) == lax.broadcasted_iota(jnp.int32, (tokens, 128), 1) * slots).astype(F32)
    apart_loss = jnp.dot(loss, chosen_lane, precision=lax.Precision.HIGHEST, preferred_element_type=F32)
    per = loss_ref.shape[1]
    for i in range(queries // per):
        loss_ref[i : i + 1, :] = apart_loss[:, i * per : (i + 1) * per]
    d_pooled = score_scale * (shifted / total - chosen) / divisor * live
    for w in range(peers):
        grad_out[w] = jnp.broadcast_to(d_pooled[w : w + 1], (8, tokens))
    each(lambda o: grad_to(o).start())
    grad_in[me] = grad_out[me]
    each(lambda o: grad_from(o).wait_recv())
    for n in groups:
        for o, at in members(n):
            factor = grad_in[o][0:1] / totals[o][0:1] * scale
            d_raw[n, :, at] = (weighed[o] * factor).astype(BF)
        both = jnp.dot(docs_t[...], d_raw[n], preferred_element_type=F32)
        for o, at in members(n):
            d_q = jnp.where(lane < half, both[0:feat, at], both[feat : 2 * feat, at])
            dq_out[o] = d_q.T.astype(BF)
    each(lambda o: dq_to(o).start())
    for n in groups:
        part = jnp.dot(d_raw[n], q_two[n], preferred_element_type=F32)
        d_docs[...] = part if n == 0 else d_docs[...] + part
    d_emb_ref[0:doc_len, :] = d_docs[:, 0:feat].astype(BF)
    d_emb_ref[doc_len : 2 * doc_len, :] = d_docs[:, feat : 2 * feat].astype(BF)
    dq_in[me] = dq_out[me]
    each(lambda o: dq_from(o).wait_recv())
    total_q = dq_in[0].astype(F32)
    for w in range(1, peers):
        total_q = total_q + dq_in[w].astype(F32)
    d_emb_ref[2 * doc_len :, :] = total_q.astype(BF)
    def sent(o):
        q_to(o).wait_send(); pool_to(o).wait_send(); grad_to(o).wait_send(); dq_to(o).wait_send()
    each(sent)

def score(emb, picks, counts, lengths, goals, loss_shape, doc_len, slots, peers):
    tokens = picks.shape[0]
    feat = emb.shape[1]
    group = min(8, peers)
    V = pltpu.VMEM
    dma = pltpu.SemaphoreType.DMA
    return pl.pallas_call(
        functools.partial(score_kernel, peers, doc_len, slots),
        out_shape=[jax.ShapeDtypeStruct(loss_shape, F32), jax.ShapeDtypeStruct(emb.shape, BF)],
        in_specs=[pl.BlockSpec(memory_space=pltpu.VMEM)] * 3 + [pl.BlockSpec(memory_space=pltpu.SMEM)] * 2,
        out_specs=[pl.BlockSpec(memory_space=pltpu.VMEM)] * 2,
        scratch_shapes=[
            V((tokens, feat), BF), V((peers, tokens, feat), BF),
            V((peers // group, group * tokens, 2 * feat), BF), V((peers // group, doc_len, group * tokens), BF),
            V((peers, doc_len, tokens), F32), V((peers, 8, tokens), F32),
            V((peers, 8, tokens), F32), V((peers, 8, tokens), F32), V((peers, 8, tokens), F32), V((peers, 8, tokens), F32),
            V((peers, tokens, feat), BF), V((peers, tokens, feat), BF), V((2 * feat, doc_len), BF), V((doc_len, 2 * feat), F32),
        ] + [dma((peers,))] * 8,
        compiler_params=pltpu.CompilerParams(collective_id=2, has_side_effects=True, vmem_limit_bytes=VMEM_ALL),
        name="score",
    )(emb, picks, counts, lengths, goals)


GELU_SCALE = 0.7978845608028654
GELU_CUBE = 0.044715

def dot(a, b):
    return jnp.dot(a, b, preferred_element_type=F32)

def dot_nt(a, b):
    return lax.dot_general(a, b, (((1,), (1,)), ((), ())), preferred_element_type=F32)

def dot_tn(a, b):
    return lax.dot_general(a, b, (((0,), (0,)), ((), ())), preferred_element_type=F32)

def inverse_rms(v):
    return lax.rsqrt(jnp.mean(v * v, axis=-1, keepdims=True) + eps_norm)

def chunks_of(total, parts):
    size = total // parts
    return [slice(i * size, (i + 1) * size) for i in range(parts)]

def ffn_kernel(parts, rows_ref, ctx_ref, wo_ref, wgu_ref, wd_ref, wp_ref, gains_ref, n2_ref, gu_ref, scale_ref, ne_ref, emb_ref, lo_ref):
    j = pl.program_id(0)
    block = wd_ref.shape[0]
    chunks = chunks_of(rows_ref.shape[0], parts)
    @pl.when(j == 0)
    def _():
        for c in chunks:
            h = rows_ref[c, :].astype(F32) + dot(ctx_ref[c, :], wo_ref[...])
            lo_ref[c, :] = h
            inv = inverse_rms(h)
            scale_ref[c, :] = jnp.broadcast_to(inv, scale_ref[c, :].shape)
            n2_ref[c, :] = (h * inv * gains_ref[1:2, :]).astype(BF)
    for c in chunks:
        gu = dot(n2_ref[c, :], wgu_ref[...])
        gu_ref[c, :] = gu.astype(BF)
        g = gu[:, :block]
        t = jnp.tanh(GELU_SCALE * (g + GELU_CUBE * (g * g * g)))
        act = (0.5 * g * (1.0 + t)) * gu[:, block:]
        lo_ref[c, :] += dot(act.astype(BF), wd_ref[...])
    @pl.when(j == pl.num_programs(0) - 1)
    def _():
        for c in chunks:
            lo = lo_ref[c, :]
            inv = inverse_rms(lo)
            lane = lax.broadcasted_iota(jnp.int32, (1, scale_ref.shape[1]), 1)
            scale_ref[c, :] = jnp.where(lane < 64, scale_ref[c, :], inv)
            ne = (lo * inv * gains_ref[2:3, :]).astype(BF)
            ne_ref[c, :] = ne
            emb_ref[c, :] = dot(ne, wp_ref[...]).astype(BF)

def ffn(rows, ctx, w_one, w_gu, w_down, gains, p_size, block):
    total, width = rows.shape
    ff = w_down.shape[0]
    once = pl.Buffered(1)
    full = lambda cols, at=0: pl.BlockSpec((total, cols), lambda j: (0, 0), pipeline_mode=once)
    return pl.pallas_call(
        functools.partial(ffn_kernel, 2),
        grid=(ff // block,),
        in_specs=[
            full(width), full(width),
            pl.BlockSpec((width, width), lambda j: (0, 3), pipeline_mode=once),
            pl.BlockSpec((width, 2 * block), lambda j: (0, j)),
            pl.BlockSpec((block, width), lambda j: (j, 0)),
            pl.BlockSpec((width, p_size), lambda j: (0, 4 * width // p_size), pipeline_mode=once),
            pl.BlockSpec(gains.shape, lambda j: (0, 0)),
        ],
        out_specs=[full(width), pl.BlockSpec((total, 2 * block), lambda j: (0, j)), full(128), full(width), full(p_size)],
        out_shape=[
            jax.ShapeDtypeStruct((total, width), BF), jax.ShapeDtypeStruct((total, 2 * ff), BF),
            jax.ShapeDtypeStruct((total, 128), F32), jax.ShapeDtypeStruct((total, width), BF),
            jax.ShapeDtypeStruct((total, p_size), BF),
        ],
        scratch_shapes=[pltpu.VMEM((total, width), F32)],
        compiler_params=pltpu.CompilerParams(vmem_limit_bytes=VMEM_ALL),
        name="feed_forward",
    )(rows, ctx, w_one, w_gu, w_down, w_one, gains)

def rms_pull_normed(normed, inv, gain, upstream):
    unit = normed.astype(F32) / gain
    scaled = upstream * gain
    d_gain = jnp.sum(upstream * unit, axis=0, keepdims=True)
    inner = jnp.mean(scaled * unit, axis=-1, keepdims=True)
    return inv * (scaled - unit * inner), d_gain


def rms_pull(v, gain, upstream):
    inv = inverse_rms(v)
    scaled = upstream * gain
    d_gain = jnp.sum(upstream * (v * inv), axis=0, keepdims=True)
    inner = jnp.mean(scaled * v, axis=-1, keepdims=True)
    return inv * scaled - v * (inv * inv * inv * inner), d_gain

def ffn_back_kernel(parts, de_ref, scale_ref, ne_ref, n2_ref, ctx_ref, wo_ref, wp_ref, gains_ref, gu_ref, wgu_ref, wd_ref,
                    dgu_w_ref, dd_w_ref, last_ref, dh_ref, dctx_ref, dgain_ref, dl_ref, low_ref, n2t_ref, acc_ref, dhl_ref):
    j = pl.program_id(0)
    block = wd_ref.shape[0]
    chunks = chunks_of(ne_ref.shape[0], parts)
    @pl.when(j == 0)
    def _():
        dgain_ref[...] = jnp.zeros_like(dgain_ref)
        for c in chunks:
            up = dot_nt(de_ref[c, :], wp_ref[...])
            dl, dg = rms_pull_normed(ne_ref[c, :], scale_ref[c, 64:65], gains_ref[2:3, :], up)
            dl_ref[c, :] = dl
            low_ref[c, :] = dl.astype(BF)
            dgain_ref[2:3, :] += dg
        width = ne_ref.shape[1]
        last_ref[:, width : width + de_ref.shape[1]] = dot_tn(ne_ref[...], de_ref[...]).astype(BF)
        n2t_ref[...] = n2_ref[...].T
        acc_ref[...] = jnp.zeros_like(acc_ref)
    acts, dgus = [], []
    for c in chunks:
        da = dot_nt(low_ref[c, :], wd_ref[...])
        g = gu_ref[c, :block].astype(F32)
        u = gu_ref[c, block:].astype(F32)
        t = jnp.tanh(GELU_SCALE * (g + GELU_CUBE * (g * g * g)))
        cdf = 0.5 * (1.0 + t)
        gel = g * cdf
        acts.append((gel * u).astype(BF))
        slope = cdf + (0.5 * GELU_SCALE) * g * (1.0 - t * t) * (1.0 + (3.0 * GELU_CUBE) * (g * g))
        dgu = jnp.concatenate([(da * u * slope).astype(BF), (da * gel).astype(BF)], axis=1)
        dgus.append(dgu)
        acc_ref[c, :] += dot_nt(dgu, wgu_ref[...])
    dgu_w_ref[...] = dot(n2t_ref[...], jnp.concatenate(dgus, axis=0)).astype(BF)
    dd_w_ref[...] = dot_tn(jnp.concatenate(acts, axis=0), low_ref[...]).astype(BF)
    @pl.when(j == pl.num_programs(0) - 1)
    def _():
        for c in chunks:
            dv, dg = rms_pull_normed(n2_ref[c, :], scale_ref[c, 0:1], gains_ref[1:2, :], acc_ref[c, :])
            dh = dl_ref[c, :] + dv
            dh_ref[c, :] = dh
            dhl = dh.astype(BF)
            dhl_ref[c, :] = dhl
            dgain_ref[1:2, :] += dg
            dctx_ref[c, :] = dot_nt(dhl, wo_ref[...]).astype(BF)
        width = ne_ref.shape[1]
        last_ref[:, :width] = dot_tn(ctx_ref[...], dhl_ref[...]).astype(BF)
        last_ref[:, width + de_ref.shape[1] :] = columns_of([dgain_ref[i : i + 1, :] for i in range(3)]).astype(BF)

def ffn_back(d_emb, scale, ne, n2, ctx, w_one, w_gu, w_down, gains, gu, p_size, block):
    total, width = ne.shape
    ff = w_down.shape[0]
    once = pl.Buffered(1)
    full = lambda cols: pl.BlockSpec((total, cols), lambda j: (0, 0), pipeline_mode=once)
    fixed = lambda shape: pl.BlockSpec(shape, lambda j: (0, 0), pipeline_mode=once)
    V = pltpu.VMEM
    return pl.pallas_call(
        functools.partial(ffn_back_kernel, 2),
        grid=(ff // block,),
        in_specs=[
            full(p_size), full(128), full(width), full(width), full(width),
            pl.BlockSpec((width, width), lambda j: (0, 3), pipeline_mode=once),
            pl.BlockSpec((width, p_size), lambda j: (0, 4 * width // p_size), pipeline_mode=once),
            fixed(gains.shape),
            pl.BlockSpec((total, 2 * block), lambda j: (0, j)),
            pl.BlockSpec((width, 2 * block), lambda j: (0, j)),
            pl.BlockSpec((block, width), lambda j: (j, 0)),
        ],
        out_specs=[
            pl.BlockSpec((width, 2 * block), lambda j: (0, j)),
            pl.BlockSpec((block, width), lambda j: (j, 0)),
            fixed((width, width + p_size + 128)), full(width), full(width),
        ],
        out_shape=[
            jax.ShapeDtypeStruct((width, 2 * ff), BF), jax.ShapeDtypeStruct((ff, width), BF),
            jax.ShapeDtypeStruct((width, width + p_size + 128), BF),
            jax.ShapeDtypeStruct((total, width), F32), jax.ShapeDtypeStruct((total, width), BF),
        ],
        scratch_shapes=[V((8, width), F32), V((total, width), F32), V((total, width), BF), V((width, total), BF), V((total, width), F32), V((total, width), BF)],
        compiler_params=pltpu.CompilerParams(vmem_limit_bytes=VMEM_ALL),
        name="feed_forward_back",
    )(d_emb, scale, ne, n2, ctx, w_one, w_one, gains, gu, w_gu, w_down)

def gate_up_columns(gate, up, block):
    rows, ff = gate.shape
    return jnp.stack([gate.reshape(rows, -1, block), up.reshape(rows, -1, block)], axis=2).reshape(rows, 2 * ff)


def contract_rows(left_mat, right_mat):
    return lax.dot_general(
        left_mat, right_mat, (((0,), (0,)), ((), ())), preferred_element_type=jnp.float32
    )


def contract_cols(left_mat, right_mat):
    return lax.dot_general(
        left_mat, right_mat, (((1,), (1,)), ((), ())), preferred_element_type=jnp.float32
    )


def matmul(left_mat, right_mat):
    return jnp.dot(left_mat, right_mat, preferred_element_type=jnp.float32)


def rms_forward(values, gain_vec):
    inverse = lax.rsqrt(jnp.mean(values * values, axis=-1, keepdims=True) + eps_norm)
    return (values * inverse * gain_vec, inverse)


def rms_backward(values, inverse, gain_vec, upstream):
    scaled = upstream * gain_vec
    gain_grad = jnp.sum(upstream * values * inverse, axis=0)
    inner_mean = jnp.mean(scaled * values, axis=-1, keepdims=True)
    return (inverse * scaled - values * inverse * inverse * inverse * inner_mean, gain_grad)


def two_level(shards):
    return (
        lax.axis_size("dp") == 4
        and lax.axis_size("wide") % 4 == 0
        and all(s.shape[0] % 8 == 0 for s in shards)
    )


def gathered(shards):
    return [lax.all_gather(s, ("dp", "wide"), axis=0, tiled=True) for s in shards]


def summed(grads, table):
    sums = [lax.psum_scatter(g.astype(F32), ("dp", "wide"), scatter_dimension=0, tiled=True) for g in grads]
    return [*sums, lax.psum(table, ("dp", "wide"))]


def local(
    doc_tokens,
    query_tokens,
    query_lengths,
    retrieved,
    targets,
    q_weight,
    k_weight,
    v_weight,
    o_weight,
    gate_weight,
    up_weight,
    down_weight,
    proj_weight,
    attn_gain,
    ffn_gain,
    final_gain,
    rel_bias,
):
    micro_count, _, doc_len, width = doc_tokens.shape
    slots = query_tokens.shape[2]
    doc_rows = micro_count * doc_len
    wide_count = lax.axis_size("wide")
    p_size = proj_weight.shape[1]
    bucket_count, head_count = rel_bias.shape
    pairs = width // 128
    ff_block = FF_BLOCK
    weights = [q_weight, k_weight, v_weight, o_weight, proj_weight]
    ffn_raw = [gate_weight, up_weight, down_weight]
    beside = two_level(weights + ffn_raw)
    picks = retrieved.reshape(-1, retrieved.shape[3])
    lengths = query_lengths
    n_dev = lax.axis_size("dp") * wide_count
    w_one = None
    if not beside:
        shard_one = jnp.concatenate(
            [pair_columns(weights[:3]), o_weight, proj_weight, jnp.pad(jnp.stack([attn_gain, ffn_gain, final_gain], axis=1), ((0, 0), (0, 125)))], axis=1
        )
        (w_one,) = gathered([shard_one])
    gain_rows = [g.reshape(1, -1) for g in (attn_gain, ffn_gain, final_gain)]
    shards = [*weights, *gain_rows, *ffn_raw] if beside else []
    rows_low, gains, normed, qkv, context, lse, table, *full = attend(
        doc_tokens.reshape(doc_rows, width),
        query_tokens.reshape(-1, width),
        rel_bias.T,
        lengths,
        slots,
        doc_len,
        micro_count,
        shards,
        picks,
        w_one,
        wide_count // 2 if beside else 0,
        n_dev,
    )
    if beside:
        w_one, w_gu, w_down, counts = full
    else:
        w_gu, w_down = gathered([gate_up_columns(gate_weight, up_weight, ff_block), down_weight])
        counts = count_all(picks.T, doc_len, wide_count)
    normed_two, gate_up, scale, normed_end, embedded = ffn(
        rows_low, context, w_one, w_gu, w_down, gains, p_size, ff_block
    )
    losses_out, d_embedded = score(
        embedded, picks, counts, lengths, targets, targets.shape, doc_len, slots, wide_count
    )
    gu_grad, down_grad, last_grad, d_hidden, d_context = ffn_back(
        d_embedded, scale, normed_end, normed_two, context, w_one, w_gu, w_down, gains, gate_up, p_size, ff_block
    )
    ff = down_grad.shape[0]
    ffn_layouts = [
        [[(2 * ff_block * i + at, ff_block) for i in range(ff // ff_block)] for at in (0, ff_block)],
        [[(0, width)]],
    ]
    one_layouts = [
        [[(384 * i + 128 * n, 128) for i in range(pairs)] for n in range(3)],
        [[(0, width)], [(width, p_size)], [(width + p_size, 128)]],
    ]
    zc = wide_count // 2 if beside else 0
    qkv_grad, packed, d_qkv, *ffn_sums = attend_back(
        qkv,
        d_context,
        lse,
        table,
        lengths,
        slots,
        bucket_count,
        normed,
        doc_len,
        micro_count,
        [gu_grad, down_grad] if beside else [],
        zc,
        n_dev,
    )
    d_rows, *one_sums = reduce_scatter(
        d_qkv, w_one, rows_low, d_hidden, gains, [qkv_grad, last_grad] if beside else [], packed, zc
    )
    if beside:
        *one_sums, s_table = one_sums
    else:
        *one_sums, s_gu, s_down, s_table = summed([qkv_grad, last_grad, gu_grad, down_grad], packed)
        ffn_sums = [s_gu, s_down]
    d_docs, d_queries, s_table, g_attn, g_ffn, g_final, s_q, s_k, s_v, s_o, s_proj, _, s_gate, s_up, s_down = apart(
        d_rows,
        s_table,
        gain_rows[0],
        weights[:3],
        [*one_sums, *ffn_sums],
        one_layouts + ffn_layouts,
        doc_rows,
        rel_bias.shape[::-1],
    )
    return (
        losses_out,
        d_docs.reshape(doc_tokens.shape),
        d_queries.reshape(query_tokens.shape),
        s_q,
        s_k,
        s_v,
        s_o,
        s_gate,
        s_up,
        s_down,
        s_proj,
        g_attn.reshape(-1),
        g_ffn.reshape(-1),
        g_final.reshape(-1),
        s_table.T,
    )


def solution(mesh):
    placed = (
        P(None, ("dp", "wide"), None, None),
        P(None, ("dp", "wide"), None, None),
        P(None, ("dp", "wide")),
        P(None, ("dp", "wide"), None, None),
        P(None, ("dp", "wide")),
        P(("dp", "wide"), None),
        P(("dp", "wide"), None),
        P(("dp", "wide"), None),
        P(("dp", "wide"), None),
        P(("dp", "wide"), None),
        P(("dp", "wide"), None),
        P(("dp", "wide"), None),
        P(("dp", "wide"), None),
        P(("dp", "wide")),
        P(("dp", "wide")),
        P(("dp", "wide")),
        P(),
    )
    return jax.shard_map(
        local,
        mesh=mesh,
        in_specs=placed,
        out_specs=(
            P(None, ("dp", "wide")),
            P(None, ("dp", "wide"), None, None),
            P(None, ("dp", "wide"), None, None),
            P(("dp", "wide"), None),
            P(("dp", "wide"), None),
            P(("dp", "wide"), None),
            P(("dp", "wide"), None),
            P(("dp", "wide"), None),
            P(("dp", "wide"), None),
            P(("dp", "wide"), None),
            P(("dp", "wide"), None),
            P(("dp", "wide")),
            P(("dp", "wide")),
            P(("dp", "wide")),
            P(),
        ),
        check_vma=False,
    )
```

```python
import functools

import jax
import jax.numpy as jnp
from jax import lax
from jax.experimental import pallas as pl
from jax.experimental.pallas import tpu as pltpu
from jax.sharding import PartitionSpec as P

eps_norm = 1e-06
score_scale = 6.0
mask_fill = -1000000000.0
top_precision = lax.Precision.HIGHEST
F32 = jnp.float32
BF = jnp.bfloat16
VMEM_ALL = 62 << 20
FF_BLOCK = 512


MESH = pl.DeviceIdType.MESH

def gray(p):
    return p + (p // 2) * (1 - 2 * (p % 2))

class Place:
    def __init__(self, zc):
        self.zc = zc
        d = lax.axis_index("dp"); w = lax.axis_index("wide")
        self.d, self.w = d, w
        self.z, self.c = w // 2, w % 2
        p = gray(d)
        self.right = gray((p + 1) % 4); self.left = gray((p + 3) % 4); self.opp = gray((p + 2) % 4)
    def dev(self, d=None, z=None, c=None):
        d = self.d if d is None else d
        z = self.z if z is None else z
        c = self.c if c is None else c
        return (d, z * 2 + c)

def enter(pos, wide=False, opp=False):
    barrier = pltpu.get_barrier_semaphore()
    def greet(dev):
        pl.semaphore_signal(barrier, inc=1, device_id=dev, device_id_type=MESH)
    greet(pos.dev(d=pos.right))
    greet(pos.dev(d=pos.left))
    if wide:
        @pl.loop(1, 2 * pos.zc)
        def _(k):
            greet((pos.d, lax.rem(pos.w + k, 2 * pos.zc)))
        pl.semaphore_wait(barrier, 1 + 2 * pos.zc)
    else:
        greet(pos.dev(c=1 - pos.c))
        @pl.loop(1, pos.zc)
        def _(k):
            greet(pos.dev(z=lax.rem(pos.z + k, pos.zc)))
        if opp:
            greet(pos.dev(d=pos.opp))
        pl.semaphore_wait(barrier, 2 + pos.zc + int(opp))


def gather_events(zc, shard, out, rest):
    count = len(shard)
    pos = Place(zc)
    comp = rest[:count]; mine = rest[count:2 * count]
    (s_col, s_ring, s_fwd, s_mate, s_pair, s_own, r_col, r_left, r_right, r_opp, r_mate, r_pair) = rest[2 * count:]
    z, c, d = pos.z, pos.c, pos.d
    rows = [o.shape[0] // (4 * zc) for o in out]
    half = [o.shape[1] // 2 for o in out]

    def part(a, ref, blk, core):
        return ref.at[pl.ds(pl.multiple_of(blk * rows[a], 16), rows[a]), pl.ds(pl.multiple_of(core * half[a], 128), half[a])]
    def own(a, core):
        return comp[a].at[:, pl.ds(pl.multiple_of(core * half[a], 128), half[a])]
    def rdma(a, src, blk, dev, ss, rs):
        return pltpu.make_async_remote_copy(src_ref=src, dst_ref=part(a, out[a], blk, c), send_sem=ss, recv_sem=rs, device_id=dev, device_id_type=MESH)
    def blk(dd, zz):
        return dd * zc + zz
    mate_dev = pos.dev(c=1 - c)
    def pair(a):
        return pltpu.make_async_remote_copy(src_ref=shard[a], dst_ref=mine[a], send_sem=s_pair.at[a], recv_sem=r_pair.at[a], device_id=mate_dev, device_id_type=MESH)
    def keep(a):
        return pltpu.make_async_copy(comp[a], out[a].at[pl.ds(pl.multiple_of(blk(d, z) * rows[a], 16), rows[a]), :], s_own.at[a])
    def up(a, src, zz):
        return rdma(a, src, blk(d, zz), pos.dev(z=lax.rem(z + 1, zc)), s_col.at[a, 0, zz], r_col.at[a, zz])
    def down(a, src, zz):
        return rdma(a, src, blk(d, zz), pos.dev(z=lax.rem(z + zc - 1, zc)), s_col.at[a, 1, zz], r_col.at[a, zz])
    def right(a, src, zz):
        return rdma(a, src, blk(d, zz), pos.dev(d=pos.right), s_ring.at[a, 0, zz], r_left.at[a, zz])
    def left(a, src, zz):
        return rdma(a, src, blk(d, zz), pos.dev(d=pos.left), s_ring.at[a, 1, zz], r_right.at[a, zz])
    def fwd_right(a, zz):
        b = blk(pos.left, zz)
        return rdma(a, part(a, out[a], b, c), b, pos.dev(d=pos.right), s_fwd.at[a, zz], r_opp.at[a, zz])
    def fwd_left(a, zz):
        b = blk(pos.right, zz)
        return rdma(a, part(a, out[a], b, c), b, pos.dev(d=pos.left), s_fwd.at[a, zz], r_opp.at[a, zz])
    def mate(a, b):
        return rdma(a, part(a, out[a], b, c), b, mate_dev, s_mate.at[a, b], r_mate.at[a, b])
    def got(a, b, sem):
        return rdma(a, part(a, out[a], b, c), b, mate_dev, s_mate.at[a, b], sem).wait_recv()
    def mate_got(a, b):
        piece = part(a, out[a], b, 1 - c)
        pltpu.make_async_remote_copy(src_ref=piece, dst_ref=piece, send_sem=s_mate.at[a, b], recv_sem=r_mate.at[a, b], device_id=mate_dev, device_id_type=MESH).wait_recv()

    def begin(wide=False):
        enter(pos, wide)
        for a in range(count):
            pair(a).start()
    def first(a):
        pair(a).wait_recv()
        r2 = rows[a] // 2
        step = 256 if half[a] * 2 % 256 == 0 else 128
        @pl.loop(0, half[a] * 2 // step)
        def _(t):
            cols = pl.ds(pl.multiple_of(t * step, 128), step)
            mn = shard[a][:, cols].astype(jnp.float32)[:r2]
            ot = mine[a][:, cols].astype(jnp.float32)[:r2]
            first = jnp.where(c == 0, mn, ot)
            second = jnp.where(c == 0, ot, mn)
            comp[a][:, cols] = jnp.concatenate([first, second], axis=0).astype(jnp.bfloat16)
        right(a, own(a, c), z).start()
        left(a, own(a, c), z).start()
        pl.when(z < zc - 1)(lambda: up(a, own(a, c), z).start())
        pl.when(z > 0)(lambda: down(a, own(a, c), z).start())
        keep(a).start()

    def column(a, j):
        @pl.when(z - j >= 0)
        def _():
            zz = z - j
            got(a, blk(d, zz), r_col.at[a, zz])
            src = part(a, out[a], blk(d, zz), c)
            pl.when(z < zc - 1)(lambda: up(a, src, zz).start())
            right(a, src, zz).start(); left(a, src, zz).start()
            mate(a, blk(d, zz)).start()
        @pl.when(z + j < zc)
        def _():
            zz = z + j
            got(a, blk(d, zz), r_col.at[a, zz])
            src = part(a, out[a], blk(d, zz), c)
            pl.when(z > 0)(lambda: down(a, src, zz).start())
            right(a, src, zz).start(); left(a, src, zz).start()
            mate(a, blk(d, zz)).start()
    def ring_one(a, zz):
        got(a, blk(pos.left, zz), r_left.at[a, zz])
        pl.when(zz % 2 == 0)(lambda: fwd_right(a, zz).start())
        mate(a, blk(pos.left, zz)).start()
        got(a, blk(pos.right, zz), r_right.at[a, zz])
        pl.when(zz % 2 == 1)(lambda: fwd_left(a, zz).start())
        mate(a, blk(pos.right, zz)).start()
    def opp_one(a, zz):
        got(a, blk(pos.opp, zz), r_opp.at[a, zz])
        mate(a, blk(pos.opp, zz)).start()
    def spread(fn, a, j):
        if j == 0:
            fn(a, z); return
        pl.when(z - j >= 0)(lambda: fn(a, z - j))
        pl.when(z + j < zc)(lambda: fn(a, z + j))
    def rounds(a):
        call = functools.partial
        steps = []
        for t in range(1, zc + 2):
            if t < zc:
                steps.append(call(column, a, t))
            if t <= zc:
                steps.append(call(spread, ring_one, a, t - 1))
            if t >= 2:
                steps.append(call(spread, opp_one, a, t - 2))
        return steps
    def finish_one(a):
        pair(a).wait_send(); keep(a).wait()
        @pl.loop(0, zc)
        def _(zz):
            src = part(a, out[a], blk(d, zz), c)
            right(a, src, zz).wait_send(); left(a, src, zz).wait_send()
            pl.when((z < zc - 1) & (zz <= z))(lambda: up(a, src, zz).wait_send())
            pl.when((z > 0) & (zz >= z))(lambda: down(a, src, zz).wait_send())
            fwd_right(a, zz).wait_send()
        @pl.loop(0, 4 * zc)
        def _(b):
            @pl.when(b != blk(d, z))
            def _():
                mate(a, b).wait_send()
                mate_got(a, b)
    return pos, begin, first, rounds, finish_one


def count_places(picks, first, out_ref, size):
    tokens = picks.shape[1]
    chunk = 64
    @pl.loop(0, size // chunk)
    def _(t):
        at = pl.multiple_of(t * chunk, chunk)
        place = lax.broadcasted_iota(jnp.int32, (chunk, tokens), 0) + (first + at)
        count = jnp.zeros((chunk, tokens), jnp.int32)
        for k in range(picks.shape[0]):
            count = count + (picks[k : k + 1, :] == place).astype(jnp.int32)
        out_ref[pl.ds(at, chunk), :] = count.astype(F32).astype(BF)


def count_kernel(doc_len, all_ref, out_ref):
    count_places(all_ref[0], lax.axis_index("wide") * doc_len, out_ref.at[0], doc_len)


def count_all(picks, doc_len, peers):
    everyone = lax.all_gather(picks, "wide", axis=0)
    shape = (1,) + picks.shape
    return pl.pallas_call(
        functools.partial(count_kernel, doc_len),
        grid=(peers,),
        in_specs=[pl.BlockSpec(shape, lambda i: (i, 0, 0))],
        out_specs=pl.BlockSpec((1, doc_len, picks.shape[1]), lambda i: (i, 0, 0)),
        out_shape=jax.ShapeDtypeStruct((peers, doc_len, picks.shape[1]), BF),
        name="count",
    )(everyone)


def put_columns(ref, at, x):
    spare = ref.shape[0] - x.shape[0]
    full = jnp.concatenate([x.astype(F32), jnp.zeros((spare, x.shape[1]), F32)], axis=0) if spare else x
    ref[:, at : at + x.shape[1]] = full.astype(ref.dtype)


def picks_events(pos, doc_len, picks_ref, counts_ref, p_all, s_p, r_p):
    peers = 2 * pos.zc
    part = doc_len // 2
    def picks_copy(k, there):
        o = lax.rem(pos.w + k, peers)
        slot = pos.w if there else o
        return pltpu.make_async_remote_copy(src_ref=picks_ref, dst_ref=p_all.at[slot], send_sem=s_p.at[o], recv_sem=r_p.at[slot], device_id=(pos.d, o), device_id_type=MESH)
    def begin():
        @pl.loop(1, peers)
        def _(k):
            picks_copy(k, True).start()
    def counted(k, h):
        o = lax.rem(pos.w + k, peers)
        if k and not h:
            picks_copy(k, False).wait_recv()
        picks = p_all[o] if k else picks_ref[...]
        count_places(picks, pos.w * doc_len + h * part, counts_ref.at[o, pl.ds(h * part, part)], part)
    def finish():
        @pl.loop(1, peers)
        def _(k):
            picks_copy(k, True).wait_send()
    return begin, [functools.partial(counted, k, h) for k in range(peers) for h in range(2)], finish


def gather_scratch(shapes, zc):
    count = len(shapes)
    comps = [pltpu.VMEM((2 * rows, cols), BF) for rows, cols in shapes]
    mines = [pltpu.VMEM((rows + -rows % 16, cols), BF) for rows, cols in shapes]
    dma = pltpu.SemaphoreType.DMA
    sems = [dma((count, 2, zc)), dma((count, 2, zc)), dma((count, zc)), dma((count, 4 * zc)), dma((count,)), dma((count,)),
            dma((count, zc)), dma((count, zc)), dma((count, zc)), dma((count, zc)), dma((count, 4 * zc)), dma((count,))]
    return comps + mines + sems


def reduce_events(zc, g, out, rest):
    count = len(g)
    pos = Place(zc)
    z, c, d = pos.z, pos.c, pos.d
    loc = rest[:count]; rxp = rest[count:2 * count]; rxf = rest[2 * count:3 * count]
    rxl = rest[3 * count:4 * count]; rxr = rest[4 * count:5 * count]
    rxz = rest[5 * count:6 * count]
    fin = rest[6 * count:7 * count]; rxm = rest[7 * count:8 * count]
    (s_pair, r_pair, s_loc, s_ring, r_fwd, r_left, r_right, s_z, r_z, s_fin, r_fin) = rest[8 * count:]
    rows = [x.shape[0] // (4 * zc) for x in g]
    half = [x.shape[1] // 2 for x in g]
    mate_dev = pos.dev(c=1 - c)
    right_dev = pos.dev(d=pos.right); left_dev = pos.dev(d=pos.left)
    def remote(src, dst, ss, rs, dev):
        return pltpu.make_async_remote_copy(src_ref=src, dst_ref=dst, send_sem=ss, recv_sem=rs, device_id=dev, device_id_type=MESH)
    def strip(a, dd):
        return pl.ds(pl.multiple_of(dd * zc * rows[a], 16), zc * rows[a])
    def cols(a, core):
        return pl.ds(pl.multiple_of(core * half[a], 128), half[a])
    def pair(a, dd):
        return remote(g[a].at[strip(a, dd), cols(a, 1 - c)], rxp[a].at[strip(a, dd), :], s_pair.at[a, dd], r_pair.at[a, dd], mate_dev)
    def local(a, dd):
        return pltpu.make_async_copy(g[a].at[strip(a, dd), cols(a, c)], loc[a].at[strip(a, dd), :], s_loc.at[a, dd])
    def first_row(a, dd, zz):
        return (dd * zc + zz) * rows[a]
    def row(a, dd, zz):
        return pl.ds(pl.multiple_of(first_row(a, dd, zz), 16), rows[a])
    def slot(a, zz):
        return pl.ds(pl.multiple_of(zz * rows[a], 16), rows[a])
    def add(a, dst, terms):
        group = 16
        while rows[a] % (2 * group) == 0 and 2 * group * half[a] <= 32768:
            group *= 2
        @pl.loop(0, rows[a] // group)
        def _(t):
            total = None
            for ref, at in terms:
                v = ref[pl.ds(pl.multiple_of(at + t * group, 16), group), :].astype(F32)
                total = v if total is None else total + v
            ref, at = dst
            ref[pl.ds(pl.multiple_of(at + t * group, 16), group), :] = total.astype(ref.dtype)
    def pair_sum(a, dd, zz, extra=()):
        r = first_row(a, dd, zz)
        add(a, (loc[a], r), [(loc[a], r), (rxp[a], r)] + list(extra))
    def first_right(a, zz):
        return remote(loc[a].at[row(a, pos.opp, zz), :], rxf[a].at[slot(a, zz), :], s_ring.at[a, 0, zz], r_fwd.at[a, zz], right_dev)
    def first_left(a, zz):
        return remote(loc[a].at[row(a, pos.opp, zz), :], rxf[a].at[slot(a, zz), :], s_ring.at[a, 0, zz], r_fwd.at[a, zz], left_dev)
    def to_right(a, zz):
        return remote(loc[a].at[row(a, pos.right, zz), :], rxl[a].at[slot(a, zz), :], s_ring.at[a, 1, zz], r_left.at[a, zz], right_dev)
    def to_left(a, zz):
        return remote(loc[a].at[row(a, pos.left, zz), :], rxr[a].at[slot(a, zz), :], s_ring.at[a, 2, zz], r_right.at[a, zz], left_dev)
    def to_line(a, zt):
        return remote(loc[a].at[row(a, d, zt), :], rxz[a].at[slot(a, z), :], s_z.at[a, zt], r_z.at[a, z], pos.dev(z=zt))
    def from_line(a, zs):
        return remote(loc[a].at[row(a, d, zs), :], rxz[a].at[slot(a, zs), :], s_z.at[a, zs], r_z.at[a, zs], pos.dev(z=zs))
    def mate_rows(a):
        r2 = rows[a] // 2
        return pl.ds(pl.multiple_of((1 - c) * r2, 8), r2)
    def my_rows(a):
        r2 = rows[a] // 2
        return pl.ds(pl.multiple_of(c * r2, 8), r2)
    def final(a):
        return remote(fin[a].at[mate_rows(a), :], rxm[a], s_fin.at[a], r_fin.at[a], mate_dev)

    order = []
    for i in range(zc // 2):
        order += [zc - 1 - i, i]
    head = order[0]
    def begin(arrays):
        for a in arrays:
            for dd in (pos.opp, pos.right, pos.left):
                pair(a, dd).start(); local(a, dd).start()
        for a in arrays:
            pair(a, d).start(); local(a, d).start()
    def opposite(a, zz):
        if zz == head:
            pair(a, pos.opp).wait_recv(); local(a, pos.opp).wait()
        pair_sum(a, pos.opp, zz)
        (first_right if zz % 2 == 0 else first_left)(a, zz).start()
    def beside(a, zz):
        if zz % 2:
            pair_sum(a, pos.right, zz); to_right(a, zz).start()
        else:
            pair_sum(a, pos.left, zz); to_left(a, zz).start()
    def neighbours(a):
        for dd in (pos.right, pos.left):
            pair(a, dd).wait_recv(); local(a, dd).wait()
    def onward(a, zz):
        if zz % 2 == 0:
            first_right(a, zz).wait_recv()
            pair_sum(a, pos.right, zz, [(rxf[a], zz * rows[a])]); to_right(a, zz).start()
        else:
            first_left(a, zz).wait_recv()
            pair_sum(a, pos.left, zz, [(rxf[a], zz * rows[a])]); to_left(a, zz).start()
    def column(a, zz, dst, extra=()):
        r = first_row(a, d, zz)
        add(a, dst, [(loc[a], r), (rxp[a], r), (rxl[a], zz * rows[a]), (rxr[a], zz * rows[a])] + list(extra))
    def arrived(a, zz):
        if zz == head:
            pair(a, d).wait_recv(); local(a, d).wait()
        to_right(a, zz).wait_recv(); to_left(a, zz).wait_recv()
    def line(a, zt):
        @pl.when(z != zt)
        def _():
            column(a, zt, (loc[a], first_row(a, d, zt)))
            to_line(a, zt).start()
    def mine(a):
        others = [lax.rem(z + k, zc) for k in range(1, zc)]
        for o in others:
            from_line(a, o).wait_recv()
        column(a, z, (fin[a], 0), [(rxz[a], o * rows[a]) for o in others])
        final(a).start()
    def whole(a):
        out[a][:, cols(a, c)] = fin[a][my_rows(a), :]
        final(a).wait_recv()
        out[a][:, cols(a, 1 - c)] = rxm[a][...]
    def steps_of(a):
        call = functools.partial
        cuts = [order[: zc // 2], order[zc // 2 :]]
        stages = [[call(opposite, a, zz) for zz in order] + [call(neighbours, a)]]
        for n, cut in enumerate(cuts):
            before = cuts[n - 1] if n else []
            stages.append(
                [call(arrived, a, zz) for zz in before]
                + [call(onward, a, zz) for zz in cut]
                + [call(beside, a, zz) for zz in cut]
                + [call(line, a, zz) for zz in before]
            )
        stages.append([call(arrived, a, zz) for zz in cuts[-1]] + [call(line, a, zz) for zz in cuts[-1]])
        stages.append([call(mine, a)])
        return stages
    def groups_of(arrays):
        parts = [steps_of(a) for a in arrays]
        depth = len(parts[0])
        groups = []
        for t in range(len(parts) + depth - 1):
            group = []
            for n, part in enumerate(parts):
                if 0 <= t - n < depth:
                    group += part[t - n]
            groups.append(group)
        return groups + [[functools.partial(whole, a) for a in arrays]]
    def finish():
        for a in range(count):
            for dd in range(4):
                pair(a, dd).wait_send()
            for zz in range(zc):
                (first_right if zz % 2 == 0 else first_left)(a, zz).wait_send()
                to_right(a, zz).wait_send(); to_left(a, zz).wait_send()
                @pl.when(zz != z)
                def _():
                    to_line(a, zz).wait_send()
            final(a).wait_send()
    return pos, begin, groups_of, finish


ROW_BLOCK = 128


def input_grad(dqkv_ref, w_ref, rows_ref, dh_ref, gains_ref, dx_ref):
    up = dot_nt(dqkv_ref[...], w_ref[...])
    dv, _ = rms_pull(rows_ref[...].astype(F32), gains_ref[0:1, :], up)
    dx_ref[...] = dh_ref[...] + dv


def reduce_scratch(grads, zc):
    count = len(grads)
    V = pltpu.VMEM
    rows = [x.shape[0] // (4 * zc) for x in grads]; half = [x.shape[1] // 2 for x in grads]
    scratch = [V((x.shape[0], h), BF) for x, h in zip(grads, half)] * 2
    for _ in range(4):
        scratch += [V((zc * r, h), BF) for r, h in zip(rows, half)]
    scratch += [V((r, h), F32) for r, h in zip(rows, half)]
    scratch += [V((r // 2, h), F32) for r, h in zip(rows, half)]
    dma = pltpu.SemaphoreType.DMA
    return scratch + [dma((count, 4)), dma((count, 4)), dma((count, 4)), dma((count, 3, zc))] + [dma((count, zc))] * 5 + [dma((count,)), dma((count,))]


def reduce_shapes(grads, n_dev):
    return [jax.ShapeDtypeStruct((x.shape[0] // n_dev, x.shape[1]), F32) for x in grads]


def input_grads(dqkv, w_one, rows, d_hidden, gains):
    total, width = rows.shape
    block = lambda cols: pl.BlockSpec((ROW_BLOCK, cols), lambda i: (i, 0))
    return pl.pallas_call(
        input_grad,
        grid=(total // ROW_BLOCK,),
        out_shape=jax.ShapeDtypeStruct(rows.shape, F32),
        in_specs=[
            block(dqkv.shape[1]),
            pl.BlockSpec((width, dqkv.shape[1]), lambda i: (0, 0), pipeline_mode=pl.Buffered(1)),
            block(width), block(width),
            pl.BlockSpec(gains.shape, lambda i: (0, 0)),
        ],
        out_specs=block(width),
        compiler_params=pltpu.CompilerParams(vmem_limit_bytes=VMEM_ALL),
        name="input_grads",
    )(dqkv, w_one, rows, d_hidden, gains)


def table_events(pos, table, table_out, refs):
    t_mate, t_ring, t_line, s_mate, r_mate, s_tr, r_tr, s_tl, r_tl = refs
    z, d, zc = pos.z, pos.d, pos.zc
    around = (pos.right, pos.left, pos.opp)
    others = [lax.rem(z + k, zc) for k in range(1, zc)]
    def tab(src, dst, ss, rs, dev):
        return pltpu.make_async_remote_copy(src_ref=src, dst_ref=dst, send_sem=ss, recv_sem=rs, device_id=dev, device_id_type=MESH)
    def tab_mate():
        return tab(table, t_mate, s_mate, r_mate, pos.dev(c=1 - pos.c))
    def tab_ring(dd, there):
        slot = d if there else dd
        return tab(t_ring.at[slot], t_ring.at[slot], s_tr.at[dd], r_tr.at[slot], pos.dev(d=dd))
    def tab_line(zz, there):
        slot = z if there else zz
        return tab(t_line.at[slot], t_line.at[slot], s_tl.at[zz], r_tl.at[slot], pos.dev(z=zz))
    def begin():
        tab_mate().start()
    def cores():
        tab_mate().wait_recv()
        t_ring[d] = table[...] + t_mate[...]
        for dd in around:
            tab_ring(dd, True).start()
    def ring():
        for dd in around:
            tab_ring(dd, False).wait_recv()
        t_line[z] = t_ring[0] + t_ring[1] + t_ring[2] + t_ring[3]
        for zz in others:
            tab_line(zz, True).start()
    def line():
        for zz in others:
            tab_line(zz, False).wait_recv()
        total = t_line[0]
        for zz in range(1, zc):
            total = total + t_line[zz]
        table_out[...] = total
        tab_mate().wait_send()
        for dd in around:
            tab_ring(dd, True).wait_send()
        for zz in others:
            tab_line(zz, True).wait_send()
    return begin, cores, ring, line


def table_scratch(shape, zc):
    V = pltpu.VMEM
    dma = pltpu.SemaphoreType.DMA
    return [V(shape, F32), V((4,) + shape, F32), V((zc,) + shape, F32), dma, dma, dma((4,)), dma((4,)), dma((zc,)), dma((zc,))]


def apart_kernel(layouts, docs_in, queries_in, packed_ref, gain_ref, wq_ref, wk_ref, wv_ref, *refs):
    count = len(layouts)
    docs_ref, queries_ref, table_ref, g_attn, g_ffn, g_end = refs[count : count + 6]
    outs = list(refs[count + 6 :])
    docs_ref[...] = docs_in[...]
    @pl.when(pl.program_id(0) == 0)
    def _():
        queries_ref[...] = queries_in[...]
        done = []
        for ref, layout in zip(refs[:count], layouts):
            for pieces in layout:
                out = outs.pop(0)
                done.append(out)
                to = 0
                for start, size in pieces:
                    out[:, to : to + size] = ref[:, start : start + size]
                    to += size
        weighed = sum(w[...].astype(F32) * g[...] for w, g in zip((wq_ref, wk_ref, wv_ref), done))
        n = weighed.shape[0]
        g_attn[...] = turned(jnp.sum(weighed, axis=1, keepdims=True))[0:1, :n] / gain_ref[...].astype(F32)
        columns = refs[1][:, refs[1].shape[1] - 128 :]
        rows = turned(columns)
        g_ffn[...] = rows[1:2, :n]
        g_end[...] = rows[2:3, :n]
        heads, buckets = table_ref.shape
        pieces = [packed_ref[:, i * buckets : (i + 1) * buckets] for i in range(-(-heads // 8))]
        table_ref[...] = jnp.concatenate(pieces, axis=0)[:heads]


def apart(dx, packed, gain, weights, sums, layouts, doc_rows, table_shape):
    total, width = dx.shape
    rest = total - doc_rows
    n = weights[0].shape[0]
    shapes = [jax.ShapeDtypeStruct(s, F32) for s in ((doc_rows, width), (rest, width), table_shape, (1, n), (1, n), (1, n))]
    shapes += [
        jax.ShapeDtypeStruct((x.shape[0], sum(size for _, size in pieces)), F32)
        for x, layout in zip(sums, layouts)
        for pieces in layout
    ]
    fixed = lambda x: pl.BlockSpec(x.shape, lambda i: (0, 0), pipeline_mode=pl.Buffered(1))
    block = pl.BlockSpec((doc_rows // 4, width), lambda i: (i, 0))
    extra = [packed, gain, *weights, *sums]
    return pl.pallas_call(
        functools.partial(apart_kernel, layouts),
        grid=(4,),
        out_shape=shapes,
        in_specs=[block, pl.BlockSpec((rest, width), lambda i: (doc_rows // rest, 0), pipeline_mode=pl.Buffered(1))] + [fixed(x) for x in extra],
        out_specs=[block] + [fixed(x) for x in shapes[1:]],
        compiler_params=pltpu.CompilerParams(vmem_limit_bytes=VMEM_ALL),
        name="apart",
    )(dx, dx, *extra)


def bucket_of(n):
    far = jnp.zeros_like(n)
    dist = jnp.abs(n)
    for power_step in range(1, 8):
        far = far + (dist * dist >= 64 * 2**power_step).astype(jnp.int32)
    return jnp.where(n > 0, 16, 0) + jnp.where(dist < 8, dist, 8 + far)

def diagonal_hot(doc_len, rows):
    span = 2 * doc_len
    i = lax.broadcasted_iota(jnp.int32, (1, span), 1)
    n = doc_len - 128 - jnp.where(i >= span - 127, i - span, i)
    inside = (n > -doc_len) & (n < doc_len)
    bucket = jnp.where(inside, bucket_of(n), -1)
    return (lax.broadcasted_iota(jnp.int32, (rows, span), 0) == bucket).astype(F32)


def padded_tile(x):
    n, m = x.shape
    x = x.astype(F32)
    if m < 128:
        x = jnp.concatenate([x, jnp.zeros((n, 128 - m), F32)], axis=1)
    if n < 128:
        x = jnp.concatenate([x, jnp.zeros((128 - n, 128), F32)], axis=0)
    return x


def turned(x):
    return padded_tile(x).T


def per_token(values, first, shape, dim, slots):
    owner = lax.broadcasted_iota(jnp.int32, shape, dim) // slots
    out = jnp.zeros(shape, jnp.int32)
    for q in range(shape[dim] // slots):
        n = first + q
        out = jnp.where(owner == q, values[n // values.shape[1], n % values.shape[1]], out)
    return out


def live_tile(lengths, tile, slots):
    shape = (128, 128)
    key = lax.broadcasted_iota(jnp.int32, shape, 0)
    query = lax.broadcasted_iota(jnp.int32, shape, 1)
    limit = per_token(lengths, tile * (128 // slots), shape, 0, slots)
    return (lax.rem(key, slots) < limit) & (key // slots == query // slots)


def cols_dot(a, b):
    return lax.dot_general(a, b, (((1,), (1,)), ((), ())), preferred_element_type=F32)

def tiles_of(table, keys, q_from, q_len, doc_len):
    parts = []
    for kb in range(keys // 128):
        at = doc_len - 128 - 128 * kb + q_from
        parts.append(table[:, at : at + q_len])
    return jnp.concatenate(parts, axis=0) if len(parts) > 1 else parts[0]

def spread_steps(steps, first_slot, slots):
    plan = {}
    for n, step in enumerate(steps):
        at = min(slots - 1, first_slot + (n * (slots - first_slot)) // len(steps))
        plan.setdefault(at, []).append(step)
    return plan


def attend_kernel(doc_len, doc_count, block, zc, slot_count, docs_ref, queries_ref, rel_ref, lengths_ref, *refs):
    beside = zc > 0
    ins = 12 if beside else 1
    raw = refs[:ins]
    rows_ref, gains_ref, normed_ref, qkv_ref, ctx_ref, lse_ref, table_ref = refs[ins : ins + 7]
    j = pl.program_id(0)
    span = 2 * doc_len
    hd = 64
    total = rows_ref.shape[0]
    width = rows_ref.shape[1]
    rest = total - doc_count * doc_len
    places = [(m * doc_len, doc_len, q_at, block, None) for m in range(doc_count) for q_at in range(0, doc_len, block)]
    places += [(doc_count * doc_len + 128 * i, 128, 0, 128, i) for i in range(rest // 128)]
    slots = len(places)
    plan = {}
    if beside:
        q_ref, k_ref, v_ref, o_ref, p_ref, *g_refs, gate_ref, up_ref, down_ref, raw_picks = raw
        outs = refs[ins + 7 : ins + 10]
        counts_ref = refs[ins + 10]
        shards = refs[ins + 11 : ins + 14]
        w_ref, load, picks_ref, p_all, s_p, r_p = refs[ins + 14 : ins + 20]
        pos, begin, first, rounds, finish_one = gather_events(zc, shards, outs, refs[ins + 20 : -1])
        begin_picks, pieces, finish_picks = picks_events(pos, doc_len, picks_ref, counts_ref, p_all, s_p, r_p)
        every = [rounds(a) for a in (1, 2)]
        steps = [step for same in zip(*every) for step in same]
        plan = spread_steps(steps, 0, slots * (width // 128))
    else:
        (w_ref,) = raw
    diag_ref = refs[-1]
    def now(i):
        for slot, steps in plan.items():
            if slot % slots == i:
                @pl.when(j == slot // slots)
                def _():
                    for step in steps:
                        step()
    def assemble():
        for i in range(width // 128):
            for n, ref in enumerate((q_ref, k_ref, v_ref)):
                put_columns(shards[0], 384 * i + 128 * n, ref[:, 128 * i : 128 * i + 128])
        put_columns(shards[0], 3 * width, o_ref[...])
        put_columns(shards[0], 4 * width, p_ref[...])
        gains = jnp.concatenate([g[...].astype(F32) for g in g_refs], axis=0)
        put_columns(shards[0], 4 * width + p_ref.shape[1], turned(gains)[: q_ref.shape[0]])
        picks_ref[...] = turned(raw_picks[...])[: picks_ref.shape[0]].astype(jnp.int32)
        size = FF_BLOCK
        for i in range(gate_ref.shape[1] // size):
            put_columns(shards[1], 2 * size * i, gate_ref[:, size * i : size * i + size])
            put_columns(shards[1], 2 * size * i + size, up_ref[:, size * i : size * i + size])
        put_columns(shards[2], 0, down_ref[...])
    @pl.when(j == 0)
    def _():
        if beside:
            assemble()
            begin(True)
            begin_picks()
            first(0)
        table = padded_tile(rel_ref[...])[: diag_ref.shape[0]].astype(BF)
        diag_ref[...] = dot(table, diagonal_hot(doc_len, 128).astype(BF))
        rows_ref[0 : docs_ref.shape[0], :] = docs_ref[...]
        rows_ref[docs_ref.shape[0] :, :] = queries_ref[...]
        if beside:
            steps = rounds(0)
            for n, step in enumerate(steps):
                if n == len(steps) - 3:
                    first(1)
                    first(2)
                for piece in pieces[len(pieces) * n // len(steps) : len(pieces) * (n + 1) // len(steps)]:
                    piece()
                step()
            finish_one(0)
            loading = pltpu.make_async_copy(outs[0], w_ref, load)
            loading.start()
            loading.wait()
        gains_ref[...] = w_ref[:, w_ref.shape[1] - 128 :].astype(F32).T[0:8]
        for c in chunks_of(total, 4):
            x = rows_ref[c, :].astype(F32)
            normed_ref[c, :] = (x * inverse_rms(x) * gains_ref[0:1, :]).astype(BF)
    w_now = w_ref[:, pl.ds(pl.multiple_of(j * 384, 128), 384)]
    for c in chunks_of(total, 4):
        qkv_ref[c, :] = dot(normed_ref[c, :], w_now).astype(BF)
    for h in range(2):
        wide = jnp.broadcast_to(diag_ref[pl.ds(2 * j + h, 1), :], (128, span))
        table_ref[h] = pltpu.roll(wide, 0, 1, stride=1, stride_axis=0)[:, : span - 128]
    lane = lax.broadcasted_iota(jnp.int32, (1, 128), 1)
    def part(rows, keys, q_at, q_len, mask):
        q2 = qkv_ref[pl.ds(rows + q_at, q_len), 0:128]
        k2 = qkv_ref[pl.ds(rows, keys), 128:256]
        v2 = qkv_ref[pl.ds(rows, keys), 256:384]
        v2t = v2.astype(F32).T.astype(BF)
        outs = []
        for h in range(2):
            qm = jnp.where((lane < hd) == (h == 0), q2, jnp.zeros_like(q2))
            s = dot_nt(k2, qm) + tiles_of(table_ref.at[h], keys, q_at, q_len, doc_len)
            if mask is not None:
                s = jnp.where(live_tile(lengths_ref, mask, slot_count), s, mask_fill)
            top = jnp.max(s, axis=0, keepdims=True)
            e = jnp.exp(s - top)
            total = jnp.sum(e, axis=0, keepdims=True)
            p = (e * (1.0 / total)).astype(BF)
            lse_ref[0, h : h + 1, pl.ds(rows + q_at, q_len)] = top + jnp.log(total)
            outs.append(dot(v2t[h * hd : (h + 1) * hd], p))
        ctx_ref[pl.ds(rows + q_at, q_len), :] = jnp.concatenate(outs, axis=0).T.astype(BF)
    for i, place in enumerate(places):
        now(i)
        part(*place)
    if beside:
        @pl.when(j == pl.num_programs(0) - 1)
        def _():
            finish_one(1)
            finish_one(2)
            finish_picks()


def attend(docs, queries, rel, lengths, slots, doc_len, doc_count, weights, picks, w_one, zc, n_dev):
    width = docs.shape[1]
    total = docs.shape[0] + queries.shape[0]
    pairs = width // 128
    span = 2 * doc_len
    once = pl.Buffered(1)
    whole = pl.BlockSpec(memory_space=pltpu.VMEM)
    fixed = lambda shape: pl.BlockSpec(shape, lambda j: (0, 0), pipeline_mode=once)
    extra_in, extra_out, extra_specs, scratch, remote = [w_one], [], [], [], {}
    if zc:
        peers = 2 * zc
        dma = pltpu.SemaphoreType.DMA
        one, (gate, up, down) = weights[:5], weights[8:]
        turned_picks = picks.shape[::-1]
        shapes = [(one[0].shape[0], sum(w.shape[1] for w in one) + 128), (gate.shape[0], 2 * gate.shape[1]), down.shape]
        extra_in = [*weights, picks]
        extra_out = [jax.ShapeDtypeStruct((r * n_dev, c), BF) for r, c in shapes]
        extra_out += [jax.ShapeDtypeStruct((peers, doc_len, picks.shape[0]), BF)]
        extra_specs = [pl.BlockSpec(memory_space=pl.ANY)] * 3 + [whole]
        scratch = [pltpu.VMEM((r + -r % 16, c), BF) for r, c in shapes]
        scratch += [pltpu.VMEM(extra_out[0].shape, BF), dma, pltpu.VMEM(turned_picks, jnp.int32), pltpu.VMEM((peers,) + turned_picks, jnp.int32), dma((peers,)), dma((peers,))]
        scratch += gather_scratch(shapes, zc)
        remote = dict(collective_id=3, has_side_effects=True)
    return pl.pallas_call(
        functools.partial(attend_kernel, doc_len, doc_count, 256, zc, slots),
        grid=(pairs,),
        in_specs=[
            fixed(docs.shape), fixed(queries.shape),
            fixed(rel.shape), pl.BlockSpec(memory_space=pltpu.SMEM),
        ] + [whole] * len(extra_in),
        out_specs=[
            fixed((total, width)), fixed((8, width)), fixed((total, width)),
            pl.BlockSpec((total, 384), lambda j: (0, j)),
            pl.BlockSpec((total, 128), lambda j: (0, j)),
            pl.BlockSpec((1, 8, total), lambda j: (j, 0, 0)),
            pl.BlockSpec((2, 128, span - 128), lambda j: (j, 0, 0)),
        ] + extra_specs,
        out_shape=[
            jax.ShapeDtypeStruct((total, width), BF),
            jax.ShapeDtypeStruct((8, width), F32),
            jax.ShapeDtypeStruct((total, width), BF),
            jax.ShapeDtypeStruct((total, pairs * 384), BF),
            jax.ShapeDtypeStruct((total, width), BF),
            jax.ShapeDtypeStruct((pairs, 8, total), F32),
            jax.ShapeDtypeStruct((pairs * 2, 128, span - 128), F32),
        ] + extra_out,
        scratch_shapes=scratch + [pltpu.VMEM((2 * pairs + -2 * pairs % 16, span), F32)],
        compiler_params=pltpu.CompilerParams(vmem_limit_bytes=VMEM_ALL, **remote),
        name="attend",
    )(docs, queries, rel, lengths, *extra_in)


BACK_SHARES = (0.0, 0.27, 0.48, 0.7, 0.88)


def attend_back_step(doc_len, doc_count, block, slot_count, bucket_count, pairs, now, qkv_ref, do_ref, lse_ref, table_ref, lengths_ref,
                     normed_ref, wg_ref, packed_ref, dqkv_ref, acc, normed_t, diag_ref):
    j = pl.program_id(0)
    span = 2 * doc_len
    hd = 64
    rest = qkv_ref.shape[0] - doc_count * doc_len
    @pl.when(j == 0)
    def _():
        normed_t[...] = normed_ref[...].T
    acc[...] = jnp.zeros_like(acc)
    lane = lax.broadcasted_iota(jnp.int32, (1, 128), 1)
    def part(rows, keys, q_len, mask):
        k2 = qkv_ref[pl.ds(rows, keys), 128:256]
        v2 = qkv_ref[pl.ds(rows, keys), 256:384]
        k2t = k2.astype(F32).T.astype(BF)
        dk = jnp.zeros((keys, 128), F32)
        dv = jnp.zeros((keys, 128), F32)
        for q_at in range(0, keys, q_len):
            now()
            qr = pl.ds(rows + q_at, q_len)
            q2 = qkv_ref[qr, 0:128]
            do2 = do_ref[qr, :]
            outs = []
            for h in range(2):
                mine = (lane < hd) == (h == 0)
                qm = jnp.where(mine, q2, jnp.zeros_like(q2))
                dom = jnp.where(mine, do2, jnp.zeros_like(do2))
                s = dot_nt(k2, qm) + tiles_of(table_ref.at[h], keys, q_at, q_len, doc_len)
                if mask is not None:
                    s = jnp.where(live_tile(lengths_ref, mask, slot_count), s, mask_fill)
                p = jnp.exp(s - lse_ref[0, h : h + 1, qr])
                dp = dot_nt(v2, dom)
                ds = p * (dp - jnp.sum(p * dp, axis=0, keepdims=True))
                for kb in range(keys // 128):
                    at = doc_len - 128 - 128 * kb + q_at
                    acc[h, :, at : at + q_len] += ds[128 * kb : 128 * (kb + 1)]
                low = ds.astype(BF)
                dv += dot(p.astype(BF), dom)
                dk += dot(low, qm)
                outs.append(dot(k2t[h * hd : (h + 1) * hd], low))
            dqkv_ref[qr, 0:128] = jnp.concatenate(outs, axis=0).T.astype(BF)
        dqkv_ref[pl.ds(rows, keys), 128:256] = dk.astype(BF)
        dqkv_ref[pl.ds(rows, keys), 256:384] = dv.astype(BF)
    for m in range(doc_count):
        part(m * doc_len, doc_len, block, None)
    for i in range(rest // 128):
        part(doc_count * doc_len + 128 * i, 128, 128, i)
    for h in range(2):
        eight = acc[h, 0:8]
        for g in range(1, 16):
            eight = eight + pltpu.roll(acc[h, 8 * g : 8 * g + 8], span - 8 * g, 1)
        one = eight[0:1]
        for r in range(1, 8):
            one = one + pltpu.roll(eight, span - r, 1)[r : r + 1]
        diag_ref[pl.ds(2 * j + h, 1), :] = one
    wg_ref[...] = dot(normed_t[...], dqkv_ref[...]).astype(BF)
    @pl.when(j == pairs - 1)
    def _():
        hot = diagonal_hot(doc_len, bucket_count)
        table = lax.dot_general(
            diag_ref[...], hot, (((1,), (1,)), ((), ())), precision=lax.Precision.HIGHEST, preferred_element_type=F32
        )
        pieces = [table[8 * i : 8 * i + 8] for i in range(table.shape[0] // 8)]
        spare = jnp.zeros((8, packed_ref.shape[1] - bucket_count * len(pieces)), F32)
        packed_ref[...] = jnp.concatenate([*pieces, spare], axis=1)

def attend_back_kernel(doc_len, doc_count, slot_count, bucket_count, pairs, *refs):
    attend_back_step(doc_len, doc_count, 256, slot_count, bucket_count, pairs, lambda: None, *refs)


def back_kernel(doc_len, doc_count, slot_count, bucket_count, pairs, zc, count, qkv_ref, do_ref, lse_ref, table_ref, lengths_ref,
                normed_ref, w_ref, rows_ref, dh_ref, gains_ref, *refs):
    grads = refs[:count]
    dx_ref = refs[count]
    outs = refs[count + 1 : 2 * count + 2]
    table_out = refs[2 * count + 2]
    acc, normed_t, diag_ref, packed_ref, dqkv_all, wg_all = refs[2 * count + 3 : 2 * count + 9]
    table_refs = refs[2 * count + 9 : 2 * count + 18]
    pos, begin, groups_of, finish = reduce_events(zc, [*grads, wg_all], outs, refs[2 * count + 18 :])
    table_begin, table_cores, table_ring, table_line = table_events(pos, packed_ref, table_out, table_refs)
    j = pl.program_id(0)
    total = qkv_ref.shape[0]
    rest = total - doc_count * doc_len
    block = 256
    slots = doc_count * (doc_len // block) + rest // 128
    groups = groups_of(range(count))
    plan = {}
    for group, share in zip(groups, BACK_SHARES):
        for n, step in enumerate(group):
            at = min(slots * pairs - 1, int(share * slots * pairs) + n // 4)
            plan.setdefault(at, []).append(step)
    slot = [0]
    def now():
        for at, steps in plan.items():
            if at % slots == slot[0]:
                @pl.when(j == at // slots)
                def _():
                    for step in steps:
                        step()
        slot[0] += 1
    @pl.when(j == 0)
    def _():
        enter(pos, opp=True)
        begin(range(count))
    @pl.when(j < pairs)
    def _():
        here = pl.ds(pl.multiple_of(j * 384, 128), 384)
        attend_back_step(
            doc_len, doc_count, block, slot_count, bucket_count, pairs, now, qkv_ref, do_ref, lse_ref, table_ref, lengths_ref,
            normed_ref, wg_all.at[:, here], packed_ref, dqkv_all.at[:, here], acc, normed_t, diag_ref,
        )
    late = groups[len(BACK_SHARES) :]
    last = groups_of([count])
    blocks = total // ROW_BLOCK
    end = blocks - 1
    after = {0: [functools.partial(begin, [count]), table_begin]}
    def put(at, steps):
        after.setdefault(min(at, end), []).extend(steps)
    for n, group in enumerate(late[:-1]):
        put(n, group)
    put(1, last[0])
    put(2, [table_cores])
    put(3, last[1])
    put(4, late[-1])
    put(5, last[2] + [table_ring])
    put(7, last[3])
    put(end, last[4] + last[5] + [table_line, finish])
    @pl.when(j >= pairs)
    def _():
        at = pl.multiple_of((j - pairs) * ROW_BLOCK, ROW_BLOCK)
        input_grad(dqkv_all.at[pl.ds(at, ROW_BLOCK), :], w_ref, rows_ref, dh_ref, gains_ref, dx_ref)
    for n, steps in sorted(after.items()):
        @pl.when(j == pairs + n)
        def _():
            for step in steps:
                step()


def back_specs(total, width, span, pairs):
    index = lambda j: jnp.minimum(j, pairs - 1)
    return [
        pl.BlockSpec((total, 384), lambda j: (0, index(j))),
        pl.BlockSpec((total, 128), lambda j: (0, index(j))),
        pl.BlockSpec((1, 8, total), lambda j: (index(j), 0, 0)),
        pl.BlockSpec((2, 128, span - 128), lambda j: (index(j), 0, 0)),
        pl.BlockSpec(memory_space=pltpu.SMEM),
        pl.BlockSpec((total, width), lambda j: (0, 0), pipeline_mode=pl.Buffered(1)),
    ]


def back_scratch(total, width, span, pairs):
    return [pltpu.VMEM((2, 128, span), F32), pltpu.VMEM((width, total), BF), pltpu.VMEM((2 * pairs + -2 * pairs % 16, span), F32)]


def attend_back(qkv, d_ctx, lse, table, lengths, slots, bucket_count, normed, doc_len, doc_count):
    total, width = normed.shape
    pairs = width // 128
    span = 2 * doc_len
    return pl.pallas_call(
        functools.partial(attend_back_kernel, doc_len, doc_count, slots, bucket_count, pairs),
        grid=(pairs,),
        in_specs=back_specs(total, width, span, pairs),
        out_specs=[
            pl.BlockSpec((width, 384), lambda j: (0, j)),
            pl.BlockSpec((8, 128), lambda j: (0, 0)),
            pl.BlockSpec((total, 384), lambda j: (0, j)),
        ],
        out_shape=[
            jax.ShapeDtypeStruct((width, 3 * width), BF),
            jax.ShapeDtypeStruct((8, 128), F32),
            jax.ShapeDtypeStruct((total, 3 * width), BF),
        ],
        scratch_shapes=back_scratch(total, width, span, pairs),
        compiler_params=pltpu.CompilerParams(vmem_limit_bytes=VMEM_ALL),
        name="attend_back",
    )(qkv, d_ctx, lse, table, lengths, normed)


def back(qkv, d_ctx, lse, table, lengths, slots, bucket_count, normed, w_one, rows, d_hidden, gains, doc_len, doc_count, grads, zc, n_dev):
    total, width = normed.shape
    pairs = width // 128
    span = 2 * doc_len
    count = len(grads)
    once = pl.Buffered(1)
    whole = pl.BlockSpec(memory_space=pltpu.VMEM)
    rows_block = pl.BlockSpec((ROW_BLOCK, width), lambda j: (jnp.maximum(j - pairs, 0), 0))
    all_grads = [*grads, jax.ShapeDtypeStruct((width, 3 * width), BF)]
    shapes = reduce_shapes(all_grads, n_dev) + [jax.ShapeDtypeStruct((8, 128), F32)]
    return pl.pallas_call(
        functools.partial(back_kernel, doc_len, doc_count, slots, bucket_count, pairs, zc, count),
        grid=(pairs + total // ROW_BLOCK,),
        in_specs=back_specs(total, width, span, pairs) + [
            pl.BlockSpec((width, 3 * width), lambda j: (0, 0), pipeline_mode=once),
            rows_block, rows_block,
            pl.BlockSpec(gains.shape, lambda j: (0, 0)),
        ] + [pl.BlockSpec(memory_space=pl.ANY)] * count,
        out_specs=[rows_block] + [whole] * len(shapes),
        out_shape=[jax.ShapeDtypeStruct((total, width), F32)] + shapes,
        scratch_shapes=back_scratch(total, width, span, pairs)
        + [pltpu.VMEM((8, 128), F32), pltpu.VMEM((total, 3 * width), BF), pltpu.VMEM((width, 3 * width), BF)]
        + table_scratch((8, 128), zc) + reduce_scratch(all_grads, zc),
        compiler_params=pltpu.CompilerParams(collective_id=4, has_side_effects=True, vmem_limit_bytes=VMEM_ALL),
        name="back",
    )(qkv, d_ctx, lse, table, lengths, normed, w_one, rows, d_hidden, gains, *grads)


def columns_of(rows):
    n = rows[0].shape[1]
    return jnp.concatenate([*rows, jnp.zeros((128 - len(rows), n), F32)], axis=0).T


def pair_columns(w):
    q, k, v = w
    rows, width = q.shape
    pack = jnp.stack([x.reshape(rows, width // 128, 128) for x in (q, k, v)], axis=2)
    return pack.reshape(rows, 3 * width)


def score_kernel(peers, doc_len, slots, emb_ref, picks_ref, counts_ref, lengths_ref, goals_ref, loss_ref, d_emb_ref,
                 q_own, q_all, q_two, d_raw, weighed, totals, pool_out, pool_in, grad_out, grad_in, dq_out, dq_in, docs_t, d_docs,
                 s_q, r_q, s_pool, r_pool, s_grad, r_grad, s_dq, r_dq):
    dp = lax.axis_index("dp"); me = lax.axis_index("wide")
    tokens = q_own.shape[0]
    feat = emb_ref.shape[1]
    half = tokens // 2
    scale = feat ** -0.5
    barrier = pltpu.get_barrier_semaphore()
    def other(k):
        return lax.rem(me + k, peers)
    def each(fn):
        @pl.loop(1, peers)
        def _(k):
            fn(other(k))
    each(lambda o: pl.semaphore_signal(barrier, inc=1, device_id=(dp, o), device_id_type=MESH))
    q_own[...] = emb_ref[2 * doc_len :, :]
    q_all[me] = q_own[...]
    pl.semaphore_wait(barrier, peers - 1)
    def send(src, dst, ss, rs, o):
        return pltpu.make_async_remote_copy(src_ref=src, dst_ref=dst, send_sem=ss, recv_sem=rs, device_id=(dp, o), device_id_type=MESH)
    def q_to(o): return send(q_own, q_all.at[me], s_q.at[o], r_q.at[me], o)
    def q_from(o): return send(q_own, q_all.at[o], s_q.at[o], r_q.at[o], o)
    def pool_to(o): return send(pool_out.at[o], pool_in.at[me], s_pool.at[o], r_pool.at[me], o)
    def pool_from(o): return send(pool_out.at[o], pool_in.at[o], s_pool.at[o], r_pool.at[o], o)
    def grad_to(o): return send(grad_out.at[o], grad_in.at[me], s_grad.at[o], r_grad.at[me], o)
    def grad_from(o): return send(grad_out.at[o], grad_in.at[o], s_grad.at[o], r_grad.at[o], o)
    def dq_to(o): return send(dq_out.at[o], dq_in.at[me], s_dq.at[o], r_dq.at[me], o)
    def dq_from(o): return send(dq_out.at[o], dq_in.at[o], s_dq.at[o], r_dq.at[o], o)
    def started(o):
        q_to(o).start()
    each(started)
    docs2 = jnp.concatenate([emb_ref[0:doc_len, :], emb_ref[doc_len : 2 * doc_len, :]], axis=1)
    docs_t[...] = docs2.astype(F32).T.astype(BF)
    row = lax.broadcasted_iota(jnp.int32, (tokens, 1), 0)
    lane = lax.broadcasted_iota(jnp.int32, (1, tokens), 1)
    group = min(8, peers)
    groups = range(peers // group)
    def members(n):
        return [(n * group + i, slice(i * tokens, (i + 1) * tokens)) for i in range(group)]
    def forward(n):
        for o, at in members(n):
            q = q_all[o]
            none = jnp.zeros_like(q)
            q_two[n, at, :] = jnp.concatenate([jnp.where(row < half, q, none), jnp.where(row < half, none, q)], axis=1)
        s = lax.dot_general(docs2, q_two[n], (((1,), (1,)), ((), ())), preferred_element_type=F32) * scale
        for o, at in members(n):
            multiple = counts_ref[o].astype(F32)
            w = multiple * jnp.exp(s[:, at])
            weighed[o] = w
            found = jnp.sum(multiple, axis=0, keepdims=True)
            weight = jnp.sum(w, axis=0, keepdims=True) + (found == 0).astype(F32)
            totals[o] = jnp.broadcast_to(weight, (8, tokens))
            pool_out[o] = jnp.broadcast_to(jnp.log(weight), (8, tokens))
    each(lambda o: q_from(o).wait_recv())
    for n in groups:
        forward(n)
    pool_in[me] = pool_out[me]
    each(lambda o: pool_to(o).start())
    each(lambda o: pool_from(o).wait_recv())
    pooled = pool_in[:, 0, :]
    mine = turned(picks_ref[...])[: picks_ref.shape[1]].astype(jnp.int32)
    hits = []
    for w in range(peers):
        inside = ((mine >= w * doc_len) & (mine < (w + 1) * doc_len)).astype(F32)
        hits.append(jnp.max(inside, axis=0, keepdims=True))
    hit = jnp.concatenate(hits, axis=0)
    live = (lax.rem(lane, slots) < per_token(lengths_ref, 0, lane.shape, 1, slots)).astype(F32)
    own_row = lax.broadcasted_iota(jnp.int32, (tokens, tokens), 0) // slots
    own_col = lax.broadcasted_iota(jnp.int32, (tokens, tokens), 1) // slots
    same = (own_row == own_col).astype(F32)
    def per_query(v):
        return jnp.dot(v, same, precision=lax.Precision.HIGHEST, preferred_element_type=F32)
    divisor = jnp.maximum(per_query(hit * live), 1.0)
    logits = score_scale * per_query(pooled * live) / divisor
    top = jnp.max(logits, axis=0, keepdims=True)
    shifted = jnp.exp(logits - top)
    total = jnp.sum(shifted, axis=0, keepdims=True)
    doc_id = lax.broadcasted_iota(jnp.int32, (peers, tokens), 0)
    chosen = (doc_id == per_token(goals_ref, 0, lane.shape, 1, slots)).astype(F32)
    loss = top + jnp.log(total) - jnp.sum(chosen * logits, axis=0, keepdims=True)
    queries = tokens // slots
    chosen_lane = (lax.broadcasted_iota(jnp.int32, (tokens, 128), 0) == lax.broadcasted_iota(jnp.int32, (tokens, 128), 1) * slots).astype(F32)
    apart_loss = jnp.dot(loss, chosen_lane, precision=lax.Precision.HIGHEST, preferred_element_type=F32)
    per = loss_ref.shape[1]
    for i in range(queries // per):
        loss_ref[i : i + 1, :] = apart_loss[:, i * per : (i + 1) * per]
    d_pooled = score_scale * (shifted / total - chosen) / divisor * live
    for w in range(peers):
        grad_out[w] = jnp.broadcast_to(d_pooled[w : w + 1], (8, tokens))
    each(lambda o: grad_to(o).start())
    grad_in[me] = grad_out[me]
    each(lambda o: grad_from(o).wait_recv())
    for n in groups:
        for o, at in members(n):
            factor = grad_in[o][0:1] / totals[o][0:1] * scale
            d_raw[n, :, at] = (weighed[o] * factor).astype(BF)
        both = jnp.dot(docs_t[...], d_raw[n], preferred_element_type=F32)
        for o, at in members(n):
            d_q = jnp.where(lane < half, both[0:feat, at], both[feat : 2 * feat, at])
            dq_out[o] = d_q.T.astype(BF)
    each(lambda o: dq_to(o).start())
    for n in groups:
        part = jnp.dot(d_raw[n], q_two[n], preferred_element_type=F32)
        d_docs[...] = part if n == 0 else d_docs[...] + part
    d_emb_ref[0:doc_len, :] = d_docs[:, 0:feat].astype(BF)
    d_emb_ref[doc_len : 2 * doc_len, :] = d_docs[:, feat : 2 * feat].astype(BF)
    dq_in[me] = dq_out[me]
    each(lambda o: dq_from(o).wait_recv())
    total_q = dq_in[0].astype(F32)
    for w in range(1, peers):
        total_q = total_q + dq_in[w].astype(F32)
    d_emb_ref[2 * doc_len :, :] = total_q.astype(BF)
    def sent(o):
        q_to(o).wait_send(); pool_to(o).wait_send(); grad_to(o).wait_send(); dq_to(o).wait_send()
    each(sent)

def score(emb, picks, counts, lengths, goals, loss_shape, doc_len, slots, peers):
    tokens = picks.shape[0]
    feat = emb.shape[1]
    group = min(8, peers)
    V = pltpu.VMEM
    dma = pltpu.SemaphoreType.DMA
    return pl.pallas_call(
        functools.partial(score_kernel, peers, doc_len, slots),
        out_shape=[jax.ShapeDtypeStruct(loss_shape, F32), jax.ShapeDtypeStruct(emb.shape, BF)],
        in_specs=[pl.BlockSpec(memory_space=pltpu.VMEM)] * 3 + [pl.BlockSpec(memory_space=pltpu.SMEM)] * 2,
        out_specs=[pl.BlockSpec(memory_space=pltpu.VMEM)] * 2,
        scratch_shapes=[
            V((tokens, feat), BF), V((peers, tokens, feat), BF),
            V((peers // group, group * tokens, 2 * feat), BF), V((peers // group, doc_len, group * tokens), BF),
            V((peers, doc_len, tokens), F32), V((peers, 8, tokens), F32),
            V((peers, 8, tokens), F32), V((peers, 8, tokens), F32), V((peers, 8, tokens), F32), V((peers, 8, tokens), F32),
            V((peers, tokens, feat), BF), V((peers, tokens, feat), BF), V((2 * feat, doc_len), BF), V((doc_len, 2 * feat), F32),
        ] + [dma((peers,))] * 8,
        compiler_params=pltpu.CompilerParams(collective_id=2, has_side_effects=True, vmem_limit_bytes=VMEM_ALL),
        name="score",
    )(emb, picks, counts, lengths, goals)


GELU_SCALE = 0.7978845608028654
GELU_CUBE = 0.044715

def dot(a, b):
    return jnp.dot(a, b, preferred_element_type=F32)

def dot_nt(a, b):
    return lax.dot_general(a, b, (((1,), (1,)), ((), ())), preferred_element_type=F32)

def dot_tn(a, b):
    return lax.dot_general(a, b, (((0,), (0,)), ((), ())), preferred_element_type=F32)

def inverse_rms(v):
    return lax.rsqrt(jnp.mean(v * v, axis=-1, keepdims=True) + eps_norm)

def chunks_of(total, parts):
    size = total // parts
    return [slice(i * size, (i + 1) * size) for i in range(parts)]

def ffn_kernel(parts, rows_ref, ctx_ref, wo_ref, wgu_ref, wd_ref, wp_ref, gains_ref, n2_ref, gu_ref, scale_ref, ne_ref, emb_ref, lo_ref):
    j = pl.program_id(0)
    block = wd_ref.shape[0]
    chunks = chunks_of(rows_ref.shape[0], parts)
    @pl.when(j == 0)
    def _():
        for c in chunks:
            h = rows_ref[c, :].astype(F32) + dot(ctx_ref[c, :], wo_ref[...])
            lo_ref[c, :] = h
            inv = inverse_rms(h)
            scale_ref[c, :] = jnp.broadcast_to(inv, scale_ref[c, :].shape)
            n2_ref[c, :] = (h * inv * gains_ref[1:2, :]).astype(BF)
    gus = [dot(n2_ref[c, :], wgu_ref[...]) for c in chunks]
    for c, gu in zip(chunks, gus):
        gu_ref[c, :] = gu.astype(BF)
        g = gu[:, :block]
        t = jnp.tanh(GELU_SCALE * (g + GELU_CUBE * (g * g * g)))
        act = (0.5 * g * (1.0 + t)) * gu[:, block:]
        lo_ref[c, :] += dot(act.astype(BF), wd_ref[...])
    @pl.when(j == pl.num_programs(0) - 1)
    def _():
        for c in chunks:
            lo = lo_ref[c, :]
            inv = inverse_rms(lo)
            lane = lax.broadcasted_iota(jnp.int32, (1, scale_ref.shape[1]), 1)
            scale_ref[c, :] = jnp.where(lane < 64, scale_ref[c, :], inv)
            ne = (lo * inv * gains_ref[2:3, :]).astype(BF)
            ne_ref[c, :] = ne
            emb_ref[c, :] = dot(ne, wp_ref[...]).astype(BF)

def ffn(rows, ctx, w_one, w_gu, w_down, gains, p_size, block):
    total, width = rows.shape
    ff = w_down.shape[0]
    once = pl.Buffered(1)
    full = lambda cols, at=0: pl.BlockSpec((total, cols), lambda j: (0, 0), pipeline_mode=once)
    return pl.pallas_call(
        functools.partial(ffn_kernel, 4),
        grid=(ff // block,),
        in_specs=[
            full(width), full(width),
            pl.BlockSpec((width, width), lambda j: (0, 3), pipeline_mode=once),
            pl.BlockSpec((width, 2 * block), lambda j: (0, j)),
            pl.BlockSpec((block, width), lambda j: (j, 0)),
            pl.BlockSpec((width, p_size), lambda j: (0, 4 * width // p_size), pipeline_mode=once),
            pl.BlockSpec(gains.shape, lambda j: (0, 0)),
        ],
        out_specs=[full(width), pl.BlockSpec((total, 2 * block), lambda j: (0, j)), full(128), full(width), full(p_size)],
        out_shape=[
            jax.ShapeDtypeStruct((total, width), BF), jax.ShapeDtypeStruct((total, 2 * ff), BF),
            jax.ShapeDtypeStruct((total, 128), F32), jax.ShapeDtypeStruct((total, width), BF),
            jax.ShapeDtypeStruct((total, p_size), BF),
        ],
        scratch_shapes=[pltpu.VMEM((total, width), F32)],
        compiler_params=pltpu.CompilerParams(vmem_limit_bytes=VMEM_ALL),
        name="feed_forward",
    )(rows, ctx, w_one, w_gu, w_down, w_one, gains)

def rms_pull_normed(normed, inv, gain, upstream):
    unit = normed.astype(F32) / gain
    scaled = upstream * gain
    d_gain = jnp.sum(upstream * unit, axis=0, keepdims=True)
    inner = jnp.mean(scaled * unit, axis=-1, keepdims=True)
    return inv * (scaled - unit * inner), d_gain


def rms_pull(v, gain, upstream):
    inv = inverse_rms(v)
    scaled = upstream * gain
    d_gain = jnp.sum(upstream * (v * inv), axis=0, keepdims=True)
    inner = jnp.mean(scaled * v, axis=-1, keepdims=True)
    return inv * scaled - v * (inv * inv * inv * inner), d_gain

def ffn_back_kernel(parts, de_ref, scale_ref, ne_ref, n2_ref, ctx_ref, wo_ref, wp_ref, gains_ref, gu_ref, wgu_ref, wd_ref,
                    dgu_w_ref, dd_w_ref, last_ref, dh_ref, dctx_ref, dgain_ref, dl_ref, low_ref, n2t_ref, acc_ref, dhl_ref):
    j = pl.program_id(0)
    block = wd_ref.shape[0]
    chunks = chunks_of(ne_ref.shape[0], parts)
    @pl.when(j == 0)
    def _():
        dgain_ref[...] = jnp.zeros_like(dgain_ref)
        for c in chunks:
            up = dot_nt(de_ref[c, :], wp_ref[...])
            dl, dg = rms_pull_normed(ne_ref[c, :], scale_ref[c, 64:65], gains_ref[2:3, :], up)
            dl_ref[c, :] = dl
            low_ref[c, :] = dl.astype(BF)
            dgain_ref[2:3, :] += dg
        width = ne_ref.shape[1]
        last_ref[:, width : width + de_ref.shape[1]] = dot_tn(ne_ref[...], de_ref[...]).astype(BF)
        n2t_ref[...] = n2_ref[...].T
        acc_ref[...] = jnp.zeros_like(acc_ref)
    acts, dgus = [], []
    das = [dot_nt(low_ref[c, :], wd_ref[...]) for c in chunks]
    for c, da in zip(chunks, das):
        g = gu_ref[c, :block].astype(F32)
        u = gu_ref[c, block:].astype(F32)
        t = jnp.tanh(GELU_SCALE * (g + GELU_CUBE * (g * g * g)))
        cdf = 0.5 * (1.0 + t)
        gel = g * cdf
        acts.append((gel * u).astype(BF))
        slope = cdf + (0.5 * GELU_SCALE) * g * (1.0 - t * t) * (1.0 + (3.0 * GELU_CUBE) * (g * g))
        dgu = jnp.concatenate([(da * u * slope).astype(BF), (da * gel).astype(BF)], axis=1)
        dgus.append(dgu)
    for c, dgu in zip(chunks, dgus):
        acc_ref[c, :] += dot_nt(dgu, wgu_ref[...])
    dgu_w_ref[...] = dot(n2t_ref[...], jnp.concatenate(dgus, axis=0)).astype(BF)
    dd_w_ref[...] = dot_tn(jnp.concatenate(acts, axis=0), low_ref[...]).astype(BF)
    @pl.when(j == pl.num_programs(0) - 1)
    def _():
        for c in chunks:
            dv, dg = rms_pull_normed(n2_ref[c, :], scale_ref[c, 0:1], gains_ref[1:2, :], acc_ref[c, :])
            dh = dl_ref[c, :] + dv
            dh_ref[c, :] = dh
            dhl = dh.astype(BF)
            dhl_ref[c, :] = dhl
            dgain_ref[1:2, :] += dg
            dctx_ref[c, :] = dot_nt(dhl, wo_ref[...]).astype(BF)
        width = ne_ref.shape[1]
        last_ref[:, :width] = dot_tn(ctx_ref[...], dhl_ref[...]).astype(BF)
        last_ref[:, width + de_ref.shape[1] :] = columns_of([dgain_ref[i : i + 1, :] for i in range(3)]).astype(BF)

def ffn_back(d_emb, scale, ne, n2, ctx, w_one, w_gu, w_down, gains, gu, p_size, block):
    total, width = ne.shape
    ff = w_down.shape[0]
    once = pl.Buffered(1)
    full = lambda cols: pl.BlockSpec((total, cols), lambda j: (0, 0), pipeline_mode=once)
    fixed = lambda shape: pl.BlockSpec(shape, lambda j: (0, 0), pipeline_mode=once)
    V = pltpu.VMEM
    return pl.pallas_call(
        functools.partial(ffn_back_kernel, 4),
        grid=(ff // block,),
        in_specs=[
            full(p_size), full(128), full(width), full(width), full(width),
            pl.BlockSpec((width, width), lambda j: (0, 3), pipeline_mode=once),
            pl.BlockSpec((width, p_size), lambda j: (0, 4 * width // p_size), pipeline_mode=once),
            fixed(gains.shape),
            pl.BlockSpec((total, 2 * block), lambda j: (0, j)),
            pl.BlockSpec((width, 2 * block), lambda j: (0, j)),
            pl.BlockSpec((block, width), lambda j: (j, 0)),
        ],
        out_specs=[
            pl.BlockSpec((width, 2 * block), lambda j: (0, j)),
            pl.BlockSpec((block, width), lambda j: (j, 0)),
            fixed((width, width + p_size + 128)), full(width), full(width),
        ],
        out_shape=[
            jax.ShapeDtypeStruct((width, 2 * ff), BF), jax.ShapeDtypeStruct((ff, width), BF),
            jax.ShapeDtypeStruct((width, width + p_size + 128), BF),
            jax.ShapeDtypeStruct((total, width), F32), jax.ShapeDtypeStruct((total, width), BF),
        ],
        scratch_shapes=[V((8, width), F32), V((total, width), F32), V((total, width), BF), V((width, total), BF), V((total, width), F32), V((total, width), BF)],
        compiler_params=pltpu.CompilerParams(vmem_limit_bytes=VMEM_ALL),
        name="feed_forward_back",
    )(d_emb, scale, ne, n2, ctx, w_one, w_one, gains, gu, w_gu, w_down)

def gate_up_columns(gate, up, block):
    rows, ff = gate.shape
    return jnp.stack([gate.reshape(rows, -1, block), up.reshape(rows, -1, block)], axis=2).reshape(rows, 2 * ff)


def contract_rows(left_mat, right_mat):
    return lax.dot_general(
        left_mat, right_mat, (((0,), (0,)), ((), ())), preferred_element_type=jnp.float32
    )


def contract_cols(left_mat, right_mat):
    return lax.dot_general(
        left_mat, right_mat, (((1,), (1,)), ((), ())), preferred_element_type=jnp.float32
    )


def matmul(left_mat, right_mat):
    return jnp.dot(left_mat, right_mat, preferred_element_type=jnp.float32)


def rms_forward(values, gain_vec):
    inverse = lax.rsqrt(jnp.mean(values * values, axis=-1, keepdims=True) + eps_norm)
    return (values * inverse * gain_vec, inverse)


def rms_backward(values, inverse, gain_vec, upstream):
    scaled = upstream * gain_vec
    gain_grad = jnp.sum(upstream * values * inverse, axis=0)
    inner_mean = jnp.mean(scaled * values, axis=-1, keepdims=True)
    return (inverse * scaled - values * inverse * inverse * inverse * inner_mean, gain_grad)


def two_level(shards):
    return (
        lax.axis_size("dp") == 4
        and lax.axis_size("wide") % 4 == 0
        and all(s.shape[0] % 8 == 0 for s in shards)
    )


def gathered(shards):
    return [lax.all_gather(s, ("dp", "wide"), axis=0, tiled=True) for s in shards]


def summed(grads, table):
    sums = [lax.psum_scatter(g.astype(F32), ("dp", "wide"), scatter_dimension=0, tiled=True) for g in grads]
    return [*sums, lax.psum(table, ("dp", "wide"))]


def local(
    doc_tokens,
    query_tokens,
    query_lengths,
    retrieved,
    targets,
    q_weight,
    k_weight,
    v_weight,
    o_weight,
    gate_weight,
    up_weight,
    down_weight,
    proj_weight,
    attn_gain,
    ffn_gain,
    final_gain,
    rel_bias,
):
    micro_count, _, doc_len, width = doc_tokens.shape
    slots = query_tokens.shape[2]
    doc_rows = micro_count * doc_len
    wide_count = lax.axis_size("wide")
    p_size = proj_weight.shape[1]
    bucket_count, head_count = rel_bias.shape
    pairs = width // 128
    ff_block = FF_BLOCK
    weights = [q_weight, k_weight, v_weight, o_weight, proj_weight]
    ffn_raw = [gate_weight, up_weight, down_weight]
    beside = two_level(weights + ffn_raw)
    picks = retrieved.reshape(-1, retrieved.shape[3])
    lengths = query_lengths
    n_dev = lax.axis_size("dp") * wide_count
    w_one = None
    if not beside:
        shard_one = jnp.concatenate(
            [pair_columns(weights[:3]), o_weight, proj_weight, jnp.pad(jnp.stack([attn_gain, ffn_gain, final_gain], axis=1), ((0, 0), (0, 125)))], axis=1
        )
        (w_one,) = gathered([shard_one])
    gain_rows = [g.reshape(1, -1) for g in (attn_gain, ffn_gain, final_gain)]
    shards = [*weights, *gain_rows, *ffn_raw] if beside else []
    rows_low, gains, normed, qkv, context, lse, table, *full = attend(
        doc_tokens.reshape(doc_rows, width),
        query_tokens.reshape(-1, width),
        rel_bias.T,
        lengths,
        slots,
        doc_len,
        micro_count,
        shards,
        picks,
        w_one,
        wide_count // 2 if beside else 0,
        n_dev,
    )
    if beside:
        w_one, w_gu, w_down, counts = full
    else:
        w_gu, w_down = gathered([gate_up_columns(gate_weight, up_weight, ff_block), down_weight])
        counts = count_all(picks.T, doc_len, wide_count)
    normed_two, gate_up, scale, normed_end, embedded = ffn(
        rows_low, context, w_one, w_gu, w_down, gains, p_size, ff_block
    )
    losses_out, d_embedded = score(
        embedded, picks, counts, lengths, targets, targets.shape, doc_len, slots, wide_count
    )
    gu_grad, down_grad, last_grad, d_hidden, d_context = ffn_back(
        d_embedded, scale, normed_end, normed_two, context, w_one, w_gu, w_down, gains, gate_up, p_size, ff_block
    )
    ff = down_grad.shape[0]
    ffn_layouts = [
        [[(2 * ff_block * i + at, ff_block) for i in range(ff // ff_block)] for at in (0, ff_block)],
        [[(0, width)]],
    ]
    one_layouts = [
        [[(384 * i + 128 * n, 128) for i in range(pairs)] for n in range(3)],
        [[(0, width)], [(width, p_size)], [(width + p_size, 128)]],
    ]
    back_args = (qkv, d_context, lse, table, lengths, slots, bucket_count, normed)
    if beside:
        d_rows, s_gu, s_down, s_last, s_qkv, s_table = back(
            *back_args,
            w_one,
            rows_low,
            d_hidden,
            gains,
            doc_len,
            micro_count,
            [gu_grad, down_grad, last_grad],
            wide_count // 2,
            n_dev,
        )
    else:
        qkv_grad, packed, d_qkv = attend_back(*back_args, doc_len, micro_count)
        d_rows = input_grads(d_qkv, w_one, rows_low, d_hidden, gains)
        s_qkv, s_last, s_gu, s_down, s_table = summed([qkv_grad, last_grad, gu_grad, down_grad], packed)
    d_docs, d_queries, s_table, g_attn, g_ffn, g_final, s_q, s_k, s_v, s_o, s_proj, _, s_gate, s_up, s_down = apart(
        d_rows,
        s_table,
        gain_rows[0],
        weights[:3],
        [s_qkv, s_last, s_gu, s_down],
        one_layouts + ffn_layouts,
        doc_rows,
        rel_bias.shape[::-1],
    )
    return (
        losses_out,
        d_docs.reshape(doc_tokens.shape),
        d_queries.reshape(query_tokens.shape),
        s_q,
        s_k,
        s_v,
        s_o,
        s_gate,
        s_up,
        s_down,
        s_proj,
        g_attn.reshape(-1),
        g_ffn.reshape(-1),
        g_final.reshape(-1),
        s_table.T,
    )


def solution(mesh):
    placed = (
        P(None, ("dp", "wide"), None, None),
        P(None, ("dp", "wide"), None, None),
        P(None, ("dp", "wide")),
        P(None, ("dp", "wide"), None, None),
        P(None, ("dp", "wide")),
        P(("dp", "wide"), None),
        P(("dp", "wide"), None),
        P(("dp", "wide"), None),
        P(("dp", "wide"), None),
        P(("dp", "wide"), None),
        P(("dp", "wide"), None),
        P(("dp", "wide"), None),
        P(("dp", "wide"), None),
        P(("dp", "wide")),
        P(("dp", "wide")),
        P(("dp", "wide")),
        P(),
    )
    return jax.shard_map(
        local,
        mesh=mesh,
        in_specs=placed,
        out_specs=(
            P(None, ("dp", "wide")),
            P(None, ("dp", "wide"), None, None),
            P(None, ("dp", "wide"), None, None),
            P(("dp", "wide"), None),
            P(("dp", "wide"), None),
            P(("dp", "wide"), None),
            P(("dp", "wide"), None),
            P(("dp", "wide"), None),
            P(("dp", "wide"), None),
            P(("dp", "wide"), None),
            P(("dp", "wide"), None),
            P(("dp", "wide")),
            P(("dp", "wide")),
            P(("dp", "wide")),
            P(),
        ),
        check_vma=False,
    )
```

```python
import functools

import jax
import jax.numpy as jnp
from jax import lax
from jax.experimental import pallas as pl
from jax.experimental.pallas import tpu as pltpu
from jax.sharding import PartitionSpec as P

eps_norm = 1e-06
score_scale = 6.0
mask_fill = -1000000000.0
top_precision = lax.Precision.HIGHEST
F32 = jnp.float32
BF = jnp.bfloat16
VMEM_ALL = 62 << 20
FF_BLOCK = 512


MESH = pl.DeviceIdType.MESH

def gray(p):
    return p + (p // 2) * (1 - 2 * (p % 2))

class Place:
    def __init__(self, zc):
        self.zc = zc
        d = lax.axis_index("dp"); w = lax.axis_index("wide")
        self.d, self.w = d, w
        self.z, self.c = w // 2, w % 2
        p = gray(d)
        self.right = gray((p + 1) % 4); self.left = gray((p + 3) % 4); self.opp = gray((p + 2) % 4)
    def dev(self, d=None, z=None, c=None):
        d = self.d if d is None else d
        z = self.z if z is None else z
        c = self.c if c is None else c
        return (d, z * 2 + c)

def enter(pos, wide=False, opp=False, between=lambda: None):
    barrier = pltpu.get_barrier_semaphore()
    def greet(dev):
        pl.semaphore_signal(barrier, inc=1, device_id=dev, device_id_type=MESH)
    greet(pos.dev(d=pos.right))
    greet(pos.dev(d=pos.left))
    if wide:
        @pl.loop(1, 2 * pos.zc)
        def _(k):
            greet((pos.d, lax.rem(pos.w + k, 2 * pos.zc)))
        between()
        pl.semaphore_wait(barrier, 1 + 2 * pos.zc)
    else:
        greet(pos.dev(c=1 - pos.c))
        @pl.loop(1, pos.zc)
        def _(k):
            greet(pos.dev(z=lax.rem(pos.z + k, pos.zc)))
        if opp:
            greet(pos.dev(d=pos.opp))
        between()
        pl.semaphore_wait(barrier, 2 + pos.zc + int(opp))


def gather_events(zc, shard, out, rest):
    count = len(shard)
    pos = Place(zc)
    comp = rest[:count]; mine = rest[count:2 * count]
    (s_col, s_ring, s_fwd, s_mate, s_pair, s_own, r_col, r_left, r_right, r_opp, r_mate, r_pair) = rest[2 * count:]
    z, c, d = pos.z, pos.c, pos.d
    rows = [o.shape[0] // (4 * zc) for o in out]
    half = [o.shape[1] // 2 for o in out]

    def part(a, ref, blk, core):
        return ref.at[pl.ds(pl.multiple_of(blk * rows[a], 16), rows[a]), pl.ds(pl.multiple_of(core * half[a], 128), half[a])]
    def own(a, core):
        return comp[a].at[:, pl.ds(pl.multiple_of(core * half[a], 128), half[a])]
    def rdma(a, src, blk, dev, ss, rs):
        return pltpu.make_async_remote_copy(src_ref=src, dst_ref=part(a, out[a], blk, c), send_sem=ss, recv_sem=rs, device_id=dev, device_id_type=MESH)
    def blk(dd, zz):
        return dd * zc + zz
    mate_dev = pos.dev(c=1 - c)
    def pair(a):
        return pltpu.make_async_remote_copy(src_ref=shard[a], dst_ref=mine[a], send_sem=s_pair.at[a], recv_sem=r_pair.at[a], device_id=mate_dev, device_id_type=MESH)
    def keep(a):
        return pltpu.make_async_copy(comp[a], out[a].at[pl.ds(pl.multiple_of(blk(d, z) * rows[a], 16), rows[a]), :], s_own.at[a])
    def up(a, src, zz):
        return rdma(a, src, blk(d, zz), pos.dev(z=lax.rem(z + 1, zc)), s_col.at[a, 0, zz], r_col.at[a, zz])
    def down(a, src, zz):
        return rdma(a, src, blk(d, zz), pos.dev(z=lax.rem(z + zc - 1, zc)), s_col.at[a, 1, zz], r_col.at[a, zz])
    def right(a, src, zz):
        return rdma(a, src, blk(d, zz), pos.dev(d=pos.right), s_ring.at[a, 0, zz], r_left.at[a, zz])
    def left(a, src, zz):
        return rdma(a, src, blk(d, zz), pos.dev(d=pos.left), s_ring.at[a, 1, zz], r_right.at[a, zz])
    def fwd_right(a, zz):
        b = blk(pos.left, zz)
        return rdma(a, part(a, out[a], b, c), b, pos.dev(d=pos.right), s_fwd.at[a, zz], r_opp.at[a, zz])
    def fwd_left(a, zz):
        b = blk(pos.right, zz)
        return rdma(a, part(a, out[a], b, c), b, pos.dev(d=pos.left), s_fwd.at[a, zz], r_opp.at[a, zz])
    def mate(a, b):
        return rdma(a, part(a, out[a], b, c), b, mate_dev, s_mate.at[a, b], r_mate.at[a, b])
    def got(a, b, sem):
        return rdma(a, part(a, out[a], b, c), b, mate_dev, s_mate.at[a, b], sem).wait_recv()
    def mate_got(a, b):
        piece = part(a, out[a], b, 1 - c)
        pltpu.make_async_remote_copy(src_ref=piece, dst_ref=piece, send_sem=s_mate.at[a, b], recv_sem=r_mate.at[a, b], device_id=mate_dev, device_id_type=MESH).wait_recv()

    def begin(between):
        enter(pos, wide=True, between=between)
        pair(0).start()
    def begin_rest():
        for a in range(1, count):
            pair(a).start()
    def first(a):
        pair(a).wait_recv()
        r2 = rows[a] // 2
        step = 256 if half[a] * 2 % 256 == 0 else 128
        @pl.loop(0, half[a] * 2 // step)
        def _(t):
            cols = pl.ds(pl.multiple_of(t * step, 128), step)
            mn = shard[a][:, cols].astype(jnp.float32)[:r2]
            ot = mine[a][:, cols].astype(jnp.float32)[:r2]
            first = jnp.where(c == 0, mn, ot)
            second = jnp.where(c == 0, ot, mn)
            comp[a][:, cols] = jnp.concatenate([first, second], axis=0).astype(jnp.bfloat16)
        right(a, own(a, c), z).start()
        left(a, own(a, c), z).start()
        pl.when(z < zc - 1)(lambda: up(a, own(a, c), z).start())
        pl.when(z > 0)(lambda: down(a, own(a, c), z).start())
        keep(a).start()

    def column(a, j):
        @pl.when(z - j >= 0)
        def _():
            zz = z - j
            got(a, blk(d, zz), r_col.at[a, zz])
            src = part(a, out[a], blk(d, zz), c)
            pl.when(z < zc - 1)(lambda: up(a, src, zz).start())
            right(a, src, zz).start(); left(a, src, zz).start()
            mate(a, blk(d, zz)).start()
        @pl.when(z + j < zc)
        def _():
            zz = z + j
            got(a, blk(d, zz), r_col.at[a, zz])
            src = part(a, out[a], blk(d, zz), c)
            pl.when(z > 0)(lambda: down(a, src, zz).start())
            right(a, src, zz).start(); left(a, src, zz).start()
            mate(a, blk(d, zz)).start()
    def ring_one(a, zz):
        got(a, blk(pos.left, zz), r_left.at[a, zz])
        pl.when(zz % 2 == 0)(lambda: fwd_right(a, zz).start())
        mate(a, blk(pos.left, zz)).start()
        got(a, blk(pos.right, zz), r_right.at[a, zz])
        pl.when(zz % 2 == 1)(lambda: fwd_left(a, zz).start())
        mate(a, blk(pos.right, zz)).start()
    def opp_one(a, zz):
        got(a, blk(pos.opp, zz), r_opp.at[a, zz])
        mate(a, blk(pos.opp, zz)).start()
    def spread(fn, a, j):
        if j == 0:
            fn(a, z); return
        pl.when(z - j >= 0)(lambda: fn(a, z - j))
        pl.when(z + j < zc)(lambda: fn(a, z + j))
    def rounds(a):
        call = functools.partial
        steps = []
        for t in range(1, zc + 2):
            if t < zc:
                steps.append(call(column, a, t))
            if t <= zc:
                steps.append(call(spread, ring_one, a, t - 1))
            if t >= 2:
                steps.append(call(spread, opp_one, a, t - 2))
        return steps
    def finish_one(a):
        pair(a).wait_send(); keep(a).wait()
        @pl.loop(0, zc)
        def _(zz):
            src = part(a, out[a], blk(d, zz), c)
            right(a, src, zz).wait_send(); left(a, src, zz).wait_send()
            pl.when((z < zc - 1) & (zz <= z))(lambda: up(a, src, zz).wait_send())
            pl.when((z > 0) & (zz >= z))(lambda: down(a, src, zz).wait_send())
            fwd_right(a, zz).wait_send()
        @pl.loop(0, 4 * zc)
        def _(b):
            @pl.when(b != blk(d, z))
            def _():
                mate(a, b).wait_send()
                mate_got(a, b)
    return pos, begin, begin_rest, first, rounds, finish_one


def count_places(picks, first, out_ref, size):
    tokens = picks.shape[1]
    chunk = 64
    @pl.loop(0, size // chunk)
    def _(t):
        at = pl.multiple_of(t * chunk, chunk)
        place = lax.broadcasted_iota(jnp.int32, (chunk, tokens), 0) + (first + at)
        count = jnp.zeros((chunk, tokens), jnp.int32)
        for k in range(picks.shape[0]):
            count = count + (picks[k : k + 1, :] == place).astype(jnp.int32)
        out_ref[pl.ds(at, chunk), :] = count.astype(F32).astype(BF)


def count_kernel(doc_len, all_ref, out_ref):
    count_places(all_ref[0], lax.axis_index("wide") * doc_len, out_ref.at[0], doc_len)


def count_all(picks, doc_len, peers):
    everyone = lax.all_gather(picks, "wide", axis=0)
    shape = (1,) + picks.shape
    return pl.pallas_call(
        functools.partial(count_kernel, doc_len),
        grid=(peers,),
        in_specs=[pl.BlockSpec(shape, lambda i: (i, 0, 0))],
        out_specs=pl.BlockSpec((1, doc_len, picks.shape[1]), lambda i: (i, 0, 0)),
        out_shape=jax.ShapeDtypeStruct((peers, doc_len, picks.shape[1]), BF),
        name="count",
    )(everyone)


def put_columns(ref, at, x):
    spare = ref.shape[0] - x.shape[0]
    full = jnp.concatenate([x.astype(F32), jnp.zeros((spare, x.shape[1]), F32)], axis=0) if spare else x
    ref[:, at : at + x.shape[1]] = full.astype(ref.dtype)


def picks_events(pos, doc_len, picks_ref, counts_ref, p_all, s_p, r_p):
    peers = 2 * pos.zc
    part = doc_len // 2
    def picks_copy(k, there):
        o = lax.rem(pos.w + k, peers)
        slot = pos.w if there else o
        return pltpu.make_async_remote_copy(src_ref=picks_ref, dst_ref=p_all.at[slot], send_sem=s_p.at[o], recv_sem=r_p.at[slot], device_id=(pos.d, o), device_id_type=MESH)
    def begin():
        @pl.loop(1, peers)
        def _(k):
            picks_copy(k, True).start()
    def counted(k, h):
        o = lax.rem(pos.w + k, peers)
        if k and not h:
            picks_copy(k, False).wait_recv()
        picks = p_all[o] if k else picks_ref[...]
        count_places(picks, pos.w * doc_len + h * part, counts_ref.at[o, pl.ds(h * part, part)], part)
    def finish():
        @pl.loop(1, peers)
        def _(k):
            picks_copy(k, True).wait_send()
    return begin, [functools.partial(counted, k, h) for k in range(peers) for h in range(2)], finish


def gather_scratch(shapes, zc):
    count = len(shapes)
    comps = [pltpu.VMEM((2 * rows, cols), BF) for rows, cols in shapes]
    mines = [pltpu.VMEM((rows + -rows % 16, cols), BF) for rows, cols in shapes]
    dma = pltpu.SemaphoreType.DMA
    sems = [dma((count, 2, zc)), dma((count, 2, zc)), dma((count, zc)), dma((count, 4 * zc)), dma((count,)), dma((count,)),
            dma((count, zc)), dma((count, zc)), dma((count, zc)), dma((count, zc)), dma((count, 4 * zc)), dma((count,))]
    return comps + mines + sems


def reduce_events(zc, g, out, rest):
    count = len(g)
    pos = Place(zc)
    z, c, d = pos.z, pos.c, pos.d
    loc = rest[:count]; rxp = rest[count:2 * count]; rxf = rest[2 * count:3 * count]
    rxl = rest[3 * count:4 * count]; rxr = rest[4 * count:5 * count]
    rxz = rest[5 * count:6 * count]
    fin = rest[6 * count:7 * count]; rxm = rest[7 * count:8 * count]
    (s_pair, r_pair, s_loc, s_ring, r_fwd, r_left, r_right, s_z, r_z, s_fin, r_fin) = rest[8 * count:]
    rows = [x.shape[0] // (4 * zc) for x in g]
    half = [x.shape[1] // 2 for x in g]
    mate_dev = pos.dev(c=1 - c)
    right_dev = pos.dev(d=pos.right); left_dev = pos.dev(d=pos.left)
    def remote(src, dst, ss, rs, dev):
        return pltpu.make_async_remote_copy(src_ref=src, dst_ref=dst, send_sem=ss, recv_sem=rs, device_id=dev, device_id_type=MESH)
    def strip(a, dd):
        return pl.ds(pl.multiple_of(dd * zc * rows[a], 16), zc * rows[a])
    def cols(a, core):
        return pl.ds(pl.multiple_of(core * half[a], 128), half[a])
    def pair(a, dd):
        return remote(g[a].at[strip(a, dd), cols(a, 1 - c)], rxp[a].at[strip(a, dd), :], s_pair.at[a, dd], r_pair.at[a, dd], mate_dev)
    def local(a, dd):
        return pltpu.make_async_copy(g[a].at[strip(a, dd), cols(a, c)], loc[a].at[strip(a, dd), :], s_loc.at[a, dd])
    def first_row(a, dd, zz):
        return (dd * zc + zz) * rows[a]
    def row(a, dd, zz):
        return pl.ds(pl.multiple_of(first_row(a, dd, zz), 16), rows[a])
    def slot(a, zz):
        return pl.ds(pl.multiple_of(zz * rows[a], 16), rows[a])
    def add(a, dst, terms):
        group = 16
        while rows[a] % (2 * group) == 0 and 2 * group * half[a] <= 32768:
            group *= 2
        @pl.loop(0, rows[a] // group)
        def _(t):
            total = None
            for ref, at in terms:
                v = ref[pl.ds(pl.multiple_of(at + t * group, 16), group), :].astype(F32)
                total = v if total is None else total + v
            ref, at = dst
            ref[pl.ds(pl.multiple_of(at + t * group, 16), group), :] = total.astype(ref.dtype)
    def pair_sum(a, dd, zz, extra=()):
        r = first_row(a, dd, zz)
        add(a, (loc[a], r), [(loc[a], r), (rxp[a], r)] + list(extra))
    def first_right(a, zz):
        return remote(loc[a].at[row(a, pos.opp, zz), :], rxf[a].at[slot(a, zz), :], s_ring.at[a, 0, zz], r_fwd.at[a, zz], right_dev)
    def first_left(a, zz):
        return remote(loc[a].at[row(a, pos.opp, zz), :], rxf[a].at[slot(a, zz), :], s_ring.at[a, 0, zz], r_fwd.at[a, zz], left_dev)
    def to_right(a, zz):
        return remote(loc[a].at[row(a, pos.right, zz), :], rxl[a].at[slot(a, zz), :], s_ring.at[a, 1, zz], r_left.at[a, zz], right_dev)
    def to_left(a, zz):
        return remote(loc[a].at[row(a, pos.left, zz), :], rxr[a].at[slot(a, zz), :], s_ring.at[a, 2, zz], r_right.at[a, zz], left_dev)
    def to_line(a, zt):
        return remote(loc[a].at[row(a, d, zt), :], rxz[a].at[slot(a, z), :], s_z.at[a, zt], r_z.at[a, z], pos.dev(z=zt))
    def from_line(a, zs):
        return remote(loc[a].at[row(a, d, zs), :], rxz[a].at[slot(a, zs), :], s_z.at[a, zs], r_z.at[a, zs], pos.dev(z=zs))
    def mate_rows(a):
        r2 = rows[a] // 2
        return pl.ds(pl.multiple_of((1 - c) * r2, 8), r2)
    def my_rows(a):
        r2 = rows[a] // 2
        return pl.ds(pl.multiple_of(c * r2, 8), r2)
    def final(a):
        return remote(fin[a].at[mate_rows(a), :], rxm[a], s_fin.at[a], r_fin.at[a], mate_dev)

    order = []
    for i in range(zc // 2):
        order += [zc - 1 - i, i]
    head = order[0]
    def begin(arrays):
        for a in arrays:
            for dd in (pos.opp, pos.right, pos.left):
                pair(a, dd).start(); local(a, dd).start()
        for a in arrays:
            pair(a, d).start(); local(a, d).start()
    def opposite(a, zz):
        if zz == head:
            pair(a, pos.opp).wait_recv(); local(a, pos.opp).wait()
        pair_sum(a, pos.opp, zz)
        (first_right if zz % 2 == 0 else first_left)(a, zz).start()
    def beside(a, zz):
        if zz % 2:
            pair_sum(a, pos.right, zz); to_right(a, zz).start()
        else:
            pair_sum(a, pos.left, zz); to_left(a, zz).start()
    def neighbours(a):
        for dd in (pos.right, pos.left):
            pair(a, dd).wait_recv(); local(a, dd).wait()
    def onward(a, zz):
        if zz % 2 == 0:
            first_right(a, zz).wait_recv()
            pair_sum(a, pos.right, zz, [(rxf[a], zz * rows[a])]); to_right(a, zz).start()
        else:
            first_left(a, zz).wait_recv()
            pair_sum(a, pos.left, zz, [(rxf[a], zz * rows[a])]); to_left(a, zz).start()
    def column(a, zz, dst, extra=()):
        r = first_row(a, d, zz)
        add(a, dst, [(loc[a], r), (rxp[a], r), (rxl[a], zz * rows[a]), (rxr[a], zz * rows[a])] + list(extra))
    def arrived(a, zz):
        if zz == head:
            pair(a, d).wait_recv(); local(a, d).wait()
        to_right(a, zz).wait_recv(); to_left(a, zz).wait_recv()
    def line(a, zt):
        @pl.when(z != zt)
        def _():
            column(a, zt, (loc[a], first_row(a, d, zt)))
            to_line(a, zt).start()
    def mine(a):
        others = [lax.rem(z + k, zc) for k in range(1, zc)]
        for o in others:
            from_line(a, o).wait_recv()
        column(a, z, (fin[a], 0), [(rxz[a], o * rows[a]) for o in others])
        final(a).start()
    def whole(a):
        out[a][:, cols(a, c)] = fin[a][my_rows(a), :]
        final(a).wait_recv()
        out[a][:, cols(a, 1 - c)] = rxm[a][...]
    def steps_of(a):
        call = functools.partial
        cuts = [order[: zc // 2], order[zc // 2 :]]
        stages = [[call(opposite, a, zz) for zz in order] + [call(neighbours, a)]]
        for n, cut in enumerate(cuts):
            before = cuts[n - 1] if n else []
            stages.append(
                [call(arrived, a, zz) for zz in before]
                + [call(onward, a, zz) for zz in cut]
                + [call(beside, a, zz) for zz in cut]
                + [call(line, a, zz) for zz in before]
            )
        stages.append([call(arrived, a, zz) for zz in cuts[-1]] + [call(line, a, zz) for zz in cuts[-1]])
        stages.append([call(mine, a)])
        return stages
    def groups_of(arrays):
        parts = [steps_of(a) for a in arrays]
        depth = len(parts[0])
        groups = []
        for t in range(len(parts) + depth - 1):
            group = []
            for n, part in enumerate(parts):
                if 0 <= t - n < depth:
                    group += part[t - n]
            groups.append(group)
        return groups + [[functools.partial(whole, a) for a in arrays]]
    def finish():
        for a in range(count):
            for dd in range(4):
                pair(a, dd).wait_send()
            for zz in range(zc):
                (first_right if zz % 2 == 0 else first_left)(a, zz).wait_send()
                to_right(a, zz).wait_send(); to_left(a, zz).wait_send()
                @pl.when(zz != z)
                def _():
                    to_line(a, zz).wait_send()
            final(a).wait_send()
    return pos, begin, groups_of, finish


ROW_BLOCK = 128


def input_grad(dqkv_ref, w_ref, rows_ref, dh_ref, gains_ref, dx_ref):
    up = dot_nt(dqkv_ref[...], w_ref[...])
    dv, _ = rms_pull(rows_ref[...].astype(F32), gains_ref[0:1, :], up)
    dx_ref[...] = dh_ref[...] + dv


def reduce_scratch(grads, zc):
    count = len(grads)
    V = pltpu.VMEM
    rows = [x.shape[0] // (4 * zc) for x in grads]; half = [x.shape[1] // 2 for x in grads]
    scratch = [V((x.shape[0], h), BF) for x, h in zip(grads, half)] * 2
    for _ in range(4):
        scratch += [V((zc * r, h), BF) for r, h in zip(rows, half)]
    scratch += [V((r, h), F32) for r, h in zip(rows, half)]
    scratch += [V((r // 2, h), F32) for r, h in zip(rows, half)]
    dma = pltpu.SemaphoreType.DMA
    return scratch + [dma((count, 4)), dma((count, 4)), dma((count, 4)), dma((count, 3, zc))] + [dma((count, zc))] * 5 + [dma((count,)), dma((count,))]


def reduce_shapes(grads, n_dev):
    return [jax.ShapeDtypeStruct((x.shape[0] // n_dev, x.shape[1]), F32) for x in grads]


def input_grads(dqkv, w_one, rows, d_hidden, gains):
    total, width = rows.shape
    block = lambda cols: pl.BlockSpec((ROW_BLOCK, cols), lambda i: (i, 0))
    return pl.pallas_call(
        input_grad,
        grid=(total // ROW_BLOCK,),
        out_shape=jax.ShapeDtypeStruct(rows.shape, F32),
        in_specs=[
            block(dqkv.shape[1]),
            pl.BlockSpec((width, dqkv.shape[1]), lambda i: (0, 0), pipeline_mode=pl.Buffered(1)),
            block(width), block(width),
            pl.BlockSpec(gains.shape, lambda i: (0, 0)),
        ],
        out_specs=block(width),
        compiler_params=pltpu.CompilerParams(vmem_limit_bytes=VMEM_ALL),
        name="input_grads",
    )(dqkv, w_one, rows, d_hidden, gains)


def table_events(pos, table, table_out, refs):
    t_mate, t_ring, t_line, s_mate, r_mate, s_tr, r_tr, s_tl, r_tl = refs
    z, d, zc = pos.z, pos.d, pos.zc
    around = (pos.right, pos.left, pos.opp)
    others = [lax.rem(z + k, zc) for k in range(1, zc)]
    def tab(src, dst, ss, rs, dev):
        return pltpu.make_async_remote_copy(src_ref=src, dst_ref=dst, send_sem=ss, recv_sem=rs, device_id=dev, device_id_type=MESH)
    def tab_mate():
        return tab(table, t_mate, s_mate, r_mate, pos.dev(c=1 - pos.c))
    def tab_ring(dd, there):
        slot = d if there else dd
        return tab(t_ring.at[slot], t_ring.at[slot], s_tr.at[dd], r_tr.at[slot], pos.dev(d=dd))
    def tab_line(zz, there):
        slot = z if there else zz
        return tab(t_line.at[slot], t_line.at[slot], s_tl.at[zz], r_tl.at[slot], pos.dev(z=zz))
    def begin():
        tab_mate().start()
    def cores():
        tab_mate().wait_recv()
        t_ring[d] = table[...] + t_mate[...]
        for dd in around:
            tab_ring(dd, True).start()
    def ring():
        for dd in around:
            tab_ring(dd, False).wait_recv()
        t_line[z] = t_ring[0] + t_ring[1] + t_ring[2] + t_ring[3]
        for zz in others:
            tab_line(zz, True).start()
    def line():
        for zz in others:
            tab_line(zz, False).wait_recv()
        total = t_line[0]
        for zz in range(1, zc):
            total = total + t_line[zz]
        table_out[...] = total
        tab_mate().wait_send()
        for dd in around:
            tab_ring(dd, True).wait_send()
        for zz in others:
            tab_line(zz, True).wait_send()
    return begin, cores, ring, line


def table_scratch(shape, zc):
    V = pltpu.VMEM
    dma = pltpu.SemaphoreType.DMA
    return [V(shape, F32), V((4,) + shape, F32), V((zc,) + shape, F32), dma, dma, dma((4,)), dma((4,)), dma((zc,)), dma((zc,))]


def apart_kernel(layouts, docs_in, queries_in, packed_ref, gain_ref, wq_ref, wk_ref, wv_ref, *refs):
    count = len(layouts)
    docs_ref, queries_ref, table_ref, g_attn, g_ffn, g_end = refs[count : count + 6]
    outs = list(refs[count + 6 :])
    docs_ref[...] = docs_in[...]
    @pl.when(pl.program_id(0) == 0)
    def _():
        queries_ref[...] = queries_in[...]
        done = []
        for ref, layout in zip(refs[:count], layouts):
            for pieces in layout:
                out = outs.pop(0)
                done.append(out)
                to = 0
                for start, size in pieces:
                    out[:, to : to + size] = ref[:, start : start + size]
                    to += size
        weighed = sum(w[...].astype(F32) * g[...] for w, g in zip((wq_ref, wk_ref, wv_ref), done))
        n = weighed.shape[0]
        g_attn[...] = turned(jnp.sum(weighed, axis=1, keepdims=True))[0:1, :n] / gain_ref[...].astype(F32)
        columns = refs[1][:, refs[1].shape[1] - 128 :]
        rows = turned(columns)
        g_ffn[...] = rows[1:2, :n]
        g_end[...] = rows[2:3, :n]
        heads, buckets = table_ref.shape
        pieces = [packed_ref[:, i * buckets : (i + 1) * buckets] for i in range(-(-heads // 8))]
        table_ref[...] = jnp.concatenate(pieces, axis=0)[:heads]


def apart(dx, packed, gain, weights, sums, layouts, doc_rows, table_shape):
    total, width = dx.shape
    rest = total - doc_rows
    n = weights[0].shape[0]
    shapes = [jax.ShapeDtypeStruct(s, F32) for s in ((doc_rows, width), (rest, width), table_shape, (1, n), (1, n), (1, n))]
    shapes += [
        jax.ShapeDtypeStruct((x.shape[0], sum(size for _, size in pieces)), F32)
        for x, layout in zip(sums, layouts)
        for pieces in layout
    ]
    fixed = lambda x: pl.BlockSpec(x.shape, lambda i: (0, 0), pipeline_mode=pl.Buffered(1))
    block = pl.BlockSpec((doc_rows // 4, width), lambda i: (i, 0))
    extra = [packed, gain, *weights, *sums]
    return pl.pallas_call(
        functools.partial(apart_kernel, layouts),
        grid=(4,),
        out_shape=shapes,
        in_specs=[block, pl.BlockSpec((rest, width), lambda i: (doc_rows // rest, 0), pipeline_mode=pl.Buffered(1))] + [fixed(x) for x in extra],
        out_specs=[block] + [fixed(x) for x in shapes[1:]],
        compiler_params=pltpu.CompilerParams(vmem_limit_bytes=VMEM_ALL),
        name="apart",
    )(dx, dx, *extra)


def bucket_of(n):
    far = jnp.zeros_like(n)
    dist = jnp.abs(n)
    for power_step in range(1, 8):
        far = far + (dist * dist >= 64 * 2**power_step).astype(jnp.int32)
    return jnp.where(n > 0, 16, 0) + jnp.where(dist < 8, dist, 8 + far)

def diagonal_hot(doc_len, rows):
    span = 2 * doc_len
    i = lax.broadcasted_iota(jnp.int32, (1, span), 1)
    n = doc_len - 128 - jnp.where(i >= span - 127, i - span, i)
    inside = (n > -doc_len) & (n < doc_len)
    bucket = jnp.where(inside, bucket_of(n), -1)
    return (lax.broadcasted_iota(jnp.int32, (rows, span), 0) == bucket).astype(F32)


def padded_tile(x):
    n, m = x.shape
    x = x.astype(F32)
    if m < 128:
        x = jnp.concatenate([x, jnp.zeros((n, 128 - m), F32)], axis=1)
    if n < 128:
        x = jnp.concatenate([x, jnp.zeros((128 - n, 128), F32)], axis=0)
    return x


def turned(x):
    return padded_tile(x).T


def per_token(values, first, shape, dim, slots):
    owner = lax.broadcasted_iota(jnp.int32, shape, dim) // slots
    out = jnp.zeros(shape, jnp.int32)
    for q in range(shape[dim] // slots):
        n = first + q
        out = jnp.where(owner == q, values[n // values.shape[1], n % values.shape[1]], out)
    return out


def live_tile(lengths, tile, slots):
    shape = (128, 128)
    key = lax.broadcasted_iota(jnp.int32, shape, 0)
    query = lax.broadcasted_iota(jnp.int32, shape, 1)
    limit = per_token(lengths, tile * (128 // slots), shape, 0, slots)
    return (lax.rem(key, slots) < limit) & (key // slots == query // slots)


def cols_dot(a, b):
    return lax.dot_general(a, b, (((1,), (1,)), ((), ())), preferred_element_type=F32)

def tiles_of(table, keys, q_from, q_len, doc_len):
    parts = []
    for kb in range(keys // 128):
        at = doc_len - 128 - 128 * kb + q_from
        parts.append(table[:, at : at + q_len])
    return jnp.concatenate(parts, axis=0) if len(parts) > 1 else parts[0]

def spread_steps(steps, first_slot, slots):
    plan = {}
    for n, step in enumerate(steps):
        at = min(slots - 1, first_slot + (n * (slots - first_slot)) // len(steps))
        plan.setdefault(at, []).append(step)
    return plan


def attend_kernel(doc_len, doc_count, block, zc, slot_count, docs_ref, queries_ref, rel_ref, lengths_ref, *refs):
    beside = zc > 0
    ins = 12 if beside else 1
    raw = refs[:ins]
    rows_ref, gains_ref, normed_ref, qkv_ref, ctx_ref, lse_ref, table_ref = refs[ins : ins + 7]
    j = pl.program_id(0)
    span = 2 * doc_len
    hd = 64
    total = rows_ref.shape[0]
    width = rows_ref.shape[1]
    rest = total - doc_count * doc_len
    places = [(m * doc_len, doc_len, q_at, block, None) for m in range(doc_count) for q_at in range(0, doc_len, block)]
    places += [(doc_count * doc_len + 128 * i, 128, 0, 128, i) for i in range(rest // 128)]
    slots = len(places)
    plan = {}
    if beside:
        q_ref, k_ref, v_ref, o_ref, p_ref, *g_refs, gate_ref, up_ref, down_ref, raw_picks = raw
        outs = refs[ins + 7 : ins + 10]
        counts_ref = refs[ins + 10]
        shards = refs[ins + 11 : ins + 14]
        w_ref, load, picks_ref, p_all, s_p, r_p = refs[ins + 14 : ins + 20]
        pos, begin, begin_rest, first, rounds, finish_one = gather_events(zc, shards, outs, refs[ins + 20 : -1])
        begin_picks, pieces, finish_picks = picks_events(pos, doc_len, picks_ref, counts_ref, p_all, s_p, r_p)
        every = [rounds(a) for a in (1, 2)]
        steps = [step for same in zip(*every) for step in same]
        plan = spread_steps(steps, 0, slots * (width // 128))
    else:
        (w_ref,) = raw
    diag_ref = refs[-1]
    def now(i):
        for slot, steps in plan.items():
            if slot % slots == i:
                @pl.when(j == slot // slots)
                def _():
                    for step in steps:
                        step()
    def assemble():
        for i in range(width // 128):
            for n, ref in enumerate((q_ref, k_ref, v_ref)):
                put_columns(shards[0], 384 * i + 128 * n, ref[:, 128 * i : 128 * i + 128])
        put_columns(shards[0], 3 * width, o_ref[...])
        put_columns(shards[0], 4 * width, p_ref[...])
        gains = jnp.concatenate([g[...].astype(F32) for g in g_refs], axis=0)
        put_columns(shards[0], 4 * width + p_ref.shape[1], turned(gains)[: q_ref.shape[0]])
    def assemble_rest():
        picks_ref[...] = turned(raw_picks[...])[: picks_ref.shape[0]].astype(jnp.int32)
        size = FF_BLOCK
        for i in range(gate_ref.shape[1] // size):
            put_columns(shards[1], 2 * size * i, gate_ref[:, size * i : size * i + size])
            put_columns(shards[1], 2 * size * i + size, up_ref[:, size * i : size * i + size])
        put_columns(shards[2], 0, down_ref[...])
    @pl.when(j == 0)
    def _():
        if beside:
            begin(assemble)
            assemble_rest()
            first(0)
            begin_picks()
            begin_rest()
        table = padded_tile(rel_ref[...])[: diag_ref.shape[0]].astype(BF)
        diag_ref[...] = dot(table, diagonal_hot(doc_len, 128).astype(BF))
        rows_ref[0 : docs_ref.shape[0], :] = docs_ref[...]
        rows_ref[docs_ref.shape[0] :, :] = queries_ref[...]
        if beside:
            steps = rounds(0)
            for n, step in enumerate(steps):
                if n == len(steps) - 3:
                    first(1)
                    first(2)
                for piece in pieces[len(pieces) * n // len(steps) : len(pieces) * (n + 1) // len(steps)]:
                    piece()
                step()
            finish_one(0)
            loading = pltpu.make_async_copy(outs[0], w_ref, load)
            loading.start()
            loading.wait()
        gains_ref[...] = w_ref[:, w_ref.shape[1] - 128 :].astype(F32).T[0:8]
        for c in chunks_of(total, 4):
            x = rows_ref[c, :].astype(F32)
            normed_ref[c, :] = (x * inverse_rms(x) * gains_ref[0:1, :]).astype(BF)
    w_now = w_ref[:, pl.ds(pl.multiple_of(j * 384, 128), 384)]
    for c in chunks_of(total, 4):
        qkv_ref[c, :] = dot(normed_ref[c, :], w_now).astype(BF)
    for h in range(2):
        wide = jnp.broadcast_to(diag_ref[pl.ds(2 * j + h, 1), :], (128, span))
        table_ref[h] = pltpu.roll(wide, 0, 1, stride=1, stride_axis=0)[:, : span - 128]
    lane = lax.broadcasted_iota(jnp.int32, (1, 128), 1)
    kept = {}
    def turned_v(rows, v2):
        if rows not in kept:
            kept[rows] = v2.astype(F32).T.astype(BF)
        return kept[rows]
    def part(rows, keys, q_at, q_len, mask):
        q2 = qkv_ref[pl.ds(rows + q_at, q_len), 0:128]
        k2 = qkv_ref[pl.ds(rows, keys), 128:256]
        v2 = qkv_ref[pl.ds(rows, keys), 256:384]
        v2t = turned_v(rows, v2)
        outs = []
        for h in range(2):
            qm = jnp.where((lane < hd) == (h == 0), q2, jnp.zeros_like(q2))
            s = dot_nt(k2, qm) + tiles_of(table_ref.at[h], keys, q_at, q_len, doc_len)
            if mask is not None:
                s = jnp.where(live_tile(lengths_ref, mask, slot_count), s, mask_fill)
            top = jnp.max(s, axis=0, keepdims=True)
            e = jnp.exp(s - top)
            total = jnp.sum(e, axis=0, keepdims=True)
            p = e.astype(BF)
            lse_ref[0, h : h + 1, pl.ds(rows + q_at, q_len)] = top + jnp.log(total)
            outs.append(dot(v2t[h * hd : (h + 1) * hd], p) * (1.0 / total))
        ctx_ref[pl.ds(rows + q_at, q_len), :] = jnp.concatenate(outs, axis=0).T.astype(BF)
    for i, place in enumerate(places):
        now(i)
        part(*place)
    if beside:
        @pl.when(j == pl.num_programs(0) - 1)
        def _():
            finish_one(1)
            finish_one(2)
            finish_picks()


def attend(docs, queries, rel, lengths, slots, doc_len, doc_count, weights, picks, w_one, zc, n_dev):
    width = docs.shape[1]
    total = docs.shape[0] + queries.shape[0]
    pairs = width // 128
    span = 2 * doc_len
    once = pl.Buffered(1)
    whole = pl.BlockSpec(memory_space=pltpu.VMEM)
    fixed = lambda shape: pl.BlockSpec(shape, lambda j: (0, 0), pipeline_mode=once)
    extra_in, extra_out, extra_specs, scratch, remote = [w_one], [], [], [], {}
    if zc:
        peers = 2 * zc
        dma = pltpu.SemaphoreType.DMA
        one, (gate, up, down) = weights[:5], weights[8:]
        turned_picks = picks.shape[::-1]
        shapes = [(one[0].shape[0], sum(w.shape[1] for w in one) + 128), (gate.shape[0], 2 * gate.shape[1]), down.shape]
        extra_in = [*weights, picks]
        extra_out = [jax.ShapeDtypeStruct((r * n_dev, c), BF) for r, c in shapes]
        extra_out += [jax.ShapeDtypeStruct((peers, doc_len, picks.shape[0]), BF)]
        extra_specs = [pl.BlockSpec(memory_space=pl.ANY)] * 3 + [whole]
        scratch = [pltpu.VMEM((r + -r % 16, c), BF) for r, c in shapes]
        scratch += [pltpu.VMEM(extra_out[0].shape, BF), dma, pltpu.VMEM(turned_picks, jnp.int32), pltpu.VMEM((peers,) + turned_picks, jnp.int32), dma((peers,)), dma((peers,))]
        scratch += gather_scratch(shapes, zc)
        remote = dict(collective_id=3, has_side_effects=True)
    return pl.pallas_call(
        functools.partial(attend_kernel, doc_len, doc_count, doc_len, zc, slots),
        grid=(pairs,),
        in_specs=[
            fixed(docs.shape), fixed(queries.shape),
            fixed(rel.shape), pl.BlockSpec(memory_space=pltpu.SMEM),
        ] + [whole] * len(extra_in),
        out_specs=[
            fixed((total, width)), fixed((8, width)), fixed((total, width)),
            pl.BlockSpec((total, 384), lambda j: (0, j)),
            pl.BlockSpec((total, 128), lambda j: (0, j)),
            pl.BlockSpec((1, 8, total), lambda j: (j, 0, 0)),
            pl.BlockSpec((2, 128, span - 128), lambda j: (j, 0, 0)),
        ] + extra_specs,
        out_shape=[
            jax.ShapeDtypeStruct((total, width), BF),
            jax.ShapeDtypeStruct((8, width), F32),
            jax.ShapeDtypeStruct((total, width), BF),
            jax.ShapeDtypeStruct((total, pairs * 384), BF),
            jax.ShapeDtypeStruct((total, width), BF),
            jax.ShapeDtypeStruct((pairs, 8, total), F32),
            jax.ShapeDtypeStruct((pairs * 2, 128, span - 128), F32),
        ] + extra_out,
        scratch_shapes=scratch + [pltpu.VMEM((2 * pairs + -2 * pairs % 16, span), F32)],
        compiler_params=pltpu.CompilerParams(vmem_limit_bytes=VMEM_ALL, **remote),
        name="attend",
    )(docs, queries, rel, lengths, *extra_in)


BACK_SHARES = (0.0, 0.27, 0.48, 0.7, 0.88)


def attend_back_step(doc_len, doc_count, block, slot_count, bucket_count, pairs, now, qkv_ref, do_ref, lse_ref, table_ref, lengths_ref,
                     normed_ref, wg_ref, packed_ref, dqkv_ref, acc, normed_t, diag_ref):
    j = pl.program_id(0)
    span = 2 * doc_len
    hd = 64
    rest = qkv_ref.shape[0] - doc_count * doc_len
    @pl.when(j == 0)
    def _():
        normed_t[...] = normed_ref[...].T
    acc[...] = jnp.zeros_like(acc)
    lane = lax.broadcasted_iota(jnp.int32, (1, 128), 1)
    def part(rows, keys, q_len, mask):
        k2 = qkv_ref[pl.ds(rows, keys), 128:256]
        v2 = qkv_ref[pl.ds(rows, keys), 256:384]
        k2t = k2.astype(F32).T.astype(BF)
        dk = jnp.zeros((keys, 128), F32)
        dv = jnp.zeros((keys, 128), F32)
        for q_at in range(0, keys, q_len):
            now()
            qr = pl.ds(rows + q_at, q_len)
            q2 = qkv_ref[qr, 0:128]
            do2 = do_ref[qr, :]
            outs = []
            for h in range(2):
                mine = (lane < hd) == (h == 0)
                qm = jnp.where(mine, q2, jnp.zeros_like(q2))
                dom = jnp.where(mine, do2, jnp.zeros_like(do2))
                s = dot_nt(k2, qm) + tiles_of(table_ref.at[h], keys, q_at, q_len, doc_len)
                if mask is not None:
                    s = jnp.where(live_tile(lengths_ref, mask, slot_count), s, mask_fill)
                p = jnp.exp(s - lse_ref[0, h : h + 1, qr])
                dp = dot_nt(v2, dom)
                ds = p * (dp - jnp.sum(p * dp, axis=0, keepdims=True))
                for kb in range(keys // 128):
                    at = doc_len - 128 - 128 * kb + q_at
                    acc[h, :, at : at + q_len] += ds[128 * kb : 128 * (kb + 1)]
                low = ds.astype(BF)
                dv += dot(p.astype(BF), dom)
                dk += dot(low, qm)
                outs.append(dot(k2t[h * hd : (h + 1) * hd], low))
            dqkv_ref[qr, 0:128] = jnp.concatenate(outs, axis=0).T.astype(BF)
        dqkv_ref[pl.ds(rows, keys), 128:256] = dk.astype(BF)
        dqkv_ref[pl.ds(rows, keys), 256:384] = dv.astype(BF)
    for m in range(doc_count):
        part(m * doc_len, doc_len, block, None)
    for i in range(rest // 128):
        part(doc_count * doc_len + 128 * i, 128, 128, i)
    for h in range(2):
        eight = acc[h, 0:8]
        for g in range(1, 16):
            eight = eight + pltpu.roll(acc[h, 8 * g : 8 * g + 8], span - 8 * g, 1)
        one = eight[0:1]
        for r in range(1, 8):
            one = one + pltpu.roll(eight, span - r, 1)[r : r + 1]
        diag_ref[pl.ds(2 * j + h, 1), :] = one
    wg_ref[...] = dot(normed_t[...], dqkv_ref[...]).astype(BF)
    @pl.when(j == pairs - 1)
    def _():
        hot = diagonal_hot(doc_len, bucket_count)
        table = lax.dot_general(
            diag_ref[...], hot, (((1,), (1,)), ((), ())), precision=lax.Precision.HIGHEST, preferred_element_type=F32
        )
        pieces = [table[8 * i : 8 * i + 8] for i in range(table.shape[0] // 8)]
        spare = jnp.zeros((8, packed_ref.shape[1] - bucket_count * len(pieces)), F32)
        packed_ref[...] = jnp.concatenate([*pieces, spare], axis=1)

def attend_back_kernel(doc_len, doc_count, slot_count, bucket_count, pairs, *refs):
    attend_back_step(doc_len, doc_count, 256, slot_count, bucket_count, pairs, lambda: None, *refs)


def back_kernel(doc_len, doc_count, slot_count, bucket_count, pairs, zc, count, qkv_ref, do_ref, lse_ref, table_ref, lengths_ref,
                normed_ref, w_ref, rows_ref, dh_ref, gains_ref, *refs):
    grads = refs[:count]
    dx_ref = refs[count]
    outs = refs[count + 1 : 2 * count + 2]
    table_out = refs[2 * count + 2]
    acc, normed_t, diag_ref, packed_ref, dqkv_all, wg_all = refs[2 * count + 3 : 2 * count + 9]
    table_refs = refs[2 * count + 9 : 2 * count + 18]
    pos, begin, groups_of, finish = reduce_events(zc, [*grads, wg_all], outs, refs[2 * count + 18 :])
    table_begin, table_cores, table_ring, table_line = table_events(pos, packed_ref, table_out, table_refs)
    j = pl.program_id(0)
    total = qkv_ref.shape[0]
    rest = total - doc_count * doc_len
    block = 256
    slots = doc_count * (doc_len // block) + rest // 128
    groups = groups_of(range(count))
    plan = {}
    for group, share in zip(groups, BACK_SHARES):
        for n, step in enumerate(group):
            at = min(slots * pairs - 1, int(share * slots * pairs) + n // 4)
            plan.setdefault(at, []).append(step)
    slot = [0]
    def now():
        for at, steps in plan.items():
            if at % slots == slot[0]:
                @pl.when(j == at // slots)
                def _():
                    for step in steps:
                        step()
        slot[0] += 1
    @pl.when(j == 0)
    def _():
        enter(pos, opp=True)
        begin(range(count))
    @pl.when(j < pairs)
    def _():
        here = pl.ds(pl.multiple_of(j * 384, 128), 384)
        attend_back_step(
            doc_len, doc_count, block, slot_count, bucket_count, pairs, now, qkv_ref, do_ref, lse_ref, table_ref, lengths_ref,
            normed_ref, wg_all.at[:, here], packed_ref, dqkv_all.at[:, here], acc, normed_t, diag_ref,
        )
    late = groups[len(BACK_SHARES) :]
    last = groups_of([count])
    blocks = total // ROW_BLOCK
    end = blocks - 1
    after = {}
    @pl.when(j == pairs)
    def _():
        begin([count])
        table_begin()
    def put(at, steps):
        after.setdefault(min(at, end), []).extend(steps)
    for n, group in enumerate(late[:-1]):
        put(n, group)
    put(1, last[0])
    put(2, [table_cores])
    put(3, last[1])
    put(4, late[-1])
    put(5, last[2] + [table_ring])
    put(7, last[3])
    put(end, last[4] + last[5] + [table_line, finish])
    @pl.when(j >= pairs)
    def _():
        at = pl.multiple_of((j - pairs) * ROW_BLOCK, ROW_BLOCK)
        input_grad(dqkv_all.at[pl.ds(at, ROW_BLOCK), :], w_ref, rows_ref, dh_ref, gains_ref, dx_ref)
    for n, steps in sorted(after.items()):
        @pl.when(j == pairs + n)
        def _():
            for step in steps:
                step()


def back_specs(total, width, span, pairs):
    index = lambda j: jnp.minimum(j, pairs - 1)
    return [
        pl.BlockSpec((total, 384), lambda j: (0, index(j))),
        pl.BlockSpec((total, 128), lambda j: (0, index(j))),
        pl.BlockSpec((1, 8, total), lambda j: (index(j), 0, 0)),
        pl.BlockSpec((2, 128, span - 128), lambda j: (index(j), 0, 0)),
        pl.BlockSpec(memory_space=pltpu.SMEM),
        pl.BlockSpec((total, width), lambda j: (0, 0), pipeline_mode=pl.Buffered(1)),
    ]


def back_scratch(total, width, span, pairs):
    return [pltpu.VMEM((2, 128, span), F32), pltpu.VMEM((width, total), BF), pltpu.VMEM((2 * pairs + -2 * pairs % 16, span), F32)]


def attend_back(qkv, d_ctx, lse, table, lengths, slots, bucket_count, normed, doc_len, doc_count):
    total, width = normed.shape
    pairs = width // 128
    span = 2 * doc_len
    return pl.pallas_call(
        functools.partial(attend_back_kernel, doc_len, doc_count, slots, bucket_count, pairs),
        grid=(pairs,),
        in_specs=back_specs(total, width, span, pairs),
        out_specs=[
            pl.BlockSpec((width, 384), lambda j: (0, j)),
            pl.BlockSpec((8, 128), lambda j: (0, 0)),
            pl.BlockSpec((total, 384), lambda j: (0, j)),
        ],
        out_shape=[
            jax.ShapeDtypeStruct((width, 3 * width), BF),
            jax.ShapeDtypeStruct((8, 128), F32),
            jax.ShapeDtypeStruct((total, 3 * width), BF),
        ],
        scratch_shapes=back_scratch(total, width, span, pairs),
        compiler_params=pltpu.CompilerParams(vmem_limit_bytes=VMEM_ALL),
        name="attend_back",
    )(qkv, d_ctx, lse, table, lengths, normed)


def back(qkv, d_ctx, lse, table, lengths, slots, bucket_count, normed, w_one, rows, d_hidden, gains, doc_len, doc_count, grads, zc, n_dev):
    total, width = normed.shape
    pairs = width // 128
    span = 2 * doc_len
    count = len(grads)
    once = pl.Buffered(1)
    whole = pl.BlockSpec(memory_space=pltpu.VMEM)
    rows_block = pl.BlockSpec((ROW_BLOCK, width), lambda j: (jnp.maximum(j - pairs, 0), 0))
    all_grads = [*grads, jax.ShapeDtypeStruct((width, 3 * width), BF)]
    shapes = reduce_shapes(all_grads, n_dev) + [jax.ShapeDtypeStruct((8, 128), F32)]
    return pl.pallas_call(
        functools.partial(back_kernel, doc_len, doc_count, slots, bucket_count, pairs, zc, count),
        grid=(pairs + total // ROW_BLOCK,),
        in_specs=back_specs(total, width, span, pairs) + [
            pl.BlockSpec((width, 3 * width), lambda j: (0, 0), pipeline_mode=once),
            rows_block, rows_block,
            pl.BlockSpec(gains.shape, lambda j: (0, 0)),
        ] + [pl.BlockSpec(memory_space=pl.ANY)] * count,
        out_specs=[rows_block] + [whole] * len(shapes),
        out_shape=[jax.ShapeDtypeStruct((total, width), F32)] + shapes,
        scratch_shapes=back_scratch(total, width, span, pairs)
        + [pltpu.VMEM((8, 128), F32), pltpu.VMEM((total, 3 * width), BF), pltpu.VMEM((width, 3 * width), BF)]
        + table_scratch((8, 128), zc) + reduce_scratch(all_grads, zc),
        compiler_params=pltpu.CompilerParams(collective_id=4, has_side_effects=True, vmem_limit_bytes=VMEM_ALL),
        name="back",
    )(qkv, d_ctx, lse, table, lengths, normed, w_one, rows, d_hidden, gains, *grads)


def columns_of(rows):
    n = rows[0].shape[1]
    return jnp.concatenate([*rows, jnp.zeros((128 - len(rows), n), F32)], axis=0).T


def pair_columns(w):
    q, k, v = w
    rows, width = q.shape
    pack = jnp.stack([x.reshape(rows, width // 128, 128) for x in (q, k, v)], axis=2)
    return pack.reshape(rows, 3 * width)


def score_kernel(peers, doc_len, slots, emb_ref, picks_ref, counts_ref, lengths_ref, goals_ref, loss_ref, d_emb_ref,
                 q_own, q_all, q_two, d_raw, weighed, totals, pool_out, pool_in, grad_out, grad_in, dq_out, dq_in, docs_t, d_docs,
                 s_q, r_q, s_pool, r_pool, s_grad, r_grad, s_dq, r_dq):
    dp = lax.axis_index("dp"); me = lax.axis_index("wide")
    tokens = q_own.shape[0]
    feat = emb_ref.shape[1]
    half = tokens // 2
    scale = feat ** -0.5
    barrier = pltpu.get_barrier_semaphore()
    def other(k):
        return lax.rem(me + k, peers)
    def each(fn):
        @pl.loop(1, peers)
        def _(k):
            fn(other(k))
    each(lambda o: pl.semaphore_signal(barrier, inc=1, device_id=(dp, o), device_id_type=MESH))
    q_own[...] = emb_ref[2 * doc_len :, :]
    q_all[me] = q_own[...]
    pl.semaphore_wait(barrier, peers - 1)
    def send(src, dst, ss, rs, o):
        return pltpu.make_async_remote_copy(src_ref=src, dst_ref=dst, send_sem=ss, recv_sem=rs, device_id=(dp, o), device_id_type=MESH)
    def q_to(o): return send(q_own, q_all.at[me], s_q.at[o], r_q.at[me], o)
    def q_from(o): return send(q_own, q_all.at[o], s_q.at[o], r_q.at[o], o)
    def pool_to(o): return send(pool_out.at[o], pool_in.at[me], s_pool.at[o], r_pool.at[me], o)
    def pool_from(o): return send(pool_out.at[o], pool_in.at[o], s_pool.at[o], r_pool.at[o], o)
    def grad_to(o): return send(grad_out.at[o], grad_in.at[me], s_grad.at[o], r_grad.at[me], o)
    def grad_from(o): return send(grad_out.at[o], grad_in.at[o], s_grad.at[o], r_grad.at[o], o)
    def dq_to(o): return send(dq_out.at[o], dq_in.at[me], s_dq.at[o], r_dq.at[me], o)
    def dq_from(o): return send(dq_out.at[o], dq_in.at[o], s_dq.at[o], r_dq.at[o], o)
    def started(o):
        q_to(o).start()
    each(started)
    docs2 = jnp.concatenate([emb_ref[0:doc_len, :], emb_ref[doc_len : 2 * doc_len, :]], axis=1)
    docs_t[...] = docs2.astype(F32).T.astype(BF)
    row = lax.broadcasted_iota(jnp.int32, (tokens, 1), 0)
    lane = lax.broadcasted_iota(jnp.int32, (1, tokens), 1)
    group = min(8, peers)
    groups = range(peers // group)
    def members(n):
        return [(n * group + i, slice(i * tokens, (i + 1) * tokens)) for i in range(group)]
    def forward(n):
        for o, at in members(n):
            q = q_all[o]
            none = jnp.zeros_like(q)
            q_two[n, at, :] = jnp.concatenate([jnp.where(row < half, q, none), jnp.where(row < half, none, q)], axis=1)
        s = lax.dot_general(docs2, q_two[n], (((1,), (1,)), ((), ())), preferred_element_type=F32) * scale
        for o, at in members(n):
            multiple = counts_ref[o].astype(F32)
            w = multiple * jnp.exp(s[:, at])
            weighed[o] = w
            found = jnp.sum(multiple, axis=0, keepdims=True)
            weight = jnp.sum(w, axis=0, keepdims=True) + (found == 0).astype(F32)
            totals[o] = jnp.broadcast_to(weight, (8, tokens))
            pool_out[o] = jnp.broadcast_to(jnp.log(weight), (8, tokens))
    each(lambda o: q_from(o).wait_recv())
    for n in groups:
        forward(n)
    pool_in[me] = pool_out[me]
    each(lambda o: pool_to(o).start())
    each(lambda o: pool_from(o).wait_recv())
    pooled = pool_in[:, 0, :]
    mine = turned(picks_ref[...])[: picks_ref.shape[1]].astype(jnp.int32)
    hits = []
    for w in range(peers):
        inside = ((mine >= w * doc_len) & (mine < (w + 1) * doc_len)).astype(F32)
        hits.append(jnp.max(inside, axis=0, keepdims=True))
    hit = jnp.concatenate(hits, axis=0)
    live = (lax.rem(lane, slots) < per_token(lengths_ref, 0, lane.shape, 1, slots)).astype(F32)
    own_row = lax.broadcasted_iota(jnp.int32, (tokens, tokens), 0) // slots
    own_col = lax.broadcasted_iota(jnp.int32, (tokens, tokens), 1) // slots
    same = (own_row == own_col).astype(F32)
    def per_query(v):
        return jnp.dot(v, same, precision=lax.Precision.HIGHEST, preferred_element_type=F32)
    divisor = jnp.maximum(per_query(hit * live), 1.0)
    logits = score_scale * per_query(pooled * live) / divisor
    top = jnp.max(logits, axis=0, keepdims=True)
    shifted = jnp.exp(logits - top)
    total = jnp.sum(shifted, axis=0, keepdims=True)
    doc_id = lax.broadcasted_iota(jnp.int32, (peers, tokens), 0)
    chosen = (doc_id == per_token(goals_ref, 0, lane.shape, 1, slots)).astype(F32)
    loss = top + jnp.log(total) - jnp.sum(chosen * logits, axis=0, keepdims=True)
    queries = tokens // slots
    chosen_lane = (lax.broadcasted_iota(jnp.int32, (tokens, 128), 0) == lax.broadcasted_iota(jnp.int32, (tokens, 128), 1) * slots).astype(F32)
    apart_loss = jnp.dot(loss, chosen_lane, precision=lax.Precision.HIGHEST, preferred_element_type=F32)
    per = loss_ref.shape[1]
    for i in range(queries // per):
        loss_ref[i : i + 1, :] = apart_loss[:, i * per : (i + 1) * per]
    d_pooled = score_scale * (shifted / total - chosen) / divisor * live
    for w in range(peers):
        grad_out[w] = jnp.broadcast_to(d_pooled[w : w + 1], (8, tokens))
    each(lambda o: grad_to(o).start())
    grad_in[me] = grad_out[me]
    each(lambda o: grad_from(o).wait_recv())
    for n in groups:
        for o, at in members(n):
            factor = grad_in[o][0:1] / totals[o][0:1] * scale
            d_raw[n, :, at] = (weighed[o] * factor).astype(BF)
        both = jnp.dot(docs_t[...], d_raw[n], preferred_element_type=F32)
        for o, at in members(n):
            d_q = jnp.where(lane < half, both[0:feat, at], both[feat : 2 * feat, at])
            dq_out[o] = d_q.T.astype(BF)
    each(lambda o: dq_to(o).start())
    for n in groups:
        part = jnp.dot(d_raw[n], q_two[n], preferred_element_type=F32)
        d_docs[...] = part if n == 0 else d_docs[...] + part
    d_emb_ref[0:doc_len, :] = d_docs[:, 0:feat].astype(BF)
    d_emb_ref[doc_len : 2 * doc_len, :] = d_docs[:, feat : 2 * feat].astype(BF)
    dq_in[me] = dq_out[me]
    each(lambda o: dq_from(o).wait_recv())
    total_q = dq_in[0].astype(F32)
    for w in range(1, peers):
        total_q = total_q + dq_in[w].astype(F32)
    d_emb_ref[2 * doc_len :, :] = total_q.astype(BF)
    def sent(o):
        q_to(o).wait_send(); pool_to(o).wait_send(); grad_to(o).wait_send(); dq_to(o).wait_send()
    each(sent)

def score(emb, picks, counts, lengths, goals, loss_shape, doc_len, slots, peers):
    tokens = picks.shape[0]
    feat = emb.shape[1]
    group = min(8, peers)
    V = pltpu.VMEM
    dma = pltpu.SemaphoreType.DMA
    return pl.pallas_call(
        functools.partial(score_kernel, peers, doc_len, slots),
        out_shape=[jax.ShapeDtypeStruct(loss_shape, F32), jax.ShapeDtypeStruct(emb.shape, BF)],
        in_specs=[pl.BlockSpec(memory_space=pltpu.VMEM)] * 3 + [pl.BlockSpec(memory_space=pltpu.SMEM)] * 2,
        out_specs=[pl.BlockSpec(memory_space=pltpu.VMEM)] * 2,
        scratch_shapes=[
            V((tokens, feat), BF), V((peers, tokens, feat), BF),
            V((peers // group, group * tokens, 2 * feat), BF), V((peers // group, doc_len, group * tokens), BF),
            V((peers, doc_len, tokens), F32), V((peers, 8, tokens), F32),
            V((peers, 8, tokens), F32), V((peers, 8, tokens), F32), V((peers, 8, tokens), F32), V((peers, 8, tokens), F32),
            V((peers, tokens, feat), BF), V((peers, tokens, feat), BF), V((2 * feat, doc_len), BF), V((doc_len, 2 * feat), F32),
        ] + [dma((peers,))] * 8,
        compiler_params=pltpu.CompilerParams(collective_id=2, has_side_effects=True, vmem_limit_bytes=VMEM_ALL),
        name="score",
    )(emb, picks, counts, lengths, goals)


GELU_SCALE = 0.7978845608028654
GELU_CUBE = 0.044715

def dot(a, b):
    return jnp.dot(a, b, preferred_element_type=F32)

def dot_nt(a, b):
    return lax.dot_general(a, b, (((1,), (1,)), ((), ())), preferred_element_type=F32)

def dot_tn(a, b):
    return lax.dot_general(a, b, (((0,), (0,)), ((), ())), preferred_element_type=F32)

def inverse_rms(v):
    return lax.rsqrt(jnp.mean(v * v, axis=-1, keepdims=True) + eps_norm)

def chunks_of(total, parts):
    size = total // parts
    return [slice(i * size, (i + 1) * size) for i in range(parts)]

def ffn_kernel(parts, rows_ref, ctx_ref, wo_ref, wgu_ref, wd_ref, wp_ref, gains_ref, n2_ref, gu_ref, scale_ref, ne_ref, emb_ref, lo_ref):
    j = pl.program_id(0)
    block = wd_ref.shape[0]
    chunks = chunks_of(rows_ref.shape[0], parts)
    @pl.when(j == 0)
    def _():
        for c in chunks:
            h = rows_ref[c, :].astype(F32) + dot(ctx_ref[c, :], wo_ref[...])
            lo_ref[c, :] = h
            inv = inverse_rms(h)
            scale_ref[c, :] = jnp.broadcast_to(inv, scale_ref[c, :].shape)
            n2_ref[c, :] = (h * inv * gains_ref[1:2, :]).astype(BF)
    gus = [dot(n2_ref[c, :], wgu_ref[...]) for c in chunks]
    for c, gu in zip(chunks, gus):
        gu_ref[c, :] = gu.astype(BF)
        g = gu[:, :block]
        t = jnp.tanh(GELU_SCALE * (g + GELU_CUBE * (g * g * g)))
        act = (0.5 * g * (1.0 + t)) * gu[:, block:]
        lo_ref[c, :] += dot(act.astype(BF), wd_ref[...])
    @pl.when(j == pl.num_programs(0) - 1)
    def _():
        for c in chunks:
            lo = lo_ref[c, :]
            inv = inverse_rms(lo)
            lane = lax.broadcasted_iota(jnp.int32, (1, scale_ref.shape[1]), 1)
            scale_ref[c, :] = jnp.where(lane < 64, scale_ref[c, :], inv)
            ne = (lo * inv * gains_ref[2:3, :]).astype(BF)
            ne_ref[c, :] = ne
            emb_ref[c, :] = dot(ne, wp_ref[...]).astype(BF)

def ffn(rows, ctx, w_one, w_gu, w_down, gains, p_size, block):
    total, width = rows.shape
    ff = w_down.shape[0]
    once = pl.Buffered(1)
    full = lambda cols, at=0: pl.BlockSpec((total, cols), lambda j: (0, 0), pipeline_mode=once)
    return pl.pallas_call(
        functools.partial(ffn_kernel, 4),
        grid=(ff // block,),
        in_specs=[
            full(width), full(width),
            pl.BlockSpec((width, width), lambda j: (0, 3), pipeline_mode=once),
            pl.BlockSpec((width, 2 * block), lambda j: (0, j)),
            pl.BlockSpec((block, width), lambda j: (j, 0)),
            pl.BlockSpec((width, p_size), lambda j: (0, 4 * width // p_size), pipeline_mode=once),
            pl.BlockSpec(gains.shape, lambda j: (0, 0)),
        ],
        out_specs=[full(width), pl.BlockSpec((total, 2 * block), lambda j: (0, j)), full(128), full(width), full(p_size)],
        out_shape=[
            jax.ShapeDtypeStruct((total, width), BF), jax.ShapeDtypeStruct((total, 2 * ff), BF),
            jax.ShapeDtypeStruct((total, 128), F32), jax.ShapeDtypeStruct((total, width), BF),
            jax.ShapeDtypeStruct((total, p_size), BF),
        ],
        scratch_shapes=[pltpu.VMEM((total, width), F32)],
        compiler_params=pltpu.CompilerParams(vmem_limit_bytes=VMEM_ALL),
        name="feed_forward",
    )(rows, ctx, w_one, w_gu, w_down, w_one, gains)

def rms_pull_normed(normed, inv, gain, upstream):
    unit = normed.astype(F32) / gain
    scaled = upstream * gain
    d_gain = jnp.sum(upstream * unit, axis=0, keepdims=True)
    inner = jnp.mean(scaled * unit, axis=-1, keepdims=True)
    return inv * (scaled - unit * inner), d_gain


def rms_pull(v, gain, upstream):
    inv = inverse_rms(v)
    scaled = upstream * gain
    d_gain = jnp.sum(upstream * (v * inv), axis=0, keepdims=True)
    inner = jnp.mean(scaled * v, axis=-1, keepdims=True)
    return inv * scaled - v * (inv * inv * inv * inner), d_gain

def ffn_back_kernel(parts, de_ref, scale_ref, ne_ref, n2_ref, ctx_ref, wo_ref, wp_ref, gains_ref, gu_ref, wgu_ref, wd_ref,
                    dgu_w_ref, dd_w_ref, last_ref, dh_ref, dctx_ref, dgain_ref, dl_ref, low_ref, n2t_ref, acc_ref, dhl_ref):
    j = pl.program_id(0)
    block = wd_ref.shape[0]
    chunks = chunks_of(ne_ref.shape[0], parts)
    @pl.when(j == 0)
    def _():
        dgain_ref[...] = jnp.zeros_like(dgain_ref)
        for c in chunks:
            up = dot_nt(de_ref[c, :], wp_ref[...])
            dl, dg = rms_pull_normed(ne_ref[c, :], scale_ref[c, 64:65], gains_ref[2:3, :], up)
            dl_ref[c, :] = dl
            low_ref[c, :] = dl.astype(BF)
            dgain_ref[2:3, :] += dg
        width = ne_ref.shape[1]
        last_ref[:, width : width + de_ref.shape[1]] = dot_tn(ne_ref[...], de_ref[...]).astype(BF)
        n2t_ref[...] = n2_ref[...].T
        acc_ref[...] = jnp.zeros_like(acc_ref)
    acts, dgus = [], []
    das = [dot_nt(low_ref[c, :], wd_ref[...]) for c in chunks]
    for c, da in zip(chunks, das):
        g = gu_ref[c, :block].astype(F32)
        u = gu_ref[c, block:].astype(F32)
        t = jnp.tanh(GELU_SCALE * (g + GELU_CUBE * (g * g * g)))
        cdf = 0.5 * (1.0 + t)
        gel = g * cdf
        acts.append((gel * u).astype(BF))
        slope = cdf + (0.5 * GELU_SCALE) * g * (1.0 - t * t) * (1.0 + (3.0 * GELU_CUBE) * (g * g))
        dgu = jnp.concatenate([(da * u * slope).astype(BF), (da * gel).astype(BF)], axis=1)
        dgus.append(dgu)
    for c, dgu in zip(chunks, dgus):
        acc_ref[c, :] += dot_nt(dgu, wgu_ref[...])
    dgu_w_ref[...] = dot(n2t_ref[...], jnp.concatenate(dgus, axis=0)).astype(BF)
    dd_w_ref[...] = dot_tn(jnp.concatenate(acts, axis=0), low_ref[...]).astype(BF)
    @pl.when(j == pl.num_programs(0) - 1)
    def _():
        for c in chunks:
            dv, dg = rms_pull_normed(n2_ref[c, :], scale_ref[c, 0:1], gains_ref[1:2, :], acc_ref[c, :])
            dh = dl_ref[c, :] + dv
            dh_ref[c, :] = dh
            dhl = dh.astype(BF)
            dhl_ref[c, :] = dhl
            dgain_ref[1:2, :] += dg
            dctx_ref[c, :] = dot_nt(dhl, wo_ref[...]).astype(BF)
        width = ne_ref.shape[1]
        last_ref[:, :width] = dot_tn(ctx_ref[...], dhl_ref[...]).astype(BF)
        last_ref[:, width + de_ref.shape[1] :] = columns_of([dgain_ref[i : i + 1, :] for i in range(3)]).astype(BF)

def ffn_back(d_emb, scale, ne, n2, ctx, w_one, w_gu, w_down, gains, gu, p_size, block):
    total, width = ne.shape
    ff = w_down.shape[0]
    once = pl.Buffered(1)
    full = lambda cols: pl.BlockSpec((total, cols), lambda j: (0, 0), pipeline_mode=once)
    fixed = lambda shape: pl.BlockSpec(shape, lambda j: (0, 0), pipeline_mode=once)
    V = pltpu.VMEM
    return pl.pallas_call(
        functools.partial(ffn_back_kernel, 4),
        grid=(ff // block,),
        in_specs=[
            full(p_size), full(128), full(width), full(width), full(width),
            pl.BlockSpec((width, width), lambda j: (0, 3), pipeline_mode=once),
            pl.BlockSpec((width, p_size), lambda j: (0, 4 * width // p_size), pipeline_mode=once),
            fixed(gains.shape),
            pl.BlockSpec((total, 2 * block), lambda j: (0, j)),
            pl.BlockSpec((width, 2 * block), lambda j: (0, j)),
            pl.BlockSpec((block, width), lambda j: (j, 0)),
        ],
        out_specs=[
            pl.BlockSpec((width, 2 * block), lambda j: (0, j)),
            pl.BlockSpec((block, width), lambda j: (j, 0)),
            fixed((width, width + p_size + 128)), full(width), full(width),
        ],
        out_shape=[
            jax.ShapeDtypeStruct((width, 2 * ff), BF), jax.ShapeDtypeStruct((ff, width), BF),
            jax.ShapeDtypeStruct((width, width + p_size + 128), BF),
            jax.ShapeDtypeStruct((total, width), F32), jax.ShapeDtypeStruct((total, width), BF),
        ],
        scratch_shapes=[V((8, width), F32), V((total, width), F32), V((total, width), BF), V((width, total), BF), V((total, width), F32), V((total, width), BF)],
        compiler_params=pltpu.CompilerParams(vmem_limit_bytes=VMEM_ALL),
        name="feed_forward_back",
    )(d_emb, scale, ne, n2, ctx, w_one, w_one, gains, gu, w_gu, w_down)

def gate_up_columns(gate, up, block):
    rows, ff = gate.shape
    return jnp.stack([gate.reshape(rows, -1, block), up.reshape(rows, -1, block)], axis=2).reshape(rows, 2 * ff)


def contract_rows(left_mat, right_mat):
    return lax.dot_general(
        left_mat, right_mat, (((0,), (0,)), ((), ())), preferred_element_type=jnp.float32
    )


def contract_cols(left_mat, right_mat):
    return lax.dot_general(
        left_mat, right_mat, (((1,), (1,)), ((), ())), preferred_element_type=jnp.float32
    )


def matmul(left_mat, right_mat):
    return jnp.dot(left_mat, right_mat, preferred_element_type=jnp.float32)


def rms_forward(values, gain_vec):
    inverse = lax.rsqrt(jnp.mean(values * values, axis=-1, keepdims=True) + eps_norm)
    return (values * inverse * gain_vec, inverse)


def rms_backward(values, inverse, gain_vec, upstream):
    scaled = upstream * gain_vec
    gain_grad = jnp.sum(upstream * values * inverse, axis=0)
    inner_mean = jnp.mean(scaled * values, axis=-1, keepdims=True)
    return (inverse * scaled - values * inverse * inverse * inverse * inner_mean, gain_grad)


def two_level(shards):
    return (
        lax.axis_size("dp") == 4
        and lax.axis_size("wide") % 4 == 0
        and all(s.shape[0] % 8 == 0 for s in shards)
    )


def gathered(shards):
    return [lax.all_gather(s, ("dp", "wide"), axis=0, tiled=True) for s in shards]


def summed(grads, table):
    sums = [lax.psum_scatter(g.astype(F32), ("dp", "wide"), scatter_dimension=0, tiled=True) for g in grads]
    return [*sums, lax.psum(table, ("dp", "wide"))]


def local(
    doc_tokens,
    query_tokens,
    query_lengths,
    retrieved,
    targets,
    q_weight,
    k_weight,
    v_weight,
    o_weight,
    gate_weight,
    up_weight,
    down_weight,
    proj_weight,
    attn_gain,
    ffn_gain,
    final_gain,
    rel_bias,
):
    micro_count, _, doc_len, width = doc_tokens.shape
    slots = query_tokens.shape[2]
    doc_rows = micro_count * doc_len
    wide_count = lax.axis_size("wide")
    p_size = proj_weight.shape[1]
    bucket_count, head_count = rel_bias.shape
    pairs = width // 128
    ff_block = FF_BLOCK
    weights = [q_weight, k_weight, v_weight, o_weight, proj_weight]
    ffn_raw = [gate_weight, up_weight, down_weight]
    beside = two_level(weights + ffn_raw)
    picks = retrieved.reshape(-1, retrieved.shape[3])
    lengths = query_lengths
    n_dev = lax.axis_size("dp") * wide_count
    w_one = None
    if not beside:
        shard_one = jnp.concatenate(
            [pair_columns(weights[:3]), o_weight, proj_weight, jnp.pad(jnp.stack([attn_gain, ffn_gain, final_gain], axis=1), ((0, 0), (0, 125)))], axis=1
        )
        (w_one,) = gathered([shard_one])
    gain_rows = [g.reshape(1, -1) for g in (attn_gain, ffn_gain, final_gain)]
    shards = [*weights, *gain_rows, *ffn_raw] if beside else []
    rows_low, gains, normed, qkv, context, lse, table, *full = attend(
        doc_tokens.reshape(doc_rows, width),
        query_tokens.reshape(-1, width),
        rel_bias.T,
        lengths,
        slots,
        doc_len,
        micro_count,
        shards,
        picks,
        w_one,
        wide_count // 2 if beside else 0,
        n_dev,
    )
    if beside:
        w_one, w_gu, w_down, counts = full
    else:
        w_gu, w_down = gathered([gate_up_columns(gate_weight, up_weight, ff_block), down_weight])
        counts = count_all(picks.T, doc_len, wide_count)
    normed_two, gate_up, scale, normed_end, embedded = ffn(
        rows_low, context, w_one, w_gu, w_down, gains, p_size, ff_block
    )
    losses_out, d_embedded = score(
        embedded, picks, counts, lengths, targets, targets.shape, doc_len, slots, wide_count
    )
    gu_grad, down_grad, last_grad, d_hidden, d_context = ffn_back(
        d_embedded, scale, normed_end, normed_two, context, w_one, w_gu, w_down, gains, gate_up, p_size, ff_block
    )
    ff = down_grad.shape[0]
    ffn_layouts = [
        [[(2 * ff_block * i + at, ff_block) for i in range(ff // ff_block)] for at in (0, ff_block)],
        [[(0, width)]],
    ]
    one_layouts = [
        [[(384 * i + 128 * n, 128) for i in range(pairs)] for n in range(3)],
        [[(0, width)], [(width, p_size)], [(width + p_size, 128)]],
    ]
    back_args = (qkv, d_context, lse, table, lengths, slots, bucket_count, normed)
    if beside:
        d_rows, s_gu, s_down, s_last, s_qkv, s_table = back(
            *back_args,
            w_one,
            rows_low,
            d_hidden,
            gains,
            doc_len,
            micro_count,
            [gu_grad, down_grad, last_grad],
            wide_count // 2,
            n_dev,
        )
    else:
        qkv_grad, packed, d_qkv = attend_back(*back_args, doc_len, micro_count)
        d_rows = input_grads(d_qkv, w_one, rows_low, d_hidden, gains)
        s_qkv, s_last, s_gu, s_down, s_table = summed([qkv_grad, last_grad, gu_grad, down_grad], packed)
    d_docs, d_queries, s_table, g_attn, g_ffn, g_final, s_q, s_k, s_v, s_o, s_proj, _, s_gate, s_up, s_down = apart(
        d_rows,
        s_table,
        gain_rows[0],
        weights[:3],
        [s_qkv, s_last, s_gu, s_down],
        one_layouts + ffn_layouts,
        doc_rows,
        rel_bias.shape[::-1],
    )
    return (
        losses_out,
        d_docs.reshape(doc_tokens.shape),
        d_queries.reshape(query_tokens.shape),
        s_q,
        s_k,
        s_v,
        s_o,
        s_gate,
        s_up,
        s_down,
        s_proj,
        g_attn.reshape(-1),
        g_ffn.reshape(-1),
        g_final.reshape(-1),
        s_table.T,
    )


def solution(mesh):
    placed = (
        P(None, ("dp", "wide"), None, None),
        P(None, ("dp", "wide"), None, None),
        P(None, ("dp", "wide")),
        P(None, ("dp", "wide"), None, None),
        P(None, ("dp", "wide")),
        P(("dp", "wide"), None),
        P(("dp", "wide"), None),
        P(("dp", "wide"), None),
        P(("dp", "wide"), None),
        P(("dp", "wide"), None),
        P(("dp", "wide"), None),
        P(("dp", "wide"), None),
        P(("dp", "wide"), None),
        P(("dp", "wide")),
        P(("dp", "wide")),
        P(("dp", "wide")),
        P(),
    )
    return jax.shard_map(
        local,
        mesh=mesh,
        in_specs=placed,
        out_specs=(
            P(None, ("dp", "wide")),
            P(None, ("dp", "wide"), None, None),
            P(None, ("dp", "wide"), None, None),
            P(("dp", "wide"), None),
            P(("dp", "wide"), None),
            P(("dp", "wide"), None),
            P(("dp", "wide"), None),
            P(("dp", "wide"), None),
            P(("dp", "wide"), None),
            P(("dp", "wide"), None),
            P(("dp", "wide"), None),
            P(("dp", "wide")),
            P(("dp", "wide")),
            P(("dp", "wide")),
            P(),
        ),
        check_vma=False,
    )
```
